32 devices in a mesh: groups: 2 (over x), wide: 16 (over z, y, core).
Axes of the slice: x: 2, y: 2, z: 4, core: 2. Of those that a mesh axis runs over, the one named last changes fastest.
Arguments:
- embeddings: bfloat16 [65536, 1024], P(('groups', 'wide')), parts along dimension 0
- basis: bfloat16 [1024, 256], replicated, may hold values from -0.1875 to 0.1875
- list_owner: int32 [65536], P(('groups', 'wide')), parts along dimension 0, may hold values from 0 to 15, as said below
- list_slot: int32 [65536], P(('groups', 'wide')), parts along dimension 0, may hold values from 0 to 1023
- centroids: bfloat16 [16384, 256], P('wide'), may hold values from -6 to 6
- rotation: bfloat16 [256, 256], replicated, may hold values from -0.375 to 0.375
Outputs:
- encoded: bfloat16 [65536, 256], P(('groups', 'wide')), parts along dimension 0
- covariance: float32 [2048, 1024], P(('groups', 'wide')), parts along dimension 0
The draws below stay inside these ranges and needn't reach their ends.
There are 2 independent parts, one for each index of `groups`. The reference program is written for one: setup_inputs(seed, part) draws one part's arguments, and reference() takes and returns one part's arrays. A program takes and returns all parts, laid end to end along the dimension named above; an argument that names none is the same for every part. Nothing has to cross between parts.
Inputs may be any that keep to these rules, and one draw needn't show every extreme that they name: `list_owner`: among the rows of one device each owner is named at most 128 times; one owner, drawn from the seed, is named exactly 128 times by the rows of every device.
All inputs are finite; a program needn't handle non-finite values.
Results may differ from the reference program's by a relative error of at most 0.0055.
Values may be sent and summed in bfloat16 or wider, within the bound.
No kernel may reach another device: no remote copies, remote signals or barrier semaphores. Data moves between devices by JAX's collectives and lax.ppermute only.
A program may use at most 64 MiB of HBM per device.

```python
import math
import jax
import jax.numpy as jnp
import numpy as np
from jax import lax

D = 1024
R = 256
LISTS_DEV = 1024
ROWS_DEV = 2048
CAP = 128
ROWS = 32768
LISTS = 16384
N_WIDE = 16


def draw_embeddings(key, part):
    key = jax.random.fold_in(key, 1)
    total = ROWS_DEV * N_WIDE
    noise = jax.random.truncated_normal(jax.random.fold_in(key, 0), -6.0, 6.0, (total, D), jnp.float32)
    offset = 0.5 * jax.random.normal(jax.random.fold_in(key, 1), (D,), jnp.float32)
    spread = jax.random.uniform(jax.random.fold_in(key, 2), (total,), jnp.float32, jnp.log(0.3), jnp.log(3.0))
    rise = 1.0 + 2.0 * jnp.arange(total, dtype=jnp.float32) / (total - 1)
    row_scale = jnp.exp(spread) * rise
    return (offset[None, :] + row_scale[:, None] * noise).astype(jnp.bfloat16)


def draw_list_owner(key, part):
    key = jax.random.fold_in(key, 2)
    hot = jax.random.randint(jax.random.fold_in(key, 0), (), 0, N_WIDE)

    def one_sender(sender_key):
        slots = jax.random.permutation(sender_key, (N_WIDE - 1) * CAP)[:ROWS_DEV - CAP]
        other = slots // CAP
        other = other + (other >= hot).astype(other.dtype)
        owners = jnp.concatenate([jnp.full((CAP,), hot, other.dtype), other])
        return jax.random.permutation(jax.random.fold_in(sender_key, 7), owners)
    sender_keys = jax.random.split(jax.random.fold_in(key, 1), N_WIDE)
    return jax.vmap(one_sender)(sender_keys).reshape(-1).astype(jnp.int32)


def touch_ends(entries, stream_key, low, top_value):
    longest = entries.shape.index(max(entries.shape))
    spots = []
    for shift in (0, 1):
        where = [jax.random.randint(jax.random.fold_in(stream_key, axis), (), 0, length) for axis, length in enumerate(entries.shape)]
        where[longest] = (where[longest] + shift) % entries.shape[longest]
        spots.append(tuple(where))
    return entries.at[spots[0]].set(low).at[spots[1]].set(top_value)


def block_levels(key, extent, cuts, smallest, top_value):
    def one(axis_at, shards_of):
        steps = jax.random.uniform(jax.random.fold_in(jax.random.fold_in(key, 6), axis_at), (shards_of,), jnp.float32, smallest / len(cuts), top_value / len(cuts))
        return jnp.repeat(jnp.exp(steps), extent[axis_at] // shards_of).reshape((-1,) + (1,) * (len(extent) - axis_at - 1))

    gain = one(*cuts[0])
    for cut in cuts[1:]:
        gain = gain * one(*cut)
    return gain


def rank_bounds(amount, slope):
    portions = [(1 << 20) // math.isqrt(standing ** slope) + 1 for standing in range(1, amount + 1)]
    scale = 1 + sum(portions) // (1 << 30)
    return np.cumsum(np.array([max(1, weight // scale) for weight in portions]))


def ranked(key, shape, number_of, skew):
    listing = rank_bounds(number_of, skew)
    pick = jax.random.randint(jax.random.fold_in(key, 1), shape, 0, int(listing[number_of - 1]))
    standing = jnp.searchsorted(jnp.asarray(listing, jnp.int32), pick, side="right")
    return jax.random.permutation(jax.random.fold_in(key, 2), number_of)[standing].astype(jnp.int32)


def scatter_about(key, extent, scale, limit, cuts=(), held_as=jnp.bfloat16):
    result = jax.random.normal(key, extent, jnp.float32) * scale
    if len(cuts) > 0:
        result = block_levels(key, extent, cuts, -0.22, 0.18) * result
    return jnp.clip(result, min=-limit, max=limit).astype(held_as)


def setup_inputs(seed: int = 0, part: int = 0) -> dict:
    key_of = jax.random.split(jax.random.key(seed), 7)
    own_keys = jax.random.split(jax.random.fold_in(key_of[6], part), 7)
    return {
        "embeddings": draw_embeddings(jax.random.fold_in(jax.random.fold_in(key_of[6], part), 71), part),
        "basis": scatter_about(key_of[1], (D, R), D ** -0.5, 0.1875),
        "list_owner": draw_list_owner(jax.random.fold_in(jax.random.fold_in(key_of[6], part), 71), part),
        "list_slot": touch_ends(ranked(own_keys[3], (ROWS,), LISTS_DEV, 2), jax.random.fold_in(own_keys[3], 3), 0, LISTS_DEV - 1).astype(jnp.int32),
        "centroids": scatter_about(key_of[4], (LISTS, R), 1.0, 6.0, ((0, 16),)),
        "rotation": scatter_about(key_of[5], (R, R), R ** -0.5, 0.375),
    }


def reference(embeddings, basis, list_owner, list_slot, centroids, rotation):
    total = embeddings.shape[0]
    column_sum = lax.optimization_barrier(jnp.sum(embeddings, 0, dtype=jnp.float32))
    moments = lax.dot_general(embeddings, embeddings, (((0,), (0,)), ((), ())), preferred_element_type=jnp.float32)
    mean = column_sum / total
    covariance = moments / total - mean[:, None] * mean[None, :]
    basis_full = basis.astype(jnp.float32)
    variance = lax.optimization_barrier(jnp.sum(basis_full * jnp.dot(covariance, basis_full, precision=lax.Precision.HIGHEST), 0))
    scale = lax.rsqrt(variance + 1e-05)
    shift = jnp.dot(mean, basis_full, precision=lax.Precision.HIGHEST)
    projected = ((jnp.dot(embeddings, basis, preferred_element_type=jnp.float32) - shift) * scale).astype(jnp.bfloat16)
    sender = jnp.arange(total, dtype=jnp.int32) // ROWS_DEV
    hits = (list_owner[:, None] == jnp.arange(N_WIDE, dtype=jnp.int32)[None, :]).astype(jnp.int32)
    running = jnp.cumsum(hits.reshape(N_WIDE, ROWS_DEV, N_WIDE), axis=1).reshape(total, N_WIDE)
    rank = lax.optimization_barrier(jnp.sum(hits * (running - 1), 1)).astype(jnp.int32)
    position = (list_owner * (N_WIDE * CAP) + sender * CAP + rank).astype(jnp.int32)
    global_list = (list_owner * LISTS_DEV + list_slot).astype(jnp.int32)
    residual = (projected.astype(jnp.float32) - centroids[global_list].astype(jnp.float32)).astype(jnp.bfloat16)
    rotated = jnp.dot(residual, rotation, preferred_element_type=jnp.float32).astype(jnp.bfloat16)
    encoded = jnp.zeros((N_WIDE * N_WIDE * CAP, R), jnp.bfloat16).at[position].set(rotated)
    return (encoded, covariance)
```

```python
import functools

import jax
import jax.numpy as jnp
from jax import lax
from jax.experimental import pallas as pl
from jax.experimental.pallas import tpu as pltpu
from jax.sharding import PartitionSpec as P

CAP = 128
LANES = 128
CHUNK = 256
GROUP = 512
VMEM_LIMIT = 50 * 1024 * 1024


def rows_kernel(width, e_ref, basis_ref, owner_ref, slot_ref, rows_ref, lists_ref, stat_ref, y_ref, yb_ref, sum_ref):
    step = pl.program_id(0)
    rows_here, feats = y_ref.shape
    y = jnp.dot(e_ref[...], basis_ref[...], preferred_element_type=jnp.float32)
    y_ref[pl.ds(pl.multiple_of(step * CHUNK, CHUNK), CHUNK), :] = y
    part = jnp.sum(y.reshape(CHUNK // 8, 8, feats), 0)

    @pl.when(step == 0)
    def _():
        sum_ref[...] = part

    @pl.when(step > 0)
    def _():
        sum_ref[...] += part

    @pl.when(step == pl.num_programs(0) - 1)
    def _():
        mean = jnp.sum(sum_ref[...], 0, keepdims=True) / rows_here
        square = jnp.zeros((8, feats), jnp.float32)
        for c in range(rows_here // CHUNK):
            centred = y_ref[c * CHUNK:(c + 1) * CHUNK, :] - mean
            square = square + jnp.sum((centred * centred).reshape(CHUNK // 8, 8, feats), 0)
            yb_ref[c * CHUNK:(c + 1) * CHUNK, :] = centred.astype(jnp.bfloat16)
        stat_ref[0:1, :] = mean
        stat_ref[1:2, :] = jnp.sum(square, 0, keepdims=True)

        chunks = rows_here // LANES
        owner = owner_ref[...]
        wanted = lax.broadcasted_iota(jnp.int32, (width, LANES), 0)
        hits = [owner[c:c + 1, :] == wanted for c in range(chunks)]
        hits_f = [jnp.where(h, 1.0, 0.0) for h in hits]
        flat = jnp.concatenate(hits_f, 0).astype(jnp.bfloat16)
        up = lax.broadcasted_iota(jnp.int32, (LANES, LANES), 0)
        to = lax.broadcasted_iota(jnp.int32, (LANES, LANES), 1)
        before = jnp.where(up < to, 1.0, 0.0).astype(jnp.bfloat16)
        every = jnp.ones((LANES, LANES), jnp.bfloat16)
        within = jnp.dot(flat, before, preferred_element_type=jnp.float32)
        totals = jnp.dot(flat, every, preferred_element_type=jnp.float32)
        carry = jnp.zeros((width, LANES), jnp.float32)
        ranks = []
        for c in range(chunks):
            at = slice(c * width, (c + 1) * width)
            ranks.append(jnp.sum(hits_f[c] * (within[at] + carry), 0, keepdims=True).astype(jnp.int32))
            carry = carry + totals[at]

        slot = slot_ref[...] + 1
        high, low = (slot >> 5).astype(jnp.float32), (slot & 31).astype(jnp.float32)
        spots = lax.broadcasted_iota(jnp.int32, (CAP, LANES), 0)
        placed = jnp.concatenate([jnp.where(ranks[c] == spots, 1.0, 0.0) for c in range(chunks)], 1).astype(jnp.bfloat16)
        digits = jnp.concatenate(
            [
                jnp.concatenate([hits_f[c] * high[c:c + 1, :] for c in range(chunks)], 1),
                jnp.concatenate([hits_f[c] * low[c:c + 1, :] for c in range(chunks)], 1),
            ],
            0,
        ).astype(jnp.bfloat16)
        found = lax.dot_general(digits, placed, (((1,), (1,)), ((), ())), preferred_element_type=jnp.float32)
        lists_ref[...] = found[:width] * 32.0 + found[width:] - 1.0

        targets = [owner[c:c + 1, :] * CAP + ranks[c] for c in range(chunks)]
        place = lax.broadcasted_iota(jnp.int32, (GROUP, LANES), 0)

        def sort_group(g, _):
            first = pl.multiple_of(g * GROUP, GROUP)
            pick = jnp.concatenate(
                [jnp.where(targets[c] - first == place, 1.0, 0.0).astype(jnp.bfloat16) for c in range(chunks)], 1
            )
            rows_ref[pl.ds(first, GROUP), :] = jnp.dot(
                pick, yb_ref[...], preferred_element_type=jnp.float32
            ).astype(jnp.bfloat16)
            return 0

        lax.fori_loop(0, width * CAP // GROUP, sort_group, 0)


def project_and_sort(width, embeddings, basis, list_owner, list_slot):
    rows_here, wide = embeddings.shape
    feats = basis.shape[1]
    lanes = rows_here // LANES
    slots = width * CAP
    return pl.pallas_call(
        functools.partial(rows_kernel, width),
        grid=(rows_here // CHUNK,),
        in_specs=[
            pl.BlockSpec((CHUNK, wide), lambda i: (i, 0)),
            pl.BlockSpec((wide, feats), lambda i: (0, 0)),
            pl.BlockSpec((lanes, LANES), lambda i: (0, 0)),
            pl.BlockSpec((lanes, LANES), lambda i: (0, 0)),
        ],
        out_specs=[
            pl.BlockSpec((slots, feats), lambda i: (0, 0)),
            pl.BlockSpec((width, CAP), lambda i: (0, 0)),
            pl.BlockSpec((2, feats), lambda i: (0, 0)),
        ],
        out_shape=[
            jax.ShapeDtypeStruct((slots, feats), jnp.bfloat16),
            jax.ShapeDtypeStruct((width, CAP), jnp.float32),
            jax.ShapeDtypeStruct((2, feats), jnp.float32),
        ],
        scratch_shapes=[
            pltpu.VMEM((rows_here, feats), jnp.float32),
            pltpu.VMEM((rows_here, feats), jnp.bfloat16),
            pltpu.VMEM((8, feats), jnp.float32),
        ],
        compiler_params=pltpu.CompilerParams(vmem_limit_bytes=VMEM_LIMIT),
        cost_estimate=pl.CostEstimate(
            flops=2 * rows_here * feats * (wide + slots), bytes_accessed=2 * rows_here * wide + 2 * slots * feats, transcendentals=0
        ),
        name="project_sort",
    )(embeddings, basis, list_owner.reshape(lanes, LANES), list_slot.reshape(lanes, LANES))


def moments_kernel(width, me_ref, e_ref, keep_ref, send_ref, mean_ref, m_ref):
    rows_here, wide = e_ref.shape
    block = wide // width
    bits = width.bit_length() - 1
    me = me_ref[0]
    total = jnp.zeros((8, wide), jnp.float32)
    for c in range(rows_here // CHUNK):
        rows = e_ref[c * CHUNK:(c + 1) * CHUNK, :].astype(jnp.float32)
        total = total + jnp.sum(rows.reshape(CHUNK // 8, 8, wide), 0)
    mean = jnp.sum(total, 0, keepdims=True) / rows_here
    mean_ref[...] = mean
    for t in range(wide // CHUNK):
        at = slice(t * CHUNK, (t + 1) * CHUNK)
        product = lax.dot_general(
            e_ref[:, at], e_ref[...], (((0,), (0,)), ((), ())), preferred_element_type=jnp.float32
        )
        down = jnp.transpose(jnp.broadcast_to(mean[:, at] * rows_here, (LANES, CHUNK)))
        for j in range(wide // LANES):
            across = slice(j * LANES, (j + 1) * LANES)
            m_ref[:, across] = product[:, across] - down * mean[:, across]
        for b in range(CHUNK // block):
            apart = (t * (CHUNK // block) + b) ^ me
            place = 0
            for k in range(1, bits):
                place = place + (((apart >> k) & 1) << (bits - 1 - k))
            first = pl.multiple_of(place * block, block)

            @pl.when((apart & 1) == 0)
            def _():
                keep_ref[pl.ds(first, block), :] = m_ref[b * block:(b + 1) * block, :]

            @pl.when((apart & 1) == 1)
            def _():
                send_ref[pl.ds(first, block), :] = m_ref[b * block:(b + 1) * block, :].astype(jnp.bfloat16)


def moments(width, me, embeddings):
    rows_here, wide = embeddings.shape
    return pl.pallas_call(
        functools.partial(moments_kernel, width),
        in_specs=[
            pl.BlockSpec(memory_space=pltpu.SMEM),
            pl.BlockSpec(memory_space=pltpu.VMEM),
        ],
        out_specs=[pl.BlockSpec(memory_space=pltpu.VMEM)] * 3,
        out_shape=[
            jax.ShapeDtypeStruct((wide // 2, wide), jnp.float32),
            jax.ShapeDtypeStruct((wide // 2, wide), jnp.bfloat16),
            jax.ShapeDtypeStruct((1, wide), jnp.float32),
        ],
        scratch_shapes=[pltpu.VMEM((CHUNK, wide), jnp.float32)],
        compiler_params=pltpu.CompilerParams(vmem_limit_bytes=VMEM_LIMIT),
        cost_estimate=pl.CostEstimate(
            flops=2 * rows_here * wide * wide, bytes_accessed=2 * rows_here * wide + 3 * wide * wide, transcendentals=0
        ),
        name="moments",
    )(me.reshape(1), embeddings)


def encode_kernel(total, rows_ref, lists_ref, stat_ref, centroid_ref, rotation_ref, out_ref, delta_ref, scale_ref):
    step = pl.program_id(0)
    width = lists_ref.shape[0]
    feats = out_ref.shape[1]
    owned = centroid_ref.shape[0]
    share = total // width

    @pl.when(step == 0)
    def _():
        means, squares = stat_ref[:, :feats], stat_ref[:, feats:]
        shift = jnp.sum(means, 0, keepdims=True) / width
        delta = means - shift
        variance = jnp.sum(squares + share * (delta * delta), 0, keepdims=True) / total
        scale_ref[...] = lax.rsqrt(variance + 1e-05)
        delta_ref[...] = delta

    senders = rows_ref.shape[0] // CAP
    first = step * senders
    columns = jnp.transpose(lists_ref[pl.ds(first, senders), :])
    names = lax.broadcasted_iota(jnp.int32, (CAP, owned), 1).astype(jnp.float32)
    for s in range(senders):
        at = slice(s * CAP, (s + 1) * CAP)
        listed = columns[:, s:s + 1]
        onehot = jnp.where(listed == names, 1.0, 0.0).astype(jnp.bfloat16)
        centre = jnp.dot(onehot, centroid_ref[...], preferred_element_type=jnp.float32)
        projected = (rows_ref[at, :].astype(jnp.float32) + delta_ref[pl.ds(first + s, 1), :]) * scale_ref[...]
        residual = jnp.where(listed >= 0, projected - centre, 0.0).astype(jnp.bfloat16)
        out_ref[at, :] = jnp.dot(residual, rotation_ref[...], preferred_element_type=jnp.float32).astype(jnp.bfloat16)


def encode(total, rows, lists, stats, centroids, rotation):
    slots, feats = rows.shape
    width = lists.shape[0]
    owned = centroids.shape[0]
    size = 8 * CAP
    whole = lambda i: (0, 0)
    return pl.pallas_call(
        functools.partial(encode_kernel, total),
        grid=(slots // size,),
        in_specs=[
            pl.BlockSpec((size, feats), lambda i: (i, 0)),
            pl.BlockSpec((width, CAP), whole),
            pl.BlockSpec((width, 2 * feats), whole),
            pl.BlockSpec((owned, feats), whole),
            pl.BlockSpec((feats, feats), whole),
        ],
        out_specs=pl.BlockSpec((size, feats), lambda i: (i, 0)),
        out_shape=jax.ShapeDtypeStruct((slots, feats), jnp.bfloat16),
        scratch_shapes=[pltpu.VMEM((width, feats), jnp.float32), pltpu.VMEM((1, feats), jnp.float32)],
        compiler_params=pltpu.CompilerParams(vmem_limit_bytes=VMEM_LIMIT),
        cost_estimate=pl.CostEstimate(
            flops=2 * slots * feats * (owned + feats), bytes_accessed=4 * slots * feats, transcendentals=0
        ),
        name="encode",
    )(rows, lists, stats, centroids, rotation)


def local(embeddings, basis, list_owner, list_slot, centroids, rotation):
    width = lax.axis_size("wide")
    me = lax.axis_index("wide")
    rows_here, wide = embeddings.shape
    feats = basis.shape[1]
    total = rows_here * width
    block = wide // width

    rows, lists, stats = project_and_sort(width, embeddings, basis, list_owner, list_slot)
    got = lax.all_to_all(rows.reshape(width, CAP, feats), "wide", split_axis=0, concat_axis=0, tiled=True)

    keep, send, mean = moments(width, me, embeddings)
    notes = jnp.concatenate(
        [lists, jnp.broadcast_to(stats.reshape(1, -1), (width, 2 * feats)), jnp.broadcast_to(mean, (width, wide))], 1
    )
    notes = lax.all_to_all(notes[:, None, :], "wide", split_axis=0, concat_axis=0, tiled=True)[:, 0, :]
    got_lists, got_stats, got_means = notes[:, :CAP], notes[:, CAP:CAP + 2 * feats], notes[:, CAP + 2 * feats:]

    step = 1
    while step < width:
        came = lax.ppermute(send, "wide", [(i, i ^ step) for i in range(width)])
        held = keep + came.astype(jnp.float32)
        half = held.shape[0] // 2
        keep, send = held[:half], held[half:].astype(jnp.bfloat16)
        step *= 2
    apart = got_means - jnp.mean(got_means, 0, keepdims=True)
    apart_here = lax.dynamic_slice_in_dim(apart, me * block, block, 1)
    between = lax.dot_general(
        apart_here, apart, (((0,), (0,)), ((), ())), precision=lax.Precision.HIGHEST, preferred_element_type=jnp.float32
    )
    covariance = (held + rows_here * between) / total

    encoded = encode(total, got.reshape(width * CAP, feats), got_lists, got_stats, centroids, rotation)
    return (encoded, covariance)


def solution(mesh):
    in_specs = (
        P(("groups", "wide"), None),
        P(),
        P(("groups", "wide")),
        P(("groups", "wide")),
        P("wide", None),
        P(),
    )
    out_specs = (P(("groups", "wide"), None), P(("groups", "wide"), None))
    return jax.shard_map(local, mesh=mesh, in_specs=in_specs, out_specs=out_specs, check_vma=False)
```

```python
import functools

import jax
import jax.numpy as jnp
from jax import lax
from jax.experimental import pallas as pl
from jax.experimental.pallas import tpu as pltpu
from jax.sharding import PartitionSpec as P

CAP = 128
LANES = 128
NOTES = 16
SPAN = CAP + NOTES
CHUNK = 512
TILE = 256
GROUP = 4
VMEM_LIMIT = 40 * 1024 * 1024


def in_three(x):
    high = x.astype(jnp.bfloat16).astype(jnp.float32)
    rest = x - high
    middle = rest.astype(jnp.bfloat16).astype(jnp.float32)
    return high, middle, (rest - middle).astype(jnp.bfloat16).astype(jnp.float32)


def rows_kernel(width, e_ref, basis_ref, owner_ref, slot_ref, rows_ref, mean_ref, y_ref, yb_ref, sum_ref, total_ref, target_ref, list_ref):
    step = pl.program_id(0)
    rows_here, feats = y_ref.shape
    wide = e_ref.shape[1]
    chunks = rows_here // LANES

    @pl.when(step == 0)
    def _():
        sum_ref[...] = jnp.zeros_like(sum_ref)
        total_ref[...] = jnp.zeros_like(total_ref)
        owner = owner_ref[...]
        wanted = lax.broadcasted_iota(jnp.int32, (width, LANES), 0)
        hits = [jnp.where(owner[c:c + 1, :] == wanted, 1.0, 0.0) for c in range(chunks)]
        flat = jnp.concatenate(hits, 0).astype(jnp.bfloat16)
        up = lax.broadcasted_iota(jnp.int32, (LANES, LANES), 0)
        to = lax.broadcasted_iota(jnp.int32, (LANES, LANES), 1)
        before = jnp.where(up < to, 1.0, 0.0).astype(jnp.bfloat16)
        every = jnp.ones((LANES, LANES), jnp.bfloat16)
        within = jnp.dot(flat, before, preferred_element_type=jnp.float32)
        counts = jnp.dot(flat, every, preferred_element_type=jnp.float32)
        carry = jnp.zeros((width, LANES), jnp.float32)
        ranks = []
        for c in range(chunks):
            at = slice(c * width, (c + 1) * width)
            ranks.append(jnp.sum(hits[c] * (within[at] + carry), 0, keepdims=True).astype(jnp.int32))
            carry = carry + counts[at]
            target_ref[c:c + 1, :] = owner[c:c + 1, :] * CAP + ranks[c]

        slot = slot_ref[...] + 1
        high, low = (slot >> 5).astype(jnp.float32), (slot & 31).astype(jnp.float32)
        spots = lax.broadcasted_iota(jnp.int32, (CAP, LANES), 0)
        placed = jnp.concatenate([jnp.where(ranks[c] == spots, 1.0, 0.0) for c in range(chunks)], 1).astype(jnp.bfloat16)
        digits = jnp.concatenate(
            [
                jnp.concatenate([hits[c] * high[c:c + 1, :] for c in range(chunks)], 1),
                jnp.concatenate([hits[c] * low[c:c + 1, :] for c in range(chunks)], 1),
            ],
            0,
        ).astype(jnp.bfloat16)
        found = lax.dot_general(digits, placed, (((1,), (1,)), ((), ())), preferred_element_type=jnp.float32)
        list_ref[:, :CAP] = found[:width]
        list_ref[:, CAP:] = found[width:]

    y = jnp.dot(e_ref[...], basis_ref[...], preferred_element_type=jnp.float32)
    y_ref[pl.ds(pl.multiple_of(step * CHUNK, CHUNK), CHUNK), :] = y
    sum_ref[...] += jnp.sum(y.reshape(CHUNK // 8, 8, feats), 0)
    total_ref[...] += jnp.sum(e_ref[...].astype(jnp.float32).reshape(CHUNK // 8, 8, wide), 0)

    @pl.when(step == pl.num_programs(0) - 1)
    def _():
        mean_y = jnp.sum(sum_ref[...], 0, keepdims=True) / rows_here
        square = jnp.zeros((8, feats), jnp.float32)
        for c in range(rows_here // CHUNK):
            at = slice(c * CHUNK, (c + 1) * CHUNK)
            centred = y_ref[at, :] - mean_y
            square = square + jnp.sum((centred * centred).reshape(CHUNK // 8, 8, feats), 0)
            yb_ref[at, :] = centred.astype(jnp.bfloat16)
        mean = jnp.sum(total_ref[...], 0, keepdims=True) / rows_here
        mean_ref[...] = mean
        parts = in_three(mean)
        common = [part[:, q * feats:(q + 1) * feats] for part in parts for q in range(wide // feats)]
        common = jnp.concatenate(common + list(in_three(jnp.sum(square, 0, keepdims=True))), 0)

        place = lax.broadcasted_iota(jnp.int32, (GROUP * CAP, LANES), 0).astype(jnp.int16)

        def sort_group(g, _):
            first = g * GROUP
            pieces = []
            for c in range(chunks):
                wanted = (target_ref[c:c + 1, :] - first * CAP).astype(jnp.int32)
                wanted = jnp.broadcast_to(wanted, (16, LANES)).astype(jnp.int16)
                wanted = jnp.concatenate([wanted] * (GROUP * CAP // 16), 0)
                pieces.append(jnp.where(wanted == place, jnp.ones((), jnp.bfloat16), jnp.zeros((), jnp.bfloat16)))
            pick = jnp.concatenate(pieces, 1)
            rows = jnp.dot(pick, yb_ref[...], preferred_element_type=jnp.float32).astype(jnp.bfloat16)
            for j in range(GROUP):
                base = pl.multiple_of((first + j) * SPAN, 16)
                rows_ref[pl.ds(base, CAP), :] = rows[j * CAP:(j + 1) * CAP]
                notes = jnp.concatenate([common, list_ref[pl.ds(first + j, 1), :]], 0)
                rows_ref[pl.ds(pl.multiple_of(base + CAP, 16), NOTES), :] = notes.astype(jnp.bfloat16)
            return 0

        groups = width // GROUP
        if groups <= 4:
            for g in range(groups):
                sort_group(g, 0)
        else:
            lax.fori_loop(0, groups, sort_group, 0)


def project_and_sort(width, embeddings, basis, list_owner, list_slot):
    rows_here, wide = embeddings.shape
    feats = basis.shape[1]
    lanes = rows_here // LANES
    slots = width * SPAN
    return pl.pallas_call(
        functools.partial(rows_kernel, width),
        grid=(rows_here // CHUNK,),
        in_specs=[
            pl.BlockSpec((CHUNK, wide), lambda i: (i, 0)),
            pl.BlockSpec((wide, feats), lambda i: (0, 0)),
            pl.BlockSpec((lanes, LANES), lambda i: (0, 0)),
            pl.BlockSpec((lanes, LANES), lambda i: (0, 0)),
        ],
        out_specs=[
            pl.BlockSpec((slots, feats), lambda i: (0, 0)),
            pl.BlockSpec((1, wide), lambda i: (0, 0)),
        ],
        out_shape=[
            jax.ShapeDtypeStruct((slots, feats), jnp.bfloat16),
            jax.ShapeDtypeStruct((1, wide), jnp.float32),
        ],
        scratch_shapes=[
            pltpu.VMEM((rows_here, feats), jnp.float32),
            pltpu.VMEM((rows_here, feats), jnp.bfloat16),
            pltpu.VMEM((8, feats), jnp.float32),
            pltpu.VMEM((8, wide), jnp.float32),
            pltpu.VMEM((lanes, LANES), jnp.int32),
            pltpu.VMEM((width, 2 * CAP), jnp.float32),
        ],
        compiler_params=pltpu.CompilerParams(vmem_limit_bytes=VMEM_LIMIT),
        cost_estimate=pl.CostEstimate(
            flops=2 * rows_here * feats * (wide + slots), bytes_accessed=2 * rows_here * wide + 2 * slots * feats, transcendentals=0
        ),
        name="project_sort",
    )(embeddings, basis, list_owner.reshape(lanes, LANES), list_slot.reshape(lanes, LANES))


def moments_kernel(width, me_ref, e_ref, mean_ref, keep_ref, send_ref, m_ref):
    step = pl.program_id(0)
    wide = e_ref.shape[1]
    rows_here = e_ref.shape[0] * pl.num_programs(0)
    block = wide // width
    bits = width.bit_length() - 1
    tiles = wide // TILE

    for t in range(tiles):
        rows, columns = slice(t * TILE, (t + 1) * TILE), slice(t * TILE, wide)
        product = lax.dot_general(
            e_ref[:, rows], e_ref[:, columns], (((0,), (0,)), ((), ())), preferred_element_type=jnp.float32
        )

        @pl.when(step == 0)
        def _():
            m_ref[rows, columns] = product

        @pl.when(step > 0)
        def _():
            m_ref[rows, columns] += product

    @pl.when(step == pl.num_programs(0) - 1)
    def _():
        me = me_ref[0]
        mean = mean_ref[...]
        for t in range(tiles):
            rows = slice(t * TILE, (t + 1) * TILE)
            for u in range(t):
                columns = slice(u * TILE, (u + 1) * TILE)
                m_ref[rows, columns] = jnp.transpose(m_ref[columns, rows])
            down = jnp.transpose(jnp.broadcast_to(mean[:, rows] * rows_here, (LANES, TILE)))
            for b in range(TILE // block):
                part = slice(b * block, (b + 1) * block)
                here = slice(t * TILE + b * block, t * TILE + (b + 1) * block)
                apart = (t * (TILE // block) + b) ^ me
                place = 0
                for k in range(1, bits):
                    place = place + (((apart >> k) & 1) << (bits - 1 - k))
                first = pl.multiple_of(place * block, block)
                centred = [
                    m_ref[here, j * LANES:(j + 1) * LANES] - down[part] * mean[:, j * LANES:(j + 1) * LANES]
                    for j in range(wide // LANES)
                ]
                centred = jnp.concatenate(centred, 1)

                @pl.when((apart & 1) == 0)
                def _():
                    keep_ref[pl.ds(first, block), :] = centred

                @pl.when((apart & 1) == 1)
                def _():
                    send_ref[pl.ds(first, block), :] = centred.astype(jnp.bfloat16)


def moments(width, me, embeddings, mean):
    rows_here, wide = embeddings.shape
    return pl.pallas_call(
        functools.partial(moments_kernel, width),
        grid=(rows_here // CHUNK,),
        in_specs=[
            pl.BlockSpec(memory_space=pltpu.SMEM),
            pl.BlockSpec((CHUNK, wide), lambda i: (i, 0)),
            pl.BlockSpec((1, wide), lambda i: (0, 0)),
        ],
        out_specs=[pl.BlockSpec((wide // 2, wide), lambda i: (0, 0))] * 2,
        out_shape=[
            jax.ShapeDtypeStruct((wide // 2, wide), jnp.float32),
            jax.ShapeDtypeStruct((wide // 2, wide), jnp.bfloat16),
        ],
        scratch_shapes=[pltpu.VMEM((wide, wide), jnp.float32)],
        compiler_params=pltpu.CompilerParams(vmem_limit_bytes=VMEM_LIMIT),
        cost_estimate=pl.CostEstimate(
            flops=2 * rows_here * wide * wide, bytes_accessed=2 * rows_here * wide + 3 * wide * wide, transcendentals=0
        ),
        name="moments",
    )(me.reshape(1), embeddings, mean)


def halve_kernel(keep_ref, came_ref, held_ref, send_ref):
    half = held_ref.shape[0]
    held_ref[...] = keep_ref[:half] + came_ref[:half].astype(jnp.float32)
    send_ref[...] = (keep_ref[half:] + came_ref[half:].astype(jnp.float32)).astype(jnp.bfloat16)


def halve(keep, came):
    rows, wide = keep.shape
    return pl.pallas_call(
        halve_kernel,
        in_specs=[pl.BlockSpec(memory_space=pltpu.VMEM)] * 2,
        out_specs=[pl.BlockSpec(memory_space=pltpu.VMEM)] * 2,
        out_shape=[
            jax.ShapeDtypeStruct((rows // 2, wide), jnp.float32),
            jax.ShapeDtypeStruct((rows // 2, wide), jnp.bfloat16),
        ],
        compiler_params=pltpu.CompilerParams(vmem_limit_bytes=VMEM_LIMIT),
        cost_estimate=pl.CostEstimate(flops=rows * wide, bytes_accessed=9 * rows * wide, transcendentals=0),
        name="halve",
    )(keep, came)


def encode_kernel(total, me_ref, got_ref, all_ref, basis_ref, centroid_ref, rotation_ref, out_ref, between_ref, delta_ref, scale_ref, list_ref, apart_ref):
    step = pl.program_id(0)
    width = delta_ref.shape[0]
    feats = out_ref.shape[1]
    owned = centroid_ref.shape[0]
    wide = basis_ref.shape[0]
    block = wide // width
    share = total // width

    @pl.when(step == 0)
    def _():
        notes = jnp.concatenate([all_ref[s * SPAN + CAP:(s + 1) * SPAN, :] for s in range(width)], 0)
        size = width * NOTES
        to = lax.broadcasted_iota(jnp.int32, (size, size), 0)
        of = lax.broadcasted_iota(jnp.int32, (size, size), 1)
        turn = jnp.where((to % width) * NOTES + to // width == of, 1.0, 0.0).astype(jnp.bfloat16)
        turned = jnp.dot(turn, notes, preferred_element_type=jnp.float32)
        row = [turned[r * width:(r + 1) * width] for r in range(NOTES)]
        quarters = wide // feats
        shifts = jnp.zeros((width, feats), jnp.float32)
        for q in range(quarters):
            parts = [row[p * quarters + q] for p in range(3)]
            mean = parts[0] + (parts[1] + parts[2])
            apart_ref[:, q * feats:(q + 1) * feats] = mean - jnp.mean(mean, 0, keepdims=True)
            terms = jnp.dot(
                jnp.concatenate(parts, 0).astype(jnp.bfloat16),
                basis_ref[q * feats:(q + 1) * feats, :],
                preferred_element_type=jnp.float32,
            )
            shifts = shifts + (terms[:width] + (terms[width:2 * width] + terms[2 * width:]))
        square = row[3 * quarters] + (row[3 * quarters + 1] + row[3 * quarters + 2])
        delta = shifts - jnp.mean(shifts, 0, keepdims=True)
        variance = jnp.sum(square + share * (delta * delta), 0, keepdims=True) / total
        scale_ref[...] = lax.rsqrt(variance + 1e-05)
        delta_ref[...] = delta
        digits = row[NOTES - 1]
        list_ref[...] = digits[:, :CAP] * 32.0 + digits[:, CAP:] - 1.0

        me = me_ref[0]
        first = me * block
        near = apart_ref[:, pl.ds(pl.multiple_of(first // LANES * LANES, LANES), LANES)]
        near = pltpu.roll(near, (LANES - first % LANES) % LANES, 1)[:, :block]
        between_ref[...] = share * lax.dot_general(
            near,
            apart_ref[...],
            (((0,), (0,)), ((), ())),
            precision=lax.Precision.HIGHEST,
            preferred_element_type=jnp.float32,
        )

    columns = jnp.transpose(list_ref[pl.ds(step * GROUP, GROUP), :])
    names = lax.broadcasted_iota(jnp.int32, (CAP, owned), 1).astype(jnp.int16)
    hits, projected, held = [], [], []
    for s in range(GROUP):
        listed = jnp.broadcast_to(columns[:, s:s + 1], (CAP, LANES))
        held.append(jnp.concatenate([listed] * (feats // LANES), 1) >= 0)
        wanted = jnp.concatenate([listed.astype(jnp.int32).astype(jnp.int16)] * (owned // LANES), 1)
        hits.append(jnp.where(wanted == names, jnp.ones((), jnp.bfloat16), jnp.zeros((), jnp.bfloat16)))
        rows = got_ref[s * SPAN:s * SPAN + CAP, :].astype(jnp.float32)
        projected.append((rows + delta_ref[pl.ds(step * GROUP + s, 1), :]) * scale_ref[...])
    centre = jnp.dot(jnp.concatenate(hits, 0), centroid_ref[...], preferred_element_type=jnp.float32)
    residual = jnp.where(jnp.concatenate(held, 0), jnp.concatenate(projected, 0) - centre, 0.0)
    out_ref[...] = jnp.dot(
        residual.astype(jnp.bfloat16), rotation_ref[...], preferred_element_type=jnp.float32
    ).astype(jnp.bfloat16)


def encode(width, total, me, got, basis, centroids, rotation):
    wide, feats = basis.shape
    owned = centroids.shape[0]
    slots = width * CAP
    whole = lambda i: (0, 0)
    return pl.pallas_call(
        functools.partial(encode_kernel, total),
        grid=(width // GROUP,),
        in_specs=[
            pl.BlockSpec(memory_space=pltpu.SMEM),
            pl.BlockSpec((GROUP * SPAN, feats), lambda i: (i, 0)),
            pl.BlockSpec((width * SPAN, feats), whole),
            pl.BlockSpec((wide, feats), whole),
            pl.BlockSpec((owned, feats), whole),
            pl.BlockSpec((feats, feats), whole),
        ],
        out_specs=[
            pl.BlockSpec((GROUP * CAP, feats), lambda i: (i, 0)),
            pl.BlockSpec((wide // width, wide), whole),
        ],
        out_shape=[
            jax.ShapeDtypeStruct((slots, feats), jnp.bfloat16),
            jax.ShapeDtypeStruct((wide // width, wide), jnp.float32),
        ],
        scratch_shapes=[
            pltpu.VMEM((width, feats), jnp.float32),
            pltpu.VMEM((1, feats), jnp.float32),
            pltpu.VMEM((width, CAP), jnp.float32),
            pltpu.VMEM((width, wide), jnp.float32),
        ],
        compiler_params=pltpu.CompilerParams(vmem_limit_bytes=VMEM_LIMIT),
        cost_estimate=pl.CostEstimate(
            flops=2 * slots * feats * (owned + feats), bytes_accessed=4 * slots * feats, transcendentals=0
        ),
        name="encode",
    )(me.reshape(1), got, got, basis, centroids, rotation)


def local(embeddings, basis, list_owner, list_slot, centroids, rotation):
    width = lax.axis_size("wide")
    me = lax.axis_index("wide")
    rows_here, wide = embeddings.shape
    feats = basis.shape[1]
    total = rows_here * width

    rows, mean = project_and_sort(width, embeddings, basis, list_owner, list_slot)
    got = lax.all_to_all(rows.reshape(width, SPAN, feats), "wide", split_axis=0, concat_axis=0, tiled=True)

    keep, send = moments(width, me, embeddings, mean)
    step = 1
    while step < width:
        came = lax.ppermute(send, "wide", [(i, i ^ step) for i in range(width)])
        step *= 2
        if step < width:
            keep, send = halve(keep, came)
    encoded, between = encode(width, total, me, got.reshape(width * SPAN, feats), basis, centroids, rotation)
    covariance = (keep + came.astype(jnp.float32) + between) / total
    return (encoded, covariance)


def solution(mesh):
    in_specs = (
        P(("groups", "wide"), None),
        P(),
        P(("groups", "wide")),
        P(("groups", "wide")),
        P("wide", None),
        P(),
    )
    out_specs = (P(("groups", "wide"), None), P(("groups", "wide"), None))
    return jax.shard_map(local, mesh=mesh, in_specs=in_specs, out_specs=out_specs, check_vma=False)
```

```python
import functools

import jax
import jax.numpy as jnp
from jax import lax
from jax.experimental import pallas as pl
from jax.experimental.pallas import tpu as pltpu
from jax.sharding import PartitionSpec as P

CAP = 128
LANES = 128
NOTES = 16
SPAN = CAP + NOTES
CHUNK = 512
TILE = 256
GROUP = 4
VMEM_ALL = 60 * 1024 * 1024
VMEM_SOME = 24 * 1024 * 1024
VMEM_MOST = 48 * 1024 * 1024


def in_three(x):
    high = x.astype(jnp.bfloat16).astype(jnp.float32)
    rest = x - high
    middle = rest.astype(jnp.bfloat16).astype(jnp.float32)
    return high, middle, (rest - middle).astype(jnp.bfloat16).astype(jnp.float32)


def rows_kernel(width, e_ref, basis_ref, owner_ref, slot_ref, rows_ref, mean_ref, y_ref, yb_ref, sum_ref, total_ref, target_ref, list_ref):
    step = pl.program_id(0)
    rows_here, feats = y_ref.shape
    wide = e_ref.shape[1]
    chunks = rows_here // LANES

    @pl.when(step == 0)
    def _():
        sum_ref[...] = jnp.zeros_like(sum_ref)
        total_ref[...] = jnp.zeros_like(total_ref)
        owner = owner_ref[...]
        wanted = lax.broadcasted_iota(jnp.int32, (width, LANES), 0)
        hits = [jnp.where(owner[c:c + 1, :] == wanted, 1.0, 0.0) for c in range(chunks)]
        flat = jnp.concatenate(hits, 0).astype(jnp.bfloat16)
        up = lax.broadcasted_iota(jnp.int32, (LANES, LANES), 0)
        to = lax.broadcasted_iota(jnp.int32, (LANES, LANES), 1)
        before = jnp.where(up < to, 1.0, 0.0).astype(jnp.bfloat16)
        every = jnp.ones((LANES, LANES), jnp.bfloat16)
        within = jnp.dot(flat, before, preferred_element_type=jnp.float32)
        counts = jnp.dot(flat, every, preferred_element_type=jnp.float32)
        carry = jnp.zeros((width, LANES), jnp.float32)
        ranks = []
        for c in range(chunks):
            at = slice(c * width, (c + 1) * width)
            ranks.append(jnp.sum(hits[c] * (within[at] + carry), 0, keepdims=True).astype(jnp.int32))
            carry = carry + counts[at]
            target_ref[c:c + 1, :] = owner[c:c + 1, :] * CAP + ranks[c]

        slot = slot_ref[...] + 1
        high, low = (slot >> 5).astype(jnp.float32), (slot & 31).astype(jnp.float32)
        spots = lax.broadcasted_iota(jnp.int32, (CAP, LANES), 0)
        placed = jnp.concatenate([jnp.where(ranks[c] == spots, 1.0, 0.0) for c in range(chunks)], 1).astype(jnp.bfloat16)
        digits = jnp.concatenate(
            [
                jnp.concatenate([hits[c] * high[c:c + 1, :] for c in range(chunks)], 1),
                jnp.concatenate([hits[c] * low[c:c + 1, :] for c in range(chunks)], 1),
            ],
            0,
        ).astype(jnp.bfloat16)
        found = lax.dot_general(digits, placed, (((1,), (1,)), ((), ())), preferred_element_type=jnp.float32)
        list_ref[:, :CAP] = found[:width]
        list_ref[:, CAP:] = found[width:]

    y = jnp.dot(e_ref[...], basis_ref[...], preferred_element_type=jnp.float32)
    y_ref[pl.ds(pl.multiple_of(step * CHUNK, CHUNK), CHUNK), :] = y
    sum_ref[...] += jnp.sum(y.reshape(CHUNK // 8, 8, feats), 0)
    total_ref[...] += jnp.sum(e_ref[...].astype(jnp.float32).reshape(CHUNK // 8, 8, wide), 0)

    @pl.when(step == pl.num_programs(0) - 1)
    def _():
        mean_y = jnp.sum(sum_ref[...], 0, keepdims=True) / rows_here
        square = jnp.zeros((8, feats), jnp.float32)
        for c in range(rows_here // CHUNK):
            at = slice(c * CHUNK, (c + 1) * CHUNK)
            centred = y_ref[at, :] - mean_y
            square = square + jnp.sum((centred * centred).reshape(CHUNK // 8, 8, feats), 0)
            yb_ref[at, :] = centred.astype(jnp.bfloat16)
        mean = jnp.sum(total_ref[...], 0, keepdims=True) / rows_here
        mean_ref[...] = mean
        parts = in_three(mean)
        common = [part[:, q * feats:(q + 1) * feats] for part in parts for q in range(wide // feats)]
        common = jnp.concatenate(common + list(in_three(jnp.sum(square, 0, keepdims=True))), 0)

        place = lax.broadcasted_iota(jnp.int32, (GROUP * CAP, LANES), 0).astype(jnp.int16)

        def sort_group(g, _):
            first = g * GROUP
            pieces = []
            for c in range(chunks):
                wanted = (target_ref[c:c + 1, :] - first * CAP).astype(jnp.int32)
                wanted = jnp.broadcast_to(wanted, (16, LANES)).astype(jnp.int16)
                wanted = jnp.concatenate([wanted] * (GROUP * CAP // 16), 0)
                pieces.append(jnp.where(wanted == place, jnp.ones((), jnp.bfloat16), jnp.zeros((), jnp.bfloat16)))
            pick = jnp.concatenate(pieces, 1)
            rows = jnp.dot(pick, yb_ref[...], preferred_element_type=jnp.float32).astype(jnp.bfloat16)
            for j in range(GROUP):
                base = pl.multiple_of((first + j) * SPAN, 16)
                rows_ref[pl.ds(base, CAP), :] = rows[j * CAP:(j + 1) * CAP]
                notes = jnp.concatenate([common, list_ref[pl.ds(first + j, 1), :]], 0)
                rows_ref[pl.ds(pl.multiple_of(base + CAP, 16), NOTES), :] = notes.astype(jnp.bfloat16)
            return 0

        groups = width // GROUP
        if groups <= 4:
            for g in range(groups):
                sort_group(g, 0)
        else:
            lax.fori_loop(0, groups, sort_group, 0)


def project_and_sort(width, embeddings, basis, list_owner, list_slot):
    rows_here, wide = embeddings.shape
    feats = basis.shape[1]
    lanes = rows_here // LANES
    slots = width * SPAN
    return pl.pallas_call(
        functools.partial(rows_kernel, width),
        grid=(rows_here // CHUNK,),
        in_specs=[
            pl.BlockSpec((CHUNK, wide), lambda i: (i, 0)),
            pl.BlockSpec((wide, feats), lambda i: (0, 0)),
            pl.BlockSpec((lanes, LANES), lambda i: (0, 0)),
            pl.BlockSpec((lanes, LANES), lambda i: (0, 0)),
        ],
        out_specs=[
            pl.BlockSpec((slots, feats), lambda i: (0, 0)),
            pl.BlockSpec((1, wide), lambda i: (0, 0)),
        ],
        out_shape=[
            jax.ShapeDtypeStruct((slots, feats), jnp.bfloat16),
            jax.ShapeDtypeStruct((1, wide), jnp.float32),
        ],
        scratch_shapes=[
            pltpu.VMEM((rows_here, feats), jnp.float32),
            pltpu.VMEM((rows_here, feats), jnp.bfloat16),
            pltpu.VMEM((8, feats), jnp.float32),
            pltpu.VMEM((8, wide), jnp.float32),
            pltpu.VMEM((lanes, LANES), jnp.int32),
            pltpu.VMEM((width, 2 * CAP), jnp.float32),
        ],
        compiler_params=pltpu.CompilerParams(vmem_limit_bytes=VMEM_ALL),
        cost_estimate=pl.CostEstimate(
            flops=2 * rows_here * feats * (wide + slots), bytes_accessed=2 * rows_here * wide + 2 * slots * feats, transcendentals=0
        ),
        name="project_sort",
    )(embeddings, basis, list_owner.reshape(lanes, LANES), list_slot.reshape(lanes, LANES))


def moments_kernel(width, me_ref, mean_hbm, e_hbm, keep_ref, send_ref, e_ref, mean_ref, m_ref, sem, mean_sem):
    rows_here, wide = e_ref.shape
    block = wide // width
    bits = width.bit_length() - 1
    mean_copy = pltpu.make_async_copy(mean_hbm, mean_ref, mean_sem)
    mean_copy.start()
    copies = []
    for c in range(rows_here // CHUNK):
        at = pl.ds(c * CHUNK, CHUNK)
        copies.append(pltpu.make_async_copy(e_hbm.at[at], e_ref.at[at], sem.at[c]))
        copies[c].start()
    me = me_ref[0]
    mean_copy.wait()
    mean = mean_ref[...]
    for t in range(wide // TILE):
        rows = slice(t * TILE, (t + 1) * TILE)
        if t == 0:
            product = jnp.zeros((TILE, wide), jnp.float32)
            for c in range(rows_here // CHUNK):
                copies[c].wait()
                at = slice(c * CHUNK, (c + 1) * CHUNK)
                product = product + lax.dot_general(
                    e_ref[at, rows], e_ref[at, :], (((0,), (0,)), ((), ())), preferred_element_type=jnp.float32
                )
        else:
            product = lax.dot_general(
                e_ref[:, rows], e_ref[...], (((0,), (0,)), ((), ())), preferred_element_type=jnp.float32
            )
        down = jnp.transpose(jnp.broadcast_to(mean[:, rows] * rows_here, (LANES, TILE)))
        for j in range(wide // LANES):
            across = slice(j * LANES, (j + 1) * LANES)
            m_ref[rows, across] = product[:, across] - down * mean[:, across]
        for pair in range(TILE // block // 2):
            first = t * (TILE // block) + 2 * pair
            apart = (first ^ me) >> 1
            place = 0
            for k in range(bits - 1):
                place = place + (((apart >> k) & 1) << (bits - 2 - k))
            to = pl.ds(pl.multiple_of(place * block, block), block)
            kept = pl.multiple_of((first + (me & 1)) * block, block)
            sent = pl.multiple_of((first + 1 - (me & 1)) * block, block)
            keep_ref[to, :] = m_ref[pl.ds(kept, block), :]
            send_ref[to, :] = m_ref[pl.ds(sent, block), :].astype(jnp.bfloat16)


def moments(width, me, embeddings, mean):
    rows_here, wide = embeddings.shape
    vmem = pl.BlockSpec(memory_space=pltpu.VMEM)
    return pl.pallas_call(
        functools.partial(moments_kernel, width),
        in_specs=[pl.BlockSpec(memory_space=pltpu.SMEM)] + [pl.BlockSpec(memory_space=pl.ANY)] * 2,
        out_specs=[vmem] * 2,
        out_shape=[
            jax.ShapeDtypeStruct((wide // 2, wide), jnp.float32),
            jax.ShapeDtypeStruct((wide // 2, wide), jnp.bfloat16),
        ],
        scratch_shapes=[
            pltpu.VMEM((rows_here, wide), jnp.bfloat16),
            pltpu.VMEM((1, wide), jnp.float32),
            pltpu.VMEM((wide, wide), jnp.float32),
            pltpu.SemaphoreType.DMA((rows_here // CHUNK,)),
            pltpu.SemaphoreType.DMA,
        ],
        compiler_params=pltpu.CompilerParams(vmem_limit_bytes=VMEM_MOST),
        cost_estimate=pl.CostEstimate(
            flops=2 * rows_here * wide * wide, bytes_accessed=2 * rows_here * wide + 3 * wide * wide, transcendentals=0
        ),
        name="moments",
    )(me.reshape(1), mean, embeddings)


def add_kernel(pieces, keep_ref, *refs):
    came, outs = refs[:-pieces], refs[-pieces:]
    size = outs[0].shape[0]
    for p in range(pieces):
        at = slice(p * size, (p + 1) * size)
        held = keep_ref[at]
        for ref in came:
            held = held + ref[at].astype(jnp.float32)
        outs[p][...] = held.astype(outs[p].dtype)


def add_and_split(keep, came, pieces):
    rows, wide = keep.shape
    vmem = pl.BlockSpec(memory_space=pltpu.VMEM)
    return pl.pallas_call(
        functools.partial(add_kernel, pieces),
        in_specs=[vmem] * (1 + len(came)),
        out_specs=[vmem] * pieces,
        out_shape=[
            jax.ShapeDtypeStruct((rows // pieces, wide), jnp.float32 if p == 0 else jnp.bfloat16) for p in range(pieces)
        ],
        compiler_params=pltpu.CompilerParams(vmem_limit_bytes=VMEM_SOME),
        cost_estimate=pl.CostEstimate(flops=2 * rows * wide, bytes_accessed=10 * rows * wide, transcendentals=0),
        name="add_and_split",
    )(keep, *came)


def partners(width, apart):
    return [(i, i ^ apart) for i in range(width)]


def halving_stages(width):
    strides = [1 << k for k in range(width.bit_length() - 1)]
    return [strides[:1], strides[1:3]] + [[s] for s in strides[3:]]


def reduce_blocks(width, keep, send):
    stages = halving_stages(width)
    out = [send]
    for n, stage in enumerate(stages):
        came = []
        for p in range(1, 1 << len(stage)):
            apart = sum(s for k, s in enumerate(stage) if (p >> (len(stage) - 1 - k)) & 1)
            came.append(lax.ppermute(out[p - 1], "wide", partners(width, apart)))
        if n + 1 < len(stages):
            keep, *out = add_and_split(keep, came, 1 << len(stages[n + 1]))
    return keep, came


def encode_kernel(total, me_ref, got_ref, all_ref, basis_ref, centroid_ref, rotation_ref, out_ref, between_ref, delta_ref, scale_ref, list_ref, apart_ref):
    step = pl.program_id(0)
    width = delta_ref.shape[0]
    feats = out_ref.shape[1]
    owned = centroid_ref.shape[0]
    wide = basis_ref.shape[0]
    block = wide // width
    share = total // width

    @pl.when(step == 0)
    def _():
        notes = jnp.concatenate([all_ref[s * SPAN + CAP:(s + 1) * SPAN, :] for s in range(width)], 0)
        size = width * NOTES
        to = lax.broadcasted_iota(jnp.int32, (size, size), 0)
        of = lax.broadcasted_iota(jnp.int32, (size, size), 1)
        turn = jnp.where((to % width) * NOTES + to // width == of, 1.0, 0.0).astype(jnp.bfloat16)
        turned = jnp.dot(turn, notes, preferred_element_type=jnp.float32)
        row = [turned[r * width:(r + 1) * width] for r in range(NOTES)]
        quarters = wide // feats
        shifts = jnp.zeros((width, feats), jnp.float32)
        for q in range(quarters):
            parts = [row[p * quarters + q] for p in range(3)]
            mean = parts[0] + (parts[1] + parts[2])
            apart_ref[:, q * feats:(q + 1) * feats] = mean - jnp.mean(mean, 0, keepdims=True)
            terms = jnp.dot(
                jnp.concatenate(parts, 0).astype(jnp.bfloat16),
                basis_ref[q * feats:(q + 1) * feats, :],
                preferred_element_type=jnp.float32,
            )
            shifts = shifts + (terms[:width] + (terms[width:2 * width] + terms[2 * width:]))
        square = row[3 * quarters] + (row[3 * quarters + 1] + row[3 * quarters + 2])
        delta = shifts - jnp.mean(shifts, 0, keepdims=True)
        variance = jnp.sum(square + share * (delta * delta), 0, keepdims=True) / total
        scale_ref[...] = lax.rsqrt(variance + 1e-05)
        delta_ref[...] = delta
        digits = row[NOTES - 1]
        list_ref[...] = digits[:, :CAP] * 32.0 + digits[:, CAP:] - 1.0

        me = me_ref[0]
        first = me * block
        near = apart_ref[:, pl.ds(pl.multiple_of(first // LANES * LANES, LANES), LANES)]
        near = pltpu.roll(near, (LANES - first % LANES) % LANES, 1)[:, :block]
        between_ref[...] = share * lax.dot_general(
            near,
            apart_ref[...],
            (((0,), (0,)), ((), ())),
            precision=lax.Precision.HIGHEST,
            preferred_element_type=jnp.float32,
        )

    columns = jnp.transpose(list_ref[pl.ds(step * GROUP, GROUP), :])
    names = lax.broadcasted_iota(jnp.int32, (CAP, owned), 1).astype(jnp.int16)
    hits, projected, held = [], [], []
    for s in range(GROUP):
        listed = jnp.broadcast_to(columns[:, s:s + 1], (CAP, LANES))
        held.append(jnp.concatenate([listed] * (feats // LANES), 1) >= 0)
        wanted = jnp.concatenate([listed.astype(jnp.int32).astype(jnp.int16)] * (owned // LANES), 1)
        hits.append(jnp.where(wanted == names, jnp.ones((), jnp.bfloat16), jnp.zeros((), jnp.bfloat16)))
        rows = got_ref[s * SPAN:s * SPAN + CAP, :].astype(jnp.float32)
        projected.append((rows + delta_ref[pl.ds(step * GROUP + s, 1), :]) * scale_ref[...])
    centre = jnp.dot(jnp.concatenate(hits, 0), centroid_ref[...], preferred_element_type=jnp.float32)
    residual = jnp.where(jnp.concatenate(held, 0), jnp.concatenate(projected, 0) - centre, 0.0)
    out_ref[...] = jnp.dot(
        residual.astype(jnp.bfloat16), rotation_ref[...], preferred_element_type=jnp.float32
    ).astype(jnp.bfloat16)


def encode(width, total, me, got, basis, centroids, rotation):
    wide, feats = basis.shape
    owned = centroids.shape[0]
    slots = width * CAP
    whole = lambda i: (0, 0)
    return pl.pallas_call(
        functools.partial(encode_kernel, total),
        grid=(width // GROUP,),
        in_specs=[
            pl.BlockSpec(memory_space=pltpu.SMEM),
            pl.BlockSpec((GROUP * SPAN, feats), lambda i: (i, 0)),
            pl.BlockSpec((width * SPAN, feats), whole),
            pl.BlockSpec((wide, feats), whole),
            pl.BlockSpec((owned, feats), whole),
            pl.BlockSpec((feats, feats), whole),
        ],
        out_specs=[
            pl.BlockSpec((GROUP * CAP, feats), lambda i: (i, 0)),
            pl.BlockSpec((wide // width, wide), whole),
        ],
        out_shape=[
            jax.ShapeDtypeStruct((slots, feats), jnp.bfloat16),
            jax.ShapeDtypeStruct((wide // width, wide), jnp.float32),
        ],
        scratch_shapes=[
            pltpu.VMEM((width, feats), jnp.float32),
            pltpu.VMEM((1, feats), jnp.float32),
            pltpu.VMEM((width, CAP), jnp.float32),
            pltpu.VMEM((width, wide), jnp.float32),
        ],
        compiler_params=pltpu.CompilerParams(vmem_limit_bytes=VMEM_SOME),
        cost_estimate=pl.CostEstimate(
            flops=2 * slots * feats * (owned + feats), bytes_accessed=4 * slots * feats, transcendentals=0
        ),
        name="encode",
    )(me.reshape(1), got, got, basis, centroids, rotation)


def local(embeddings, basis, list_owner, list_slot, centroids, rotation):
    width = lax.axis_size("wide")
    me = lax.axis_index("wide")
    rows_here, wide = embeddings.shape
    feats = basis.shape[1]
    total = rows_here * width

    rows, mean = project_and_sort(width, embeddings, basis, list_owner, list_slot)
    got = lax.all_to_all(rows.reshape(width, SPAN, feats), "wide", split_axis=0, concat_axis=0, tiled=True)

    keep, send = moments(width, me, embeddings, mean)
    keep, came = reduce_blocks(width, keep, send)
    encoded, between = encode(width, total, me, got.reshape(width * SPAN, feats), basis, centroids, rotation)
    for block in came:
        keep = keep + block.astype(jnp.float32)
    covariance = (keep + between) / total
    return (encoded, covariance)


def solution(mesh):
    in_specs = (
        P(("groups", "wide"), None),
        P(),
        P(("groups", "wide")),
        P(("groups", "wide")),
        P("wide", None),
        P(),
    )
    out_specs = (P(("groups", "wide"), None), P(("groups", "wide"), None))
    return jax.shard_map(local, mesh=mesh, in_specs=in_specs, out_specs=out_specs, check_vma=False)
```

```python
import functools

import jax
import jax.numpy as jnp
from jax import lax
from jax.experimental import pallas as pl
from jax.experimental.pallas import tpu as pltpu
from jax.sharding import PartitionSpec as P

CAP = 128
LANES = 128
NOTES = 16
SPAN = CAP + NOTES
CHUNK = 512
TILE = 256
GROUP = 4
VMEM_SOME = 24 * 1024 * 1024
VMEM_MOST = 57 * 1024 * 1024


def in_three(x):
    high = x.astype(jnp.bfloat16).astype(jnp.float32)
    rest = x - high
    middle = rest.astype(jnp.bfloat16).astype(jnp.float32)
    return high, middle, (rest - middle).astype(jnp.bfloat16).astype(jnp.float32)


def first_kernel(
    width, me_ref, e_hbm, basis_hbm, owner_ref, slot_ref,
    rows_hbm, keep_hbm, send_hbm,
    e_ref, basis_ref, y_ref, yb_ref, pick_ref, rows_ref, m_ref, list_ref, e_sem, basis_sem, rows_sem, block_sem,
):
    rows_here, wide = e_ref.shape
    feats = basis_ref.shape[1]
    chunks = rows_here // LANES
    parts = rows_here // CHUNK
    block = wide // width
    bits = width.bit_length() - 1

    e_copies = []
    for c in range(parts):
        at = pl.ds(c * CHUNK, CHUNK)
        e_copies.append(pltpu.make_async_copy(e_hbm.at[at], e_ref.at[at], e_sem.at[c]))
        e_copies[c].start()
        if c == 0:
            basis_copy = pltpu.make_async_copy(basis_hbm, basis_ref, basis_sem)
            basis_copy.start()

    owner = owner_ref[...]
    wanted = lax.broadcasted_iota(jnp.int32, (width, LANES), 0)
    hits = [jnp.where(owner[c:c + 1, :] == wanted, 1.0, 0.0) for c in range(chunks)]
    flat = jnp.concatenate(hits, 0).astype(jnp.bfloat16)
    up = lax.broadcasted_iota(jnp.int32, (LANES, LANES), 0)
    to = lax.broadcasted_iota(jnp.int32, (LANES, LANES), 1)
    before = jnp.where(up < to, 1.0, 0.0).astype(jnp.bfloat16)
    every = jnp.ones((LANES, LANES), jnp.bfloat16)
    within = jnp.dot(flat, before, preferred_element_type=jnp.float32)
    counts = jnp.dot(flat, every, preferred_element_type=jnp.float32)
    carry = jnp.zeros((width, LANES), jnp.float32)
    ranks, targets = [], []
    for c in range(chunks):
        at = slice(c * width, (c + 1) * width)
        ranks.append(jnp.sum(hits[c] * (within[at] + carry), 0, keepdims=True).astype(jnp.int32))
        carry = carry + counts[at]
        targets.append(owner[c:c + 1, :] * CAP + ranks[c])
    slot = slot_ref[...] + 1
    high, low = (slot >> 5).astype(jnp.float32), (slot & 31).astype(jnp.float32)
    spots = lax.broadcasted_iota(jnp.int32, (CAP, LANES), 0)
    placed = jnp.concatenate([jnp.where(ranks[c] == spots, 1.0, 0.0) for c in range(chunks)], 1).astype(jnp.bfloat16)
    digits = jnp.concatenate(
        [
            jnp.concatenate([hits[c] * high[c:c + 1, :] for c in range(chunks)], 1),
            jnp.concatenate([hits[c] * low[c:c + 1, :] for c in range(chunks)], 1),
        ],
        0,
    ).astype(jnp.bfloat16)
    found = lax.dot_general(digits, placed, (((1,), (1,)), ((), ())), preferred_element_type=jnp.float32)
    list_ref[:, :CAP] = found[:width]
    list_ref[:, CAP:] = found[width:]

    groups = width // GROUP
    held = pick_ref.shape[0]
    place = lax.broadcasted_iota(jnp.int32, (GROUP * CAP, LANES), 0).astype(jnp.int16)

    def pick_group(g, into):
        for c in range(chunks):
            aim = jnp.broadcast_to(targets[c] - g * (GROUP * CAP), (16, LANES)).astype(jnp.int16)
            aim = jnp.concatenate([aim] * (GROUP * CAP // 16), 0)
            pick_ref[into, :, c * LANES:(c + 1) * LANES] = jnp.where(
                aim == place, jnp.ones((), jnp.bfloat16), jnp.zeros((), jnp.bfloat16)
            )

    basis_copy.wait()
    sum_y = jnp.zeros((8, feats), jnp.float32)
    sum_e = jnp.zeros((8, wide), jnp.float32)
    for c in range(parts):
        at = slice(c * CHUNK, (c + 1) * CHUNK)
        e_copies[c].wait()
        rows = e_ref[at, :]
        y = jnp.dot(rows, basis_ref[...], preferred_element_type=jnp.float32)
        y_ref[at, :] = y
        sum_y = sum_y + jnp.sum(y.reshape(CHUNK // 8, 8, feats), 0)
        sum_e = sum_e + jnp.sum(rows.astype(jnp.float32).reshape(CHUNK // 8, 8, wide), 0)
        if c < held:
            pick_group(c, c)

    mean_y = jnp.sum(sum_y, 0, keepdims=True) / rows_here
    square = jnp.zeros((8, feats), jnp.float32)
    for c in range(parts):
        at = slice(c * CHUNK, (c + 1) * CHUNK)
        centred = y_ref[at, :] - mean_y
        square = square + jnp.sum((centred * centred).reshape(CHUNK // 8, 8, feats), 0)
        yb_ref[at, :] = centred.astype(jnp.bfloat16)
    mean = jnp.sum(sum_e, 0, keepdims=True) / rows_here
    common = [part[:, q * feats:(q + 1) * feats] for part in in_three(mean) for q in range(wide // feats)]
    common = jnp.concatenate(common + list(in_three(jnp.sum(square, 0, keepdims=True))), 0)

    def sort_group(g, into):
        rows = jnp.dot(pick_ref[into], yb_ref[...], preferred_element_type=jnp.float32).astype(jnp.bfloat16)
        for j in range(GROUP):
            base = pl.multiple_of((g * GROUP + j) * SPAN, 16)
            rows_ref[pl.ds(base, CAP), :] = rows[j * CAP:(j + 1) * CAP]
            notes = jnp.concatenate([common, list_ref[pl.ds(g * GROUP + j, 1), :]], 0)
            rows_ref[pl.ds(pl.multiple_of(base + CAP, 16), NOTES), :] = notes.astype(jnp.bfloat16)

    if groups <= held:
        for g in range(groups):
            sort_group(g, g)
    else:

        @pl.loop(0, groups)
        def _(g):
            pick_group(g, 0)
            sort_group(g, 0)

    whole_copy = pltpu.make_async_copy(rows_ref, rows_hbm, rows_sem)
    whole_copy.start()

    me = me_ref[0]
    copies = []
    for t in range(wide // TILE):
        rows = slice(t * TILE, (t + 1) * TILE)
        product = lax.dot_general(
            e_ref[:, rows], e_ref[...], (((0,), (0,)), ((), ())), preferred_element_type=jnp.float32
        )
        down = jnp.transpose(jnp.broadcast_to(mean[:, rows] * rows_here, (LANES, TILE)))
        for j in range(wide // LANES):
            across = slice(j * LANES, (j + 1) * LANES)
            m_ref[rows, across] = (product[:, across] - down * mean[:, across]).astype(jnp.bfloat16)
        for pair in range(TILE // block // 2):
            first = t * (TILE // block) + 2 * pair
            apart = (first ^ me) >> 1
            spot = 0
            for k in range(bits - 1):
                spot = spot + (((apart >> k) & 1) << (bits - 2 - k))
            at = pl.ds(pl.multiple_of(spot * block, block), block)
            kept = pl.multiple_of((first + (me & 1)) * block, block)
            sent = pl.multiple_of((first + 1 - (me & 1)) * block, block)
            for here, there in ((kept, keep_hbm), (sent, send_hbm)):
                copy = pltpu.make_async_copy(m_ref.at[pl.ds(here, block)], there.at[at], block_sem.at[len(copies)])
                copy.start()
                copies.append(copy)
    for copy in copies:
        copy.wait()
    whole_copy.wait()


def first(width, me, embeddings, basis, list_owner, list_slot):
    rows_here, wide = embeddings.shape
    feats = basis.shape[1]
    lanes = rows_here // LANES
    slots = width * SPAN
    groups = width // GROUP
    vmem, anywhere = pl.BlockSpec(memory_space=pltpu.VMEM), pl.BlockSpec(memory_space=pl.ANY)
    return pl.pallas_call(
        functools.partial(first_kernel, width),
        in_specs=[pl.BlockSpec(memory_space=pltpu.SMEM), anywhere, anywhere, vmem, vmem],
        out_specs=[anywhere] * 3,
        out_shape=[jax.ShapeDtypeStruct((slots, feats), jnp.bfloat16)]
        + [jax.ShapeDtypeStruct((wide // 2, wide), jnp.bfloat16)] * 2,
        scratch_shapes=[
            pltpu.VMEM((rows_here, wide), jnp.bfloat16),
            pltpu.VMEM((wide, feats), jnp.bfloat16),
            pltpu.VMEM((rows_here, feats), jnp.float32),
            pltpu.VMEM((rows_here, feats), jnp.bfloat16),
            pltpu.VMEM((groups if groups <= rows_here // CHUNK else 1, GROUP * CAP, rows_here), jnp.bfloat16),
            pltpu.VMEM((slots, feats), jnp.bfloat16),
            pltpu.VMEM((wide, wide), jnp.bfloat16),
            pltpu.VMEM((width, 2 * CAP), jnp.float32),
            pltpu.SemaphoreType.DMA((rows_here // CHUNK,)),
            pltpu.SemaphoreType.DMA,
            pltpu.SemaphoreType.DMA,
            pltpu.SemaphoreType.DMA((width,)),
        ],
        compiler_params=pltpu.CompilerParams(vmem_limit_bytes=VMEM_MOST),
        cost_estimate=pl.CostEstimate(
            flops=2 * rows_here * (feats * (wide + slots) + wide * wide),
            bytes_accessed=2 * rows_here * wide + 2 * slots * feats + 2 * wide * wide,
            transcendentals=0,
        ),
        name="first",
    )(me.reshape(1), embeddings, basis, list_owner.reshape(lanes, LANES), list_slot.reshape(lanes, LANES))


def add_kernel(pieces, keep_ref, *refs):
    came, outs = refs[:-pieces], refs[-pieces:]
    size = outs[0].shape[0]
    for p in range(pieces):
        at = slice(p * size, (p + 1) * size)
        held = keep_ref[at].astype(jnp.float32)
        for ref in came:
            held = held + ref[at].astype(jnp.float32)
        outs[p][...] = held.astype(outs[p].dtype)


def add_and_split(keep, came, pieces):
    rows, wide = keep.shape
    vmem = pl.BlockSpec(memory_space=pltpu.VMEM)
    return pl.pallas_call(
        functools.partial(add_kernel, pieces),
        in_specs=[vmem] * (1 + len(came)),
        out_specs=[vmem] * pieces,
        out_shape=[
            jax.ShapeDtypeStruct((rows // pieces, wide), jnp.float32 if p == 0 else jnp.bfloat16) for p in range(pieces)
        ],
        compiler_params=pltpu.CompilerParams(vmem_limit_bytes=VMEM_SOME),
        cost_estimate=pl.CostEstimate(flops=2 * rows * wide, bytes_accessed=10 * rows * wide, transcendentals=0),
        name="add_and_split",
    )(keep, *came)


def partners(width, apart):
    return [(i, i ^ apart) for i in range(width)]


def halving_stages(width):
    strides = [1 << k for k in range(width.bit_length() - 1)]
    return [strides[:1], strides[1:3]] + [[s] for s in strides[3:]]


def reduce_blocks(width, keep, send):
    stages = halving_stages(width)
    out = [send]
    for n, stage in enumerate(stages):
        came = []
        for p in range(1, 1 << len(stage)):
            apart = sum(s for k, s in enumerate(stage) if (p >> (len(stage) - 1 - k)) & 1)
            came.append(lax.ppermute(out[p - 1], "wide", partners(width, apart)))
        if n + 1 < len(stages):
            keep, *out = add_and_split(keep, came, 1 << len(stages[n + 1]))
    return keep, came


def encode_kernel(total, me_ref, got_ref, all_ref, basis_ref, centroid_ref, rotation_ref, out_ref, between_ref, delta_ref, scale_ref, list_ref, apart_ref):
    step = pl.program_id(0)
    width = delta_ref.shape[0]
    feats = out_ref.shape[1]
    owned = centroid_ref.shape[0]
    wide = basis_ref.shape[0]
    block = wide // width
    share = total // width

    @pl.when(step == 0)
    def _():
        notes = jnp.concatenate([all_ref[s * SPAN + CAP:(s + 1) * SPAN, :] for s in range(width)], 0)
        size = width * NOTES
        to = lax.broadcasted_iota(jnp.int32, (size, size), 0)
        of = lax.broadcasted_iota(jnp.int32, (size, size), 1)
        turn = jnp.where((to % width) * NOTES + to // width == of, 1.0, 0.0).astype(jnp.bfloat16)
        turned = jnp.dot(turn, notes, preferred_element_type=jnp.float32)
        row = [turned[r * width:(r + 1) * width] for r in range(NOTES)]
        quarters = wide // feats
        shifts = jnp.zeros((width, feats), jnp.float32)
        for q in range(quarters):
            parts = [row[p * quarters + q] for p in range(3)]
            mean = parts[0] + (parts[1] + parts[2])
            apart_ref[:, q * feats:(q + 1) * feats] = mean - jnp.mean(mean, 0, keepdims=True)
            terms = jnp.dot(
                jnp.concatenate(parts, 0).astype(jnp.bfloat16),
                basis_ref[q * feats:(q + 1) * feats, :],
                preferred_element_type=jnp.float32,
            )
            shifts = shifts + (terms[:width] + (terms[width:2 * width] + terms[2 * width:]))
        square = row[3 * quarters] + (row[3 * quarters + 1] + row[3 * quarters + 2])
        delta = shifts - jnp.mean(shifts, 0, keepdims=True)
        variance = jnp.sum(square + share * (delta * delta), 0, keepdims=True) / total
        scale_ref[...] = lax.rsqrt(variance + 1e-05)
        delta_ref[...] = delta
        digits = row[NOTES - 1]
        list_ref[...] = digits[:, :CAP] * 32.0 + digits[:, CAP:] - 1.0

        me = me_ref[0]
        first = me * block
        near = apart_ref[:, pl.ds(pl.multiple_of(first // LANES * LANES, LANES), LANES)]
        near = pltpu.roll(near, (LANES - first % LANES) % LANES, 1)[:, :block]
        between_ref[...] = share * lax.dot_general(
            near,
            apart_ref[...],
            (((0,), (0,)), ((), ())),
            precision=lax.Precision.HIGHEST,
            preferred_element_type=jnp.float32,
        )

    columns = jnp.transpose(list_ref[pl.ds(step * GROUP, GROUP), :])
    names = lax.broadcasted_iota(jnp.int32, (CAP, owned), 1).astype(jnp.int16)
    hits, projected, held = [], [], []
    for s in range(GROUP):
        listed = jnp.broadcast_to(columns[:, s:s + 1], (CAP, LANES))
        held.append(jnp.concatenate([listed] * (feats // LANES), 1) >= 0)
        wanted = jnp.concatenate([listed.astype(jnp.int32).astype(jnp.int16)] * (owned // LANES), 1)
        hits.append(jnp.where(wanted == names, jnp.ones((), jnp.bfloat16), jnp.zeros((), jnp.bfloat16)))
        rows = got_ref[s * SPAN:s * SPAN + CAP, :].astype(jnp.float32)
        projected.append((rows + delta_ref[pl.ds(step * GROUP + s, 1), :]) * scale_ref[...])
    centre = jnp.dot(jnp.concatenate(hits, 0), centroid_ref[...], preferred_element_type=jnp.float32)
    residual = jnp.where(jnp.concatenate(held, 0), jnp.concatenate(projected, 0) - centre, 0.0)
    out_ref[...] = jnp.dot(
        residual.astype(jnp.bfloat16), rotation_ref[...], preferred_element_type=jnp.float32
    ).astype(jnp.bfloat16)


def encode(width, total, me, got, basis, centroids, rotation):
    wide, feats = basis.shape
    owned = centroids.shape[0]
    slots = width * CAP
    whole = lambda i: (0, 0)
    return pl.pallas_call(
        functools.partial(encode_kernel, total),
        grid=(width // GROUP,),
        in_specs=[
            pl.BlockSpec(memory_space=pltpu.SMEM),
            pl.BlockSpec((GROUP * SPAN, feats), lambda i: (i, 0)),
            pl.BlockSpec((width * SPAN, feats), whole),
            pl.BlockSpec((wide, feats), whole),
            pl.BlockSpec((owned, feats), whole),
            pl.BlockSpec((feats, feats), whole),
        ],
        out_specs=[
            pl.BlockSpec((GROUP * CAP, feats), lambda i: (i, 0)),
            pl.BlockSpec((wide // width, wide), whole),
        ],
        out_shape=[
            jax.ShapeDtypeStruct((slots, feats), jnp.bfloat16),
            jax.ShapeDtypeStruct((wide // width, wide), jnp.float32),
        ],
        scratch_shapes=[
            pltpu.VMEM((width, feats), jnp.float32),
            pltpu.VMEM((1, feats), jnp.float32),
            pltpu.VMEM((width, CAP), jnp.float32),
            pltpu.VMEM((width, wide), jnp.float32),
        ],
        compiler_params=pltpu.CompilerParams(vmem_limit_bytes=VMEM_SOME),
        cost_estimate=pl.CostEstimate(
            flops=2 * slots * feats * (owned + feats), bytes_accessed=4 * slots * feats, transcendentals=0
        ),
        name="encode",
    )(me.reshape(1), got, got, basis, centroids, rotation)


def local(embeddings, basis, list_owner, list_slot, centroids, rotation):
    width = lax.axis_size("wide")
    me = lax.axis_index("wide")
    rows_here, wide = embeddings.shape
    feats = basis.shape[1]
    total = rows_here * width

    rows, keep, send = first(width, me, embeddings, basis, list_owner, list_slot)
    got = lax.all_to_all(rows.reshape(width, SPAN, feats), "wide", split_axis=0, concat_axis=0, tiled=True)
    keep, came = reduce_blocks(width, keep, send)
    encoded, between = encode(width, total, me, got.reshape(width * SPAN, feats), basis, centroids, rotation)
    for block in came:
        keep = keep + block.astype(jnp.float32)
    covariance = (keep + between) / total
    return (encoded, covariance)


def solution(mesh):
    in_specs = (
        P(("groups", "wide"), None),
        P(),
        P(("groups", "wide")),
        P(("groups", "wide")),
        P("wide", None),
        P(),
    )
    out_specs = (P(("groups", "wide"), None), P(("groups", "wide"), None))
    return jax.shard_map(local, mesh=mesh, in_specs=in_specs, out_specs=out_specs, check_vma=False)
```

```python
import functools

import jax
import jax.numpy as jnp
from jax import lax
from jax.experimental import pallas as pl
from jax.experimental.pallas import tpu as pltpu
from jax.sharding import PartitionSpec as P

CAP = 128
LANES = 128
NOTES = 16
SPAN = CAP + NOTES
CHUNK = 512
TILE = 256
GROUP = 4
VMEM_SOME = 24 * 1024 * 1024
VMEM_MOST = 57 * 1024 * 1024
VMEM_MUCH = 48 * 1024 * 1024


def in_three(x):
    high = x.astype(jnp.bfloat16).astype(jnp.float32)
    rest = x - high
    middle = rest.astype(jnp.bfloat16).astype(jnp.float32)
    return high, middle, (rest - middle).astype(jnp.bfloat16).astype(jnp.float32)


def moments_kernel(width, me_ref, e_hbm, keep_hbm, send_hbm, mean_ref, e_ref, m_ref, e_sem, block_sem):
    rows_here, wide = e_ref.shape
    block = wide // width
    bits = width.bit_length() - 1
    parts = rows_here // CHUNK
    tiles = wide // TILE
    e_copies = []
    for c in range(parts):
        at = pl.ds(c * CHUNK, CHUNK)
        e_copies.append(pltpu.make_async_copy(e_hbm.at[at], e_ref.at[at], e_sem.at[c]))
        e_copies[c].start()
    me = me_ref[0]
    copies = []
    for t in range(tiles):
        rows, columns = slice(t * TILE, (t + 1) * TILE), slice(t * TILE, wide)
        if t == 0:
            product = jnp.zeros((TILE, wide), jnp.float32)
            sum_e = jnp.zeros((8, wide), jnp.float32)
            for c in range(parts):
                e_copies[c].wait()
                at = slice(c * CHUNK, (c + 1) * CHUNK)
                product = product + lax.dot_general(
                    e_ref[at, rows], e_ref[at, :], (((0,), (0,)), ((), ())), preferred_element_type=jnp.float32
                )
                sum_e = sum_e + jnp.sum(e_ref[at, :].astype(jnp.float32).reshape(CHUNK // 8, 8, wide), 0)
            mean = jnp.sum(sum_e, 0, keepdims=True) / rows_here
            mean_ref[...] = mean
        else:
            product = lax.dot_general(
                e_ref[:, rows], e_ref[:, columns], (((0,), (0,)), ((), ())), preferred_element_type=jnp.float32
            )
        down = jnp.transpose(jnp.broadcast_to(mean[:, rows] * rows_here, (LANES, TILE)))
        for u in range(t, tiles):
            pieces = []
            for j in range(u * TILE // LANES, (u + 1) * TILE // LANES):
                across = slice(j * LANES, (j + 1) * LANES)
                within = slice(j * LANES - t * TILE, (j + 1) * LANES - t * TILE)
                pieces.append((product[:, within] - down * mean[:, across]).astype(jnp.bfloat16))
            piece = jnp.concatenate(pieces, 1)
            other = slice(u * TILE, (u + 1) * TILE)
            m_ref[rows, other] = piece
            if u > t:
                m_ref[other, rows] = jnp.transpose(piece)
        for pair in range(TILE // block // 2):
            first = t * (TILE // block) + 2 * pair
            apart = (first ^ me) >> 1
            spot = 0
            for k in range(bits - 1):
                spot = spot + (((apart >> k) & 1) << (bits - 2 - k))
            at = pl.ds(pl.multiple_of(spot * block, block), block)
            kept = pl.multiple_of((first + (me & 1)) * block, block)
            sent = pl.multiple_of((first + 1 - (me & 1)) * block, block)
            for here, there in ((kept, keep_hbm), (sent, send_hbm)):
                copy = pltpu.make_async_copy(m_ref.at[pl.ds(here, block)], there.at[at], block_sem.at[len(copies)])
                copy.start()
                copies.append(copy)
    for copy in copies:
        copy.wait()


def moments(width, me, embeddings):
    rows_here, wide = embeddings.shape
    anywhere = pl.BlockSpec(memory_space=pl.ANY)
    return pl.pallas_call(
        functools.partial(moments_kernel, width),
        in_specs=[pl.BlockSpec(memory_space=pltpu.SMEM), anywhere],
        out_specs=[anywhere, anywhere, pl.BlockSpec(memory_space=pltpu.VMEM)],
        out_shape=[jax.ShapeDtypeStruct((wide // 2, wide), jnp.bfloat16)] * 2 + [jax.ShapeDtypeStruct((1, wide), jnp.float32)],
        scratch_shapes=[
            pltpu.VMEM((rows_here, wide), jnp.bfloat16),
            pltpu.VMEM((wide, wide), jnp.bfloat16),
            pltpu.SemaphoreType.DMA((rows_here // CHUNK,)),
            pltpu.SemaphoreType.DMA((width,)),
        ],
        compiler_params=pltpu.CompilerParams(vmem_limit_bytes=VMEM_MOST),
        cost_estimate=pl.CostEstimate(
            flops=2 * rows_here * wide * wide, bytes_accessed=2 * rows_here * wide + 2 * wide * wide, transcendentals=0
        ),
        name="moments",
    )(me.reshape(1), embeddings)


def project_kernel(
    width, e_hbm, basis_ref, owner_ref, slot_ref, mean_ref,
    yb_ref, target_ref, list_ref, notes_ref,
    e_ref, y_ref, e_sem,
):
    rows_here, wide = e_ref.shape
    feats = basis_ref.shape[1]
    chunks = rows_here // LANES
    parts = rows_here // CHUNK

    e_copies = []
    for c in range(parts):
        at = pl.ds(c * CHUNK, CHUNK)
        e_copies.append(pltpu.make_async_copy(e_hbm.at[at], e_ref.at[at], e_sem.at[c]))
        e_copies[c].start()

    owner = owner_ref[...]
    wanted = lax.broadcasted_iota(jnp.int32, (width, LANES), 0)
    hits = [jnp.where(owner[c:c + 1, :] == wanted, 1.0, 0.0) for c in range(chunks)]
    flat = jnp.concatenate(hits, 0).astype(jnp.bfloat16)
    up = lax.broadcasted_iota(jnp.int32, (LANES, LANES), 0)
    to = lax.broadcasted_iota(jnp.int32, (LANES, LANES), 1)
    before = jnp.where(up < to, 1.0, 0.0).astype(jnp.bfloat16)
    every = jnp.ones((LANES, LANES), jnp.bfloat16)
    within = jnp.dot(flat, before, preferred_element_type=jnp.float32)
    counts = jnp.dot(flat, every, preferred_element_type=jnp.float32)
    carry = jnp.zeros((width, LANES), jnp.float32)
    ranks = []
    for c in range(chunks):
        at = slice(c * width, (c + 1) * width)
        ranks.append(jnp.sum(hits[c] * (within[at] + carry), 0, keepdims=True).astype(jnp.int32))
        carry = carry + counts[at]
        target_ref[c:c + 1, :] = owner[c:c + 1, :] * CAP + ranks[c]
    slot = slot_ref[...] + 1
    high, low = (slot >> 5).astype(jnp.float32), (slot & 31).astype(jnp.float32)
    spots = lax.broadcasted_iota(jnp.int32, (CAP, LANES), 0)
    placed = jnp.concatenate([jnp.where(ranks[c] == spots, 1.0, 0.0) for c in range(chunks)], 1).astype(jnp.bfloat16)
    digits = jnp.concatenate(
        [
            jnp.concatenate([hits[c] * high[c:c + 1, :] for c in range(chunks)], 1),
            jnp.concatenate([hits[c] * low[c:c + 1, :] for c in range(chunks)], 1),
        ],
        0,
    ).astype(jnp.bfloat16)
    found = lax.dot_general(digits, placed, (((1,), (1,)), ((), ())), preferred_element_type=jnp.float32)
    list_ref[:, :CAP] = found[:width]
    list_ref[:, CAP:] = found[width:]

    sum_y = jnp.zeros((8, feats), jnp.float32)
    for c in range(parts):
        at = slice(c * CHUNK, (c + 1) * CHUNK)
        e_copies[c].wait()
        y = jnp.dot(e_ref[at, :], basis_ref[...], preferred_element_type=jnp.float32)
        y_ref[at, :] = y
        sum_y = sum_y + jnp.sum(y.reshape(CHUNK // 8, 8, feats), 0)
    mean_y = jnp.sum(sum_y, 0, keepdims=True) / rows_here
    square = jnp.zeros((8, feats), jnp.float32)
    for c in range(parts):
        at = slice(c * CHUNK, (c + 1) * CHUNK)
        centred = y_ref[at, :] - mean_y
        square = square + jnp.sum((centred * centred).reshape(CHUNK // 8, 8, feats), 0)
        yb_ref[at, :] = centred.astype(jnp.bfloat16)
    notes = [part[:, q * feats:(q + 1) * feats] for part in in_three(mean_ref[...]) for q in range(wide // feats)]
    notes = notes + list(in_three(jnp.sum(square, 0, keepdims=True)))
    notes_ref[:len(notes), :] = jnp.concatenate(notes, 0)
    notes_ref[len(notes):, :] = jnp.zeros((NOTES - len(notes), feats), jnp.float32)


def project(width, embeddings, basis, list_owner, list_slot, mean):
    rows_here, wide = embeddings.shape
    feats = basis.shape[1]
    lanes = rows_here // LANES
    vmem, anywhere = pl.BlockSpec(memory_space=pltpu.VMEM), pl.BlockSpec(memory_space=pl.ANY)
    return pl.pallas_call(
        functools.partial(project_kernel, width),
        in_specs=[anywhere, vmem, vmem, vmem, vmem],
        out_specs=[vmem] * 4,
        out_shape=[
            jax.ShapeDtypeStruct((rows_here, feats), jnp.bfloat16),
            jax.ShapeDtypeStruct((lanes, LANES), jnp.int32),
            jax.ShapeDtypeStruct((width, 2 * CAP), jnp.float32),
            jax.ShapeDtypeStruct((NOTES, feats), jnp.float32),
        ],
        scratch_shapes=[
            pltpu.VMEM((rows_here, wide), jnp.bfloat16),
            pltpu.VMEM((rows_here, feats), jnp.float32),
            pltpu.SemaphoreType.DMA((rows_here // CHUNK,)),
        ],
        compiler_params=pltpu.CompilerParams(vmem_limit_bytes=VMEM_MUCH),
        cost_estimate=pl.CostEstimate(
            flops=2 * rows_here * feats * wide, bytes_accessed=2 * rows_here * (wide + feats), transcendentals=0
        ),
        name="project",
    )(embeddings, basis, list_owner.reshape(lanes, LANES), list_slot.reshape(lanes, LANES), mean)


def sort_kernel(yb_ref, target_ref, list_ref, notes_ref, after_hbm, rows_hbm, rows_ref, sem):
    rows_here, feats = yb_ref.shape
    width = list_ref.shape[0]
    chunks = rows_here // LANES
    groups = width // GROUP
    place = lax.broadcasted_iota(jnp.int32, (GROUP * CAP, LANES), 0).astype(jnp.int16)

    def sort_group(g):
        pieces = []
        for c in range(chunks):
            aim = jnp.broadcast_to(target_ref[c:c + 1, :] - g * (GROUP * CAP), (16, LANES)).astype(jnp.int16)
            aim = jnp.concatenate([aim] * (GROUP * CAP // 16), 0)
            pieces.append(jnp.where(aim == place, jnp.ones((), jnp.bfloat16), jnp.zeros((), jnp.bfloat16)))
        rows = jnp.dot(jnp.concatenate(pieces, 1), yb_ref[...], preferred_element_type=jnp.float32).astype(jnp.bfloat16)
        for j in range(GROUP):
            base = pl.multiple_of((g * GROUP + j) * SPAN, 16)
            rows_ref[pl.ds(base, CAP), :] = rows[j * CAP:(j + 1) * CAP]
            notes = jnp.concatenate([notes_ref[:NOTES - 1, :], list_ref[pl.ds(g * GROUP + j, 1), :]], 0)
            rows_ref[pl.ds(pl.multiple_of(base + CAP, 16), NOTES), :] = notes.astype(jnp.bfloat16)
        at = pl.ds(pl.multiple_of(g * (GROUP * SPAN), 16), GROUP * SPAN)
        return pltpu.make_async_copy(rows_ref.at[at], rows_hbm.at[at], sem.at[g])

    if groups <= 4:
        copies = []
        for g in range(groups):
            copies.append(sort_group(g))
            copies[g].start()
        for copy in copies:
            copy.wait()
    else:

        @pl.loop(0, groups)
        def _(g):
            copy = sort_group(g)
            copy.start()
            copy.wait()


def sort(yb, targets, lists, notes, after):
    rows_here, feats = yb.shape
    width = lists.shape[0]
    slots = width * SPAN
    vmem, anywhere = pl.BlockSpec(memory_space=pltpu.VMEM), pl.BlockSpec(memory_space=pl.ANY)
    return pl.pallas_call(
        sort_kernel,
        in_specs=[vmem] * 4 + [anywhere],
        out_specs=anywhere,
        out_shape=jax.ShapeDtypeStruct((slots, feats), jnp.bfloat16),
        scratch_shapes=[pltpu.VMEM((slots, feats), jnp.bfloat16), pltpu.SemaphoreType.DMA((width // GROUP,))],
        compiler_params=pltpu.CompilerParams(vmem_limit_bytes=VMEM_SOME),
        cost_estimate=pl.CostEstimate(
            flops=2 * rows_here * feats * slots, bytes_accessed=2 * (rows_here + slots) * feats, transcendentals=0
        ),
        name="sort",
    )(yb, targets, lists, notes, after)


def add_kernel(pieces, arrived, keep_ref, *refs):
    came, outs = refs[:arrived], refs[-pieces:]
    size = outs[0].shape[0]
    for p in range(pieces):
        at = slice(p * size, (p + 1) * size)
        held = keep_ref[at].astype(jnp.float32)
        for ref in came:
            held = held + ref[at].astype(jnp.float32)
        outs[p][...] = held.astype(outs[p].dtype)


def add_and_split(keep, came, pieces, after=()):
    rows, wide = keep.shape
    vmem, anywhere = pl.BlockSpec(memory_space=pltpu.VMEM), pl.BlockSpec(memory_space=pl.ANY)
    return pl.pallas_call(
        functools.partial(add_kernel, pieces, len(came)),
        in_specs=[vmem] * (1 + len(came)) + [anywhere] * len(after),
        out_specs=[vmem] * pieces,
        out_shape=[
            jax.ShapeDtypeStruct((rows // pieces, wide), jnp.float32 if p == 0 else jnp.bfloat16) for p in range(pieces)
        ],
        compiler_params=pltpu.CompilerParams(vmem_limit_bytes=VMEM_SOME),
        cost_estimate=pl.CostEstimate(flops=2 * rows * wide, bytes_accessed=10 * rows * wide, transcendentals=0),
        name="add_and_split",
    )(keep, *came, *after)


def partners(width, apart):
    return [(i, i ^ apart) for i in range(width)]


def halving_stages(width):
    strides = [1 << k for k in range(width.bit_length() - 1)]
    return [strides[:1], strides[1:3]] + [[s] for s in strides[3:]]


def exchange(width, stage, out):
    came = []
    for p in range(1, 1 << len(stage)):
        apart = sum(s for k, s in enumerate(stage) if (p >> (len(stage) - 1 - k)) & 1)
        came.append(lax.ppermute(out[p - 1], "wide", partners(width, apart)))
    return came


def encode_kernel(total, me_ref, got_ref, all_ref, basis_ref, centroid_ref, rotation_ref, out_ref, between_ref, delta_ref, scale_ref, list_ref, apart_ref):
    step = pl.program_id(0)
    width = delta_ref.shape[0]
    feats = out_ref.shape[1]
    owned = centroid_ref.shape[0]
    wide = basis_ref.shape[0]
    block = wide // width
    share = total // width

    @pl.when(step == 0)
    def _():
        notes = jnp.concatenate([all_ref[s * SPAN + CAP:(s + 1) * SPAN, :] for s in range(width)], 0)
        size = width * NOTES
        to = lax.broadcasted_iota(jnp.int32, (size, size), 0)
        of = lax.broadcasted_iota(jnp.int32, (size, size), 1)
        turn = jnp.where((to % width) * NOTES + to // width == of, 1.0, 0.0).astype(jnp.bfloat16)
        turned = jnp.dot(turn, notes, preferred_element_type=jnp.float32)
        row = [turned[r * width:(r + 1) * width] for r in range(NOTES)]
        quarters = wide // feats
        shifts = jnp.zeros((width, feats), jnp.float32)
        for q in range(quarters):
            parts = [row[p * quarters + q] for p in range(3)]
            mean = parts[0] + (parts[1] + parts[2])
            apart_ref[:, q * feats:(q + 1) * feats] = mean - jnp.mean(mean, 0, keepdims=True)
            terms = jnp.dot(
                jnp.concatenate(parts, 0).astype(jnp.bfloat16),
                basis_ref[q * feats:(q + 1) * feats, :],
                preferred_element_type=jnp.float32,
            )
            shifts = shifts + (terms[:width] + (terms[width:2 * width] + terms[2 * width:]))
        square = row[3 * quarters] + (row[3 * quarters + 1] + row[3 * quarters + 2])
        delta = shifts - jnp.mean(shifts, 0, keepdims=True)
        variance = jnp.sum(square + share * (delta * delta), 0, keepdims=True) / total
        scale_ref[...] = lax.rsqrt(variance + 1e-05)
        delta_ref[...] = delta
        digits = row[NOTES - 1]
        list_ref[...] = digits[:, :CAP] * 32.0 + digits[:, CAP:] - 1.0

        me = me_ref[0]
        first = me * block
        near = apart_ref[:, pl.ds(pl.multiple_of(first // LANES * LANES, LANES), LANES)]
        near = pltpu.roll(near, (LANES - first % LANES) % LANES, 1)[:, :block]
        between_ref[...] = share * lax.dot_general(
            near,
            apart_ref[...],
            (((0,), (0,)), ((), ())),
            precision=lax.Precision.HIGHEST,
            preferred_element_type=jnp.float32,
        )

    columns = jnp.transpose(list_ref[pl.ds(step * GROUP, GROUP), :])
    names = lax.broadcasted_iota(jnp.int32, (CAP, owned), 1).astype(jnp.int16)
    hits, projected, held = [], [], []
    for s in range(GROUP):
        listed = jnp.broadcast_to(columns[:, s:s + 1], (CAP, LANES))
        held.append(jnp.concatenate([listed] * (feats // LANES), 1) >= 0)
        wanted = jnp.concatenate([listed.astype(jnp.int32).astype(jnp.int16)] * (owned // LANES), 1)
        hits.append(jnp.where(wanted == names, jnp.ones((), jnp.bfloat16), jnp.zeros((), jnp.bfloat16)))
        rows = got_ref[s * SPAN:s * SPAN + CAP, :].astype(jnp.float32)
        projected.append((rows + delta_ref[pl.ds(step * GROUP + s, 1), :]) * scale_ref[...])
    centre = jnp.dot(jnp.concatenate(hits, 0), centroid_ref[...], preferred_element_type=jnp.float32)
    residual = jnp.where(jnp.concatenate(held, 0), jnp.concatenate(projected, 0) - centre, 0.0)
    out_ref[...] = jnp.dot(
        residual.astype(jnp.bfloat16), rotation_ref[...], preferred_element_type=jnp.float32
    ).astype(jnp.bfloat16)


def encode(width, total, me, got, basis, centroids, rotation):
    wide, feats = basis.shape
    owned = centroids.shape[0]
    slots = width * CAP
    whole = lambda i: (0, 0)
    return pl.pallas_call(
        functools.partial(encode_kernel, total),
        grid=(width // GROUP,),
        in_specs=[
            pl.BlockSpec(memory_space=pltpu.SMEM),
            pl.BlockSpec((GROUP * SPAN, feats), lambda i: (i, 0)),
            pl.BlockSpec((width * SPAN, feats), whole),
            pl.BlockSpec((wide, feats), whole),
            pl.BlockSpec((owned, feats), whole),
            pl.BlockSpec((feats, feats), whole),
        ],
        out_specs=[
            pl.BlockSpec((GROUP * CAP, feats), lambda i: (i, 0)),
            pl.BlockSpec((wide // width, wide), whole),
        ],
        out_shape=[
            jax.ShapeDtypeStruct((slots, feats), jnp.bfloat16),
            jax.ShapeDtypeStruct((wide // width, wide), jnp.float32),
        ],
        scratch_shapes=[
            pltpu.VMEM((width, feats), jnp.float32),
            pltpu.VMEM((1, feats), jnp.float32),
            pltpu.VMEM((width, CAP), jnp.float32),
            pltpu.VMEM((width, wide), jnp.float32),
        ],
        compiler_params=pltpu.CompilerParams(vmem_limit_bytes=VMEM_SOME),
        cost_estimate=pl.CostEstimate(
            flops=2 * slots * feats * (owned + feats), bytes_accessed=4 * slots * feats, transcendentals=0
        ),
        name="encode",
    )(me.reshape(1), got, got, basis, centroids, rotation)


def local(embeddings, basis, list_owner, list_slot, centroids, rotation):
    width = lax.axis_size("wide")
    me = lax.axis_index("wide")
    rows_here, wide = embeddings.shape
    feats = basis.shape[1]
    total = rows_here * width

    stages = halving_stages(width)
    keep, send, mean = moments(width, me, embeddings)
    came = exchange(width, stages[0], [send])
    yb, targets, lists, notes = project(width, embeddings, basis, list_owner, list_slot, mean)
    keep, *out = add_and_split(keep, came, 1 << len(stages[1]), after=[notes])
    rows = sort(yb, targets, lists, notes, out[0])
    got = lax.all_to_all(rows.reshape(width, SPAN, feats), "wide", split_axis=0, concat_axis=0, tiled=True)
    for n in range(1, len(stages)):
        came = exchange(width, stages[n], out)
        if n + 1 < len(stages):
            keep, *out = add_and_split(keep, came, 1 << len(stages[n + 1]))
    encoded, between = encode(width, total, me, got.reshape(width * SPAN, feats), basis, centroids, rotation)
    for block in came:
        keep = keep + block.astype(jnp.float32)
    covariance = (keep + between) / total
    return (encoded, covariance)


def solution(mesh):
    in_specs = (
        P(("groups", "wide"), None),
        P(),
        P(("groups", "wide")),
        P(("groups", "wide")),
        P("wide", None),
        P(),
    )
    out_specs = (P(("groups", "wide"), None), P(("groups", "wide"), None))
    return jax.shard_map(local, mesh=mesh, in_specs=in_specs, out_specs=out_specs, check_vma=False)
```

```python
import functools

import jax
import jax.numpy as jnp
from jax import lax
from jax.experimental import pallas as pl
from jax.experimental.pallas import tpu as pltpu
from jax.sharding import PartitionSpec as P

CAP = 128
LANES = 128
NOTES = 16
SPAN = CAP + NOTES
CHUNK = 512
TILE = 256
GROUP = 4
VMEM_SOME = 24 * 1024 * 1024
VMEM_MOST = 57 * 1024 * 1024
VMEM_MUCH = 48 * 1024 * 1024


def in_three(x):
    high = x.astype(jnp.bfloat16).astype(jnp.float32)
    rest = x - high
    middle = rest.astype(jnp.bfloat16).astype(jnp.float32)
    return high, middle, (rest - middle).astype(jnp.bfloat16).astype(jnp.float32)


def rows_kernel(
    width, e_hbm, basis_hbm, owner_ref, slot_ref,
    rows_hbm, mean_ref,
    e_ref, basis_ref, y_ref, yb_ref, pick_ref, rows_ref, list_ref, e_sem, basis_sem, rows_sem,
):
    rows_here, wide = e_ref.shape
    feats = basis_ref.shape[1]
    chunks = rows_here // LANES
    parts = rows_here // CHUNK

    e_copies = []
    for c in range(parts):
        at = pl.ds(c * CHUNK, CHUNK)
        e_copies.append(pltpu.make_async_copy(e_hbm.at[at], e_ref.at[at], e_sem.at[c]))
        e_copies[c].start()
        if c == 0:
            basis_copy = pltpu.make_async_copy(basis_hbm, basis_ref, basis_sem)
            basis_copy.start()

    owner = owner_ref[...]
    wanted = lax.broadcasted_iota(jnp.int32, (width, LANES), 0)
    hits = [jnp.where(owner[c:c + 1, :] == wanted, 1.0, 0.0) for c in range(chunks)]
    flat = jnp.concatenate(hits, 0).astype(jnp.bfloat16)
    up = lax.broadcasted_iota(jnp.int32, (LANES, LANES), 0)
    to = lax.broadcasted_iota(jnp.int32, (LANES, LANES), 1)
    before = jnp.where(up < to, 1.0, 0.0).astype(jnp.bfloat16)
    every = jnp.ones((LANES, LANES), jnp.bfloat16)
    within = jnp.dot(flat, before, preferred_element_type=jnp.float32)
    counts = jnp.dot(flat, every, preferred_element_type=jnp.float32)
    carry = jnp.zeros((width, LANES), jnp.float32)
    ranks, targets = [], []
    for c in range(chunks):
        at = slice(c * width, (c + 1) * width)
        ranks.append(jnp.sum(hits[c] * (within[at] + carry), 0, keepdims=True).astype(jnp.int32))
        carry = carry + counts[at]
        targets.append(owner[c:c + 1, :] * CAP + ranks[c])
    slot = slot_ref[...] + 1
    high, low = (slot >> 5).astype(jnp.float32), (slot & 31).astype(jnp.float32)
    spots = lax.broadcasted_iota(jnp.int32, (CAP, LANES), 0)
    placed = jnp.concatenate([jnp.where(ranks[c] == spots, 1.0, 0.0) for c in range(chunks)], 1).astype(jnp.bfloat16)
    digits = jnp.concatenate(
        [
            jnp.concatenate([hits[c] * high[c:c + 1, :] for c in range(chunks)], 1),
            jnp.concatenate([hits[c] * low[c:c + 1, :] for c in range(chunks)], 1),
        ],
        0,
    ).astype(jnp.bfloat16)
    found = lax.dot_general(digits, placed, (((1,), (1,)), ((), ())), preferred_element_type=jnp.float32)
    list_ref[:, :CAP] = found[:width]
    list_ref[:, CAP:] = found[width:]

    groups = width // GROUP
    held = pick_ref.shape[0]
    place = lax.broadcasted_iota(jnp.int32, (GROUP * CAP, LANES), 0).astype(jnp.int16)

    def pick_group(g, into):
        for c in range(chunks):
            aim = jnp.broadcast_to(targets[c] - g * (GROUP * CAP), (16, LANES)).astype(jnp.int16)
            aim = jnp.concatenate([aim] * (GROUP * CAP // 16), 0)
            pick_ref[into, :, c * LANES:(c + 1) * LANES] = jnp.where(
                aim == place, jnp.ones((), jnp.bfloat16), jnp.zeros((), jnp.bfloat16)
            )

    basis_copy.wait()
    sum_y = jnp.zeros((8, feats), jnp.float32)
    sum_e = jnp.zeros((8, wide), jnp.float32)
    for c in range(parts):
        at = slice(c * CHUNK, (c + 1) * CHUNK)
        e_copies[c].wait()
        rows = e_ref[at, :]
        y = jnp.dot(rows, basis_ref[...], preferred_element_type=jnp.float32)
        y_ref[at, :] = y
        sum_y = sum_y + jnp.sum(y.reshape(CHUNK // 8, 8, feats), 0)
        sum_e = sum_e + jnp.sum(rows.astype(jnp.float32).reshape(CHUNK // 8, 8, wide), 0)
        if c < held:
            pick_group(c, c)

    mean_y = jnp.sum(sum_y, 0, keepdims=True) / rows_here
    square = jnp.zeros((8, feats), jnp.float32)
    for c in range(parts):
        at = slice(c * CHUNK, (c + 1) * CHUNK)
        centred = y_ref[at, :] - mean_y
        square = square + jnp.sum((centred * centred).reshape(CHUNK // 8, 8, feats), 0)
        yb_ref[at, :] = centred.astype(jnp.bfloat16)
    mean = jnp.sum(sum_e, 0, keepdims=True) / rows_here
    mean_ref[...] = mean
    common = [part[:, q * feats:(q + 1) * feats] for part in in_three(mean) for q in range(wide // feats)]
    common = jnp.concatenate(common + list(in_three(jnp.sum(square, 0, keepdims=True))), 0)

    def sort_group(g, into):
        rows = jnp.dot(pick_ref[into], yb_ref[...], preferred_element_type=jnp.float32).astype(jnp.bfloat16)
        for j in range(GROUP):
            base = pl.multiple_of((g * GROUP + j) * SPAN, 16)
            rows_ref[pl.ds(base, CAP), :] = rows[j * CAP:(j + 1) * CAP]
            notes = jnp.concatenate([common, list_ref[pl.ds(g * GROUP + j, 1), :]], 0)
            rows_ref[pl.ds(pl.multiple_of(base + CAP, 16), NOTES), :] = notes.astype(jnp.bfloat16)
        at = pl.ds(pl.multiple_of(g * (GROUP * SPAN), 16), GROUP * SPAN)
        return pltpu.make_async_copy(rows_ref.at[at], rows_hbm.at[at], rows_sem.at[into])

    if groups <= held:
        copies = []
        for g in range(groups):
            copies.append(sort_group(g, g))
            copies[g].start()
        for copy in copies:
            copy.wait()
    else:

        @pl.loop(0, groups)
        def _(g):
            pick_group(g, 0)
            copy = sort_group(g, 0)
            copy.start()
            copy.wait()


def project_and_sort(width, embeddings, basis, list_owner, list_slot):
    rows_here, wide = embeddings.shape
    feats = basis.shape[1]
    lanes = rows_here // LANES
    slots = width * SPAN
    groups = width // GROUP
    held = groups if groups <= rows_here // CHUNK else 1
    vmem, anywhere = pl.BlockSpec(memory_space=pltpu.VMEM), pl.BlockSpec(memory_space=pl.ANY)
    return pl.pallas_call(
        functools.partial(rows_kernel, width),
        in_specs=[anywhere, anywhere, vmem, vmem],
        out_specs=[anywhere, vmem],
        out_shape=[jax.ShapeDtypeStruct((slots, feats), jnp.bfloat16), jax.ShapeDtypeStruct((1, wide), jnp.float32)],
        scratch_shapes=[
            pltpu.VMEM((rows_here, wide), jnp.bfloat16),
            pltpu.VMEM((wide, feats), jnp.bfloat16),
            pltpu.VMEM((rows_here, feats), jnp.float32),
            pltpu.VMEM((rows_here, feats), jnp.bfloat16),
            pltpu.VMEM((held, GROUP * CAP, rows_here), jnp.bfloat16),
            pltpu.VMEM((slots, feats), jnp.bfloat16),
            pltpu.VMEM((width, 2 * CAP), jnp.float32),
            pltpu.SemaphoreType.DMA((rows_here // CHUNK,)),
            pltpu.SemaphoreType.DMA,
            pltpu.SemaphoreType.DMA((held,)),
        ],
        compiler_params=pltpu.CompilerParams(vmem_limit_bytes=VMEM_MOST),
        cost_estimate=pl.CostEstimate(
            flops=2 * rows_here * feats * (wide + slots), bytes_accessed=2 * rows_here * wide + 2 * slots * feats, transcendentals=0
        ),
        name="project_sort",
    )(embeddings, basis, list_owner.reshape(lanes, LANES), list_slot.reshape(lanes, LANES))


def moments_kernel(
    width, me_ref, mean_hbm, e_hbm, keep_hbm, send_hbm, e_ref, mean_ref, m_ref, e_sem, mean_sem, block_sem
):
    rows_here, wide = e_ref.shape
    block = wide // width
    bits = width.bit_length() - 1
    parts = rows_here // CHUNK
    tiles = wide // TILE
    e_copies = []
    for c in range(parts):
        at = pl.ds(c * CHUNK, CHUNK)
        e_copies.append(pltpu.make_async_copy(e_hbm.at[at], e_ref.at[at], e_sem.at[c]))
        e_copies[c].start()
    mean_copy = pltpu.make_async_copy(mean_hbm, mean_ref, mean_sem)
    mean_copy.start()
    me = me_ref[0]
    copies = []
    for t in range(tiles):
        rows, columns = slice(t * TILE, (t + 1) * TILE), slice(t * TILE, wide)
        if t == 0:
            product = jnp.zeros((TILE, wide), jnp.float32)
            for c in range(parts):
                e_copies[c].wait()
                at = slice(c * CHUNK, (c + 1) * CHUNK)
                product = product + lax.dot_general(
                    e_ref[at, rows], e_ref[at, :], (((0,), (0,)), ((), ())), preferred_element_type=jnp.float32
                )
            mean_copy.wait()
            mean = mean_ref[...]
        else:
            product = lax.dot_general(
                e_ref[:, rows], e_ref[:, columns], (((0,), (0,)), ((), ())), preferred_element_type=jnp.float32
            )
        down = jnp.transpose(jnp.broadcast_to(mean[:, rows] * rows_here, (LANES, TILE)))
        for u in range(t, tiles):
            pieces = []
            for j in range(u * TILE // LANES, (u + 1) * TILE // LANES):
                across = slice(j * LANES, (j + 1) * LANES)
                within = slice(j * LANES - t * TILE, (j + 1) * LANES - t * TILE)
                pieces.append((product[:, within] - down * mean[:, across]).astype(jnp.bfloat16))
            piece = jnp.concatenate(pieces, 1)
            other = slice(u * TILE, (u + 1) * TILE)
            m_ref[rows, other] = piece
            if u > t:
                m_ref[other, rows] = jnp.transpose(piece)
        for pair in range(TILE // block // 2):
            first = t * (TILE // block) + 2 * pair
            apart = (first ^ me) >> 1
            spot = 0
            for k in range(bits - 1):
                spot = spot + (((apart >> k) & 1) << (bits - 2 - k))
            at = pl.ds(pl.multiple_of(spot * block, block), block)
            kept = pl.multiple_of((first + (me & 1)) * block, block)
            sent = pl.multiple_of((first + 1 - (me & 1)) * block, block)
            for here, there in ((kept, keep_hbm), (sent, send_hbm)):
                copy = pltpu.make_async_copy(m_ref.at[pl.ds(here, block)], there.at[at], block_sem.at[len(copies)])
                copy.start()
                copies.append(copy)
    for copy in copies:
        copy.wait()


def moments(width, me, embeddings, mean):
    rows_here, wide = embeddings.shape
    anywhere = pl.BlockSpec(memory_space=pl.ANY)
    return pl.pallas_call(
        functools.partial(moments_kernel, width),
        in_specs=[pl.BlockSpec(memory_space=pltpu.SMEM), anywhere, anywhere],
        out_specs=[anywhere] * 2,
        out_shape=[jax.ShapeDtypeStruct((wide // 2, wide), jnp.bfloat16)] * 2,
        scratch_shapes=[
            pltpu.VMEM((rows_here, wide), jnp.bfloat16),
            pltpu.VMEM((1, wide), jnp.float32),
            pltpu.VMEM((wide, wide), jnp.bfloat16),
            pltpu.SemaphoreType.DMA((rows_here // CHUNK,)),
            pltpu.SemaphoreType.DMA,
            pltpu.SemaphoreType.DMA((width,)),
        ],
        compiler_params=pltpu.CompilerParams(vmem_limit_bytes=VMEM_MUCH),
        cost_estimate=pl.CostEstimate(
            flops=2 * rows_here * wide * wide, bytes_accessed=2 * rows_here * wide + 2 * wide * wide, transcendentals=0
        ),
        name="moments",
    )(me.reshape(1), mean, embeddings)


def add_kernel(pieces, arrived, keep_ref, *refs):
    came, outs = refs[:arrived], refs[-pieces:]
    size = outs[0].shape[0]
    for p in range(pieces):
        at = slice(p * size, (p + 1) * size)
        held = keep_ref[at].astype(jnp.float32)
        for ref in came:
            held = held + ref[at].astype(jnp.float32)
        outs[p][...] = held.astype(outs[p].dtype)


def add_and_split(keep, came, pieces):
    rows, wide = keep.shape
    vmem = pl.BlockSpec(memory_space=pltpu.VMEM)
    return pl.pallas_call(
        functools.partial(add_kernel, pieces, len(came)),
        in_specs=[vmem] * (1 + len(came)),
        out_specs=[vmem] * pieces,
        out_shape=[
            jax.ShapeDtypeStruct((rows // pieces, wide), jnp.float32 if p == 0 else jnp.bfloat16) for p in range(pieces)
        ],
        compiler_params=pltpu.CompilerParams(vmem_limit_bytes=VMEM_SOME),
        cost_estimate=pl.CostEstimate(flops=2 * rows * wide, bytes_accessed=10 * rows * wide, transcendentals=0),
        name="add_and_split",
    )(keep, *came)


def partners(width, apart):
    return [(i, i ^ apart) for i in range(width)]


def halving_stages(width):
    strides = [1 << k for k in range(width.bit_length() - 1)]
    return [[s] for s in strides[:-2]] + [strides[-2:]]


def exchange(width, stage, out):
    came = []
    for p in range(1, 1 << len(stage)):
        apart = sum(s for k, s in enumerate(stage) if (p >> (len(stage) - 1 - k)) & 1)
        came.append(lax.ppermute(out[p - 1], "wide", partners(width, apart)))
    return came


def encode_kernel(total, me_ref, got_ref, all_ref, basis_ref, centroid_ref, rotation_ref, out_ref, between_ref, delta_ref, scale_ref, list_ref, apart_ref):
    step = pl.program_id(0)
    width = delta_ref.shape[0]
    feats = out_ref.shape[1]
    owned = centroid_ref.shape[0]
    wide = basis_ref.shape[0]
    block = wide // width
    share = total // width

    @pl.when(step == 0)
    def _():
        notes = jnp.concatenate([all_ref[s * SPAN + CAP:(s + 1) * SPAN, :] for s in range(width)], 0)
        size = width * NOTES
        to = lax.broadcasted_iota(jnp.int32, (size, size), 0)
        of = lax.broadcasted_iota(jnp.int32, (size, size), 1)
        turn = jnp.where((to % width) * NOTES + to // width == of, 1.0, 0.0).astype(jnp.bfloat16)
        turned = jnp.dot(turn, notes, preferred_element_type=jnp.float32)
        row = [turned[r * width:(r + 1) * width] for r in range(NOTES)]
        quarters = wide // feats
        shifts = jnp.zeros((width, feats), jnp.float32)
        for q in range(quarters):
            parts = [row[p * quarters + q] for p in range(3)]
            mean = parts[0] + (parts[1] + parts[2])
            apart_ref[:, q * feats:(q + 1) * feats] = mean - jnp.mean(mean, 0, keepdims=True)
            terms = jnp.dot(
                jnp.concatenate(parts, 0).astype(jnp.bfloat16),
                basis_ref[q * feats:(q + 1) * feats, :],
                preferred_element_type=jnp.float32,
            )
            shifts = shifts + (terms[:width] + (terms[width:2 * width] + terms[2 * width:]))
        square = row[3 * quarters] + (row[3 * quarters + 1] + row[3 * quarters + 2])
        delta = shifts - jnp.mean(shifts, 0, keepdims=True)
        variance = jnp.sum(square + share * (delta * delta), 0, keepdims=True) / total
        scale_ref[...] = lax.rsqrt(variance + 1e-05)
        delta_ref[...] = delta
        digits = row[NOTES - 1]
        list_ref[...] = digits[:, :CAP] * 32.0 + digits[:, CAP:] - 1.0

        me = me_ref[0]
        first = me * block
        near = apart_ref[:, pl.ds(pl.multiple_of(first // LANES * LANES, LANES), LANES)]
        near = pltpu.roll(near, (LANES - first % LANES) % LANES, 1)[:, :block]
        between_ref[...] = share * lax.dot_general(
            near,
            apart_ref[...],
            (((0,), (0,)), ((), ())),
            precision=lax.Precision.HIGHEST,
            preferred_element_type=jnp.float32,
        )

    columns = jnp.transpose(list_ref[pl.ds(step * GROUP, GROUP), :])
    names = lax.broadcasted_iota(jnp.int32, (CAP, owned), 1).astype(jnp.int16)
    hits, projected, held = [], [], []
    for s in range(GROUP):
        listed = jnp.broadcast_to(columns[:, s:s + 1], (CAP, LANES))
        held.append(jnp.concatenate([listed] * (feats // LANES), 1) >= 0)
        wanted = jnp.concatenate([listed.astype(jnp.int32).astype(jnp.int16)] * (owned // LANES), 1)
        hits.append(jnp.where(wanted == names, jnp.ones((), jnp.bfloat16), jnp.zeros((), jnp.bfloat16)))
        rows = got_ref[s * SPAN:s * SPAN + CAP, :].astype(jnp.float32)
        projected.append((rows + delta_ref[pl.ds(step * GROUP + s, 1), :]) * scale_ref[...])
    centre = jnp.dot(jnp.concatenate(hits, 0), centroid_ref[...], preferred_element_type=jnp.float32)
    residual = jnp.where(jnp.concatenate(held, 0), jnp.concatenate(projected, 0) - centre, 0.0)
    out_ref[...] = jnp.dot(
        residual.astype(jnp.bfloat16), rotation_ref[...], preferred_element_type=jnp.float32
    ).astype(jnp.bfloat16)


def encode(width, total, me, got, basis, centroids, rotation):
    wide, feats = basis.shape
    owned = centroids.shape[0]
    slots = width * CAP
    whole = lambda i: (0, 0)
    return pl.pallas_call(
        functools.partial(encode_kernel, total),
        grid=(width // GROUP,),
        in_specs=[
            pl.BlockSpec(memory_space=pltpu.SMEM),
            pl.BlockSpec((GROUP * SPAN, feats), lambda i: (i, 0)),
            pl.BlockSpec((width * SPAN, feats), whole),
            pl.BlockSpec((wide, feats), whole),
            pl.BlockSpec((owned, feats), whole),
            pl.BlockSpec((feats, feats), whole),
        ],
        out_specs=[
            pl.BlockSpec((GROUP * CAP, feats), lambda i: (i, 0)),
            pl.BlockSpec((wide // width, wide), whole),
        ],
        out_shape=[
            jax.ShapeDtypeStruct((slots, feats), jnp.bfloat16),
            jax.ShapeDtypeStruct((wide // width, wide), jnp.float32),
        ],
        scratch_shapes=[
            pltpu.VMEM((width, feats), jnp.float32),
            pltpu.VMEM((1, feats), jnp.float32),
            pltpu.VMEM((width, CAP), jnp.float32),
            pltpu.VMEM((width, wide), jnp.float32),
        ],
        compiler_params=pltpu.CompilerParams(vmem_limit_bytes=VMEM_SOME),
        cost_estimate=pl.CostEstimate(
            flops=2 * slots * feats * (owned + feats), bytes_accessed=4 * slots * feats, transcendentals=0
        ),
        name="encode",
    )(me.reshape(1), got, got, basis, centroids, rotation)


def local(embeddings, basis, list_owner, list_slot, centroids, rotation):
    width = lax.axis_size("wide")
    me = lax.axis_index("wide")
    rows_here, wide = embeddings.shape
    feats = basis.shape[1]
    total = rows_here * width

    rows, mean = project_and_sort(width, embeddings, basis, list_owner, list_slot)
    got = lax.all_to_all(rows.reshape(width, SPAN, feats), "wide", split_axis=0, concat_axis=0, tiled=True)
    stages = halving_stages(width)
    keep, *out = moments(width, me, embeddings, mean)
    for n, stage in enumerate(stages):
        came = exchange(width, stage, out)
        if n + 1 < len(stages):
            keep, *out = add_and_split(keep, came, 1 << len(stages[n + 1]))
    encoded, between = encode(width, total, me, got.reshape(width * SPAN, feats), basis, centroids, rotation)
    for block in came:
        keep = keep + block.astype(jnp.float32)
    covariance = (keep + between) / total
    return (encoded, covariance)


def solution(mesh):
    in_specs = (
        P(("groups", "wide"), None),
        P(),
        P(("groups", "wide")),
        P(("groups", "wide")),
        P("wide", None),
        P(),
    )
    out_specs = (P(("groups", "wide"), None), P(("groups", "wide"), None))
    return jax.shard_map(local, mesh=mesh, in_specs=in_specs, out_specs=out_specs, check_vma=False)
```

```python
import functools

import jax
import jax.numpy as jnp
from jax import lax
from jax.experimental import pallas as pl
from jax.experimental.pallas import tpu as pltpu
from jax.sharding import PartitionSpec as P

CAP = 128
LANES = 128
NOTES = 16
SPAN = CAP + NOTES
CHUNK = 512
TILE = 256
GROUP = 4
SHARES = 2
VMEM_ALL = 60 * 1024 * 1024
VMEM_SOME = 24 * 1024 * 1024
VMEM_MOST = 48 * 1024 * 1024


def in_three(x):
    high = x.astype(jnp.bfloat16).astype(jnp.float32)
    rest = x - high
    middle = rest.astype(jnp.bfloat16).astype(jnp.float32)
    return high, middle, (rest - middle).astype(jnp.bfloat16).astype(jnp.float32)


def rows_kernel(
    width, e_hbm, basis_ref, owner_ref, slot_ref,
    rows_hbm, mean_ref,
    e_ref, rows_ref, y_ref, yb_ref, sum_ref, total_ref, target_ref, list_ref, e_sem, sem,
):
    step = pl.program_id(0)
    rows_here, feats = y_ref.shape
    wide = e_ref.shape[1]
    chunks = rows_here // LANES

    def e_copy(c):
        at = pl.ds(pl.multiple_of(c * CHUNK, CHUNK), CHUNK)
        return pltpu.make_async_copy(e_hbm.at[at], e_ref.at[at], e_sem.at[c])

    @pl.when(step == 0)
    def _():
        for c in range(rows_here // CHUNK):
            e_copy(c).start()
        sum_ref[...] = jnp.zeros_like(sum_ref)
        total_ref[...] = jnp.zeros_like(total_ref)
        owner = owner_ref[...]
        wanted = lax.broadcasted_iota(jnp.int32, (width, LANES), 0)
        hits = [jnp.where(owner[c:c + 1, :] == wanted, 1.0, 0.0) for c in range(chunks)]
        flat = jnp.concatenate(hits, 0).astype(jnp.bfloat16)
        up = lax.broadcasted_iota(jnp.int32, (LANES, LANES), 0)
        to = lax.broadcasted_iota(jnp.int32, (LANES, LANES), 1)
        before = jnp.where(up < to, 1.0, 0.0).astype(jnp.bfloat16)
        every = jnp.ones((LANES, LANES), jnp.bfloat16)
        within = jnp.dot(flat, before, preferred_element_type=jnp.float32)
        counts = jnp.dot(flat, every, preferred_element_type=jnp.float32)
        carry = jnp.zeros((width, LANES), jnp.float32)
        ranks = []
        for c in range(chunks):
            at = slice(c * width, (c + 1) * width)
            ranks.append(jnp.sum(hits[c] * (within[at] + carry), 0, keepdims=True).astype(jnp.int32))
            carry = carry + counts[at]
            target_ref[c:c + 1, :] = owner[c:c + 1, :] * CAP + ranks[c]

        slot = slot_ref[...] + 1
        high, low = (slot >> 5).astype(jnp.float32), (slot & 31).astype(jnp.float32)
        spots = lax.broadcasted_iota(jnp.int32, (CAP, LANES), 0)
        placed = jnp.concatenate([jnp.where(ranks[c] == spots, 1.0, 0.0) for c in range(chunks)], 1).astype(jnp.bfloat16)
        digits = jnp.concatenate(
            [
                jnp.concatenate([hits[c] * high[c:c + 1, :] for c in range(chunks)], 1),
                jnp.concatenate([hits[c] * low[c:c + 1, :] for c in range(chunks)], 1),
            ],
            0,
        ).astype(jnp.bfloat16)
        found = lax.dot_general(digits, placed, (((1,), (1,)), ((), ())), preferred_element_type=jnp.float32)
        list_ref[:, :CAP] = found[:width]
        list_ref[:, CAP:] = found[width:]

    e_copy(step).wait()
    here = pl.ds(pl.multiple_of(step * CHUNK, CHUNK), CHUNK)
    rows = e_ref[here, :]
    y = jnp.dot(rows, basis_ref[...], preferred_element_type=jnp.float32)
    y_ref[here, :] = y
    sum_ref[...] += jnp.sum(y.reshape(CHUNK // 8, 8, feats), 0)
    total_ref[...] += jnp.sum(rows.astype(jnp.float32).reshape(CHUNK // 8, 8, wide), 0)

    @pl.when(step == pl.num_programs(0) - 1)
    def _():
        mean_y = jnp.sum(sum_ref[...], 0, keepdims=True) / rows_here
        square = jnp.zeros((8, feats), jnp.float32)
        for c in range(rows_here // CHUNK):
            at = slice(c * CHUNK, (c + 1) * CHUNK)
            centred = y_ref[at, :] - mean_y
            square = square + jnp.sum((centred * centred).reshape(CHUNK // 8, 8, feats), 0)
            yb_ref[at, :] = centred.astype(jnp.bfloat16)
        mean = jnp.sum(total_ref[...], 0, keepdims=True) / rows_here
        mean_ref[...] = mean
        parts = in_three(mean)
        common = [part[:, q * feats:(q + 1) * feats] for part in parts for q in range(wide // feats)]
        common = jnp.concatenate(common + list(in_three(jnp.sum(square, 0, keepdims=True))), 0)

        place = lax.broadcasted_iota(jnp.int32, (GROUP * CAP, LANES), 0).astype(jnp.int16)

        def sort_group(g):
            first = g * GROUP
            pieces = []
            for c in range(chunks):
                wanted = (target_ref[c:c + 1, :] - first * CAP).astype(jnp.int32)
                wanted = jnp.broadcast_to(wanted, (16, LANES)).astype(jnp.int16)
                wanted = jnp.concatenate([wanted] * (GROUP * CAP // 16), 0)
                pieces.append(jnp.where(wanted == place, jnp.ones((), jnp.bfloat16), jnp.zeros((), jnp.bfloat16)))
            pick = jnp.concatenate(pieces, 1)
            rows = jnp.dot(pick, yb_ref[...], preferred_element_type=jnp.float32).astype(jnp.bfloat16)
            for j in range(GROUP):
                base = pl.multiple_of((first + j) * SPAN, 16)
                rows_ref[pl.ds(base, CAP), :] = rows[j * CAP:(j + 1) * CAP]
                notes = jnp.concatenate([common, list_ref[pl.ds(first + j, 1), :]], 0)
                rows_ref[pl.ds(pl.multiple_of(base + CAP, 16), NOTES), :] = notes.astype(jnp.bfloat16)
            at = pl.ds(pl.multiple_of(g * (GROUP * SPAN), 16), GROUP * SPAN)
            return pltpu.make_async_copy(rows_ref.at[at], rows_hbm.at[at], sem.at[g])

        groups = width // GROUP
        if groups <= 4:
            copies = []
            for g in range(groups):
                copies.append(sort_group(g))
                copies[g].start()
            for copy in copies:
                copy.wait()
        else:

            @pl.loop(0, groups)
            def _(g):
                copy = sort_group(g)
                copy.start()
                copy.wait()


def project_and_sort(width, embeddings, basis, list_owner, list_slot):
    rows_here, wide = embeddings.shape
    feats = basis.shape[1]
    lanes = rows_here // LANES
    slots = width * SPAN
    return pl.pallas_call(
        functools.partial(rows_kernel, width),
        grid=(rows_here // CHUNK,),
        in_specs=[
            pl.BlockSpec(memory_space=pl.ANY),
            pl.BlockSpec((wide, feats), lambda i: (0, 0)),
            pl.BlockSpec((lanes, LANES), lambda i: (0, 0)),
            pl.BlockSpec((lanes, LANES), lambda i: (0, 0)),
        ],
        out_specs=[
            pl.BlockSpec(memory_space=pl.ANY),
            pl.BlockSpec((1, wide), lambda i: (0, 0)),
        ],
        out_shape=[
            jax.ShapeDtypeStruct((slots, feats), jnp.bfloat16),
            jax.ShapeDtypeStruct((1, wide), jnp.float32),
        ],
        scratch_shapes=[
            pltpu.VMEM((rows_here, wide), jnp.bfloat16),
            pltpu.VMEM((slots, feats), jnp.bfloat16),
            pltpu.VMEM((rows_here, feats), jnp.float32),
            pltpu.VMEM((rows_here, feats), jnp.bfloat16),
            pltpu.VMEM((8, feats), jnp.float32),
            pltpu.VMEM((8, wide), jnp.float32),
            pltpu.VMEM((lanes, LANES), jnp.int32),
            pltpu.VMEM((width, 2 * CAP), jnp.float32),
            pltpu.SemaphoreType.DMA((rows_here // CHUNK,)),
            pltpu.SemaphoreType.DMA((width // GROUP,)),
        ],
        compiler_params=pltpu.CompilerParams(vmem_limit_bytes=VMEM_ALL),
        cost_estimate=pl.CostEstimate(
            flops=2 * rows_here * feats * (wide + slots), bytes_accessed=2 * rows_here * wide + 2 * slots * feats, transcendentals=0
        ),
        name="project_sort",
    )(embeddings, basis, list_owner.reshape(lanes, LANES), list_slot.reshape(lanes, LANES))


def moments_kernel(width, me_ref, mean_hbm, e_hbm, keep_ref, send_ref, e_ref, mean_ref, m_ref, sem, mean_sem):
    rows_here, wide = e_ref.shape
    block = wide // width
    bits = width.bit_length() - 1
    mean_copy = pltpu.make_async_copy(mean_hbm, mean_ref, mean_sem)
    mean_copy.start()
    copies = []
    for c in range(rows_here // CHUNK):
        at = pl.ds(c * CHUNK, CHUNK)
        copies.append(pltpu.make_async_copy(e_hbm.at[at], e_ref.at[at], sem.at[c]))
        copies[c].start()
    me = me_ref[0]
    mean_copy.wait()
    mean = mean_ref[...]
    for t in range(wide // TILE):
        rows = slice(t * TILE, (t + 1) * TILE)
        if t == 0:
            product = jnp.zeros((TILE, wide), jnp.float32)
            for c in range(rows_here // CHUNK):
                copies[c].wait()
                at = slice(c * CHUNK, (c + 1) * CHUNK)
                product = product + lax.dot_general(
                    e_ref[at, rows], e_ref[at, :], (((0,), (0,)), ((), ())), preferred_element_type=jnp.float32
                )
        else:
            product = lax.dot_general(
                e_ref[:, rows], e_ref[...], (((0,), (0,)), ((), ())), preferred_element_type=jnp.float32
            )
        down = jnp.transpose(jnp.broadcast_to(mean[:, rows] * rows_here, (LANES, TILE)))
        for j in range(wide // LANES):
            across = slice(j * LANES, (j + 1) * LANES)
            m_ref[rows, across] = product[:, across] - down * mean[:, across]
        for pair in range(TILE // block // 2):
            first = t * (TILE // block) + 2 * pair
            apart = (first ^ me) >> 1
            place = 0
            for k in range(bits - 1):
                place = place + (((apart >> k) & 1) << (bits - 2 - k))
            to = pl.ds(pl.multiple_of(place * block, block), block)
            kept = pl.multiple_of((first + (me & 1)) * block, block)
            sent = pl.multiple_of((first + 1 - (me & 1)) * block, block)
            keep_ref[to, :] = m_ref[pl.ds(kept, block), :]
            send_ref[to, :] = m_ref[pl.ds(sent, block), :].astype(jnp.bfloat16)


def moments(width, me, embeddings, mean):
    rows_here, wide = embeddings.shape
    vmem = pl.BlockSpec(memory_space=pltpu.VMEM)
    return pl.pallas_call(
        functools.partial(moments_kernel, width),
        in_specs=[pl.BlockSpec(memory_space=pltpu.SMEM)] + [pl.BlockSpec(memory_space=pl.ANY)] * 2,
        out_specs=[vmem] * 2,
        out_shape=[
            jax.ShapeDtypeStruct((wide // 2, wide), jnp.float32),
            jax.ShapeDtypeStruct((wide // 2, wide), jnp.bfloat16),
        ],
        scratch_shapes=[
            pltpu.VMEM((rows_here, wide), jnp.bfloat16),
            pltpu.VMEM((1, wide), jnp.float32),
            pltpu.VMEM((wide, wide), jnp.float32),
            pltpu.SemaphoreType.DMA((rows_here // CHUNK,)),
            pltpu.SemaphoreType.DMA,
        ],
        compiler_params=pltpu.CompilerParams(vmem_limit_bytes=VMEM_MOST),
        cost_estimate=pl.CostEstimate(
            flops=2 * rows_here * wide * wide, bytes_accessed=2 * rows_here * wide + 3 * wide * wide, transcendentals=0
        ),
        name="moments",
    )(me.reshape(1), mean, embeddings)


def add_kernel(shares, pieces, keep_ref, *refs):
    outs = refs[len(refs) - shares * pieces:]
    came = refs[:len(refs) - shares * pieces]
    rows, columns = outs[0].shape
    for h in range(shares):
        across = slice(h * columns, (h + 1) * columns)
        for p in range(pieces):
            at = slice(p * rows, (p + 1) * rows)
            held = keep_ref[at, across]
            for ref in came:
                held = held + ref[at, across].astype(jnp.float32)
            out = outs[h * pieces + p]
            out[...] = held.astype(out.dtype)


def add_and_split(keep, came, shares, pieces):
    rows, columns = keep.shape
    vmem = pl.BlockSpec(memory_space=pltpu.VMEM)
    shape = (rows // pieces, columns // shares)
    kinds = [jnp.float32] + [jnp.bfloat16] * (pieces - 1)
    outs = pl.pallas_call(
        functools.partial(add_kernel, shares, pieces),
        in_specs=[vmem] * (1 + len(came)),
        out_specs=[vmem] * (shares * pieces),
        out_shape=[jax.ShapeDtypeStruct(shape, kind) for kind in kinds * shares],
        compiler_params=pltpu.CompilerParams(vmem_limit_bytes=VMEM_SOME),
        cost_estimate=pl.CostEstimate(flops=2 * rows * columns, bytes_accessed=10 * rows * columns, transcendentals=0),
        name="add_and_split",
    )(keep, *came)
    return [outs[h * pieces:(h + 1) * pieces] for h in range(shares)]


def finish_kernel(total, between_ref, *refs):
    out_ref = refs[-1]
    each = (len(refs) - 1) // SHARES
    columns = out_ref.shape[1] // SHARES
    for h in range(SHARES):
        across = slice(h * columns, (h + 1) * columns)
        held = refs[h * each][...]
        for ref in refs[h * each + 1:(h + 1) * each]:
            held = held + ref[...].astype(jnp.float32)
        out_ref[:, across] = (held + between_ref[:, across]) / total


def finish(total, between, keeps, came):
    parts = [part for keep, pieces in zip(keeps, came) for part in (keep, *pieces)]
    vmem = pl.BlockSpec(memory_space=pltpu.VMEM)
    return pl.pallas_call(
        functools.partial(finish_kernel, total),
        in_specs=[vmem] * (1 + len(parts)),
        out_specs=vmem,
        out_shape=jax.ShapeDtypeStruct(between.shape, jnp.float32),
        compiler_params=pltpu.CompilerParams(vmem_limit_bytes=VMEM_SOME),
        cost_estimate=pl.CostEstimate(flops=8 * between.size, bytes_accessed=16 * between.size, transcendentals=0),
        name="finish",
    )(between, *parts)


def halving_stages(width):
    strides = [1 << k for k in range(width.bit_length() - 1)]
    return [[s] for s in strides[:-2]] + [strides[-2:]]


def exchange(width, stage, out):
    came = []
    for p in range(1, 1 << len(stage)):
        apart = sum(s for k, s in enumerate(stage) if (p >> (len(stage) - 1 - k)) & 1)
        came.append(lax.ppermute(out[p - 1], "wide", [(i, i ^ apart) for i in range(width)]))
    return came


def encode_kernel(total, me_ref, got_ref, all_ref, basis_ref, centroid_ref, rotation_ref, *refs):
    out_ref, between_ref, delta_ref, scale_ref, list_ref, apart_ref = refs[-6:]
    step = pl.program_id(0)
    width = delta_ref.shape[0]
    feats = out_ref.shape[1]
    owned = centroid_ref.shape[0]
    wide = basis_ref.shape[0]
    block = wide // width
    share = total // width

    @pl.when(step == 0)
    def _():
        notes = jnp.concatenate([all_ref[s * SPAN + CAP:(s + 1) * SPAN, :] for s in range(width)], 0)
        size = width * NOTES
        to = lax.broadcasted_iota(jnp.int32, (size, size), 0)
        of = lax.broadcasted_iota(jnp.int32, (size, size), 1)
        turn = jnp.where((to % width) * NOTES + to // width == of, 1.0, 0.0).astype(jnp.bfloat16)
        turned = jnp.dot(turn, notes, preferred_element_type=jnp.float32)
        row = [turned[r * width:(r + 1) * width] for r in range(NOTES)]
        quarters = wide // feats
        shifts = jnp.zeros((width, feats), jnp.float32)
        for q in range(quarters):
            parts = [row[p * quarters + q] for p in range(3)]
            mean = parts[0] + (parts[1] + parts[2])
            apart_ref[:, q * feats:(q + 1) * feats] = mean - jnp.mean(mean, 0, keepdims=True)
            terms = jnp.dot(
                jnp.concatenate(parts, 0).astype(jnp.bfloat16),
                basis_ref[q * feats:(q + 1) * feats, :],
                preferred_element_type=jnp.float32,
            )
            shifts = shifts + (terms[:width] + (terms[width:2 * width] + terms[2 * width:]))
        square = row[3 * quarters] + (row[3 * quarters + 1] + row[3 * quarters + 2])
        delta = shifts - jnp.mean(shifts, 0, keepdims=True)
        variance = jnp.sum(square + share * (delta * delta), 0, keepdims=True) / total
        scale_ref[...] = lax.rsqrt(variance + 1e-05)
        delta_ref[...] = delta
        digits = row[NOTES - 1]
        list_ref[...] = digits[:, :CAP] * 32.0 + digits[:, CAP:] - 1.0

        me = me_ref[0]
        first = me * block
        near = apart_ref[:, pl.ds(pl.multiple_of(first // LANES * LANES, LANES), LANES)]
        near = pltpu.roll(near, (LANES - first % LANES) % LANES, 1)[:, :block]
        between_ref[...] = share * lax.dot_general(
            near,
            apart_ref[...],
            (((0,), (0,)), ((), ())),
            precision=lax.Precision.HIGHEST,
            preferred_element_type=jnp.float32,
        )

    columns = jnp.transpose(list_ref[pl.ds(step * GROUP, GROUP), :])
    names = lax.broadcasted_iota(jnp.int32, (CAP, owned), 1).astype(jnp.int16)
    hits, projected, held = [], [], []
    for s in range(GROUP):
        listed = jnp.broadcast_to(columns[:, s:s + 1], (CAP, LANES))
        held.append(jnp.concatenate([listed] * (feats // LANES), 1) >= 0)
        wanted = jnp.concatenate([listed.astype(jnp.int32).astype(jnp.int16)] * (owned // LANES), 1)
        hits.append(jnp.where(wanted == names, jnp.ones((), jnp.bfloat16), jnp.zeros((), jnp.bfloat16)))
        rows = got_ref[s * SPAN:s * SPAN + CAP, :].astype(jnp.float32)
        projected.append((rows + delta_ref[pl.ds(step * GROUP + s, 1), :]) * scale_ref[...])
    centre = jnp.dot(jnp.concatenate(hits, 0), centroid_ref[...], preferred_element_type=jnp.float32)
    residual = jnp.where(jnp.concatenate(held, 0), jnp.concatenate(projected, 0) - centre, 0.0)
    out_ref[...] = jnp.dot(
        residual.astype(jnp.bfloat16), rotation_ref[...], preferred_element_type=jnp.float32
    ).astype(jnp.bfloat16)


def encode(width, total, me, got, basis, centroids, rotation, after):
    wide, feats = basis.shape
    owned = centroids.shape[0]
    slots = width * CAP
    whole = lambda i: (0, 0)
    return pl.pallas_call(
        functools.partial(encode_kernel, total),
        grid=(width // GROUP,),
        in_specs=[
            pl.BlockSpec(memory_space=pltpu.SMEM),
            pl.BlockSpec((GROUP * SPAN, feats), lambda i: (i, 0)),
            pl.BlockSpec((width * SPAN, feats), whole),
            pl.BlockSpec((wide, feats), whole),
            pl.BlockSpec((owned, feats), whole),
            pl.BlockSpec((feats, feats), whole),
        ]
        + [pl.BlockSpec(memory_space=pl.ANY)] * len(after),
        out_specs=[
            pl.BlockSpec((GROUP * CAP, feats), lambda i: (i, 0)),
            pl.BlockSpec((wide // width, wide), whole),
        ],
        out_shape=[
            jax.ShapeDtypeStruct((slots, feats), jnp.bfloat16),
            jax.ShapeDtypeStruct((wide // width, wide), jnp.float32),
        ],
        scratch_shapes=[
            pltpu.VMEM((width, feats), jnp.float32),
            pltpu.VMEM((1, feats), jnp.float32),
            pltpu.VMEM((width, CAP), jnp.float32),
            pltpu.VMEM((width, wide), jnp.float32),
        ],
        compiler_params=pltpu.CompilerParams(vmem_limit_bytes=VMEM_SOME),
        cost_estimate=pl.CostEstimate(
            flops=2 * slots * feats * (owned + feats), bytes_accessed=4 * slots * feats, transcendentals=0
        ),
        name="encode",
    )(me.reshape(1), got, got, basis, centroids, rotation, *after)


def local(embeddings, basis, list_owner, list_slot, centroids, rotation):
    width = lax.axis_size("wide")
    me = lax.axis_index("wide")
    rows_here, wide = embeddings.shape
    feats = basis.shape[1]
    total = rows_here * width

    rows, mean = project_and_sort(width, embeddings, basis, list_owner, list_slot)
    got = lax.all_to_all(rows.reshape(width, SPAN, feats), "wide", split_axis=0, concat_axis=0, tiled=True)

    keep, send = moments(width, me, embeddings, mean)
    stages = halving_stages(width)
    came = exchange(width, stages[0], [send])
    shares = add_and_split(keep, came, SHARES, 1 << len(stages[1]))
    last = []
    for share in shares:
        for n in range(1, len(stages) - 1):
            came = exchange(width, stages[n], share[1:])
            (share,) = add_and_split(share[0], came, 1, 1 << len(stages[n + 1]))
        last.append(share)
    came = [exchange(width, stages[-1], share[1:]) for share in last]
    encoded, between = encode(
        width, total, me, got.reshape(width * SPAN, feats), basis, centroids, rotation, [share[1] for share in last]
    )
    covariance = finish(total, between, [share[0] for share in last], came)
    return (encoded, covariance)


def solution(mesh):
    in_specs = (
        P(("groups", "wide"), None),
        P(),
        P(("groups", "wide")),
        P(("groups", "wide")),
        P("wide", None),
        P(),
    )
    out_specs = (P(("groups", "wide"), None), P(("groups", "wide"), None))
    return jax.shard_map(local, mesh=mesh, in_specs=in_specs, out_specs=out_specs, check_vma=False)
```

```python
import functools

import jax
import jax.numpy as jnp
from jax import lax
from jax.experimental import pallas as pl
from jax.experimental.pallas import tpu as pltpu
from jax.sharding import PartitionSpec as P

CAP = 128
LANES = 128
NOTES = 16
SPAN = CAP + NOTES
CHUNK = 512
TILE = 256
GROUP = 4
SHARES = 2
VMEM_ALL = 60 * 1024 * 1024
VMEM_SOME = 24 * 1024 * 1024
VMEM_MOST = 48 * 1024 * 1024


def in_three(x):
    high = x.astype(jnp.bfloat16).astype(jnp.float32)
    rest = x - high
    middle = rest.astype(jnp.bfloat16).astype(jnp.float32)
    return high, middle, (rest - middle).astype(jnp.bfloat16).astype(jnp.float32)


def rows_kernel(
    width, e_hbm, basis_hbm, owner_hbm, slot_hbm,
    rows_hbm, mean_hbm,
    owner_ref, slot_ref, mean_ref, basis_ref, e_ref, rows_ref, y_ref, yb_ref, sum_ref, total_ref, target_ref, list_ref, e_sem, small_sem, sem,
):
    step = pl.program_id(0)
    rows_here, feats = y_ref.shape
    wide = e_ref.shape[1]
    chunks = rows_here // LANES

    def e_copy(c):
        at = pl.ds(pl.multiple_of(c * CHUNK, CHUNK), CHUNK)
        return pltpu.make_async_copy(e_hbm.at[at], e_ref.at[at], e_sem.at[c])

    @pl.when(step == 0)
    def _():
        owner_copy = pltpu.make_async_copy(owner_hbm, owner_ref, small_sem.at[0])
        slot_copy = pltpu.make_async_copy(slot_hbm, slot_ref, small_sem.at[1])
        basis_copy = pltpu.make_async_copy(basis_hbm, basis_ref, small_sem.at[2])
        owner_copy.start()
        e_copy(0).start()
        slot_copy.start()
        basis_copy.start()
        for c in range(1, rows_here // CHUNK):
            e_copy(c).start()
        owner_copy.wait()
        sum_ref[...] = jnp.zeros_like(sum_ref)
        total_ref[...] = jnp.zeros_like(total_ref)
        owner = owner_ref[...]
        wanted = lax.broadcasted_iota(jnp.int32, (width, LANES), 0)
        hits = [jnp.where(owner[c:c + 1, :] == wanted, 1.0, 0.0) for c in range(chunks)]
        flat = jnp.concatenate(hits, 0).astype(jnp.bfloat16)
        up = lax.broadcasted_iota(jnp.int32, (LANES, LANES), 0)
        to = lax.broadcasted_iota(jnp.int32, (LANES, LANES), 1)
        before = jnp.where(up < to, 1.0, 0.0).astype(jnp.bfloat16)
        every = jnp.ones((LANES, LANES), jnp.bfloat16)
        within = jnp.dot(flat, before, preferred_element_type=jnp.float32)
        counts = jnp.dot(flat, every, preferred_element_type=jnp.float32)
        carry = jnp.zeros((width, LANES), jnp.float32)
        ranks = []
        for c in range(chunks):
            at = slice(c * width, (c + 1) * width)
            ranks.append(jnp.sum(hits[c] * (within[at] + carry), 0, keepdims=True).astype(jnp.int32))
            carry = carry + counts[at]
            target_ref[c:c + 1, :] = owner[c:c + 1, :] * CAP + ranks[c]

        slot_copy.wait()
        slot = slot_ref[...] + 1
        high, low = (slot >> 5).astype(jnp.float32), (slot & 31).astype(jnp.float32)
        spots = lax.broadcasted_iota(jnp.int32, (CAP, LANES), 0)
        placed = jnp.concatenate([jnp.where(ranks[c] == spots, 1.0, 0.0) for c in range(chunks)], 1).astype(jnp.bfloat16)
        digits = jnp.concatenate(
            [
                jnp.concatenate([hits[c] * high[c:c + 1, :] for c in range(chunks)], 1),
                jnp.concatenate([hits[c] * low[c:c + 1, :] for c in range(chunks)], 1),
            ],
            0,
        ).astype(jnp.bfloat16)
        found = lax.dot_general(digits, placed, (((1,), (1,)), ((), ())), preferred_element_type=jnp.float32)
        list_ref[:, :CAP] = found[:width]
        list_ref[:, CAP:] = found[width:]
        basis_copy.wait()

    e_copy(step).wait()
    here = pl.ds(pl.multiple_of(step * CHUNK, CHUNK), CHUNK)
    rows = e_ref[here, :]
    y = jnp.dot(rows, basis_ref[...], preferred_element_type=jnp.float32)
    y_ref[here, :] = y
    sum_ref[...] += jnp.sum(y.reshape(CHUNK // 8, 8, feats), 0)
    total_ref[...] += jnp.sum(rows.astype(jnp.float32).reshape(CHUNK // 8, 8, wide), 0)

    @pl.when(step == pl.num_programs(0) - 1)
    def _():
        mean_y = jnp.sum(sum_ref[...], 0, keepdims=True) / rows_here
        square = jnp.zeros((8, feats), jnp.float32)
        for c in range(rows_here // CHUNK):
            at = slice(c * CHUNK, (c + 1) * CHUNK)
            centred = y_ref[at, :] - mean_y
            square = square + jnp.sum((centred * centred).reshape(CHUNK // 8, 8, feats), 0)
            yb_ref[at, :] = centred.astype(jnp.bfloat16)
        mean = jnp.sum(total_ref[...], 0, keepdims=True) / rows_here
        mean_ref[...] = mean
        mean_copy = pltpu.make_async_copy(mean_ref, mean_hbm, small_sem.at[3])
        mean_copy.start()
        parts = in_three(mean)
        common = [part[:, q * feats:(q + 1) * feats] for part in parts for q in range(wide // feats)]
        common = jnp.concatenate(common + list(in_three(jnp.sum(square, 0, keepdims=True))), 0)

        place = lax.broadcasted_iota(jnp.int32, (GROUP * CAP, LANES), 0).astype(jnp.int16)

        def sort_group(g):
            first = g * GROUP
            pieces = []
            for c in range(chunks):
                wanted = (target_ref[c:c + 1, :] - first * CAP).astype(jnp.int32)
                wanted = jnp.broadcast_to(wanted, (16, LANES)).astype(jnp.int16)
                wanted = jnp.concatenate([wanted] * (GROUP * CAP // 16), 0)
                pieces.append(jnp.where(wanted == place, jnp.ones((), jnp.bfloat16), jnp.zeros((), jnp.bfloat16)))
            pick = jnp.concatenate(pieces, 1)
            rows = jnp.dot(pick, yb_ref[...], preferred_element_type=jnp.float32).astype(jnp.bfloat16)
            for j in range(GROUP):
                base = pl.multiple_of((first + j) * SPAN, 16)
                rows_ref[pl.ds(base, CAP), :] = rows[j * CAP:(j + 1) * CAP]
                notes = jnp.concatenate([common, list_ref[pl.ds(first + j, 1), :]], 0)
                rows_ref[pl.ds(pl.multiple_of(base + CAP, 16), NOTES), :] = notes.astype(jnp.bfloat16)
            at = pl.ds(pl.multiple_of(g * (GROUP * SPAN), 16), GROUP * SPAN)
            return pltpu.make_async_copy(rows_ref.at[at], rows_hbm.at[at], sem.at[g])

        groups = width // GROUP
        if groups <= 4:
            copies = []
            for g in range(groups):
                copies.append(sort_group(g))
                copies[g].start()
            for copy in copies:
                copy.wait()
        else:

            @pl.loop(0, groups)
            def _(g):
                copy = sort_group(g)
                copy.start()
                copy.wait()

        mean_copy.wait()


def project_and_sort(width, embeddings, basis, list_owner, list_slot):
    rows_here, wide = embeddings.shape
    feats = basis.shape[1]
    lanes = rows_here // LANES
    slots = width * SPAN
    return pl.pallas_call(
        functools.partial(rows_kernel, width),
        grid=(rows_here // CHUNK,),
        in_specs=[pl.BlockSpec(memory_space=pl.ANY)] * 4,
        out_specs=[pl.BlockSpec(memory_space=pl.ANY)] * 2,
        out_shape=[
            jax.ShapeDtypeStruct((slots, feats), jnp.bfloat16),
            jax.ShapeDtypeStruct((1, wide), jnp.float32),
        ],
        scratch_shapes=[
            pltpu.VMEM((lanes, LANES), jnp.int32),
            pltpu.VMEM((lanes, LANES), jnp.int32),
            pltpu.VMEM((1, wide), jnp.float32),
            pltpu.VMEM((wide, feats), jnp.bfloat16),
            pltpu.VMEM((rows_here, wide), jnp.bfloat16),
            pltpu.VMEM((slots, feats), jnp.bfloat16),
            pltpu.VMEM((rows_here, feats), jnp.float32),
            pltpu.VMEM((rows_here, feats), jnp.bfloat16),
            pltpu.VMEM((8, feats), jnp.float32),
            pltpu.VMEM((8, wide), jnp.float32),
            pltpu.VMEM((lanes, LANES), jnp.int32),
            pltpu.VMEM((width, 2 * CAP), jnp.float32),
            pltpu.SemaphoreType.DMA((rows_here // CHUNK,)),
            pltpu.SemaphoreType.DMA((4,)),
            pltpu.SemaphoreType.DMA((width // GROUP,)),
        ],
        compiler_params=pltpu.CompilerParams(vmem_limit_bytes=VMEM_ALL),
        cost_estimate=pl.CostEstimate(
            flops=2 * rows_here * feats * (wide + slots), bytes_accessed=2 * rows_here * wide + 2 * slots * feats, transcendentals=0
        ),
        name="project_sort",
    )(embeddings, basis, list_owner.reshape(lanes, LANES), list_slot.reshape(lanes, LANES))


def moments_kernel(width, me_ref, mean_hbm, e_hbm, keep_ref, send_ref, e_ref, mean_ref, m_ref, sem, mean_sem):
    rows_here, wide = e_ref.shape
    block = wide // width
    bits = width.bit_length() - 1
    mean_copy = pltpu.make_async_copy(mean_hbm, mean_ref, mean_sem)
    mean_copy.start()
    copies = []
    for c in range(rows_here // CHUNK):
        at = pl.ds(c * CHUNK, CHUNK)
        copies.append(pltpu.make_async_copy(e_hbm.at[at], e_ref.at[at], sem.at[c]))
        copies[c].start()
    me = me_ref[0]
    mean_copy.wait()
    mean = mean_ref[...]
    for t in range(wide // TILE):
        rows = slice(t * TILE, (t + 1) * TILE)
        if t == 0:
            product = jnp.zeros((TILE, wide), jnp.float32)
            for c in range(rows_here // CHUNK):
                copies[c].wait()
                at = slice(c * CHUNK, (c + 1) * CHUNK)
                product = product + lax.dot_general(
                    e_ref[at, rows], e_ref[at, :], (((0,), (0,)), ((), ())), preferred_element_type=jnp.float32
                )
        else:
            product = lax.dot_general(
                e_ref[:, rows], e_ref[...], (((0,), (0,)), ((), ())), preferred_element_type=jnp.float32
            )
        down = jnp.transpose(jnp.broadcast_to(mean[:, rows] * rows_here, (LANES, TILE)))
        for j in range(wide // LANES):
            across = slice(j * LANES, (j + 1) * LANES)
            m_ref[rows, across] = product[:, across] - down * mean[:, across]
        for pair in range(TILE // block // 2):
            first = t * (TILE // block) + 2 * pair
            apart = (first ^ me) >> 1
            place = 0
            for k in range(bits - 1):
                place = place + (((apart >> k) & 1) << (bits - 2 - k))
            to = pl.ds(pl.multiple_of(place * block, block), block)
            kept = pl.multiple_of((first + (me & 1)) * block, block)
            sent = pl.multiple_of((first + 1 - (me & 1)) * block, block)
            keep_ref[to, :] = m_ref[pl.ds(kept, block), :]
            send_ref[to, :] = m_ref[pl.ds(sent, block), :].astype(jnp.bfloat16)


def moments(width, me, embeddings, mean):
    rows_here, wide = embeddings.shape
    vmem = pl.BlockSpec(memory_space=pltpu.VMEM)
    return pl.pallas_call(
        functools.partial(moments_kernel, width),
        in_specs=[pl.BlockSpec(memory_space=pltpu.SMEM)] + [pl.BlockSpec(memory_space=pl.ANY)] * 2,
        out_specs=[vmem] * 2,
        out_shape=[
            jax.ShapeDtypeStruct((wide // 2, wide), jnp.float32),
            jax.ShapeDtypeStruct((wide // 2, wide), jnp.bfloat16),
        ],
        scratch_shapes=[
            pltpu.VMEM((rows_here, wide), jnp.bfloat16),
            pltpu.VMEM((1, wide), jnp.float32),
            pltpu.VMEM((wide, wide), jnp.float32),
            pltpu.SemaphoreType.DMA((rows_here // CHUNK,)),
            pltpu.SemaphoreType.DMA,
        ],
        compiler_params=pltpu.CompilerParams(vmem_limit_bytes=VMEM_MOST),
        cost_estimate=pl.CostEstimate(
            flops=2 * rows_here * wide * wide, bytes_accessed=2 * rows_here * wide + 3 * wide * wide, transcendentals=0
        ),
        name="moments",
    )(me.reshape(1), mean, embeddings)


def add_kernel(shares, pieces, keep_ref, *refs):
    outs = refs[len(refs) - shares * pieces:]
    came = refs[:len(refs) - shares * pieces]
    rows, columns = outs[0].shape
    for h in range(shares):
        across = slice(h * columns, (h + 1) * columns)
        for p in range(pieces):
            at = slice(p * rows, (p + 1) * rows)
            held = keep_ref[at, across]
            for ref in came:
                held = held + ref[at, across].astype(jnp.float32)
            out = outs[h * pieces + p]
            out[...] = held.astype(out.dtype)


def add_and_split(keep, came, shares, pieces):
    rows, columns = keep.shape
    vmem = pl.BlockSpec(memory_space=pltpu.VMEM)
    shape = (rows // pieces, columns // shares)
    kinds = [jnp.float32] + [jnp.bfloat16] * (pieces - 1)
    outs = pl.pallas_call(
        functools.partial(add_kernel, shares, pieces),
        in_specs=[vmem] * (1 + len(came)),
        out_specs=[vmem] * (shares * pieces),
        out_shape=[jax.ShapeDtypeStruct(shape, kind) for kind in kinds * shares],
        compiler_params=pltpu.CompilerParams(vmem_limit_bytes=VMEM_SOME),
        cost_estimate=pl.CostEstimate(flops=2 * rows * columns, bytes_accessed=10 * rows * columns, transcendentals=0),
        name="add_and_split",
    )(keep, *came)
    return [outs[h * pieces:(h + 1) * pieces] for h in range(shares)]


def finish_kernel(total, between_ref, *refs):
    out_ref = refs[-1]
    each = (len(refs) - 1) // SHARES
    columns = out_ref.shape[1] // SHARES
    for h in range(SHARES):
        across = slice(h * columns, (h + 1) * columns)
        held = refs[h * each][...]
        for ref in refs[h * each + 1:(h + 1) * each]:
            held = held + ref[...].astype(jnp.float32)
        out_ref[:, across] = (held + between_ref[:, across]) / total


def finish(total, between, keeps, came):
    parts = [part for keep, pieces in zip(keeps, came) for part in (keep, *pieces)]
    vmem = pl.BlockSpec(memory_space=pltpu.VMEM)
    return pl.pallas_call(
        functools.partial(finish_kernel, total),
        in_specs=[vmem] * (1 + len(parts)),
        out_specs=vmem,
        out_shape=jax.ShapeDtypeStruct(between.shape, jnp.float32),
        compiler_params=pltpu.CompilerParams(vmem_limit_bytes=VMEM_SOME),
        cost_estimate=pl.CostEstimate(flops=8 * between.size, bytes_accessed=16 * between.size, transcendentals=0),
        name="finish",
    )(between, *parts)


def halving_stages(width):
    strides = [1 << k for k in range(width.bit_length() - 1)]
    return [[s] for s in strides[:-2]] + [strides[-2:]]


def exchange(width, stage, out):
    came = []
    for p in range(1, 1 << len(stage)):
        apart = sum(s for k, s in enumerate(stage) if (p >> (len(stage) - 1 - k)) & 1)
        came.append(lax.ppermute(out[p - 1], "wide", [(i, i ^ apart) for i in range(width)]))
    return came


def encode_kernel(total, me_ref, got_ref, basis_ref, centroid_ref, rotation_ref, *refs):
    out_hbm, between_ref, out_ref, delta_ref, list_ref, apart_ref, sem = refs[-7:]
    width = delta_ref.shape[0]
    feats = out_ref.shape[1]
    owned = centroid_ref.shape[0]
    wide = basis_ref.shape[0]
    block = wide // width
    share = total // width

    notes = jnp.concatenate([got_ref[s * SPAN + CAP:(s + 1) * SPAN, :] for s in range(width)], 0)
    size = width * NOTES
    to = lax.broadcasted_iota(jnp.int32, (size, size), 0)
    of = lax.broadcasted_iota(jnp.int32, (size, size), 1)
    turn = jnp.where((to % width) * NOTES + to // width == of, 1.0, 0.0).astype(jnp.bfloat16)
    turned = jnp.dot(turn, notes, preferred_element_type=jnp.float32)
    row = [turned[r * width:(r + 1) * width] for r in range(NOTES)]
    digits = row[NOTES - 1]
    list_ref[...] = digits[:, :CAP] * 32.0 + digits[:, CAP:] - 1.0
    quarters = wide // feats
    shifts = jnp.zeros((width, feats), jnp.float32)
    for q in range(quarters):
        parts = [row[p * quarters + q] for p in range(3)]
        mean = parts[0] + (parts[1] + parts[2])
        apart_ref[:, q * feats:(q + 1) * feats] = mean - jnp.mean(mean, 0, keepdims=True)
        terms = jnp.dot(
            jnp.concatenate(parts, 0).astype(jnp.bfloat16),
            basis_ref[q * feats:(q + 1) * feats, :],
            preferred_element_type=jnp.float32,
        )
        shifts = shifts + (terms[:width] + (terms[width:2 * width] + terms[2 * width:]))
    square = row[3 * quarters] + (row[3 * quarters + 1] + row[3 * quarters + 2])
    delta = shifts - jnp.mean(shifts, 0, keepdims=True)
    variance = jnp.sum(square + share * (delta * delta), 0, keepdims=True) / total
    scale = lax.rsqrt(variance + 1e-05)
    delta_ref[...] = delta

    names = lax.broadcasted_iota(jnp.int32, (CAP, owned), 1).astype(jnp.int16)

    def encode_group(g):
        columns = jnp.transpose(list_ref[pl.ds(g * GROUP, GROUP), :])
        hits, projected, held = [], [], []
        for s in range(GROUP):
            listed = jnp.broadcast_to(columns[:, s:s + 1], (CAP, LANES))
            held.append(jnp.concatenate([listed] * (feats // LANES), 1) >= 0)
            wanted = jnp.concatenate([listed.astype(jnp.int32).astype(jnp.int16)] * (owned // LANES), 1)
            hits.append(jnp.where(wanted == names, jnp.ones((), jnp.bfloat16), jnp.zeros((), jnp.bfloat16)))
            base = pl.multiple_of((g * GROUP + s) * SPAN, 16)
            rows = got_ref[pl.ds(base, CAP), :].astype(jnp.float32)
            projected.append((rows + delta_ref[pl.ds(g * GROUP + s, 1), :]) * scale)
        centre = jnp.dot(jnp.concatenate(hits, 0), centroid_ref[...], preferred_element_type=jnp.float32)
        residual = jnp.where(jnp.concatenate(held, 0), jnp.concatenate(projected, 0) - centre, 0.0)
        at = pl.ds(pl.multiple_of(g * (GROUP * CAP), GROUP * CAP), GROUP * CAP)
        out_ref[at, :] = jnp.dot(
            residual.astype(jnp.bfloat16), rotation_ref[...], preferred_element_type=jnp.float32
        ).astype(jnp.bfloat16)
        return pltpu.make_async_copy(out_ref.at[at], out_hbm.at[at], sem.at[g])

    groups = width // GROUP
    copies = []
    if groups <= 4:
        for g in range(groups):
            copies.append(encode_group(g))
            copies[g].start()
    else:

        @pl.loop(0, groups)
        def _(g):
            copy = encode_group(g)
            copy.start()
            copy.wait()

    first = me_ref[0] * block
    near = apart_ref[:, pl.ds(pl.multiple_of(first // LANES * LANES, LANES), LANES)]
    near = pltpu.roll(near, (LANES - first % LANES) % LANES, 1)[:, :block]
    between_ref[...] = share * lax.dot_general(
        near,
        apart_ref[...],
        (((0,), (0,)), ((), ())),
        precision=lax.Precision.HIGHEST,
        preferred_element_type=jnp.float32,
    )
    for copy in copies:
        copy.wait()


def encode(width, total, me, got, basis, centroids, rotation, after):
    wide, feats = basis.shape
    owned = centroids.shape[0]
    slots = width * CAP
    vmem, anywhere = pl.BlockSpec(memory_space=pltpu.VMEM), pl.BlockSpec(memory_space=pl.ANY)
    return pl.pallas_call(
        functools.partial(encode_kernel, total),
        in_specs=[pl.BlockSpec(memory_space=pltpu.SMEM)] + [vmem] * 4 + [anywhere] * len(after),
        out_specs=[anywhere, vmem],
        out_shape=[
            jax.ShapeDtypeStruct((slots, feats), jnp.bfloat16),
            jax.ShapeDtypeStruct((wide // width, wide), jnp.float32),
        ],
        scratch_shapes=[
            pltpu.VMEM((slots, feats), jnp.bfloat16),
            pltpu.VMEM((width, feats), jnp.float32),
            pltpu.VMEM((width, CAP), jnp.float32),
            pltpu.VMEM((width, wide), jnp.float32),
            pltpu.SemaphoreType.DMA((width // GROUP,)),
        ],
        compiler_params=pltpu.CompilerParams(vmem_limit_bytes=VMEM_SOME),
        cost_estimate=pl.CostEstimate(
            flops=2 * slots * feats * (owned + feats), bytes_accessed=4 * slots * feats, transcendentals=0
        ),
        name="encode",
    )(me.reshape(1), got, basis, centroids, rotation, *after)


def local(embeddings, basis, list_owner, list_slot, centroids, rotation):
    width = lax.axis_size("wide")
    me = lax.axis_index("wide")
    rows_here, wide = embeddings.shape
    feats = basis.shape[1]
    total = rows_here * width

    rows, mean = project_and_sort(width, embeddings, basis, list_owner, list_slot)
    got = lax.all_to_all(rows.reshape(width, SPAN, feats), "wide", split_axis=0, concat_axis=0, tiled=True)

    keep, send = moments(width, me, embeddings, mean)
    stages = halving_stages(width)
    came = exchange(width, stages[0], [send])
    shares = add_and_split(keep, came, SHARES, 1 << len(stages[1]))
    last = []
    for share in shares:
        for n in range(1, len(stages) - 1):
            came = exchange(width, stages[n], share[1:])
            (share,) = add_and_split(share[0], came, 1, 1 << len(stages[n + 1]))
        last.append(share)
    came = [exchange(width, stages[-1], share[1:]) for share in last]
    encoded, between = encode(
        width, total, me, got.reshape(width * SPAN, feats), basis, centroids, rotation, [share[1] for share in last]
    )
    covariance = finish(total, between, [share[0] for share in last], came)
    return (encoded, covariance)


def solution(mesh):
    in_specs = (
        P(("groups", "wide"), None),
        P(),
        P(("groups", "wide")),
        P(("groups", "wide")),
        P("wide", None),
        P(),
    )
    out_specs = (P(("groups", "wide"), None), P(("groups", "wide"), None))
    return jax.shard_map(local, mesh=mesh, in_specs=in_specs, out_specs=out_specs, check_vma=False)
```

```python
import functools

import jax
import jax.numpy as jnp
from jax import lax
from jax.experimental import pallas as pl
from jax.experimental.pallas import tpu as pltpu
from jax.sharding import PartitionSpec as P

CAP = 128
LANES = 128
NOTES = 16
SPAN = CAP + NOTES
CHUNK = 512
TILE = 256
GROUP = 4
SHARES = (5, 3)
VMEM_ALL = 60 * 1024 * 1024
VMEM_SOME = 24 * 1024 * 1024
VMEM_MOST = 48 * 1024 * 1024


def in_two(x):
    high = x.astype(jnp.bfloat16).astype(jnp.float32)
    return [high, (x - high).astype(jnp.bfloat16).astype(jnp.float32)]


def rows_kernel(
    width, e_hbm, basis_hbm, owner_hbm, slot_hbm,
    rows_hbm, mean_hbm,
    owner_ref, slot_ref, mean_ref, basis_ref, e_ref, rows_ref, sorted_ref, centre_ref, sum_ref, square_ref, total_ref, target_ref, list_ref, e_sem, small_sem, sem,
):
    step = pl.program_id(0)
    rows_here, wide = e_ref.shape
    feats = basis_ref.shape[1]
    groups = width // GROUP
    chunks = rows_here // LANES

    def e_copy(c):
        at = pl.ds(pl.multiple_of(c * CHUNK, CHUNK), CHUNK)
        return pltpu.make_async_copy(e_hbm.at[at], e_ref.at[at], e_sem.at[c])

    @pl.when(step == 0)
    def _():
        owner_copy = pltpu.make_async_copy(owner_hbm, owner_ref, small_sem.at[0])
        slot_copy = pltpu.make_async_copy(slot_hbm, slot_ref, small_sem.at[1])
        basis_copy = pltpu.make_async_copy(basis_hbm, basis_ref, small_sem.at[2])
        owner_copy.start()
        e_copy(0).start()
        slot_copy.start()
        basis_copy.start()
        for c in range(1, rows_here // CHUNK):
            e_copy(c).start()
        owner_copy.wait()
        sorted_ref[...] = jnp.zeros_like(sorted_ref)
        sum_ref[...] = jnp.zeros_like(sum_ref)
        square_ref[...] = jnp.zeros_like(square_ref)
        total_ref[...] = jnp.zeros_like(total_ref)
        owner = owner_ref[...]
        wanted = lax.broadcasted_iota(jnp.int32, (width, LANES), 0)
        hits = [jnp.where(owner[c:c + 1, :] == wanted, 1.0, 0.0) for c in range(chunks)]
        flat = jnp.concatenate(hits, 0).astype(jnp.bfloat16)
        up = lax.broadcasted_iota(jnp.int32, (LANES, LANES), 0)
        to = lax.broadcasted_iota(jnp.int32, (LANES, LANES), 1)
        before = jnp.where(up < to, 1.0, 0.0).astype(jnp.bfloat16)
        every = jnp.ones((LANES, LANES), jnp.bfloat16)
        within = jnp.dot(flat, before, preferred_element_type=jnp.float32)
        counts = jnp.dot(flat, every, preferred_element_type=jnp.float32)
        carry = jnp.zeros((width, LANES), jnp.float32)
        ranks = []
        for c in range(chunks):
            at = slice(c * width, (c + 1) * width)
            ranks.append(jnp.sum(hits[c] * (within[at] + carry), 0, keepdims=True).astype(jnp.int32))
            carry = carry + counts[at]
            target_ref[c:c + 1, :] = owner[c:c + 1, :] * CAP + ranks[c]

        slot_copy.wait()
        slot = slot_ref[...] + 1
        high, low = (slot >> 5).astype(jnp.float32), (slot & 31).astype(jnp.float32)
        spots = lax.broadcasted_iota(jnp.int32, (CAP, LANES), 0)
        placed = jnp.concatenate([jnp.where(ranks[c] == spots, 1.0, 0.0) for c in range(chunks)], 1).astype(jnp.bfloat16)
        digits = jnp.concatenate(
            [
                jnp.concatenate([hits[c] * high[c:c + 1, :] for c in range(chunks)], 1),
                jnp.concatenate([hits[c] * low[c:c + 1, :] for c in range(chunks)], 1),
            ],
            0,
        ).astype(jnp.bfloat16)
        found = lax.dot_general(digits, placed, (((1,), (1,)), ((), ())), preferred_element_type=jnp.float32)
        list_ref[:, :CAP] = found[:width]
        list_ref[:, CAP:] = found[width:]
        basis_copy.wait()

    e_copy(step).wait()
    here = pl.ds(pl.multiple_of(step * CHUNK, CHUNK), CHUNK)
    rows = e_ref[here, :]
    y = jnp.dot(rows, basis_ref[...], preferred_element_type=jnp.float32)

    @pl.when(step == 0)
    def _():
        high, low = in_two(jnp.mean(y, 0, keepdims=True))
        centre_ref[0:1, :] = high
        centre_ref[1:2, :] = low

    y = y - (centre_ref[0:1, :] + centre_ref[1:2, :])
    sum_ref[...] += jnp.sum(y.reshape(CHUNK // 8, 8, feats), 0)
    square_ref[...] += jnp.sum((y * y).reshape(CHUNK // 8, 8, feats), 0)
    total_ref[...] += jnp.sum(rows.astype(jnp.float32).reshape(CHUNK // 8, 8, wide), 0)
    y = y.astype(jnp.bfloat16)

    place = lax.broadcasted_iota(jnp.int32, (GROUP * CAP, LANES), 0).astype(jnp.int16)

    def sort_group(g):
        pieces = []
        for c in range(CHUNK // LANES):
            aim = target_ref[pl.ds(step * (CHUNK // LANES) + c, 1), :] - g * (GROUP * CAP)
            aim = jnp.broadcast_to(aim, (16, LANES)).astype(jnp.int16)
            aim = jnp.concatenate([aim] * (GROUP * CAP // 16), 0)
            pieces.append(jnp.where(aim == place, jnp.ones((), jnp.bfloat16), jnp.zeros((), jnp.bfloat16)))
        at = pl.ds(pl.multiple_of(g * (GROUP * CAP), GROUP * CAP), GROUP * CAP)
        sorted_ref[at, :] += jnp.dot(jnp.concatenate(pieces, 1), y, preferred_element_type=jnp.float32)

    if groups <= 4:
        for g in range(groups):
            sort_group(g)
    else:

        @pl.loop(0, groups)
        def _(g):
            sort_group(g)

    @pl.when(step == pl.num_programs(0) - 1)
    def _():
        mean = jnp.sum(total_ref[...], 0, keepdims=True) / rows_here
        mean_ref[...] = mean
        mean_copy = pltpu.make_async_copy(mean_ref, mean_hbm, small_sem.at[3])
        mean_copy.start()
        offset = jnp.sum(sum_ref[...], 0, keepdims=True) / rows_here
        square = jnp.sum(square_ref[...], 0, keepdims=True) - rows_here * (offset * offset)
        common = [part[:, q * feats:(q + 1) * feats] for part in in_two(mean) for q in range(wide // feats)]
        common = common + [centre_ref[0:1, :], centre_ref[1:2, :]] + in_two(offset) + in_two(square)
        common = common + [jnp.zeros((1, feats), jnp.float32)] * (NOTES - 1 - len(common))
        common = jnp.concatenate(common, 0)

        def rows_copy(g):
            at = pl.ds(pl.multiple_of(g * (GROUP * SPAN), 16), GROUP * SPAN)
            return pltpu.make_async_copy(rows_ref.at[at], rows_hbm.at[at], sem.at[g])

        def place_group(g):
            for j in range(GROUP):
                base = pl.multiple_of((g * GROUP + j) * SPAN, 16)
                from_here = pl.ds(pl.multiple_of((g * GROUP + j) * CAP, CAP), CAP)
                rows_ref[pl.ds(base, CAP), :] = sorted_ref[from_here, :].astype(jnp.bfloat16)
                notes = jnp.concatenate([common, list_ref[pl.ds(g * GROUP + j, 1), :]], 0)
                rows_ref[pl.ds(pl.multiple_of(base + CAP, 16), NOTES), :] = notes.astype(jnp.bfloat16)
            rows_copy(g).start()

        if groups <= 4:
            for g in range(groups):
                place_group(g)
        else:

            @pl.loop(0, groups)
            def _(g):
                place_group(g)

        for g in range(groups):
            rows_copy(g).wait()
        mean_copy.wait()


def project_and_sort(width, embeddings, basis, list_owner, list_slot):
    rows_here, wide = embeddings.shape
    feats = basis.shape[1]
    lanes = rows_here // LANES
    slots = width * SPAN
    return pl.pallas_call(
        functools.partial(rows_kernel, width),
        grid=(rows_here // CHUNK,),
        in_specs=[pl.BlockSpec(memory_space=pl.ANY)] * 4,
        out_specs=[pl.BlockSpec(memory_space=pl.ANY)] * 2,
        out_shape=[
            jax.ShapeDtypeStruct((slots, feats), jnp.bfloat16),
            jax.ShapeDtypeStruct((1, wide), jnp.float32),
        ],
        scratch_shapes=[
            pltpu.VMEM((lanes, LANES), jnp.int32),
            pltpu.VMEM((lanes, LANES), jnp.int32),
            pltpu.VMEM((1, wide), jnp.float32),
            pltpu.VMEM((wide, feats), jnp.bfloat16),
            pltpu.VMEM((rows_here, wide), jnp.bfloat16),
            pltpu.VMEM((slots, feats), jnp.bfloat16),
            pltpu.VMEM((width * CAP, feats), jnp.float32),
            pltpu.VMEM((2, feats), jnp.float32),
            pltpu.VMEM((8, feats), jnp.float32),
            pltpu.VMEM((8, feats), jnp.float32),
            pltpu.VMEM((8, wide), jnp.float32),
            pltpu.VMEM((lanes, LANES), jnp.int32),
            pltpu.VMEM((width, 2 * CAP), jnp.float32),
            pltpu.SemaphoreType.DMA((rows_here // CHUNK,)),
            pltpu.SemaphoreType.DMA((4,)),
            pltpu.SemaphoreType.DMA((width // GROUP,)),
        ],
        compiler_params=pltpu.CompilerParams(vmem_limit_bytes=VMEM_ALL),
        cost_estimate=pl.CostEstimate(
            flops=2 * rows_here * feats * (wide + slots), bytes_accessed=2 * rows_here * wide + 2 * slots * feats, transcendentals=0
        ),
        name="project_sort",
    )(embeddings, basis, list_owner.reshape(lanes, LANES), list_slot.reshape(lanes, LANES))


def moments_kernel(width, me_ref, mean_hbm, e_hbm, keep_ref, send_ref, e_ref, mean_ref, m_ref, sem, mean_sem):
    rows_here, wide = e_ref.shape
    block = wide // width
    bits = width.bit_length() - 1
    mean_copy = pltpu.make_async_copy(mean_hbm, mean_ref, mean_sem)
    mean_copy.start()
    copies = []
    for c in range(rows_here // CHUNK):
        at = pl.ds(c * CHUNK, CHUNK)
        copies.append(pltpu.make_async_copy(e_hbm.at[at], e_ref.at[at], sem.at[c]))
        copies[c].start()
    me = me_ref[0]
    mean_copy.wait()
    mean = mean_ref[...]
    for t in range(wide // TILE):
        rows = slice(t * TILE, (t + 1) * TILE)
        if t == 0:
            product = jnp.zeros((TILE, wide), jnp.float32)
            for c in range(rows_here // CHUNK):
                copies[c].wait()
                at = slice(c * CHUNK, (c + 1) * CHUNK)
                product = product + lax.dot_general(
                    e_ref[at, rows], e_ref[at, :], (((0,), (0,)), ((), ())), preferred_element_type=jnp.float32
                )
        else:
            product = lax.dot_general(
                e_ref[:, rows], e_ref[...], (((0,), (0,)), ((), ())), preferred_element_type=jnp.float32
            )
        down = jnp.transpose(jnp.broadcast_to(mean[:, rows] * rows_here, (LANES, TILE)))
        for j in range(wide // LANES):
            across = slice(j * LANES, (j + 1) * LANES)
            m_ref[rows, across] = product[:, across] - down * mean[:, across]
        for pair in range(TILE // block // 2):
            first = t * (TILE // block) + 2 * pair
            apart = (first ^ me) >> 1
            place = 0
            for k in range(bits - 1):
                place = place + (((apart >> k) & 1) << (bits - 2 - k))
            to = pl.ds(pl.multiple_of(place * block, block), block)
            kept = pl.multiple_of((first + (me & 1)) * block, block)
            sent = pl.multiple_of((first + 1 - (me & 1)) * block, block)
            keep_ref[to, :] = m_ref[pl.ds(kept, block), :]
            send_ref[to, :] = m_ref[pl.ds(sent, block), :].astype(jnp.bfloat16)


def moments(width, me, embeddings, mean):
    rows_here, wide = embeddings.shape
    vmem = pl.BlockSpec(memory_space=pltpu.VMEM)
    return pl.pallas_call(
        functools.partial(moments_kernel, width),
        in_specs=[pl.BlockSpec(memory_space=pltpu.SMEM)] + [pl.BlockSpec(memory_space=pl.ANY)] * 2,
        out_specs=[vmem] * 2,
        out_shape=[
            jax.ShapeDtypeStruct((wide // 2, wide), jnp.float32),
            jax.ShapeDtypeStruct((wide // 2, wide), jnp.bfloat16),
        ],
        scratch_shapes=[
            pltpu.VMEM((rows_here, wide), jnp.bfloat16),
            pltpu.VMEM((1, wide), jnp.float32),
            pltpu.VMEM((wide, wide), jnp.float32),
            pltpu.SemaphoreType.DMA((rows_here // CHUNK,)),
            pltpu.SemaphoreType.DMA,
        ],
        compiler_params=pltpu.CompilerParams(vmem_limit_bytes=VMEM_MOST),
        cost_estimate=pl.CostEstimate(
            flops=2 * rows_here * wide * wide, bytes_accessed=2 * rows_here * wide + 3 * wide * wide, transcendentals=0
        ),
        name="moments",
    )(me.reshape(1), mean, embeddings)


def cuts(columns, shares):
    unit = columns // sum(shares)
    ends = [unit * sum(shares[:h + 1]) for h in range(len(shares))]
    return list(zip([0] + ends[:-1], ends))


def add_kernel(shares, pieces, keep_ref, *refs):
    count = len(shares) * pieces
    came, outs = refs[:-count], refs[-count:]
    for h, (first, end) in enumerate(cuts(keep_ref.shape[1], shares)):
        for p in range(pieces):
            out = outs[h * pieces + p]
            at = slice(p * out.shape[0], (p + 1) * out.shape[0])
            held = keep_ref[at, first:end].astype(jnp.float32)
            for ref in came:
                held = held + ref[at, first:end].astype(jnp.float32)
            out[...] = held.astype(out.dtype)


def add_and_split(keep, came, shares, pieces):
    rows, columns = keep.shape
    vmem = pl.BlockSpec(memory_space=pltpu.VMEM)
    kinds = [jnp.float32] + [jnp.bfloat16] * (pieces - 1)
    outs = pl.pallas_call(
        functools.partial(add_kernel, shares, pieces),
        in_specs=[vmem] * (1 + len(came)),
        out_specs=[vmem] * (len(shares) * pieces),
        out_shape=[
            jax.ShapeDtypeStruct((rows // pieces, end - first), kind) for first, end in cuts(columns, shares) for kind in kinds
        ],
        compiler_params=pltpu.CompilerParams(vmem_limit_bytes=VMEM_SOME),
        cost_estimate=pl.CostEstimate(flops=2 * rows * columns, bytes_accessed=10 * rows * columns, transcendentals=0),
        name="add_and_split",
    )(keep, *came)
    return [outs[h * pieces:(h + 1) * pieces] for h in range(len(shares))]


def finish_kernel(total, between_ref, *refs):
    out_ref = refs[-1]
    each = (len(refs) - 1) // len(SHARES)
    for h, (first, end) in enumerate(cuts(out_ref.shape[1], SHARES)):
        held = refs[h * each][...]
        for ref in refs[h * each + 1:(h + 1) * each]:
            held = held + ref[...].astype(jnp.float32)
        out_ref[:, first:end] = (held + between_ref[:, first:end]) / total


def finish(total, between, keeps, came):
    parts = [part for keep, pieces in zip(keeps, came) for part in (keep, *pieces)]
    vmem = pl.BlockSpec(memory_space=pltpu.VMEM)
    return pl.pallas_call(
        functools.partial(finish_kernel, total),
        in_specs=[vmem] * (1 + len(parts)),
        out_specs=vmem,
        out_shape=jax.ShapeDtypeStruct(between.shape, jnp.float32),
        compiler_params=pltpu.CompilerParams(vmem_limit_bytes=VMEM_SOME),
        cost_estimate=pl.CostEstimate(flops=8 * between.size, bytes_accessed=16 * between.size, transcendentals=0),
        name="finish",
    )(between, *parts)


def halving_stages(width):
    strides = [1 << k for k in range(width.bit_length() - 1)]
    return [[s] for s in strides[:-2]] + [strides[-2:]]


def exchange(width, stage, out):
    came = []
    for p in range(1, 1 << len(stage)):
        apart = sum(s for k, s in enumerate(stage) if (p >> (len(stage) - 1 - k)) & 1)
        came.append(lax.ppermute(out[p - 1], "wide", [(i, i ^ apart) for i in range(width)]))
    return came


def encode_kernel(total, me_ref, got_ref, centroid_ref, rotation_ref, *refs):
    out_hbm, between_ref, out_ref, delta_ref, list_ref, apart_ref, sem = refs[-7:]
    width = delta_ref.shape[0]
    feats = out_ref.shape[1]
    owned = centroid_ref.shape[0]
    wide = apart_ref.shape[1]
    block = wide // width
    share = total // width

    notes = jnp.concatenate([got_ref[s * SPAN + CAP:(s + 1) * SPAN, :] for s in range(width)], 0)
    size = width * NOTES
    to = lax.broadcasted_iota(jnp.int32, (size, size), 0)
    of = lax.broadcasted_iota(jnp.int32, (size, size), 1)
    turn = jnp.where((to % width) * NOTES + to // width == of, 1.0, 0.0).astype(jnp.bfloat16)
    turned = jnp.dot(turn, notes, preferred_element_type=jnp.float32)
    row = [turned[r * width:(r + 1) * width] for r in range(NOTES)]
    digits = row[NOTES - 1]
    list_ref[...] = digits[:, :CAP] * 32.0 + digits[:, CAP:] - 1.0
    quarters = wide // feats
    for q in range(quarters):
        mean = row[q] + row[quarters + q]
        apart_ref[:, q * feats:(q + 1) * feats] = mean - jnp.mean(mean, 0, keepdims=True)
    centre, offset, square = [row[n] + row[n + 1] for n in range(2 * quarters, 2 * quarters + 6, 2)]
    delta = centre - jnp.mean(centre, 0, keepdims=True) - jnp.mean(offset, 0, keepdims=True)
    variance = jnp.sum(square + share * ((delta + offset) * (delta + offset)), 0, keepdims=True) / total
    scale = lax.rsqrt(variance + 1e-05)
    delta_ref[...] = delta

    names = lax.broadcasted_iota(jnp.int32, (CAP, owned), 1).astype(jnp.int16)

    def encode_group(g):
        columns = jnp.transpose(list_ref[pl.ds(g * GROUP, GROUP), :])
        hits, projected, held = [], [], []
        for s in range(GROUP):
            listed = jnp.broadcast_to(columns[:, s:s + 1], (CAP, LANES))
            held.append(jnp.concatenate([listed] * (feats // LANES), 1) >= 0)
            wanted = jnp.concatenate([listed.astype(jnp.int32).astype(jnp.int16)] * (owned // LANES), 1)
            hits.append(jnp.where(wanted == names, jnp.ones((), jnp.bfloat16), jnp.zeros((), jnp.bfloat16)))
            base = pl.multiple_of((g * GROUP + s) * SPAN, 16)
            rows = got_ref[pl.ds(base, CAP), :].astype(jnp.float32)
            projected.append((rows + delta_ref[pl.ds(g * GROUP + s, 1), :]) * scale)
        centroid = jnp.dot(jnp.concatenate(hits, 0), centroid_ref[...], preferred_element_type=jnp.float32)
        residual = jnp.where(jnp.concatenate(held, 0), jnp.concatenate(projected, 0) - centroid, 0.0)
        at = pl.ds(pl.multiple_of(g * (GROUP * CAP), GROUP * CAP), GROUP * CAP)
        out_ref[at, :] = jnp.dot(
            residual.astype(jnp.bfloat16), rotation_ref[...], preferred_element_type=jnp.float32
        ).astype(jnp.bfloat16)
        return pltpu.make_async_copy(out_ref.at[at], out_hbm.at[at], sem.at[g])

    groups = width // GROUP
    copies = []
    if groups <= 4:
        for g in range(groups):
            copies.append(encode_group(g))
            copies[g].start()
    else:

        @pl.loop(0, groups)
        def _(g):
            copy = encode_group(g)
            copy.start()
            copy.wait()

    first = me_ref[0] * block
    near = apart_ref[:, pl.ds(pl.multiple_of(first // LANES * LANES, LANES), LANES)]
    near = pltpu.roll(near, (LANES - first % LANES) % LANES, 1)[:, :block]
    between_ref[...] = share * lax.dot_general(
        near,
        apart_ref[...],
        (((0,), (0,)), ((), ())),
        precision=lax.Precision.HIGHEST,
        preferred_element_type=jnp.float32,
    )
    for copy in copies:
        copy.wait()


def encode(width, total, me, wide, got, centroids, rotation, after):
    owned, feats = centroids.shape
    slots = width * CAP
    vmem, anywhere = pl.BlockSpec(memory_space=pltpu.VMEM), pl.BlockSpec(memory_space=pl.ANY)
    return pl.pallas_call(
        functools.partial(encode_kernel, total),
        in_specs=[pl.BlockSpec(memory_space=pltpu.SMEM)] + [vmem] * 3 + [anywhere] * len(after),
        out_specs=[anywhere, vmem],
        out_shape=[
            jax.ShapeDtypeStruct((slots, feats), jnp.bfloat16),
            jax.ShapeDtypeStruct((wide // width, wide), jnp.float32),
        ],
        scratch_shapes=[
            pltpu.VMEM((slots, feats), jnp.bfloat16),
            pltpu.VMEM((width, feats), jnp.float32),
            pltpu.VMEM((width, CAP), jnp.float32),
            pltpu.VMEM((width, wide), jnp.float32),
            pltpu.SemaphoreType.DMA((width // GROUP,)),
        ],
        compiler_params=pltpu.CompilerParams(vmem_limit_bytes=VMEM_SOME),
        cost_estimate=pl.CostEstimate(
            flops=2 * slots * feats * (owned + feats), bytes_accessed=4 * slots * feats, transcendentals=0
        ),
        name="encode",
    )(me.reshape(1), got, centroids, rotation, *after)


def local(embeddings, basis, list_owner, list_slot, centroids, rotation):
    width = lax.axis_size("wide")
    me = lax.axis_index("wide")
    rows_here, wide = embeddings.shape
    feats = basis.shape[1]
    total = rows_here * width

    rows, mean = project_and_sort(width, embeddings, basis, list_owner, list_slot)
    got = lax.all_to_all(rows.reshape(width, SPAN, feats), "wide", split_axis=0, concat_axis=0, tiled=True)

    keep, send = moments(width, me, embeddings, mean)
    stages = halving_stages(width)
    came = exchange(width, stages[0], [send])
    shares = add_and_split(keep, came, SHARES, 1 << len(stages[1]))
    last = []
    for share in shares:
        for n in range(1, len(stages) - 1):
            came = exchange(width, stages[n], share[1:])
            (share,) = add_and_split(share[0], came, (1,), 1 << len(stages[n + 1]))
        last.append(share)
    came = [exchange(width, stages[-1], share[1:]) for share in last]
    encoded, between = encode(
        width, total, me, wide, got.reshape(width * SPAN, feats), centroids, rotation, [share[1] for share in last]
    )
    covariance = finish(total, between, [share[0] for share in last], came)
    return (encoded, covariance)


def solution(mesh):
    in_specs = (
        P(("groups", "wide"), None),
        P(),
        P(("groups", "wide")),
        P(("groups", "wide")),
        P("wide", None),
        P(),
    )
    out_specs = (P(("groups", "wide"), None), P(("groups", "wide"), None))
    return jax.shard_map(local, mesh=mesh, in_specs=in_specs, out_specs=out_specs, check_vma=False)
```

```python
import functools

import jax
import jax.numpy as jnp
from jax import lax
from jax.experimental import pallas as pl
from jax.experimental.pallas import tpu as pltpu
from jax.sharding import PartitionSpec as P

CAP = 128
LANES = 128
NOTES = 16
SPAN = CAP + NOTES
CHUNK = 512
TILE = 256
GROUP = 4
SHARES = (5, 3)
VMEM_ALL = 60 * 1024 * 1024
VMEM_SOME = 24 * 1024 * 1024
VMEM_MOST = 48 * 1024 * 1024


def in_two(x):
    high = x.astype(jnp.bfloat16).astype(jnp.float32)
    return [high, (x - high).astype(jnp.bfloat16).astype(jnp.float32)]


def rows_kernel(
    width, e_hbm, basis_hbm, owner_hbm, slot_hbm,
    rows_hbm, mean_hbm,
    owner_ref, slot_ref, mean_ref, basis_ref, e_ref, rows_ref, yb_ref, centre_ref, sum_ref, square_ref, total_ref, target_ref, list_ref, e_sem, small_sem, sem,
):
    step = pl.program_id(0)
    rows_here, wide = e_ref.shape
    feats = basis_ref.shape[1]
    groups = width // GROUP
    chunks = rows_here // LANES

    def e_copy(c):
        at = pl.ds(pl.multiple_of(c * CHUNK, CHUNK), CHUNK)
        return pltpu.make_async_copy(e_hbm.at[at], e_ref.at[at], e_sem.at[c])

    @pl.when(step == 0)
    def _():
        owner_copy = pltpu.make_async_copy(owner_hbm, owner_ref, small_sem.at[0])
        slot_copy = pltpu.make_async_copy(slot_hbm, slot_ref, small_sem.at[1])
        basis_copy = pltpu.make_async_copy(basis_hbm, basis_ref, small_sem.at[2])
        owner_copy.start()
        e_copy(0).start()
        slot_copy.start()
        basis_copy.start()
        for c in range(1, rows_here // CHUNK):
            e_copy(c).start()
        owner_copy.wait()
        sum_ref[...] = jnp.zeros_like(sum_ref)
        square_ref[...] = jnp.zeros_like(square_ref)
        total_ref[...] = jnp.zeros_like(total_ref)
        owner = owner_ref[...]
        wanted = lax.broadcasted_iota(jnp.int32, (width, LANES), 0)
        hits = [jnp.where(owner[c:c + 1, :] == wanted, 1.0, 0.0) for c in range(chunks)]
        flat = jnp.concatenate(hits, 0).astype(jnp.bfloat16)
        up = lax.broadcasted_iota(jnp.int32, (LANES, LANES), 0)
        to = lax.broadcasted_iota(jnp.int32, (LANES, LANES), 1)
        before = jnp.where(up < to, 1.0, 0.0).astype(jnp.bfloat16)
        every = jnp.ones((LANES, LANES), jnp.bfloat16)
        within = jnp.dot(flat, before, preferred_element_type=jnp.float32)
        counts = jnp.dot(flat, every, preferred_element_type=jnp.float32)
        carry = jnp.zeros((width, LANES), jnp.float32)
        ranks = []
        for c in range(chunks):
            at = slice(c * width, (c + 1) * width)
            ranks.append(jnp.sum(hits[c] * (within[at] + carry), 0, keepdims=True).astype(jnp.int32))
            carry = carry + counts[at]
            target_ref[c:c + 1, :] = owner[c:c + 1, :] * CAP + ranks[c]

        slot_copy.wait()
        slot = slot_ref[...] + 1
        high, low = (slot >> 5).astype(jnp.float32), (slot & 31).astype(jnp.float32)
        spots = lax.broadcasted_iota(jnp.int32, (CAP, LANES), 0)
        placed = jnp.concatenate([jnp.where(ranks[c] == spots, 1.0, 0.0) for c in range(chunks)], 1).astype(jnp.bfloat16)
        digits = jnp.concatenate(
            [
                jnp.concatenate([hits[c] * high[c:c + 1, :] for c in range(chunks)], 1),
                jnp.concatenate([hits[c] * low[c:c + 1, :] for c in range(chunks)], 1),
            ],
            0,
        ).astype(jnp.bfloat16)
        found = lax.dot_general(digits, placed, (((1,), (1,)), ((), ())), preferred_element_type=jnp.float32)
        list_ref[:, :CAP] = found[:width]
        list_ref[:, CAP:] = found[width:]
        basis_copy.wait()

    e_copy(step).wait()
    here = pl.ds(pl.multiple_of(step * CHUNK, CHUNK), CHUNK)
    rows = e_ref[here, :]
    y = jnp.dot(rows, basis_ref[...], preferred_element_type=jnp.float32)

    @pl.when(step == 0)
    def _():
        high, low = in_two(jnp.mean(y, 0, keepdims=True))
        centre_ref[0:1, :] = high
        centre_ref[1:2, :] = low

    y = y - (centre_ref[0:1, :] + centre_ref[1:2, :])
    sum_ref[...] += jnp.sum(y.reshape(CHUNK // 8, 8, feats), 0)
    square_ref[...] += jnp.sum((y * y).reshape(CHUNK // 8, 8, feats), 0)
    total_ref[...] += jnp.sum(rows.astype(jnp.float32).reshape(CHUNK // 8, 8, wide), 0)
    yb_ref[here, :] = y.astype(jnp.bfloat16)

    @pl.when(step == pl.num_programs(0) - 1)
    def _():
        mean = jnp.sum(total_ref[...], 0, keepdims=True) / rows_here
        mean_ref[...] = mean
        mean_copy = pltpu.make_async_copy(mean_ref, mean_hbm, small_sem.at[3])
        mean_copy.start()
        offset = jnp.sum(sum_ref[...], 0, keepdims=True) / rows_here
        square = jnp.sum(square_ref[...], 0, keepdims=True) - rows_here * (offset * offset)
        common = [part[:, q * feats:(q + 1) * feats] for part in in_two(mean) for q in range(wide // feats)]
        common = common + [centre_ref[0:1, :], centre_ref[1:2, :]] + in_two(offset) + in_two(square)
        common = common + [jnp.zeros((1, feats), jnp.float32)] * (NOTES - 1 - len(common))
        common = jnp.concatenate(common, 0)

        place = lax.broadcasted_iota(jnp.int32, (GROUP * CAP, LANES), 0).astype(jnp.int16)

        def sort_group(g):
            first = g * GROUP
            pieces = []
            for c in range(chunks):
                aim = target_ref[c:c + 1, :] - first * CAP
                aim = jnp.broadcast_to(aim, (16, LANES)).astype(jnp.int16)
                aim = jnp.concatenate([aim] * (GROUP * CAP // 16), 0)
                pieces.append(jnp.where(aim == place, jnp.ones((), jnp.bfloat16), jnp.zeros((), jnp.bfloat16)))
            pick = jnp.concatenate(pieces, 1)
            rows = jnp.dot(pick, yb_ref[...], preferred_element_type=jnp.float32).astype(jnp.bfloat16)
            for j in range(GROUP):
                base = pl.multiple_of((first + j) * SPAN, 16)
                rows_ref[pl.ds(base, CAP), :] = rows[j * CAP:(j + 1) * CAP]
                notes = jnp.concatenate([common, list_ref[pl.ds(first + j, 1), :]], 0)
                rows_ref[pl.ds(pl.multiple_of(base + CAP, 16), NOTES), :] = notes.astype(jnp.bfloat16)
            at = pl.ds(pl.multiple_of(g * (GROUP * SPAN), 16), GROUP * SPAN)
            return pltpu.make_async_copy(rows_ref.at[at], rows_hbm.at[at], sem.at[g])

        if groups <= 4:
            copies = []
            for g in range(groups):
                copies.append(sort_group(g))
                copies[g].start()
            for copy in copies:
                copy.wait()
        else:

            @pl.loop(0, groups)
            def _(g):
                copy = sort_group(g)
                copy.start()
                copy.wait()

        mean_copy.wait()


def project_and_sort(width, embeddings, basis, list_owner, list_slot):
    rows_here, wide = embeddings.shape
    feats = basis.shape[1]
    lanes = rows_here // LANES
    slots = width * SPAN
    return pl.pallas_call(
        functools.partial(rows_kernel, width),
        grid=(rows_here // CHUNK,),
        in_specs=[pl.BlockSpec(memory_space=pl.ANY)] * 4,
        out_specs=[pl.BlockSpec(memory_space=pl.ANY)] * 2,
        out_shape=[
            jax.ShapeDtypeStruct((slots, feats), jnp.bfloat16),
            jax.ShapeDtypeStruct((1, wide), jnp.float32),
        ],
        scratch_shapes=[
            pltpu.VMEM((lanes, LANES), jnp.int32),
            pltpu.VMEM((lanes, LANES), jnp.int32),
            pltpu.VMEM((1, wide), jnp.float32),
            pltpu.VMEM((wide, feats), jnp.bfloat16),
            pltpu.VMEM((rows_here, wide), jnp.bfloat16),
            pltpu.VMEM((slots, feats), jnp.bfloat16),
            pltpu.VMEM((rows_here, feats), jnp.bfloat16),
            pltpu.VMEM((2, feats), jnp.float32),
            pltpu.VMEM((8, feats), jnp.float32),
            pltpu.VMEM((8, feats), jnp.float32),
            pltpu.VMEM((8, wide), jnp.float32),
            pltpu.VMEM((lanes, LANES), jnp.int32),
            pltpu.VMEM((width, 2 * CAP), jnp.float32),
            pltpu.SemaphoreType.DMA((rows_here // CHUNK,)),
            pltpu.SemaphoreType.DMA((4,)),
            pltpu.SemaphoreType.DMA((width // GROUP,)),
        ],
        compiler_params=pltpu.CompilerParams(vmem_limit_bytes=VMEM_ALL),
        cost_estimate=pl.CostEstimate(
            flops=2 * rows_here * feats * (wide + slots), bytes_accessed=2 * rows_here * wide + 2 * slots * feats, transcendentals=0
        ),
        name="project_sort",
    )(embeddings, basis, list_owner.reshape(lanes, LANES), list_slot.reshape(lanes, LANES))


def moments_kernel(width, me_ref, mean_hbm, e_hbm, keep_ref, send_ref, e_ref, mean_ref, m_ref, sem, mean_sem):
    rows_here, wide = e_ref.shape
    block = wide // width
    bits = width.bit_length() - 1
    mean_copy = pltpu.make_async_copy(mean_hbm, mean_ref, mean_sem)
    mean_copy.start()
    copies = []
    for c in range(rows_here // CHUNK):
        at = pl.ds(c * CHUNK, CHUNK)
        copies.append(pltpu.make_async_copy(e_hbm.at[at], e_ref.at[at], sem.at[c]))
        copies[c].start()
    me = me_ref[0]
    mean_copy.wait()
    mean = mean_ref[...]
    for t in range(wide // TILE):
        rows = slice(t * TILE, (t + 1) * TILE)
        if t == 0:
            product = jnp.zeros((TILE, wide), jnp.float32)
            for c in range(rows_here // CHUNK):
                copies[c].wait()
                at = slice(c * CHUNK, (c + 1) * CHUNK)
                product = product + lax.dot_general(
                    e_ref[at, rows], e_ref[at, :], (((0,), (0,)), ((), ())), preferred_element_type=jnp.float32
                )
        else:
            product = lax.dot_general(
                e_ref[:, rows], e_ref[...], (((0,), (0,)), ((), ())), preferred_element_type=jnp.float32
            )
        down = jnp.transpose(jnp.broadcast_to(mean[:, rows] * rows_here, (LANES, TILE)))
        for j in range(wide // LANES):
            across = slice(j * LANES, (j + 1) * LANES)
            m_ref[rows, across] = product[:, across] - down * mean[:, across]
        for pair in range(TILE // block // 2):
            first = t * (TILE // block) + 2 * pair
            apart = (first ^ me) >> 1
            place = 0
            for k in range(bits - 1):
                place = place + (((apart >> k) & 1) << (bits - 2 - k))
            to = pl.ds(pl.multiple_of(place * block, block), block)
            kept = pl.multiple_of((first + (me & 1)) * block, block)
            sent = pl.multiple_of((first + 1 - (me & 1)) * block, block)
            keep_ref[to, :] = m_ref[pl.ds(kept, block), :]
            send_ref[to, :] = m_ref[pl.ds(sent, block), :].astype(jnp.bfloat16)


def moments(width, me, embeddings, mean):
    rows_here, wide = embeddings.shape
    vmem = pl.BlockSpec(memory_space=pltpu.VMEM)
    return pl.pallas_call(
        functools.partial(moments_kernel, width),
        in_specs=[pl.BlockSpec(memory_space=pltpu.SMEM)] + [pl.BlockSpec(memory_space=pl.ANY)] * 2,
        out_specs=[vmem] * 2,
        out_shape=[
            jax.ShapeDtypeStruct((wide // 2, wide), jnp.float32),
            jax.ShapeDtypeStruct((wide // 2, wide), jnp.bfloat16),
        ],
        scratch_shapes=[
            pltpu.VMEM((rows_here, wide), jnp.bfloat16),
            pltpu.VMEM((1, wide), jnp.float32),
            pltpu.VMEM((wide, wide), jnp.float32),
            pltpu.SemaphoreType.DMA((rows_here // CHUNK,)),
            pltpu.SemaphoreType.DMA,
        ],
        compiler_params=pltpu.CompilerParams(vmem_limit_bytes=VMEM_MOST),
        cost_estimate=pl.CostEstimate(
            flops=2 * rows_here * wide * wide, bytes_accessed=2 * rows_here * wide + 3 * wide * wide, transcendentals=0
        ),
        name="moments",
    )(me.reshape(1), mean, embeddings)


def cuts(columns, shares):
    unit = columns // sum(shares)
    ends = [unit * sum(shares[:h + 1]) for h in range(len(shares))]
    return list(zip([0] + ends[:-1], ends))


def add_kernel(shares, pieces, arrived, keep_ref, *refs):
    count = len(shares) * pieces
    came, outs = refs[:arrived], refs[-count:]
    for h, (first, end) in enumerate(cuts(keep_ref.shape[1], shares)):
        for p in range(pieces):
            out = outs[h * pieces + p]
            at = slice(p * out.shape[0], (p + 1) * out.shape[0])
            held = keep_ref[at, first:end].astype(jnp.float32)
            for ref in came:
                held = held + ref[at, first:end].astype(jnp.float32)
            out[...] = held.astype(out.dtype)


def add_and_split(keep, came, shares, pieces, after=()):
    rows, columns = keep.shape
    vmem = pl.BlockSpec(memory_space=pltpu.VMEM)
    kinds = [jnp.float32] + [jnp.bfloat16] * (pieces - 1)
    outs = pl.pallas_call(
        functools.partial(add_kernel, shares, pieces, len(came)),
        in_specs=[vmem] * (1 + len(came)) + [pl.BlockSpec(memory_space=pl.ANY)] * len(after),
        out_specs=[vmem] * (len(shares) * pieces),
        out_shape=[
            jax.ShapeDtypeStruct((rows // pieces, end - first), kind) for first, end in cuts(columns, shares) for kind in kinds
        ],
        compiler_params=pltpu.CompilerParams(vmem_limit_bytes=VMEM_SOME),
        cost_estimate=pl.CostEstimate(flops=2 * rows * columns, bytes_accessed=10 * rows * columns, transcendentals=0),
        name="add_and_split",
    )(keep, *came, *after)
    return [outs[h * pieces:(h + 1) * pieces] for h in range(len(shares))]


def finish_kernel(total, between_ref, *refs):
    out_ref = refs[-1]
    each = (len(refs) - 1) // len(SHARES)
    for h, (first, end) in enumerate(cuts(out_ref.shape[1], SHARES)):
        held = refs[h * each][...]
        for ref in refs[h * each + 1:(h + 1) * each]:
            held = held + ref[...].astype(jnp.float32)
        out_ref[:, first:end] = (held + between_ref[:, first:end]) / total


def finish(total, between, keeps, came):
    parts = [part for keep, pieces in zip(keeps, came) for part in (keep, *pieces)]
    vmem = pl.BlockSpec(memory_space=pltpu.VMEM)
    return pl.pallas_call(
        functools.partial(finish_kernel, total),
        in_specs=[vmem] * (1 + len(parts)),
        out_specs=vmem,
        out_shape=jax.ShapeDtypeStruct(between.shape, jnp.float32),
        compiler_params=pltpu.CompilerParams(vmem_limit_bytes=VMEM_SOME),
        cost_estimate=pl.CostEstimate(flops=8 * between.size, bytes_accessed=16 * between.size, transcendentals=0),
        name="finish",
    )(between, *parts)


def halving_stages(width):
    strides = [1 << k for k in range(width.bit_length() - 1)]
    return [[s] for s in strides[:-2]] + [strides[-2:]]


def exchange(width, stage, out):
    came = []
    for p in range(1, 1 << len(stage)):
        apart = sum(s for k, s in enumerate(stage) if (p >> (len(stage) - 1 - k)) & 1)
        came.append(lax.ppermute(out[p - 1], "wide", [(i, i ^ apart) for i in range(width)]))
    return came


def encode_kernel(total, me_ref, got_ref, centroid_ref, rotation_ref, *refs):
    out_hbm, between_ref, out_ref, delta_ref, list_ref, apart_ref, sem = refs[-7:]
    width = delta_ref.shape[0]
    feats = out_ref.shape[1]
    owned = centroid_ref.shape[0]
    wide = apart_ref.shape[1]
    block = wide // width
    share = total // width

    notes = jnp.concatenate([got_ref[s * SPAN + CAP:(s + 1) * SPAN, :] for s in range(width)], 0)
    size = width * NOTES
    to = lax.broadcasted_iota(jnp.int32, (size, size), 0)
    of = lax.broadcasted_iota(jnp.int32, (size, size), 1)
    turn = jnp.where((to % width) * NOTES + to // width == of, 1.0, 0.0).astype(jnp.bfloat16)
    turned = jnp.dot(turn, notes, preferred_element_type=jnp.float32)
    row = [turned[r * width:(r + 1) * width] for r in range(NOTES)]
    digits = row[NOTES - 1]
    list_ref[...] = digits[:, :CAP] * 32.0 + digits[:, CAP:] - 1.0
    quarters = wide // feats
    for q in range(quarters):
        mean = row[q] + row[quarters + q]
        apart_ref[:, q * feats:(q + 1) * feats] = mean - jnp.mean(mean, 0, keepdims=True)
    centre, offset, square = [row[n] + row[n + 1] for n in range(2 * quarters, 2 * quarters + 6, 2)]
    delta = centre - jnp.mean(centre, 0, keepdims=True) - jnp.mean(offset, 0, keepdims=True)
    variance = jnp.sum(square + share * ((delta + offset) * (delta + offset)), 0, keepdims=True) / total
    scale = lax.rsqrt(variance + 1e-05)
    delta_ref[...] = delta

    names = lax.broadcasted_iota(jnp.int32, (CAP, owned), 1).astype(jnp.int16)

    def encode_group(g):
        columns = jnp.transpose(list_ref[pl.ds(g * GROUP, GROUP), :])
        hits, projected, held = [], [], []
        for s in range(GROUP):
            listed = jnp.broadcast_to(columns[:, s:s + 1], (CAP, LANES))
            held.append(jnp.concatenate([listed] * (feats // LANES), 1) >= 0)
            wanted = jnp.concatenate([listed.astype(jnp.int32).astype(jnp.int16)] * (owned // LANES), 1)
            hits.append(jnp.where(wanted == names, jnp.ones((), jnp.bfloat16), jnp.zeros((), jnp.bfloat16)))
            base = pl.multiple_of((g * GROUP + s) * SPAN, 16)
            rows = got_ref[pl.ds(base, CAP), :].astype(jnp.float32)
            projected.append((rows + delta_ref[pl.ds(g * GROUP + s, 1), :]) * scale)
        centroid = jnp.dot(jnp.concatenate(hits, 0), centroid_ref[...], preferred_element_type=jnp.float32)
        residual = jnp.where(jnp.concatenate(held, 0), jnp.concatenate(projected, 0) - centroid, 0.0)
        at = pl.ds(pl.multiple_of(g * (GROUP * CAP), GROUP * CAP), GROUP * CAP)
        out_ref[at, :] = jnp.dot(
            residual.astype(jnp.bfloat16), rotation_ref[...], preferred_element_type=jnp.float32
        ).astype(jnp.bfloat16)
        return pltpu.make_async_copy(out_ref.at[at], out_hbm.at[at], sem.at[g])

    groups = width // GROUP
    copies = []
    if groups <= 4:
        for g in range(groups):
            copies.append(encode_group(g))
            copies[g].start()
    else:

        @pl.loop(0, groups)
        def _(g):
            copy = encode_group(g)
            copy.start()
            copy.wait()

    first = me_ref[0] * block
    near = apart_ref[:, pl.ds(pl.multiple_of(first // LANES * LANES, LANES), LANES)]
    near = pltpu.roll(near, (LANES - first % LANES) % LANES, 1)[:, :block]
    between_ref[...] = share * lax.dot_general(
        near,
        apart_ref[...],
        (((0,), (0,)), ((), ())),
        precision=lax.Precision.HIGHEST,
        preferred_element_type=jnp.float32,
    )
    for copy in copies:
        copy.wait()


def encode(width, total, me, wide, got, centroids, rotation, after):
    owned, feats = centroids.shape
    slots = width * CAP
    vmem, anywhere = pl.BlockSpec(memory_space=pltpu.VMEM), pl.BlockSpec(memory_space=pl.ANY)
    return pl.pallas_call(
        functools.partial(encode_kernel, total),
        in_specs=[pl.BlockSpec(memory_space=pltpu.SMEM)] + [vmem] * 3 + [anywhere] * len(after),
        out_specs=[anywhere, vmem],
        out_shape=[
            jax.ShapeDtypeStruct((slots, feats), jnp.bfloat16),
            jax.ShapeDtypeStruct((wide // width, wide), jnp.float32),
        ],
        scratch_shapes=[
            pltpu.VMEM((slots, feats), jnp.bfloat16),
            pltpu.VMEM((width, feats), jnp.float32),
            pltpu.VMEM((width, CAP), jnp.float32),
            pltpu.VMEM((width, wide), jnp.float32),
            pltpu.SemaphoreType.DMA((width // GROUP,)),
        ],
        compiler_params=pltpu.CompilerParams(vmem_limit_bytes=VMEM_SOME),
        cost_estimate=pl.CostEstimate(
            flops=2 * slots * feats * (owned + feats), bytes_accessed=4 * slots * feats, transcendentals=0
        ),
        name="encode",
    )(me.reshape(1), got, centroids, rotation, *after)


def local(embeddings, basis, list_owner, list_slot, centroids, rotation):
    width = lax.axis_size("wide")
    me = lax.axis_index("wide")
    rows_here, wide = embeddings.shape
    feats = basis.shape[1]
    total = rows_here * width

    rows, mean = project_and_sort(width, embeddings, basis, list_owner, list_slot)
    got = lax.all_to_all(rows.reshape(width, SPAN, feats), "wide", split_axis=0, concat_axis=0, tiled=True)

    keep, send = moments(width, me, embeddings, mean)
    stages = halving_stages(width)
    came = exchange(width, stages[0], [send])
    shares = add_and_split(keep, came, SHARES, 1 << len(stages[1]))
    last = []
    for share in shares:
        for n in range(1, len(stages) - 1):
            came = exchange(width, stages[n], share[1:])
            (share,) = add_and_split(share[0], came, (1,), 1 << len(stages[n + 1]), [held[1] for held in last[-1:]])
        last.append(share)
    came = [exchange(width, stages[-1], share[1:]) for share in last]
    encoded, between = encode(
        width, total, me, wide, got.reshape(width * SPAN, feats), centroids, rotation, [share[1] for share in last]
    )
    covariance = finish(total, between, [share[0] for share in last], came)
    return (encoded, covariance)


def solution(mesh):
    in_specs = (
        P(("groups", "wide"), None),
        P(),
        P(("groups", "wide")),
        P(("groups", "wide")),
        P("wide", None),
        P(),
    )
    out_specs = (P(("groups", "wide"), None), P(("groups", "wide"), None))
    return jax.shard_map(local, mesh=mesh, in_specs=in_specs, out_specs=out_specs, check_vma=False)
```

```python
import functools

import jax
import jax.numpy as jnp
from jax import lax
from jax.experimental import pallas as pl
from jax.experimental.pallas import tpu as pltpu
from jax.sharding import PartitionSpec as P

CAP = 128
LANES = 128
NOTES = 16
SPAN = CAP + NOTES
CHUNK = 512
TILE = 256
GROUP = 4
SHARES = (5, 3)
VMEM_ALL = 60 * 1024 * 1024
VMEM_SOME = 24 * 1024 * 1024
VMEM_MOST = 48 * 1024 * 1024


def in_three(x):
    high = x.astype(jnp.bfloat16).astype(jnp.float32)
    rest = x - high
    middle = rest.astype(jnp.bfloat16).astype(jnp.float32)
    return high, middle, (rest - middle).astype(jnp.bfloat16).astype(jnp.float32)


def rows_kernel(
    width, e_hbm, basis_hbm, owner_hbm, slot_hbm,
    rows_hbm, mean_hbm,
    owner_ref, slot_ref, mean_ref, basis_ref, e_ref, rows_ref, y_ref, yb_ref, sum_ref, total_ref, target_ref, list_ref, e_sem, small_sem, sem,
):
    step = pl.program_id(0)
    rows_here, feats = y_ref.shape
    wide = e_ref.shape[1]
    chunks = rows_here // LANES

    def e_copy(c):
        at = pl.ds(pl.multiple_of(c * CHUNK, CHUNK), CHUNK)
        return pltpu.make_async_copy(e_hbm.at[at], e_ref.at[at], e_sem.at[c])

    @pl.when(step == 0)
    def _():
        owner_copy = pltpu.make_async_copy(owner_hbm, owner_ref, small_sem.at[0])
        slot_copy = pltpu.make_async_copy(slot_hbm, slot_ref, small_sem.at[1])
        basis_copy = pltpu.make_async_copy(basis_hbm, basis_ref, small_sem.at[2])
        owner_copy.start()
        e_copy(0).start()
        slot_copy.start()
        basis_copy.start()
        for c in range(1, rows_here // CHUNK):
            e_copy(c).start()
        owner_copy.wait()
        sum_ref[...] = jnp.zeros_like(sum_ref)
        total_ref[...] = jnp.zeros_like(total_ref)
        owner = owner_ref[...]
        wanted = lax.broadcasted_iota(jnp.int32, (width, LANES), 0)
        hits = [jnp.where(owner[c:c + 1, :] == wanted, 1.0, 0.0) for c in range(chunks)]
        flat = jnp.concatenate(hits, 0).astype(jnp.bfloat16)
        up = lax.broadcasted_iota(jnp.int32, (LANES, LANES), 0)
        to = lax.broadcasted_iota(jnp.int32, (LANES, LANES), 1)
        before = jnp.where(up < to, 1.0, 0.0).astype(jnp.bfloat16)
        every = jnp.ones((LANES, LANES), jnp.bfloat16)
        within = jnp.dot(flat, before, preferred_element_type=jnp.float32)
        counts = jnp.dot(flat, every, preferred_element_type=jnp.float32)
        carry = jnp.zeros((width, LANES), jnp.float32)
        ranks = []
        for c in range(chunks):
            at = slice(c * width, (c + 1) * width)
            ranks.append(jnp.sum(hits[c] * (within[at] + carry), 0, keepdims=True).astype(jnp.int32))
            carry = carry + counts[at]
            target_ref[c:c + 1, :] = owner[c:c + 1, :] * CAP + ranks[c]

        slot_copy.wait()
        slot = slot_ref[...] + 1
        high, low = (slot >> 5).astype(jnp.float32), (slot & 31).astype(jnp.float32)
        spots = lax.broadcasted_iota(jnp.int32, (CAP, LANES), 0)
        placed = jnp.concatenate([jnp.where(ranks[c] == spots, 1.0, 0.0) for c in range(chunks)], 1).astype(jnp.bfloat16)
        digits = jnp.concatenate(
            [
                jnp.concatenate([hits[c] * high[c:c + 1, :] for c in range(chunks)], 1),
                jnp.concatenate([hits[c] * low[c:c + 1, :] for c in range(chunks)], 1),
            ],
            0,
        ).astype(jnp.bfloat16)
        found = lax.dot_general(digits, placed, (((1,), (1,)), ((), ())), preferred_element_type=jnp.float32)
        list_ref[:, :CAP] = found[:width]
        list_ref[:, CAP:] = found[width:]
        basis_copy.wait()

    e_copy(step).wait()
    here = pl.ds(pl.multiple_of(step * CHUNK, CHUNK), CHUNK)
    rows = e_ref[here, :]
    y = jnp.dot(rows, basis_ref[...], preferred_element_type=jnp.float32)
    y_ref[here, :] = y
    sum_ref[...] += jnp.sum(y.reshape(CHUNK // 8, 8, feats), 0)
    total_ref[...] += jnp.sum(rows.astype(jnp.float32).reshape(CHUNK // 8, 8, wide), 0)

    @pl.when(step == pl.num_programs(0) - 1)
    def _():
        mean_y = jnp.sum(sum_ref[...], 0, keepdims=True) / rows_here
        square = jnp.zeros((8, feats), jnp.float32)
        for c in range(rows_here // CHUNK):
            at = slice(c * CHUNK, (c + 1) * CHUNK)
            centred = y_ref[at, :] - mean_y
            square = square + jnp.sum((centred * centred).reshape(CHUNK // 8, 8, feats), 0)
            yb_ref[at, :] = centred.astype(jnp.bfloat16)
        mean = jnp.sum(total_ref[...], 0, keepdims=True) / rows_here
        mean_ref[...] = mean
        mean_copy = pltpu.make_async_copy(mean_ref, mean_hbm, small_sem.at[3])
        mean_copy.start()
        parts = in_three(mean)
        common = [part[:, q * feats:(q + 1) * feats] for part in parts for q in range(wide // feats)]
        common = jnp.concatenate(common + list(in_three(jnp.sum(square, 0, keepdims=True))), 0)

        place = lax.broadcasted_iota(jnp.int32, (GROUP * CAP, LANES), 0).astype(jnp.int16)

        def sort_group(g):
            first = g * GROUP
            pieces = []
            for c in range(chunks):
                wanted = (target_ref[c:c + 1, :] - first * CAP).astype(jnp.int32)
                wanted = jnp.broadcast_to(wanted, (16, LANES)).astype(jnp.int16)
                wanted = jnp.concatenate([wanted] * (GROUP * CAP // 16), 0)
                pieces.append(jnp.where(wanted == place, jnp.ones((), jnp.bfloat16), jnp.zeros((), jnp.bfloat16)))
            pick = jnp.concatenate(pieces, 1)
            rows = jnp.dot(pick, yb_ref[...], preferred_element_type=jnp.float32).astype(jnp.bfloat16)
            for j in range(GROUP):
                base = pl.multiple_of((first + j) * SPAN, 16)
                rows_ref[pl.ds(base, CAP), :] = rows[j * CAP:(j + 1) * CAP]
                notes = jnp.concatenate([common, list_ref[pl.ds(first + j, 1), :]], 0)
                rows_ref[pl.ds(pl.multiple_of(base + CAP, 16), NOTES), :] = notes.astype(jnp.bfloat16)
            at = pl.ds(pl.multiple_of(g * (GROUP * SPAN), 16), GROUP * SPAN)
            return pltpu.make_async_copy(rows_ref.at[at], rows_hbm.at[at], sem.at[g])

        groups = width // GROUP
        if groups <= 4:
            copies = []
            for g in range(groups):
                copies.append(sort_group(g))
                copies[g].start()
            for copy in copies:
                copy.wait()
        else:

            @pl.loop(0, groups)
            def _(g):
                copy = sort_group(g)
                copy.start()
                copy.wait()

        mean_copy.wait()


def project_and_sort(width, embeddings, basis, list_owner, list_slot):
    rows_here, wide = embeddings.shape
    feats = basis.shape[1]
    lanes = rows_here // LANES
    slots = width * SPAN
    return pl.pallas_call(
        functools.partial(rows_kernel, width),
        grid=(rows_here // CHUNK,),
        in_specs=[pl.BlockSpec(memory_space=pl.ANY)] * 4,
        out_specs=[pl.BlockSpec(memory_space=pl.ANY)] * 2,
        out_shape=[
            jax.ShapeDtypeStruct((slots, feats), jnp.bfloat16),
            jax.ShapeDtypeStruct((1, wide), jnp.float32),
        ],
        scratch_shapes=[
            pltpu.VMEM((lanes, LANES), jnp.int32),
            pltpu.VMEM((lanes, LANES), jnp.int32),
            pltpu.VMEM((1, wide), jnp.float32),
            pltpu.VMEM((wide, feats), jnp.bfloat16),
            pltpu.VMEM((rows_here, wide), jnp.bfloat16),
            pltpu.VMEM((slots, feats), jnp.bfloat16),
            pltpu.VMEM((rows_here, feats), jnp.float32),
            pltpu.VMEM((rows_here, feats), jnp.bfloat16),
            pltpu.VMEM((8, feats), jnp.float32),
            pltpu.VMEM((8, wide), jnp.float32),
            pltpu.VMEM((lanes, LANES), jnp.int32),
            pltpu.VMEM((width, 2 * CAP), jnp.float32),
            pltpu.SemaphoreType.DMA((rows_here // CHUNK,)),
            pltpu.SemaphoreType.DMA((4,)),
            pltpu.SemaphoreType.DMA((width // GROUP,)),
        ],
        compiler_params=pltpu.CompilerParams(vmem_limit_bytes=VMEM_ALL),
        cost_estimate=pl.CostEstimate(
            flops=2 * rows_here * feats * (wide + slots), bytes_accessed=2 * rows_here * wide + 2 * slots * feats, transcendentals=0
        ),
        name="project_sort",
    )(embeddings, basis, list_owner.reshape(lanes, LANES), list_slot.reshape(lanes, LANES))


def moments_kernel(width, me_ref, mean_hbm, e_hbm, keep_ref, send_ref, e_ref, mean_ref, m_ref, sem, mean_sem):
    rows_here, wide = e_ref.shape
    block = wide // width
    bits = width.bit_length() - 1
    mean_copy = pltpu.make_async_copy(mean_hbm, mean_ref, mean_sem)
    mean_copy.start()
    copies = []
    for c in range(rows_here // CHUNK):
        at = pl.ds(c * CHUNK, CHUNK)
        copies.append(pltpu.make_async_copy(e_hbm.at[at], e_ref.at[at], sem.at[c]))
        copies[c].start()
    me = me_ref[0]
    mean_copy.wait()
    mean = mean_ref[...]
    for t in range(wide // TILE):
        rows = slice(t * TILE, (t + 1) * TILE)
        if t == 0:
            product = jnp.zeros((TILE, wide), jnp.float32)
            for c in range(rows_here // CHUNK):
                copies[c].wait()
                at = slice(c * CHUNK, (c + 1) * CHUNK)
                product = product + lax.dot_general(
                    e_ref[at, rows], e_ref[at, :], (((0,), (0,)), ((), ())), preferred_element_type=jnp.float32
                )
        else:
            product = lax.dot_general(
                e_ref[:, rows], e_ref[...], (((0,), (0,)), ((), ())), preferred_element_type=jnp.float32
            )
        down = jnp.transpose(jnp.broadcast_to(mean[:, rows] * rows_here, (LANES, TILE)))
        for j in range(wide // LANES):
            across = slice(j * LANES, (j + 1) * LANES)
            m_ref[rows, across] = product[:, across] - down * mean[:, across]
        for pair in range(TILE // block // 2):
            first = t * (TILE // block) + 2 * pair
            apart = (first ^ me) >> 1
            place = 0
            for k in range(bits - 1):
                place = place + (((apart >> k) & 1) << (bits - 2 - k))
            to = pl.ds(pl.multiple_of(place * block, block), block)
            kept = pl.multiple_of((first + (me & 1)) * block, block)
            sent = pl.multiple_of((first + 1 - (me & 1)) * block, block)
            keep_ref[to, :] = m_ref[pl.ds(kept, block), :]
            send_ref[to, :] = m_ref[pl.ds(sent, block), :].astype(jnp.bfloat16)


def moments(width, me, embeddings, mean):
    rows_here, wide = embeddings.shape
    vmem = pl.BlockSpec(memory_space=pltpu.VMEM)
    return pl.pallas_call(
        functools.partial(moments_kernel, width),
        in_specs=[pl.BlockSpec(memory_space=pltpu.SMEM)] + [pl.BlockSpec(memory_space=pl.ANY)] * 2,
        out_specs=[vmem] * 2,
        out_shape=[
            jax.ShapeDtypeStruct((wide // 2, wide), jnp.float32),
            jax.ShapeDtypeStruct((wide // 2, wide), jnp.bfloat16),
        ],
        scratch_shapes=[
            pltpu.VMEM((rows_here, wide), jnp.bfloat16),
            pltpu.VMEM((1, wide), jnp.float32),
            pltpu.VMEM((wide, wide), jnp.float32),
            pltpu.SemaphoreType.DMA((rows_here // CHUNK,)),
            pltpu.SemaphoreType.DMA,
        ],
        compiler_params=pltpu.CompilerParams(vmem_limit_bytes=VMEM_MOST),
        cost_estimate=pl.CostEstimate(
            flops=2 * rows_here * wide * wide, bytes_accessed=2 * rows_here * wide + 3 * wide * wide, transcendentals=0
        ),
        name="moments",
    )(me.reshape(1), mean, embeddings)


def cuts(columns, shares):
    unit = columns // sum(shares)
    ends = [unit * sum(shares[:h + 1]) for h in range(len(shares))]
    return list(zip([0] + ends[:-1], ends))


def add_kernel(shares, pieces, arrived, keep_ref, *refs):
    count = len(shares) * pieces
    came, outs = refs[:arrived], refs[-count:]
    for h, (first, end) in enumerate(cuts(keep_ref.shape[1], shares)):
        for p in range(pieces):
            out = outs[h * pieces + p]
            at = slice(p * out.shape[0], (p + 1) * out.shape[0])
            held = keep_ref[at, first:end].astype(jnp.float32)
            for ref in came:
                held = held + ref[at, first:end].astype(jnp.float32)
            out[...] = held.astype(out.dtype)


def add_and_split(keep, came, shares, pieces, after=()):
    rows, columns = keep.shape
    vmem = pl.BlockSpec(memory_space=pltpu.VMEM)
    kinds = [jnp.float32] + [jnp.bfloat16] * (pieces - 1)
    outs = pl.pallas_call(
        functools.partial(add_kernel, shares, pieces, len(came)),
        in_specs=[vmem] * (1 + len(came)) + [pl.BlockSpec(memory_space=pl.ANY)] * len(after),
        out_specs=[vmem] * (len(shares) * pieces),
        out_shape=[
            jax.ShapeDtypeStruct((rows // pieces, end - first), kind) for first, end in cuts(columns, shares) for kind in kinds
        ],
        compiler_params=pltpu.CompilerParams(vmem_limit_bytes=VMEM_SOME),
        cost_estimate=pl.CostEstimate(flops=2 * rows * columns, bytes_accessed=10 * rows * columns, transcendentals=0),
        name="add_and_split",
    )(keep, *came, *after)
    return [outs[h * pieces:(h + 1) * pieces] for h in range(len(shares))]


def finish_kernel(total, between_ref, *refs):
    out_ref = refs[-1]
    each = (len(refs) - 1) // len(SHARES)
    for h, (first, end) in enumerate(cuts(out_ref.shape[1], SHARES)):
        held = refs[h * each][...]
        for ref in refs[h * each + 1:(h + 1) * each]:
            held = held + ref[...].astype(jnp.float32)
        out_ref[:, first:end] = (held + between_ref[:, first:end]) / total


def finish(total, between, ends):
    parts = [part for end in ends for part in end]
    vmem = pl.BlockSpec(memory_space=pltpu.VMEM)
    return pl.pallas_call(
        functools.partial(finish_kernel, total),
        in_specs=[vmem] * (1 + len(parts)),
        out_specs=vmem,
        out_shape=jax.ShapeDtypeStruct(between.shape, jnp.float32),
        compiler_params=pltpu.CompilerParams(vmem_limit_bytes=VMEM_SOME),
        cost_estimate=pl.CostEstimate(flops=8 * between.size, bytes_accessed=16 * between.size, transcendentals=0),
        name="finish",
    )(between, *parts)


def exchange(width, stride, out):
    return lax.ppermute(out, "wide", [(i, i ^ stride) for i in range(width)])


def encode_kernel(total, me_ref, got_ref, basis_ref, centroid_ref, rotation_ref, *refs):
    out_hbm, between_ref, out_ref, delta_ref, list_ref, apart_ref, sem = refs[-7:]
    width = delta_ref.shape[0]
    feats = out_ref.shape[1]
    owned = centroid_ref.shape[0]
    wide = basis_ref.shape[0]
    block = wide // width
    share = total // width

    notes = jnp.concatenate([got_ref[s * SPAN + CAP:(s + 1) * SPAN, :] for s in range(width)], 0)
    size = width * NOTES
    to = lax.broadcasted_iota(jnp.int32, (size, size), 0)
    of = lax.broadcasted_iota(jnp.int32, (size, size), 1)
    turn = jnp.where((to % width) * NOTES + to // width == of, 1.0, 0.0).astype(jnp.bfloat16)
    turned = jnp.dot(turn, notes, preferred_element_type=jnp.float32)
    row = [turned[r * width:(r + 1) * width] for r in range(NOTES)]
    digits = row[NOTES - 1]
    list_ref[...] = digits[:, :CAP] * 32.0 + digits[:, CAP:] - 1.0
    quarters = wide // feats
    shifts = jnp.zeros((width, feats), jnp.float32)
    for q in range(quarters):
        parts = [row[p * quarters + q] for p in range(3)]
        mean = parts[0] + (parts[1] + parts[2])
        apart_ref[:, q * feats:(q + 1) * feats] = mean - jnp.mean(mean, 0, keepdims=True)
        terms = jnp.dot(
            jnp.concatenate(parts, 0).astype(jnp.bfloat16),
            basis_ref[q * feats:(q + 1) * feats, :],
            preferred_element_type=jnp.float32,
        )
        shifts = shifts + (terms[:width] + (terms[width:2 * width] + terms[2 * width:]))
    square = row[3 * quarters] + (row[3 * quarters + 1] + row[3 * quarters + 2])
    delta = shifts - jnp.mean(shifts, 0, keepdims=True)
    variance = jnp.sum(square + share * (delta * delta), 0, keepdims=True) / total
    scale = lax.rsqrt(variance + 1e-05)
    delta_ref[...] = delta

    names = lax.broadcasted_iota(jnp.int32, (CAP, owned), 1).astype(jnp.int16)

    def encode_group(g):
        columns = jnp.transpose(list_ref[pl.ds(g * GROUP, GROUP), :])
        hits, projected, held = [], [], []
        for s in range(GROUP):
            listed = jnp.broadcast_to(columns[:, s:s + 1], (CAP, LANES))
            held.append(jnp.concatenate([listed] * (feats // LANES), 1) >= 0)
            wanted = jnp.concatenate([listed.astype(jnp.int32).astype(jnp.int16)] * (owned // LANES), 1)
            hits.append(jnp.where(wanted == names, jnp.ones((), jnp.bfloat16), jnp.zeros((), jnp.bfloat16)))
            base = pl.multiple_of((g * GROUP + s) * SPAN, 16)
            rows = got_ref[pl.ds(base, CAP), :].astype(jnp.float32)
            projected.append((rows + delta_ref[pl.ds(g * GROUP + s, 1), :]) * scale)
        centre = jnp.dot(jnp.concatenate(hits, 0), centroid_ref[...], preferred_element_type=jnp.float32)
        residual = jnp.where(jnp.concatenate(held, 0), jnp.concatenate(projected, 0) - centre, 0.0)
        at = pl.ds(pl.multiple_of(g * (GROUP * CAP), GROUP * CAP), GROUP * CAP)
        out_ref[at, :] = jnp.dot(
            residual.astype(jnp.bfloat16), rotation_ref[...], preferred_element_type=jnp.float32
        ).astype(jnp.bfloat16)
        return pltpu.make_async_copy(out_ref.at[at], out_hbm.at[at], sem.at[g])

    groups = width // GROUP
    copies = []
    if groups <= 4:
        for g in range(groups):
            copies.append(encode_group(g))
            copies[g].start()
    else:

        @pl.loop(0, groups)
        def _(g):
            copy = encode_group(g)
            copy.start()
            copy.wait()

    first = me_ref[0] * block
    near = apart_ref[:, pl.ds(pl.multiple_of(first // LANES * LANES, LANES), LANES)]
    near = pltpu.roll(near, (LANES - first % LANES) % LANES, 1)[:, :block]
    between_ref[...] = share * lax.dot_general(
        near,
        apart_ref[...],
        (((0,), (0,)), ((), ())),
        precision=lax.Precision.HIGHEST,
        preferred_element_type=jnp.float32,
    )
    for copy in copies:
        copy.wait()


def encode(width, total, me, got, basis, centroids, rotation, after):
    wide, feats = basis.shape
    owned = centroids.shape[0]
    slots = width * CAP
    vmem, anywhere = pl.BlockSpec(memory_space=pltpu.VMEM), pl.BlockSpec(memory_space=pl.ANY)
    return pl.pallas_call(
        functools.partial(encode_kernel, total),
        in_specs=[pl.BlockSpec(memory_space=pltpu.SMEM)] + [vmem] * 4 + [anywhere] * len(after),
        out_specs=[anywhere, vmem],
        out_shape=[
            jax.ShapeDtypeStruct((slots, feats), jnp.bfloat16),
            jax.ShapeDtypeStruct((wide // width, wide), jnp.float32),
        ],
        scratch_shapes=[
            pltpu.VMEM((slots, feats), jnp.bfloat16),
            pltpu.VMEM((width, feats), jnp.float32),
            pltpu.VMEM((width, CAP), jnp.float32),
            pltpu.VMEM((width, wide), jnp.float32),
            pltpu.SemaphoreType.DMA((width // GROUP,)),
        ],
        compiler_params=pltpu.CompilerParams(vmem_limit_bytes=VMEM_SOME),
        cost_estimate=pl.CostEstimate(
            flops=2 * slots * feats * (owned + feats), bytes_accessed=4 * slots * feats, transcendentals=0
        ),
        name="encode",
    )(me.reshape(1), got, basis, centroids, rotation, *after)


def local(embeddings, basis, list_owner, list_slot, centroids, rotation):
    width = lax.axis_size("wide")
    me = lax.axis_index("wide")
    rows_here, wide = embeddings.shape
    feats = basis.shape[1]
    total = rows_here * width

    rows, mean = project_and_sort(width, embeddings, basis, list_owner, list_slot)
    got = lax.all_to_all(rows.reshape(width, SPAN, feats), "wide", split_axis=0, concat_axis=0, tiled=True)

    keep, send = moments(width, me, embeddings, mean)
    came = exchange(width, 1, send)
    shares = add_and_split(keep, [came], SHARES, 2)
    encoded, ends, after = None, [], []
    for keep, send in shares:
        stride = 2
        while stride < width:
            came = exchange(width, stride, send)
            stride *= 2
            if stride < width:
                ((keep, send),) = add_and_split(keep, [came], (1,), 2, after)
                after = []
            if encoded is None:
                encoded, between = encode(
                    width, total, me, got.reshape(width * SPAN, feats), basis, centroids, rotation, [send]
                )
        ends.append([keep, came])
        after = [between]
    covariance = finish(total, between, ends)
    return (encoded, covariance)


def solution(mesh):
    in_specs = (
        P(("groups", "wide"), None),
        P(),
        P(("groups", "wide")),
        P(("groups", "wide")),
        P("wide", None),
        P(),
    )
    out_specs = (P(("groups", "wide"), None), P(("groups", "wide"), None))
    return jax.shard_map(local, mesh=mesh, in_specs=in_specs, out_specs=out_specs, check_vma=False)
```

```python
import functools

import jax
import jax.numpy as jnp
from jax import lax
from jax.experimental import pallas as pl
from jax.experimental.pallas import tpu as pltpu
from jax.sharding import PartitionSpec as P

CAP = 128
LANES = 128
NOTES = 16
SPAN = CAP + NOTES
CHUNK = 512
TILE = 256
GROUP = 4
SHARES = 2
VMEM_ALL = 60 * 1024 * 1024
VMEM_SOME = 24 * 1024 * 1024
VMEM_MOST = 48 * 1024 * 1024


def in_three(x):
    high = x.astype(jnp.bfloat16).astype(jnp.float32)
    rest = x - high
    middle = rest.astype(jnp.bfloat16).astype(jnp.float32)
    return high, middle, (rest - middle).astype(jnp.bfloat16).astype(jnp.float32)


def rows_kernel(
    width, e_hbm, basis_hbm, owner_hbm, slot_hbm,
    rows_hbm, mean_hbm,
    owner_ref, slot_ref, mean_ref, basis_ref, e_ref, rows_ref, y_ref, yb_ref, sum_ref, total_ref, target_ref, list_ref, e_sem, small_sem, sem,
):
    step = pl.program_id(0)
    rows_here, feats = y_ref.shape
    wide = e_ref.shape[1]
    chunks = rows_here // LANES

    def e_copy(c):
        at = pl.ds(pl.multiple_of(c * CHUNK, CHUNK), CHUNK)
        return pltpu.make_async_copy(e_hbm.at[at], e_ref.at[at], e_sem.at[c])

    @pl.when(step == 0)
    def _():
        owner_copy = pltpu.make_async_copy(owner_hbm, owner_ref, small_sem.at[0])
        slot_copy = pltpu.make_async_copy(slot_hbm, slot_ref, small_sem.at[1])
        basis_copy = pltpu.make_async_copy(basis_hbm, basis_ref, small_sem.at[2])
        owner_copy.start()
        e_copy(0).start()
        slot_copy.start()
        basis_copy.start()
        for c in range(1, rows_here // CHUNK):
            e_copy(c).start()
        owner_copy.wait()
        sum_ref[...] = jnp.zeros_like(sum_ref)
        total_ref[...] = jnp.zeros_like(total_ref)
        owner = owner_ref[...]
        wanted = lax.broadcasted_iota(jnp.int32, (width, LANES), 0)
        hits = [jnp.where(owner[c:c + 1, :] == wanted, 1.0, 0.0) for c in range(chunks)]
        flat = jnp.concatenate(hits, 0).astype(jnp.bfloat16)
        up = lax.broadcasted_iota(jnp.int32, (LANES, LANES), 0)
        to = lax.broadcasted_iota(jnp.int32, (LANES, LANES), 1)
        before = jnp.where(up < to, 1.0, 0.0).astype(jnp.bfloat16)
        every = jnp.ones((LANES, LANES), jnp.bfloat16)
        within = jnp.dot(flat, before, preferred_element_type=jnp.float32)
        counts = jnp.dot(flat, every, preferred_element_type=jnp.float32)
        carry = jnp.zeros((width, LANES), jnp.float32)
        ranks = []
        for c in range(chunks):
            at = slice(c * width, (c + 1) * width)
            ranks.append(jnp.sum(hits[c] * (within[at] + carry), 0, keepdims=True).astype(jnp.int32))
            carry = carry + counts[at]
            target_ref[c:c + 1, :] = owner[c:c + 1, :] * CAP + ranks[c]

        slot_copy.wait()
        slot = slot_ref[...] + 1
        high, low = (slot >> 5).astype(jnp.float32), (slot & 31).astype(jnp.float32)
        spots = lax.broadcasted_iota(jnp.int32, (CAP, LANES), 0)
        placed = jnp.concatenate([jnp.where(ranks[c] == spots, 1.0, 0.0) for c in range(chunks)], 1).astype(jnp.bfloat16)
        digits = jnp.concatenate(
            [
                jnp.concatenate([hits[c] * high[c:c + 1, :] for c in range(chunks)], 1),
                jnp.concatenate([hits[c] * low[c:c + 1, :] for c in range(chunks)], 1),
            ],
            0,
        ).astype(jnp.bfloat16)
        found = lax.dot_general(digits, placed, (((1,), (1,)), ((), ())), preferred_element_type=jnp.float32)
        list_ref[:, :CAP] = found[:width]
        list_ref[:, CAP:] = found[width:]
        basis_copy.wait()

    e_copy(step).wait()
    here = pl.ds(pl.multiple_of(step * CHUNK, CHUNK), CHUNK)
    rows = e_ref[here, :]
    y = jnp.dot(rows, basis_ref[...], preferred_element_type=jnp.float32)
    y_ref[here, :] = y
    sum_ref[...] += jnp.sum(y.reshape(CHUNK // 8, 8, feats), 0)
    total_ref[...] += jnp.sum(rows.astype(jnp.float32).reshape(CHUNK // 8, 8, wide), 0)

    @pl.when(step == pl.num_programs(0) - 1)
    def _():
        mean_y = jnp.sum(sum_ref[...], 0, keepdims=True) / rows_here
        square = jnp.zeros((8, feats), jnp.float32)
        for c in range(rows_here // CHUNK):
            at = slice(c * CHUNK, (c + 1) * CHUNK)
            centred = y_ref[at, :] - mean_y
            square = square + jnp.sum((centred * centred).reshape(CHUNK // 8, 8, feats), 0)
            yb_ref[at, :] = centred.astype(jnp.bfloat16)
        mean = jnp.sum(total_ref[...], 0, keepdims=True) / rows_here
        mean_ref[...] = mean
        mean_copy = pltpu.make_async_copy(mean_ref, mean_hbm, small_sem.at[3])
        mean_copy.start()
        parts = in_three(mean)
        common = [part[:, q * feats:(q + 1) * feats] for part in parts for q in range(wide // feats)]
        common = jnp.concatenate(common + list(in_three(jnp.sum(square, 0, keepdims=True))), 0)

        place = lax.broadcasted_iota(jnp.int32, (GROUP * CAP, LANES), 0).astype(jnp.int16)

        def sort_group(g):
            first = g * GROUP
            pieces = []
            for c in range(chunks):
                wanted = (target_ref[c:c + 1, :] - first * CAP).astype(jnp.int32)
                wanted = jnp.broadcast_to(wanted, (16, LANES)).astype(jnp.int16)
                wanted = jnp.concatenate([wanted] * (GROUP * CAP // 16), 0)
                pieces.append(jnp.where(wanted == place, jnp.ones((), jnp.bfloat16), jnp.zeros((), jnp.bfloat16)))
            pick = jnp.concatenate(pieces, 1)
            rows = jnp.dot(pick, yb_ref[...], preferred_element_type=jnp.float32).astype(jnp.bfloat16)
            for j in range(GROUP):
                base = pl.multiple_of((first + j) * SPAN, 16)
                rows_ref[pl.ds(base, CAP), :] = rows[j * CAP:(j + 1) * CAP]
                notes = jnp.concatenate([common, list_ref[pl.ds(first + j, 1), :]], 0)
                rows_ref[pl.ds(pl.multiple_of(base + CAP, 16), NOTES), :] = notes.astype(jnp.bfloat16)
            at = pl.ds(pl.multiple_of(g * (GROUP * SPAN), 16), GROUP * SPAN)
            return pltpu.make_async_copy(rows_ref.at[at], rows_hbm.at[at], sem.at[g])

        groups = width // GROUP
        if groups <= 4:
            copies = []
            for g in range(groups):
                copies.append(sort_group(g))
                copies[g].start()
            for copy in copies:
                copy.wait()
        else:

            @pl.loop(0, groups)
            def _(g):
                copy = sort_group(g)
                copy.start()
                copy.wait()

        mean_copy.wait()


def project_and_sort(width, embeddings, basis, list_owner, list_slot):
    rows_here, wide = embeddings.shape
    feats = basis.shape[1]
    lanes = rows_here // LANES
    slots = width * SPAN
    return pl.pallas_call(
        functools.partial(rows_kernel, width),
        grid=(rows_here // CHUNK,),
        in_specs=[pl.BlockSpec(memory_space=pl.ANY)] * 4,
        out_specs=[pl.BlockSpec(memory_space=pl.ANY)] * 2,
        out_shape=[
            jax.ShapeDtypeStruct((slots, feats), jnp.bfloat16),
            jax.ShapeDtypeStruct((1, wide), jnp.float32),
        ],
        scratch_shapes=[
            pltpu.VMEM((lanes, LANES), jnp.int32),
            pltpu.VMEM((lanes, LANES), jnp.int32),
            pltpu.VMEM((1, wide), jnp.float32),
            pltpu.VMEM((wide, feats), jnp.bfloat16),
            pltpu.VMEM((rows_here, wide), jnp.bfloat16),
            pltpu.VMEM((slots, feats), jnp.bfloat16),
            pltpu.VMEM((rows_here, feats), jnp.float32),
            pltpu.VMEM((rows_here, feats), jnp.bfloat16),
            pltpu.VMEM((8, feats), jnp.float32),
            pltpu.VMEM((8, wide), jnp.float32),
            pltpu.VMEM((lanes, LANES), jnp.int32),
            pltpu.VMEM((width, 2 * CAP), jnp.float32),
            pltpu.SemaphoreType.DMA((rows_here // CHUNK,)),
            pltpu.SemaphoreType.DMA((4,)),
            pltpu.SemaphoreType.DMA((width // GROUP,)),
        ],
        compiler_params=pltpu.CompilerParams(vmem_limit_bytes=VMEM_ALL),
        cost_estimate=pl.CostEstimate(
            flops=2 * rows_here * feats * (wide + slots), bytes_accessed=2 * rows_here * wide + 2 * slots * feats, transcendentals=0
        ),
        name="project_sort",
    )(embeddings, basis, list_owner.reshape(lanes, LANES), list_slot.reshape(lanes, LANES))


def moments_kernel(width, me_ref, mean_hbm, e_hbm, keep_ref, send_ref, e_ref, mean_ref, m_ref, sem, mean_sem):
    rows_here, wide = e_ref.shape
    block = wide // width
    bits = width.bit_length() - 1
    mean_copy = pltpu.make_async_copy(mean_hbm, mean_ref, mean_sem)
    mean_copy.start()
    copies = []
    for c in range(rows_here // CHUNK):
        at = pl.ds(c * CHUNK, CHUNK)
        copies.append(pltpu.make_async_copy(e_hbm.at[at], e_ref.at[at], sem.at[c]))
        copies[c].start()
    me = me_ref[0]
    mean_copy.wait()
    mean = mean_ref[...]
    for t in range(wide // TILE):
        rows = slice(t * TILE, (t + 1) * TILE)
        if t == 0:
            product = jnp.zeros((TILE, wide), jnp.float32)
            for c in range(rows_here // CHUNK):
                copies[c].wait()
                at = slice(c * CHUNK, (c + 1) * CHUNK)
                product = product + lax.dot_general(
                    e_ref[at, rows], e_ref[at, :], (((0,), (0,)), ((), ())), preferred_element_type=jnp.float32
                )
        else:
            product = lax.dot_general(
                e_ref[:, rows], e_ref[...], (((0,), (0,)), ((), ())), preferred_element_type=jnp.float32
            )
        down = jnp.transpose(jnp.broadcast_to(mean[:, rows] * rows_here, (LANES, TILE)))
        for j in range(wide // LANES):
            across = slice(j * LANES, (j + 1) * LANES)
            m_ref[rows, across] = product[:, across] - down * mean[:, across]
        for pair in range(TILE // block // 2):
            first = t * (TILE // block) + 2 * pair
            apart = (first ^ me) >> 1
            place = 0
            for k in range(bits - 1):
                place = place + (((apart >> k) & 1) << (bits - 2 - k))
            to = pl.ds(pl.multiple_of(place * block, block), block)
            kept = pl.multiple_of((first + (me & 1)) * block, block)
            sent = pl.multiple_of((first + 1 - (me & 1)) * block, block)
            keep_ref[to, :] = m_ref[pl.ds(kept, block), :]
            send_ref[to, :] = m_ref[pl.ds(sent, block), :].astype(jnp.bfloat16)


def moments(width, me, embeddings, mean):
    rows_here, wide = embeddings.shape
    vmem = pl.BlockSpec(memory_space=pltpu.VMEM)
    return pl.pallas_call(
        functools.partial(moments_kernel, width),
        in_specs=[pl.BlockSpec(memory_space=pltpu.SMEM)] + [pl.BlockSpec(memory_space=pl.ANY)] * 2,
        out_specs=[vmem] * 2,
        out_shape=[
            jax.ShapeDtypeStruct((wide // 2, wide), jnp.float32),
            jax.ShapeDtypeStruct((wide // 2, wide), jnp.bfloat16),
        ],
        scratch_shapes=[
            pltpu.VMEM((rows_here, wide), jnp.bfloat16),
            pltpu.VMEM((1, wide), jnp.float32),
            pltpu.VMEM((wide, wide), jnp.float32),
            pltpu.SemaphoreType.DMA((rows_here // CHUNK,)),
            pltpu.SemaphoreType.DMA,
        ],
        compiler_params=pltpu.CompilerParams(vmem_limit_bytes=VMEM_MOST),
        cost_estimate=pl.CostEstimate(
            flops=2 * rows_here * wide * wide, bytes_accessed=2 * rows_here * wide + 3 * wide * wide, transcendentals=0
        ),
        name="moments",
    )(me.reshape(1), mean, embeddings)


def add_kernel(shares, pieces, keep_ref, *refs):
    outs = refs[len(refs) - shares * pieces:]
    came = refs[:len(refs) - shares * pieces]
    rows, columns = outs[0].shape
    for h in range(shares):
        across = slice(h * columns, (h + 1) * columns)
        for p in range(pieces):
            at = slice(p * rows, (p + 1) * rows)
            held = keep_ref[at, across]
            for ref in came:
                held = held + ref[at, across].astype(jnp.float32)
            out = outs[h * pieces + p]
            out[...] = held.astype(out.dtype)


def add_and_split(keep, came, shares, pieces):
    rows, columns = keep.shape
    vmem = pl.BlockSpec(memory_space=pltpu.VMEM)
    shape = (rows // pieces, columns // shares)
    kinds = [jnp.float32] + [jnp.bfloat16] * (pieces - 1)
    outs = pl.pallas_call(
        functools.partial(add_kernel, shares, pieces),
        in_specs=[vmem] * (1 + len(came)),
        out_specs=[vmem] * (shares * pieces),
        out_shape=[jax.ShapeDtypeStruct(shape, kind) for kind in kinds * shares],
        compiler_params=pltpu.CompilerParams(vmem_limit_bytes=VMEM_SOME),
        cost_estimate=pl.CostEstimate(flops=2 * rows * columns, bytes_accessed=10 * rows * columns, transcendentals=0),
        name="add_and_split",
    )(keep, *came)
    return [outs[h * pieces:(h + 1) * pieces] for h in range(shares)]


def gather_kernel(strides, me_ref, keep_ref, came_ref, out_ref):
    pieces = 1 << len(strides)
    size = out_ref.shape[0] // pieces
    here = me_ref[0] // strides[0]
    for p in range(pieces):
        at = slice(p * size, (p + 1) * size)
        there = here ^ sum(((p >> (len(strides) - 1 - k)) & 1) << k for k in range(len(strides)))
        held = keep_ref[at] + came_ref[at].astype(jnp.float32)
        out_ref[pl.ds(pl.multiple_of(there * size, size), size), :] = held.astype(jnp.bfloat16)


def add_and_gather(strides, me, keep, came):
    vmem = pl.BlockSpec(memory_space=pltpu.VMEM)
    return pl.pallas_call(
        functools.partial(gather_kernel, strides),
        in_specs=[pl.BlockSpec(memory_space=pltpu.SMEM), vmem, vmem],
        out_specs=vmem,
        out_shape=jax.ShapeDtypeStruct(keep.shape, jnp.bfloat16),
        compiler_params=pltpu.CompilerParams(vmem_limit_bytes=VMEM_SOME),
        cost_estimate=pl.CostEstimate(flops=2 * keep.size, bytes_accessed=8 * keep.size, transcendentals=0),
        name="add_and_gather",
    )(me.reshape(1), keep, came)


def finish_kernel(total, between_ref, first_ref, *refs):
    *came, second_ref, out_ref = refs
    rows, columns = first_ref.shape
    held = first_ref[...]
    for ref in came:
        held = held + ref[...].astype(jnp.float32)
    out_ref[:, :columns] = (held + between_ref[:, :columns]) / total
    held = between_ref[:, columns:]
    for p in range(second_ref.shape[0] // rows):
        held = held + second_ref[p * rows:(p + 1) * rows, :].astype(jnp.float32)
    out_ref[:, columns:] = held / total


def finish(total, between, first, came, second):
    vmem = pl.BlockSpec(memory_space=pltpu.VMEM)
    return pl.pallas_call(
        functools.partial(finish_kernel, total),
        in_specs=[vmem] * (3 + len(came)),
        out_specs=vmem,
        out_shape=jax.ShapeDtypeStruct(between.shape, jnp.float32),
        compiler_params=pltpu.CompilerParams(vmem_limit_bytes=VMEM_SOME),
        cost_estimate=pl.CostEstimate(flops=8 * between.size, bytes_accessed=16 * between.size, transcendentals=0),
        name="finish",
    )(between, first, *came, second)


def halving_stages(width):
    strides = [1 << k for k in range(width.bit_length() - 1)]
    return [[s] for s in strides[:-2]] + [strides[-2:]]


def exchange(width, stage, out):
    came = []
    for p in range(1, 1 << len(stage)):
        apart = sum(s for k, s in enumerate(stage) if (p >> (len(stage) - 1 - k)) & 1)
        came.append(lax.ppermute(out[p - 1], "wide", [(i, i ^ apart) for i in range(width)]))
    return came


def encode_kernel(total, me_ref, got_ref, basis_ref, centroid_ref, rotation_ref, *refs):
    out_hbm, between_ref, out_ref, delta_ref, list_ref, apart_ref, sem = refs[-7:]
    width = delta_ref.shape[0]
    feats = out_ref.shape[1]
    owned = centroid_ref.shape[0]
    wide = basis_ref.shape[0]
    block = wide // width
    share = total // width

    notes = jnp.concatenate([got_ref[s * SPAN + CAP:(s + 1) * SPAN, :] for s in range(width)], 0)
    size = width * NOTES
    to = lax.broadcasted_iota(jnp.int32, (size, size), 0)
    of = lax.broadcasted_iota(jnp.int32, (size, size), 1)
    turn = jnp.where((to % width) * NOTES + to // width == of, 1.0, 0.0).astype(jnp.bfloat16)
    turned = jnp.dot(turn, notes, preferred_element_type=jnp.float32)
    row = [turned[r * width:(r + 1) * width] for r in range(NOTES)]
    digits = row[NOTES - 1]
    list_ref[...] = digits[:, :CAP] * 32.0 + digits[:, CAP:] - 1.0
    quarters = wide // feats
    shifts = jnp.zeros((width, feats), jnp.float32)
    for q in range(quarters):
        parts = [row[p * quarters + q] for p in range(3)]
        mean = parts[0] + (parts[1] + parts[2])
        apart_ref[:, q * feats:(q + 1) * feats] = mean - jnp.mean(mean, 0, keepdims=True)
        terms = jnp.dot(
            jnp.concatenate(parts, 0).astype(jnp.bfloat16),
            basis_ref[q * feats:(q + 1) * feats, :],
            preferred_element_type=jnp.float32,
        )
        shifts = shifts + (terms[:width] + (terms[width:2 * width] + terms[2 * width:]))
    square = row[3 * quarters] + (row[3 * quarters + 1] + row[3 * quarters + 2])
    delta = shifts - jnp.mean(shifts, 0, keepdims=True)
    variance = jnp.sum(square + share * (delta * delta), 0, keepdims=True) / total
    scale = lax.rsqrt(variance + 1e-05)
    delta_ref[...] = delta

    names = lax.broadcasted_iota(jnp.int32, (CAP, owned), 1).astype(jnp.int16)

    def encode_group(g):
        columns = jnp.transpose(list_ref[pl.ds(g * GROUP, GROUP), :])
        hits, projected, held = [], [], []
        for s in range(GROUP):
            listed = jnp.broadcast_to(columns[:, s:s + 1], (CAP, LANES))
            held.append(jnp.concatenate([listed] * (feats // LANES), 1) >= 0)
            wanted = jnp.concatenate([listed.astype(jnp.int32).astype(jnp.int16)] * (owned // LANES), 1)
            hits.append(jnp.where(wanted == names, jnp.ones((), jnp.bfloat16), jnp.zeros((), jnp.bfloat16)))
            base = pl.multiple_of((g * GROUP + s) * SPAN, 16)
            rows = got_ref[pl.ds(base, CAP), :].astype(jnp.float32)
            projected.append((rows + delta_ref[pl.ds(g * GROUP + s, 1), :]) * scale)
        centre = jnp.dot(jnp.concatenate(hits, 0), centroid_ref[...], preferred_element_type=jnp.float32)
        residual = jnp.where(jnp.concatenate(held, 0), jnp.concatenate(projected, 0) - centre, 0.0)
        at = pl.ds(pl.multiple_of(g * (GROUP * CAP), GROUP * CAP), GROUP * CAP)
        out_ref[at, :] = jnp.dot(
            residual.astype(jnp.bfloat16), rotation_ref[...], preferred_element_type=jnp.float32
        ).astype(jnp.bfloat16)
        return pltpu.make_async_copy(out_ref.at[at], out_hbm.at[at], sem.at[g])

    groups = width // GROUP
    copies = []
    if groups <= 4:
        for g in range(groups):
            copies.append(encode_group(g))
            copies[g].start()
    else:

        @pl.loop(0, groups)
        def _(g):
            copy = encode_group(g)
            copy.start()
            copy.wait()

    first = me_ref[0] * block
    near = apart_ref[:, pl.ds(pl.multiple_of(first // LANES * LANES, LANES), LANES)]
    near = pltpu.roll(near, (LANES - first % LANES) % LANES, 1)[:, :block]
    between_ref[...] = share * lax.dot_general(
        near,
        apart_ref[...],
        (((0,), (0,)), ((), ())),
        precision=lax.Precision.HIGHEST,
        preferred_element_type=jnp.float32,
    )
    for copy in copies:
        copy.wait()


def encode(width, total, me, got, basis, centroids, rotation, after):
    wide, feats = basis.shape
    owned = centroids.shape[0]
    slots = width * CAP
    vmem, anywhere = pl.BlockSpec(memory_space=pltpu.VMEM), pl.BlockSpec(memory_space=pl.ANY)
    return pl.pallas_call(
        functools.partial(encode_kernel, total),
        in_specs=[pl.BlockSpec(memory_space=pltpu.SMEM)] + [vmem] * 4 + [anywhere] * len(after),
        out_specs=[anywhere, vmem],
        out_shape=[
            jax.ShapeDtypeStruct((slots, feats), jnp.bfloat16),
            jax.ShapeDtypeStruct((wide // width, wide), jnp.float32),
        ],
        scratch_shapes=[
            pltpu.VMEM((slots, feats), jnp.bfloat16),
            pltpu.VMEM((width, feats), jnp.float32),
            pltpu.VMEM((width, CAP), jnp.float32),
            pltpu.VMEM((width, wide), jnp.float32),
            pltpu.SemaphoreType.DMA((width // GROUP,)),
        ],
        compiler_params=pltpu.CompilerParams(vmem_limit_bytes=VMEM_SOME),
        cost_estimate=pl.CostEstimate(
            flops=2 * slots * feats * (owned + feats), bytes_accessed=4 * slots * feats, transcendentals=0
        ),
        name="encode",
    )(me.reshape(1), got, basis, centroids, rotation, *after)


def local(embeddings, basis, list_owner, list_slot, centroids, rotation):
    width = lax.axis_size("wide")
    me = lax.axis_index("wide")
    rows_here, wide = embeddings.shape
    feats = basis.shape[1]
    total = rows_here * width

    rows, mean = project_and_sort(width, embeddings, basis, list_owner, list_slot)
    got = lax.all_to_all(rows.reshape(width, SPAN, feats), "wide", split_axis=0, concat_axis=0, tiled=True)

    keep, send = moments(width, me, embeddings, mean)
    stages = halving_stages(width)
    came = exchange(width, stages[0], [send])
    shares = add_and_split(keep, came, SHARES, 1 << len(stages[1]))
    first, second = shares
    for n in range(1, len(stages) - 2):
        came = exchange(width, stages[n], first[1:])
        (first,) = add_and_split(first[0], came, 1, 2)
        came = exchange(width, stages[n], second[1:])
        (second,) = add_and_split(second[0], came, 1, 2)
    came = exchange(width, stages[-2], first[1:])
    (first,) = add_and_split(first[0], came, 1, 1 << len(stages[-1]))
    came = exchange(width, stages[-1], first[1:])
    (last,) = exchange(width, stages[-2], second[1:])
    second = add_and_gather(stages[-1], me, second[0], last)
    stride = stages[-1][0]
    lines = [list(range(i, width, stride)) for i in range(stride)]
    blocks = second.reshape(width // stride, second.shape[0] * stride // width, -1)
    gathered = lax.all_to_all(blocks, "wide", split_axis=0, concat_axis=0, tiled=True, axis_index_groups=lines)
    encoded, between = encode(
        width, total, me, got.reshape(width * SPAN, feats), basis, centroids, rotation, [first[1], second]
    )
    covariance = finish(total, between, first[0], came, gathered.reshape(second.shape))
    return (encoded, covariance)


def solution(mesh):
    in_specs = (
        P(("groups", "wide"), None),
        P(),
        P(("groups", "wide")),
        P(("groups", "wide")),
        P("wide", None),
        P(),
    )
    out_specs = (P(("groups", "wide"), None), P(("groups", "wide"), None))
    return jax.shard_map(local, mesh=mesh, in_specs=in_specs, out_specs=out_specs, check_vma=False)
```

```python
import functools

import jax
import jax.numpy as jnp
from jax import lax
from jax.experimental import pallas as pl
from jax.experimental.pallas import tpu as pltpu
from jax.sharding import PartitionSpec as P

CAP = 128
LANES = 128
NOTES = 16
SPAN = CAP + NOTES
CHUNK = 512
TILE = 512
GROUP = 8
SHARES = 2
VMEM_ALL = 60 * 1024 * 1024
VMEM_SOME = 24 * 1024 * 1024
VMEM_MOST = 48 * 1024 * 1024


def in_three(x):
    high = x.astype(jnp.bfloat16).astype(jnp.float32)
    rest = x - high
    middle = rest.astype(jnp.bfloat16).astype(jnp.float32)
    return high, middle, (rest - middle).astype(jnp.bfloat16).astype(jnp.float32)


def rows_kernel(
    width, e_hbm, basis_hbm, owner_hbm, slot_hbm,
    rows_hbm, mean_hbm,
    owner_ref, slot_ref, mean_ref, basis_ref, e_ref, rows_ref, y_ref, yb_ref, sum_ref, total_ref, target_ref, list_ref, e_sem, small_sem, sem,
):
    step = pl.program_id(0)
    rows_here, feats = y_ref.shape
    wide = e_ref.shape[1]
    chunks = rows_here // LANES

    def e_copy(c):
        at = pl.ds(pl.multiple_of(c * CHUNK, CHUNK), CHUNK)
        return pltpu.make_async_copy(e_hbm.at[at], e_ref.at[at], e_sem.at[c])

    @pl.when(step == 0)
    def _():
        owner_copy = pltpu.make_async_copy(owner_hbm, owner_ref, small_sem.at[0])
        slot_copy = pltpu.make_async_copy(slot_hbm, slot_ref, small_sem.at[1])
        basis_copy = pltpu.make_async_copy(basis_hbm, basis_ref, small_sem.at[2])
        owner_copy.start()
        e_copy(0).start()
        slot_copy.start()
        basis_copy.start()
        for c in range(1, rows_here // CHUNK):
            e_copy(c).start()
        owner_copy.wait()
        sum_ref[...] = jnp.zeros_like(sum_ref)
        total_ref[...] = jnp.zeros_like(total_ref)
        owner = owner_ref[...]
        wanted = lax.broadcasted_iota(jnp.int32, (width, LANES), 0)
        hits = [jnp.where(owner[c:c + 1, :] == wanted, 1.0, 0.0) for c in range(chunks)]
        flat = jnp.concatenate(hits, 0).astype(jnp.bfloat16)
        up = lax.broadcasted_iota(jnp.int32, (LANES, LANES), 0)
        to = lax.broadcasted_iota(jnp.int32, (LANES, LANES), 1)
        before = jnp.where(up < to, 1.0, 0.0).astype(jnp.bfloat16)
        every = jnp.ones((LANES, LANES), jnp.bfloat16)
        within = jnp.dot(flat, before, preferred_element_type=jnp.float32)
        counts = jnp.dot(flat, every, preferred_element_type=jnp.float32)
        carry = jnp.zeros((width, LANES), jnp.float32)
        ranks = []
        for c in range(chunks):
            at = slice(c * width, (c + 1) * width)
            ranks.append(jnp.sum(hits[c] * (within[at] + carry), 0, keepdims=True).astype(jnp.int32))
            carry = carry + counts[at]
            target_ref[c:c + 1, :] = owner[c:c + 1, :] * CAP + ranks[c]

        slot_copy.wait()
        slot = slot_ref[...] + 1
        high, low = (slot >> 5).astype(jnp.float32), (slot & 31).astype(jnp.float32)
        spots = lax.broadcasted_iota(jnp.int32, (CAP, LANES), 0)
        placed = jnp.concatenate([jnp.where(ranks[c] == spots, 1.0, 0.0) for c in range(chunks)], 1).astype(jnp.bfloat16)
        digits = jnp.concatenate(
            [
                jnp.concatenate([hits[c] * high[c:c + 1, :] for c in range(chunks)], 1),
                jnp.concatenate([hits[c] * low[c:c + 1, :] for c in range(chunks)], 1),
            ],
            0,
        ).astype(jnp.bfloat16)
        found = lax.dot_general(digits, placed, (((1,), (1,)), ((), ())), preferred_element_type=jnp.float32)
        list_ref[:, :CAP] = found[:width]
        list_ref[:, CAP:] = found[width:]
        basis_copy.wait()

    e_copy(step).wait()
    here = pl.ds(pl.multiple_of(step * CHUNK, CHUNK), CHUNK)
    rows = e_ref[here, :]
    y = jnp.dot(rows, basis_ref[...], preferred_element_type=jnp.float32)
    y_ref[here, :] = y
    sum_ref[...] += jnp.sum(y.reshape(CHUNK // 8, 8, feats), 0)
    total_ref[...] += jnp.sum(rows.astype(jnp.float32).reshape(CHUNK // 8, 8, wide), 0)

    @pl.when(step == pl.num_programs(0) - 1)
    def _():
        mean_y = jnp.sum(sum_ref[...], 0, keepdims=True) / rows_here
        square = jnp.zeros((8, feats), jnp.float32)
        for c in range(rows_here // CHUNK):
            at = slice(c * CHUNK, (c + 1) * CHUNK)
            centred = y_ref[at, :] - mean_y
            square = square + jnp.sum((centred * centred).reshape(CHUNK // 8, 8, feats), 0)
            yb_ref[at, :] = centred.astype(jnp.bfloat16)
        mean = jnp.sum(total_ref[...], 0, keepdims=True) / rows_here
        mean_ref[...] = mean
        mean_copy = pltpu.make_async_copy(mean_ref, mean_hbm, small_sem.at[3])
        mean_copy.start()
        parts = in_three(mean)
        common = [part[:, q * feats:(q + 1) * feats] for part in parts for q in range(wide // feats)]
        common = jnp.concatenate(common + list(in_three(jnp.sum(square, 0, keepdims=True))), 0)

        place = lax.broadcasted_iota(jnp.int32, (GROUP * CAP, LANES), 0).astype(jnp.int16)

        def sort_group(g):
            first = g * GROUP
            pieces = []
            for c in range(chunks):
                wanted = (target_ref[c:c + 1, :] - first * CAP).astype(jnp.int32)
                wanted = jnp.broadcast_to(wanted, (16, LANES)).astype(jnp.int16)
                wanted = jnp.concatenate([wanted] * (GROUP * CAP // 16), 0)
                pieces.append(jnp.where(wanted == place, jnp.ones((), jnp.bfloat16), jnp.zeros((), jnp.bfloat16)))
            pick = jnp.concatenate(pieces, 1)
            rows = jnp.dot(pick, yb_ref[...], preferred_element_type=jnp.float32).astype(jnp.bfloat16)
            for j in range(GROUP):
                base = pl.multiple_of((first + j) * SPAN, 16)
                rows_ref[pl.ds(base, CAP), :] = rows[j * CAP:(j + 1) * CAP]
                notes = jnp.concatenate([common, list_ref[pl.ds(first + j, 1), :]], 0)
                rows_ref[pl.ds(pl.multiple_of(base + CAP, 16), NOTES), :] = notes.astype(jnp.bfloat16)
            at = pl.ds(pl.multiple_of(g * (GROUP * SPAN), 16), GROUP * SPAN)
            return pltpu.make_async_copy(rows_ref.at[at], rows_hbm.at[at], sem.at[g])

        groups = width // GROUP
        if groups <= 4:
            copies = []
            for g in range(groups):
                copies.append(sort_group(g))
                copies[g].start()
            for copy in copies:
                copy.wait()
        else:

            @pl.loop(0, groups)
            def _(g):
                copy = sort_group(g)
                copy.start()
                copy.wait()

        mean_copy.wait()


def project_and_sort(width, embeddings, basis, list_owner, list_slot):
    rows_here, wide = embeddings.shape
    feats = basis.shape[1]
    lanes = rows_here // LANES
    slots = width * SPAN
    return pl.pallas_call(
        functools.partial(rows_kernel, width),
        grid=(rows_here // CHUNK,),
        in_specs=[pl.BlockSpec(memory_space=pl.ANY)] * 4,
        out_specs=[pl.BlockSpec(memory_space=pl.ANY)] * 2,
        out_shape=[
            jax.ShapeDtypeStruct((slots, feats), jnp.bfloat16),
            jax.ShapeDtypeStruct((1, wide), jnp.float32),
        ],
        scratch_shapes=[
            pltpu.VMEM((lanes, LANES), jnp.int32),
            pltpu.VMEM((lanes, LANES), jnp.int32),
            pltpu.VMEM((1, wide), jnp.float32),
            pltpu.VMEM((wide, feats), jnp.bfloat16),
            pltpu.VMEM((rows_here, wide), jnp.bfloat16),
            pltpu.VMEM((slots, feats), jnp.bfloat16),
            pltpu.VMEM((rows_here, feats), jnp.float32),
            pltpu.VMEM((rows_here, feats), jnp.bfloat16),
            pltpu.VMEM((8, feats), jnp.float32),
            pltpu.VMEM((8, wide), jnp.float32),
            pltpu.VMEM((lanes, LANES), jnp.int32),
            pltpu.VMEM((width, 2 * CAP), jnp.float32),
            pltpu.SemaphoreType.DMA((rows_here // CHUNK,)),
            pltpu.SemaphoreType.DMA((4,)),
            pltpu.SemaphoreType.DMA((width // GROUP,)),
        ],
        compiler_params=pltpu.CompilerParams(vmem_limit_bytes=VMEM_ALL),
        cost_estimate=pl.CostEstimate(
            flops=2 * rows_here * feats * (wide + slots), bytes_accessed=2 * rows_here * wide + 2 * slots * feats, transcendentals=0
        ),
        name="project_sort",
    )(embeddings, basis, list_owner.reshape(lanes, LANES), list_slot.reshape(lanes, LANES))


def moments_kernel(width, me_ref, mean_hbm, e_hbm, keep_ref, send_ref, e_ref, mean_ref, m_ref, sem, mean_sem):
    rows_here, wide = e_ref.shape
    block = wide // width
    bits = width.bit_length() - 1
    mean_copy = pltpu.make_async_copy(mean_hbm, mean_ref, mean_sem)
    mean_copy.start()
    copies = []
    for c in range(rows_here // CHUNK):
        at = pl.ds(c * CHUNK, CHUNK)
        copies.append(pltpu.make_async_copy(e_hbm.at[at], e_ref.at[at], sem.at[c]))
        copies[c].start()
    me = me_ref[0]
    mean_copy.wait()
    mean = mean_ref[...]
    for t in range(wide // TILE):
        rows = slice(t * TILE, (t + 1) * TILE)
        if t == 0:
            product = jnp.zeros((TILE, wide), jnp.float32)
            for c in range(rows_here // CHUNK):
                copies[c].wait()
                at = slice(c * CHUNK, (c + 1) * CHUNK)
                product = product + lax.dot_general(
                    e_ref[at, rows], e_ref[at, :], (((0,), (0,)), ((), ())), preferred_element_type=jnp.float32
                )
        else:
            product = lax.dot_general(
                e_ref[:, rows], e_ref[...], (((0,), (0,)), ((), ())), preferred_element_type=jnp.float32
            )
        down = jnp.transpose(jnp.broadcast_to(mean[:, rows] * rows_here, (LANES, TILE)))
        for j in range(wide // LANES):
            across = slice(j * LANES, (j + 1) * LANES)
            m_ref[rows, across] = product[:, across] - down * mean[:, across]
        for pair in range(TILE // block // 2):
            first = t * (TILE // block) + 2 * pair
            apart = (first ^ me) >> 1
            place = 0
            for k in range(bits - 1):
                place = place + (((apart >> k) & 1) << (bits - 2 - k))
            to = pl.ds(pl.multiple_of(place * block, block), block)
            kept = pl.multiple_of((first + (me & 1)) * block, block)
            sent = pl.multiple_of((first + 1 - (me & 1)) * block, block)
            keep_ref[to, :] = m_ref[pl.ds(kept, block), :]
            send_ref[to, :] = m_ref[pl.ds(sent, block), :].astype(jnp.bfloat16)


def moments(width, me, embeddings, mean):
    rows_here, wide = embeddings.shape
    vmem = pl.BlockSpec(memory_space=pltpu.VMEM)
    return pl.pallas_call(
        functools.partial(moments_kernel, width),
        in_specs=[pl.BlockSpec(memory_space=pltpu.SMEM)] + [pl.BlockSpec(memory_space=pl.ANY)] * 2,
        out_specs=[vmem] * 2,
        out_shape=[
            jax.ShapeDtypeStruct((wide // 2, wide), jnp.float32),
            jax.ShapeDtypeStruct((wide // 2, wide), jnp.bfloat16),
        ],
        scratch_shapes=[
            pltpu.VMEM((rows_here, wide), jnp.bfloat16),
            pltpu.VMEM((1, wide), jnp.float32),
            pltpu.VMEM((wide, wide), jnp.float32),
            pltpu.SemaphoreType.DMA((rows_here // CHUNK,)),
            pltpu.SemaphoreType.DMA,
        ],
        compiler_params=pltpu.CompilerParams(vmem_limit_bytes=VMEM_MOST),
        cost_estimate=pl.CostEstimate(
            flops=2 * rows_here * wide * wide, bytes_accessed=2 * rows_here * wide + 3 * wide * wide, transcendentals=0
        ),
        name="moments",
    )(me.reshape(1), mean, embeddings)


def add_kernel(shares, pieces, arrived, keep_ref, *refs):
    outs = refs[len(refs) - shares * pieces:]
    came = refs[:arrived]
    rows, columns = outs[0].shape
    for h in range(shares):
        across = slice(h * columns, (h + 1) * columns)
        for p in range(pieces):
            at = slice(p * rows, (p + 1) * rows)
            held = keep_ref[at, across]
            for ref in came:
                held = held + ref[at, across].astype(jnp.float32)
            out = outs[h * pieces + p]
            out[...] = held.astype(out.dtype)


def add_and_split(keep, came, shares, pieces, after=()):
    rows, columns = keep.shape
    vmem = pl.BlockSpec(memory_space=pltpu.VMEM)
    shape = (rows // pieces, columns // shares)
    kinds = [jnp.float32] + [jnp.bfloat16] * (pieces - 1)
    outs = pl.pallas_call(
        functools.partial(add_kernel, shares, pieces, len(came)),
        in_specs=[vmem] * (1 + len(came)) + [pl.BlockSpec(memory_space=pl.ANY)] * len(after),
        out_specs=[vmem] * (shares * pieces),
        out_shape=[jax.ShapeDtypeStruct(shape, kind) for kind in kinds * shares],
        compiler_params=pltpu.CompilerParams(vmem_limit_bytes=VMEM_SOME),
        cost_estimate=pl.CostEstimate(flops=2 * rows * columns, bytes_accessed=10 * rows * columns, transcendentals=0),
        name="add_and_split",
    )(keep, *came, *after)
    return [outs[h * pieces:(h + 1) * pieces] for h in range(shares)]


def finish_kernel(total, between_ref, *refs):
    out_ref = refs[-1]
    each = (len(refs) - 1) // SHARES
    columns = out_ref.shape[1] // SHARES
    for h in range(SHARES):
        across = slice(h * columns, (h + 1) * columns)
        held = refs[h * each][...]
        for ref in refs[h * each + 1:(h + 1) * each]:
            held = held + ref[...].astype(jnp.float32)
        out_ref[:, across] = (held + between_ref[:, across]) / total


def finish(total, between, keeps, came):
    parts = [part for keep, pieces in zip(keeps, came) for part in (keep, *pieces)]
    vmem = pl.BlockSpec(memory_space=pltpu.VMEM)
    return pl.pallas_call(
        functools.partial(finish_kernel, total),
        in_specs=[vmem] * (1 + len(parts)),
        out_specs=vmem,
        out_shape=jax.ShapeDtypeStruct(between.shape, jnp.float32),
        compiler_params=pltpu.CompilerParams(vmem_limit_bytes=VMEM_SOME),
        cost_estimate=pl.CostEstimate(flops=8 * between.size, bytes_accessed=16 * between.size, transcendentals=0),
        name="finish",
    )(between, *parts)


def halving_stages(width):
    strides = [1 << k for k in range(width.bit_length() - 1)]
    return [[s] for s in strides[:-2]] + [strides[-2:]]


def exchange(width, stage, out):
    came = []
    for p in range(1, 1 << len(stage)):
        apart = sum(s for k, s in enumerate(stage) if (p >> (len(stage) - 1 - k)) & 1)
        came.append(lax.ppermute(out[p - 1], "wide", [(i, i ^ apart) for i in range(width)]))
    return came


def encode_kernel(total, me_ref, got_ref, basis_ref, centroid_ref, rotation_ref, *refs):
    out_hbm, between_ref, out_ref, delta_ref, list_ref, apart_ref, sem = refs[-7:]
    width = delta_ref.shape[0]
    feats = out_ref.shape[1]
    owned = centroid_ref.shape[0]
    wide = basis_ref.shape[0]
    block = wide // width
    share = total // width

    notes = jnp.concatenate([got_ref[s * SPAN + CAP:(s + 1) * SPAN, :] for s in range(width)], 0)
    size = width * NOTES
    to = lax.broadcasted_iota(jnp.int32, (size, size), 0)
    of = lax.broadcasted_iota(jnp.int32, (size, size), 1)
    turn = jnp.where((to % width) * NOTES + to // width == of, 1.0, 0.0).astype(jnp.bfloat16)
    turned = jnp.dot(turn, notes, preferred_element_type=jnp.float32)
    row = [turned[r * width:(r + 1) * width] for r in range(NOTES)]
    digits = row[NOTES - 1]
    list_ref[...] = digits[:, :CAP] * 32.0 + digits[:, CAP:] - 1.0
    quarters = wide // feats
    shifts = jnp.zeros((width, feats), jnp.float32)
    for q in range(quarters):
        parts = [row[p * quarters + q] for p in range(3)]
        mean = parts[0] + (parts[1] + parts[2])
        apart_ref[:, q * feats:(q + 1) * feats] = mean - jnp.mean(mean, 0, keepdims=True)
        terms = jnp.dot(
            jnp.concatenate(parts, 0).astype(jnp.bfloat16),
            basis_ref[q * feats:(q + 1) * feats, :],
            preferred_element_type=jnp.float32,
        )
        shifts = shifts + (terms[:width] + (terms[width:2 * width] + terms[2 * width:]))
    square = row[3 * quarters] + (row[3 * quarters + 1] + row[3 * quarters + 2])
    delta = shifts - jnp.mean(shifts, 0, keepdims=True)
    variance = jnp.sum(square + share * (delta * delta), 0, keepdims=True) / total
    scale = lax.rsqrt(variance + 1e-05)
    delta_ref[...] = delta

    names = lax.broadcasted_iota(jnp.int32, (CAP, owned), 1).astype(jnp.int16)

    def encode_group(g):
        columns = jnp.transpose(list_ref[pl.ds(g * GROUP, GROUP), :])
        hits, projected, held = [], [], []
        for s in range(GROUP):
            listed = jnp.broadcast_to(columns[:, s:s + 1], (CAP, LANES))
            held.append(jnp.concatenate([listed] * (feats // LANES), 1) >= 0)
            wanted = jnp.concatenate([listed.astype(jnp.int32).astype(jnp.int16)] * (owned // LANES), 1)
            hits.append(jnp.where(wanted == names, jnp.ones((), jnp.bfloat16), jnp.zeros((), jnp.bfloat16)))
            base = pl.multiple_of((g * GROUP + s) * SPAN, 16)
            rows = got_ref[pl.ds(base, CAP), :].astype(jnp.float32)
            projected.append((rows + delta_ref[pl.ds(g * GROUP + s, 1), :]) * scale)
        centre = jnp.dot(jnp.concatenate(hits, 0), centroid_ref[...], preferred_element_type=jnp.float32)
        residual = jnp.where(jnp.concatenate(held, 0), jnp.concatenate(projected, 0) - centre, 0.0)
        at = pl.ds(pl.multiple_of(g * (GROUP * CAP), GROUP * CAP), GROUP * CAP)
        out_ref[at, :] = jnp.dot(
            residual.astype(jnp.bfloat16), rotation_ref[...], preferred_element_type=jnp.float32
        ).astype(jnp.bfloat16)
        return pltpu.make_async_copy(out_ref.at[at], out_hbm.at[at], sem.at[g])

    groups = width // GROUP
    copies = []
    if groups <= 4:
        for g in range(groups):
            copies.append(encode_group(g))
            copies[g].start()
    else:

        @pl.loop(0, groups)
        def _(g):
            copy = encode_group(g)
            copy.start()
            copy.wait()

    first = me_ref[0] * block
    near = apart_ref[:, pl.ds(pl.multiple_of(first // LANES * LANES, LANES), LANES)]
    near = pltpu.roll(near, (LANES - first % LANES) % LANES, 1)[:, :block]
    between_ref[...] = share * lax.dot_general(
        near,
        apart_ref[...],
        (((0,), (0,)), ((), ())),
        precision=lax.Precision.HIGHEST,
        preferred_element_type=jnp.float32,
    )
    for copy in copies:
        copy.wait()


def encode(width, total, me, got, basis, centroids, rotation, after):
    wide, feats = basis.shape
    owned = centroids.shape[0]
    slots = width * CAP
    vmem, anywhere = pl.BlockSpec(memory_space=pltpu.VMEM), pl.BlockSpec(memory_space=pl.ANY)
    return pl.pallas_call(
        functools.partial(encode_kernel, total),
        in_specs=[pl.BlockSpec(memory_space=pltpu.SMEM)] + [vmem] * 4 + [anywhere] * len(after),
        out_specs=[anywhere, vmem],
        out_shape=[
            jax.ShapeDtypeStruct((slots, feats), jnp.bfloat16),
            jax.ShapeDtypeStruct((wide // width, wide), jnp.float32),
        ],
        scratch_shapes=[
            pltpu.VMEM((slots, feats), jnp.bfloat16),
            pltpu.VMEM((width, feats), jnp.float32),
            pltpu.VMEM((width, CAP), jnp.float32),
            pltpu.VMEM((width, wide), jnp.float32),
            pltpu.SemaphoreType.DMA((width // GROUP,)),
        ],
        compiler_params=pltpu.CompilerParams(vmem_limit_bytes=VMEM_SOME),
        cost_estimate=pl.CostEstimate(
            flops=2 * slots * feats * (owned + feats), bytes_accessed=4 * slots * feats, transcendentals=0
        ),
        name="encode",
    )(me.reshape(1), got, basis, centroids, rotation, *after)


def local(embeddings, basis, list_owner, list_slot, centroids, rotation):
    width = lax.axis_size("wide")
    me = lax.axis_index("wide")
    rows_here, wide = embeddings.shape
    feats = basis.shape[1]
    total = rows_here * width

    rows, mean = project_and_sort(width, embeddings, basis, list_owner, list_slot)
    got = lax.all_to_all(rows.reshape(width, SPAN, feats), "wide", split_axis=0, concat_axis=0, tiled=True)

    keep, send = moments(width, me, embeddings, mean)
    stages = halving_stages(width)
    came = exchange(width, stages[0], [send])
    shares = add_and_split(keep, came, SHARES, 1 << len(stages[1]))
    keeps, ends, after = [], [], []
    for share in shares:
        for n in range(1, len(stages) - 1):
            came = exchange(width, stages[n], share[1:])
            (share,) = add_and_split(share[0], came, 1, 1 << len(stages[n + 1]), after if n == 1 else [])
        keeps.append(share[0])
        ends.append(exchange(width, stages[-1], share[1:]))
        if not after:
            encoded, between = encode(
                width, total, me, got.reshape(width * SPAN, feats), basis, centroids, rotation, [share[1]]
            )
            after = [between, *ends[0]]
    covariance = finish(total, between, keeps, ends)
    return (encoded, covariance)


def solution(mesh):
    in_specs = (
        P(("groups", "wide"), None),
        P(),
        P(("groups", "wide")),
        P(("groups", "wide")),
        P("wide", None),
        P(),
    )
    out_specs = (P(("groups", "wide"), None), P(("groups", "wide"), None))
    return jax.shard_map(local, mesh=mesh, in_specs=in_specs, out_specs=out_specs, check_vma=False)
```

```python
import functools

import jax
import jax.numpy as jnp
from jax import lax
from jax.experimental import pallas as pl
from jax.experimental.pallas import tpu as pltpu
from jax.sharding import PartitionSpec as P

CAP = 128
LANES = 128
NOTES = 16
SPAN = CAP + NOTES
CHUNK = 512
TILE = 256
GROUP = 4
SHARES = (5, 3)
VMEM_ALL = 60 * 1024 * 1024
VMEM_SOME = 24 * 1024 * 1024
VMEM_MOST = 48 * 1024 * 1024


def in_three(x):
    high = x.astype(jnp.bfloat16).astype(jnp.float32)
    rest = x - high
    middle = rest.astype(jnp.bfloat16).astype(jnp.float32)
    return high, middle, (rest - middle).astype(jnp.bfloat16).astype(jnp.float32)


def rows_kernel(
    width, e_hbm, basis_hbm, owner_hbm, slot_hbm,
    rows_hbm, mean_hbm,
    owner_ref, slot_ref, mean_ref, basis_ref, e_ref, rows_ref, y_ref, yb_ref, sum_ref, total_ref, target_ref, list_ref, e_sem, small_sem, sem,
):
    step = pl.program_id(0)
    rows_here, feats = y_ref.shape
    wide = e_ref.shape[1]
    chunks = rows_here // LANES

    def e_copy(c):
        at = pl.ds(pl.multiple_of(c * CHUNK, CHUNK), CHUNK)
        return pltpu.make_async_copy(e_hbm.at[at], e_ref.at[at], e_sem.at[c])

    @pl.when(step == 0)
    def _():
        owner_copy = pltpu.make_async_copy(owner_hbm, owner_ref, small_sem.at[0])
        slot_copy = pltpu.make_async_copy(slot_hbm, slot_ref, small_sem.at[1])
        basis_copy = pltpu.make_async_copy(basis_hbm, basis_ref, small_sem.at[2])
        owner_copy.start()
        e_copy(0).start()
        slot_copy.start()
        basis_copy.start()
        for c in range(1, rows_here // CHUNK):
            e_copy(c).start()
        owner_copy.wait()
        sum_ref[...] = jnp.zeros_like(sum_ref)
        total_ref[...] = jnp.zeros_like(total_ref)
        owner = owner_ref[...]
        wanted = lax.broadcasted_iota(jnp.int32, (width, LANES), 0)
        hits = [jnp.where(owner[c:c + 1, :] == wanted, 1.0, 0.0) for c in range(chunks)]
        flat = jnp.concatenate(hits, 0).astype(jnp.bfloat16)
        up = lax.broadcasted_iota(jnp.int32, (LANES, LANES), 0)
        to = lax.broadcasted_iota(jnp.int32, (LANES, LANES), 1)
        before = jnp.where(up < to, 1.0, 0.0).astype(jnp.bfloat16)
        every = jnp.ones((LANES, LANES), jnp.bfloat16)
        within = jnp.dot(flat, before, preferred_element_type=jnp.float32)
        counts = jnp.dot(flat, every, preferred_element_type=jnp.float32)
        carry = jnp.zeros((width, LANES), jnp.float32)
        ranks = []
        for c in range(chunks):
            at = slice(c * width, (c + 1) * width)
            ranks.append(jnp.sum(hits[c] * (within[at] + carry), 0, keepdims=True).astype(jnp.int32))
            carry = carry + counts[at]
            target_ref[c:c + 1, :] = owner[c:c + 1, :] * CAP + ranks[c]

        slot_copy.wait()
        slot = slot_ref[...] + 1
        high, low = (slot >> 5).astype(jnp.float32), (slot & 31).astype(jnp.float32)
        spots = lax.broadcasted_iota(jnp.int32, (CAP, LANES), 0)
        placed = jnp.concatenate([jnp.where(ranks[c] == spots, 1.0, 0.0) for c in range(chunks)], 1).astype(jnp.bfloat16)
        digits = jnp.concatenate(
            [
                jnp.concatenate([hits[c] * high[c:c + 1, :] for c in range(chunks)], 1),
                jnp.concatenate([hits[c] * low[c:c + 1, :] for c in range(chunks)], 1),
            ],
            0,
        ).astype(jnp.bfloat16)
        found = lax.dot_general(digits, placed, (((1,), (1,)), ((), ())), preferred_element_type=jnp.float32)
        list_ref[:, :CAP] = found[:width]
        list_ref[:, CAP:] = found[width:]
        basis_copy.wait()

    e_copy(step).wait()
    here = pl.ds(pl.multiple_of(step * CHUNK, CHUNK), CHUNK)
    rows = e_ref[here, :]
    y = jnp.dot(rows, basis_ref[...], preferred_element_type=jnp.float32)
    y_ref[here, :] = y
    sum_ref[...] += jnp.sum(y.reshape(CHUNK // 8, 8, feats), 0)
    total_ref[...] += jnp.sum(rows.astype(jnp.float32).reshape(CHUNK // 8, 8, wide), 0)

    @pl.when(step == pl.num_programs(0) - 1)
    def _():
        mean_y = jnp.sum(sum_ref[...], 0, keepdims=True) / rows_here
        square = jnp.zeros((8, feats), jnp.float32)
        for c in range(rows_here // CHUNK):
            at = slice(c * CHUNK, (c + 1) * CHUNK)
            centred = y_ref[at, :] - mean_y
            square = square + jnp.sum((centred * centred).reshape(CHUNK // 8, 8, feats), 0)
            yb_ref[at, :] = centred.astype(jnp.bfloat16)
        mean = jnp.sum(total_ref[...], 0, keepdims=True) / rows_here
        mean_ref[...] = mean
        mean_copy = pltpu.make_async_copy(mean_ref, mean_hbm, small_sem.at[3])
        mean_copy.start()
        parts = in_three(mean)
        common = [part[:, q * feats:(q + 1) * feats] for part in parts for q in range(wide // feats)]
        common = jnp.concatenate(common + list(in_three(jnp.sum(square, 0, keepdims=True))), 0)

        place = lax.broadcasted_iota(jnp.int32, (GROUP * CAP, LANES), 0).astype(jnp.int16)

        def sort_group(g):
            first = g * GROUP
            pieces = []
            for c in range(chunks):
                wanted = (target_ref[c:c + 1, :] - first * CAP).astype(jnp.int32)
                wanted = jnp.broadcast_to(wanted, (16, LANES)).astype(jnp.int16)
                wanted = jnp.concatenate([wanted] * (GROUP * CAP // 16), 0)
                pieces.append(jnp.where(wanted == place, jnp.ones((), jnp.bfloat16), jnp.zeros((), jnp.bfloat16)))
            pick = jnp.concatenate(pieces, 1)
            rows = jnp.dot(pick, yb_ref[...], preferred_element_type=jnp.float32).astype(jnp.bfloat16)
            for j in range(GROUP):
                base = pl.multiple_of((first + j) * SPAN, 16)
                rows_ref[pl.ds(base, CAP), :] = rows[j * CAP:(j + 1) * CAP]
                notes = jnp.concatenate([common, list_ref[pl.ds(first + j, 1), :]], 0)
                rows_ref[pl.ds(pl.multiple_of(base + CAP, 16), NOTES), :] = notes.astype(jnp.bfloat16)
            at = pl.ds(pl.multiple_of(g * (GROUP * SPAN), 16), GROUP * SPAN)
            return pltpu.make_async_copy(rows_ref.at[at], rows_hbm.at[at], sem.at[g])

        groups = width // GROUP
        if groups <= 4:
            copies = []
            for g in range(groups):
                copies.append(sort_group(g))
                copies[g].start()
            for copy in copies:
                copy.wait()
        else:

            @pl.loop(0, groups)
            def _(g):
                copy = sort_group(g)
                copy.start()
                copy.wait()

        mean_copy.wait()


def project_and_sort(width, embeddings, basis, list_owner, list_slot):
    rows_here, wide = embeddings.shape
    feats = basis.shape[1]
    lanes = rows_here // LANES
    slots = width * SPAN
    return pl.pallas_call(
        functools.partial(rows_kernel, width),
        grid=(rows_here // CHUNK,),
        in_specs=[pl.BlockSpec(memory_space=pl.ANY)] * 4,
        out_specs=[pl.BlockSpec(memory_space=pl.ANY)] * 2,
        out_shape=[
            jax.ShapeDtypeStruct((slots, feats), jnp.bfloat16),
            jax.ShapeDtypeStruct((1, wide), jnp.float32),
        ],
        scratch_shapes=[
            pltpu.VMEM((lanes, LANES), jnp.int32),
            pltpu.VMEM((lanes, LANES), jnp.int32),
            pltpu.VMEM((1, wide), jnp.float32),
            pltpu.VMEM((wide, feats), jnp.bfloat16),
            pltpu.VMEM((rows_here, wide), jnp.bfloat16),
            pltpu.VMEM((slots, feats), jnp.bfloat16),
            pltpu.VMEM((rows_here, feats), jnp.float32),
            pltpu.VMEM((rows_here, feats), jnp.bfloat16),
            pltpu.VMEM((8, feats), jnp.float32),
            pltpu.VMEM((8, wide), jnp.float32),
            pltpu.VMEM((lanes, LANES), jnp.int32),
            pltpu.VMEM((width, 2 * CAP), jnp.float32),
            pltpu.SemaphoreType.DMA((rows_here // CHUNK,)),
            pltpu.SemaphoreType.DMA((4,)),
            pltpu.SemaphoreType.DMA((width // GROUP,)),
        ],
        compiler_params=pltpu.CompilerParams(vmem_limit_bytes=VMEM_ALL),
        cost_estimate=pl.CostEstimate(
            flops=2 * rows_here * feats * (wide + slots), bytes_accessed=2 * rows_here * wide + 2 * slots * feats, transcendentals=0
        ),
        name="project_sort",
    )(embeddings, basis, list_owner.reshape(lanes, LANES), list_slot.reshape(lanes, LANES))


def moments_kernel(width, me_ref, mean_hbm, e_hbm, keep_ref, send_ref, e_ref, mean_ref, m_ref, sem, mean_sem):
    rows_here, wide = e_ref.shape
    block = wide // width
    bits = width.bit_length() - 1
    mean_copy = pltpu.make_async_copy(mean_hbm, mean_ref, mean_sem)
    mean_copy.start()
    copies = []
    for c in range(rows_here // CHUNK):
        at = pl.ds(c * CHUNK, CHUNK)
        copies.append(pltpu.make_async_copy(e_hbm.at[at], e_ref.at[at], sem.at[c]))
        copies[c].start()
    me = me_ref[0]
    mean_copy.wait()
    mean = mean_ref[...]
    for t in range(wide // TILE):
        rows = slice(t * TILE, (t + 1) * TILE)
        if t == 0:
            product = jnp.zeros((TILE, wide), jnp.float32)
            for c in range(rows_here // CHUNK):
                copies[c].wait()
                at = slice(c * CHUNK, (c + 1) * CHUNK)
                product = product + lax.dot_general(
                    e_ref[at, rows], e_ref[at, :], (((0,), (0,)), ((), ())), preferred_element_type=jnp.float32
                )
        else:
            product = lax.dot_general(
                e_ref[:, rows], e_ref[...], (((0,), (0,)), ((), ())), preferred_element_type=jnp.float32
            )
        down = jnp.transpose(jnp.broadcast_to(mean[:, rows] * rows_here, (LANES, TILE)))
        for j in range(wide // LANES):
            across = slice(j * LANES, (j + 1) * LANES)
            m_ref[rows, across] = product[:, across] - down * mean[:, across]
        for pair in range(TILE // block // 2):
            first = t * (TILE // block) + 2 * pair
            apart = (first ^ me) >> 1
            place = 0
            for k in range(bits - 1):
                place = place + (((apart >> k) & 1) << (bits - 2 - k))
            to = pl.ds(pl.multiple_of(place * block, block), block)
            kept = pl.multiple_of((first + (me & 1)) * block, block)
            sent = pl.multiple_of((first + 1 - (me & 1)) * block, block)
            keep_ref[to, :] = m_ref[pl.ds(kept, block), :]
            send_ref[to, :] = m_ref[pl.ds(sent, block), :].astype(jnp.bfloat16)


def moments(width, me, embeddings, mean):
    rows_here, wide = embeddings.shape
    vmem = pl.BlockSpec(memory_space=pltpu.VMEM)
    return pl.pallas_call(
        functools.partial(moments_kernel, width),
        in_specs=[pl.BlockSpec(memory_space=pltpu.SMEM)] + [pl.BlockSpec(memory_space=pl.ANY)] * 2,
        out_specs=[vmem] * 2,
        out_shape=[
            jax.ShapeDtypeStruct((wide // 2, wide), jnp.float32),
            jax.ShapeDtypeStruct((wide // 2, wide), jnp.bfloat16),
        ],
        scratch_shapes=[
            pltpu.VMEM((rows_here, wide), jnp.bfloat16),
            pltpu.VMEM((1, wide), jnp.float32),
            pltpu.VMEM((wide, wide), jnp.float32),
            pltpu.SemaphoreType.DMA((rows_here // CHUNK,)),
            pltpu.SemaphoreType.DMA,
        ],
        compiler_params=pltpu.CompilerParams(vmem_limit_bytes=VMEM_MOST),
        cost_estimate=pl.CostEstimate(
            flops=2 * rows_here * wide * wide, bytes_accessed=2 * rows_here * wide + 3 * wide * wide, transcendentals=0
        ),
        name="moments",
    )(me.reshape(1), mean, embeddings)


def cuts(columns):
    ends = [columns * sum(SHARES[:h + 1]) // sum(SHARES) for h in range(len(SHARES))]
    return list(zip([0] + ends[:-1], ends))


def add_kernel(first, arrived, pieces, keep_ref, *refs):
    came, outs = refs[:arrived], refs[-pieces:]
    rows, columns = outs[0].shape
    across = slice(first, first + columns)
    for p in range(pieces):
        at = slice(p * rows, (p + 1) * rows)
        held = keep_ref[at, across]
        for ref in came:
            held = held + ref[at, across].astype(jnp.float32)
        outs[p][...] = held.astype(outs[p].dtype)


def add_and_split(keep, came, pieces, share=None, after=()):
    rows, columns = keep.shape
    first, end = share or (0, columns)
    vmem = pl.BlockSpec(memory_space=pltpu.VMEM)
    shape = (rows // pieces, end - first)
    return pl.pallas_call(
        functools.partial(add_kernel, first, len(came), pieces),
        in_specs=[vmem] * (1 + len(came)) + [pl.BlockSpec(memory_space=pl.ANY)] * len(after),
        out_specs=[vmem] * pieces,
        out_shape=[jax.ShapeDtypeStruct(shape, jnp.float32 if p == 0 else jnp.bfloat16) for p in range(pieces)],
        compiler_params=pltpu.CompilerParams(vmem_limit_bytes=VMEM_SOME),
        cost_estimate=pl.CostEstimate(flops=2 * rows * (end - first), bytes_accessed=10 * rows * (end - first), transcendentals=0),
        name="add_and_split",
    )(keep, *came, *after)


def finish_kernel(total, between_ref, *refs):
    out_ref = refs[-1]
    each = (len(refs) - 1) // len(SHARES)
    for h, (first, end) in enumerate(cuts(out_ref.shape[1])):
        held = refs[h * each][...]
        for ref in refs[h * each + 1:(h + 1) * each]:
            held = held + ref[...].astype(jnp.float32)
        out_ref[:, first:end] = (held + between_ref[:, first:end]) / total


def finish(total, between, keeps, came):
    parts = [part for keep, pieces in zip(keeps, came) for part in (keep, *pieces)]
    vmem = pl.BlockSpec(memory_space=pltpu.VMEM)
    return pl.pallas_call(
        functools.partial(finish_kernel, total),
        in_specs=[vmem] * (1 + len(parts)),
        out_specs=vmem,
        out_shape=jax.ShapeDtypeStruct(between.shape, jnp.float32),
        compiler_params=pltpu.CompilerParams(vmem_limit_bytes=VMEM_SOME),
        cost_estimate=pl.CostEstimate(flops=8 * between.size, bytes_accessed=16 * between.size, transcendentals=0),
        name="finish",
    )(between, *parts)


def halving_stages(width):
    strides = [1 << k for k in range(width.bit_length() - 1)]
    return [[s] for s in strides[:-2]] + [strides[-2:]]


def exchange(width, stage, out):
    came = []
    for p in range(1, 1 << len(stage)):
        apart = sum(s for k, s in enumerate(stage) if (p >> (len(stage) - 1 - k)) & 1)
        came.append(lax.ppermute(out[p - 1], "wide", [(i, i ^ apart) for i in range(width)]))
    return came


def encode_kernel(total, me_ref, got_ref, basis_ref, centroid_ref, rotation_ref, *refs):
    out_hbm, between_ref, out_ref, delta_ref, list_ref, apart_ref, sem = refs[-7:]
    width = delta_ref.shape[0]
    feats = out_ref.shape[1]
    owned = centroid_ref.shape[0]
    wide = basis_ref.shape[0]
    block = wide // width
    share = total // width

    notes = jnp.concatenate([got_ref[s * SPAN + CAP:(s + 1) * SPAN, :] for s in range(width)], 0)
    size = width * NOTES
    to = lax.broadcasted_iota(jnp.int32, (size, size), 0)
    of = lax.broadcasted_iota(jnp.int32, (size, size), 1)
    turn = jnp.where((to % width) * NOTES + to // width == of, 1.0, 0.0).astype(jnp.bfloat16)
    turned = jnp.dot(turn, notes, preferred_element_type=jnp.float32)
    row = [turned[r * width:(r + 1) * width] for r in range(NOTES)]
    digits = row[NOTES - 1]
    list_ref[...] = digits[:, :CAP] * 32.0 + digits[:, CAP:] - 1.0
    quarters = wide // feats
    shifts = jnp.zeros((width, feats), jnp.float32)
    for q in range(quarters):
        parts = [row[p * quarters + q] for p in range(3)]
        mean = parts[0] + (parts[1] + parts[2])
        apart_ref[:, q * feats:(q + 1) * feats] = mean - jnp.mean(mean, 0, keepdims=True)
        terms = jnp.dot(
            jnp.concatenate(parts, 0).astype(jnp.bfloat16),
            basis_ref[q * feats:(q + 1) * feats, :],
            preferred_element_type=jnp.float32,
        )
        shifts = shifts + (terms[:width] + (terms[width:2 * width] + terms[2 * width:]))
    square = row[3 * quarters] + (row[3 * quarters + 1] + row[3 * quarters + 2])
    delta = shifts - jnp.mean(shifts, 0, keepdims=True)
    variance = jnp.sum(square + share * (delta * delta), 0, keepdims=True) / total
    scale = lax.rsqrt(variance + 1e-05)
    delta_ref[...] = delta

    names = lax.broadcasted_iota(jnp.int32, (CAP, owned), 1).astype(jnp.int16)

    def encode_group(g):
        columns = jnp.transpose(list_ref[pl.ds(g * GROUP, GROUP), :])
        hits, projected, held = [], [], []
        for s in range(GROUP):
            listed = jnp.broadcast_to(columns[:, s:s + 1], (CAP, LANES))
            held.append(jnp.concatenate([listed] * (feats // LANES), 1) >= 0)
            wanted = jnp.concatenate([listed.astype(jnp.int32).astype(jnp.int16)] * (owned // LANES), 1)
            hits.append(jnp.where(wanted == names, jnp.ones((), jnp.bfloat16), jnp.zeros((), jnp.bfloat16)))
            base = pl.multiple_of((g * GROUP + s) * SPAN, 16)
            rows = got_ref[pl.ds(base, CAP), :].astype(jnp.float32)
            projected.append((rows + delta_ref[pl.ds(g * GROUP + s, 1), :]) * scale)
        centre = jnp.dot(jnp.concatenate(hits, 0), centroid_ref[...], preferred_element_type=jnp.float32)
        residual = jnp.where(jnp.concatenate(held, 0), jnp.concatenate(projected, 0) - centre, 0.0)
        at = pl.ds(pl.multiple_of(g * (GROUP * CAP), GROUP * CAP), GROUP * CAP)
        out_ref[at, :] = jnp.dot(
            residual.astype(jnp.bfloat16), rotation_ref[...], preferred_element_type=jnp.float32
        ).astype(jnp.bfloat16)
        return pltpu.make_async_copy(out_ref.at[at], out_hbm.at[at], sem.at[g])

    groups = width // GROUP
    copies = []
    if groups <= 4:
        for g in range(groups):
            copies.append(encode_group(g))
            copies[g].start()
    else:

        @pl.loop(0, groups)
        def _(g):
            copy = encode_group(g)
            copy.start()
            copy.wait()

    first = me_ref[0] * block
    near = apart_ref[:, pl.ds(pl.multiple_of(first // LANES * LANES, LANES), LANES)]
    near = pltpu.roll(near, (LANES - first % LANES) % LANES, 1)[:, :block]
    between_ref[...] = share * lax.dot_general(
        near,
        apart_ref[...],
        (((0,), (0,)), ((), ())),
        precision=lax.Precision.HIGHEST,
        preferred_element_type=jnp.float32,
    )
    for copy in copies:
        copy.wait()


def encode(width, total, me, got, basis, centroids, rotation, after):
    wide, feats = basis.shape
    owned = centroids.shape[0]
    slots = width * CAP
    vmem, anywhere = pl.BlockSpec(memory_space=pltpu.VMEM), pl.BlockSpec(memory_space=pl.ANY)
    return pl.pallas_call(
        functools.partial(encode_kernel, total),
        in_specs=[pl.BlockSpec(memory_space=pltpu.SMEM)] + [vmem] * 4 + [anywhere] * len(after),
        out_specs=[anywhere, vmem],
        out_shape=[
            jax.ShapeDtypeStruct((slots, feats), jnp.bfloat16),
            jax.ShapeDtypeStruct((wide // width, wide), jnp.float32),
        ],
        scratch_shapes=[
            pltpu.VMEM((slots, feats), jnp.bfloat16),
            pltpu.VMEM((width, feats), jnp.float32),
            pltpu.VMEM((width, CAP), jnp.float32),
            pltpu.VMEM((width, wide), jnp.float32),
            pltpu.SemaphoreType.DMA((width // GROUP,)),
        ],
        compiler_params=pltpu.CompilerParams(vmem_limit_bytes=VMEM_SOME),
        cost_estimate=pl.CostEstimate(
            flops=2 * slots * feats * (owned + feats), bytes_accessed=4 * slots * feats, transcendentals=0
        ),
        name="encode",
    )(me.reshape(1), got, basis, centroids, rotation, *after)


def local(embeddings, basis, list_owner, list_slot, centroids, rotation):
    width = lax.axis_size("wide")
    me = lax.axis_index("wide")
    rows_here, wide = embeddings.shape
    feats = basis.shape[1]
    total = rows_here * width

    rows, mean = project_and_sort(width, embeddings, basis, list_owner, list_slot)
    got = lax.all_to_all(rows.reshape(width, SPAN, feats), "wide", split_axis=0, concat_axis=0, tiled=True)

    keep, send = moments(width, me, embeddings, mean)
    stages = halving_stages(width)
    came = exchange(width, stages[0], [send])
    last, after = [], []
    for cut in cuts(wide):
        share = add_and_split(keep, came, 1 << len(stages[1]), cut, after)
        for n in range(1, len(stages) - 1):
            moved = exchange(width, stages[n], share[1:])
            share = add_and_split(share[0], moved, 1 << len(stages[n + 1]))
            if n == 1:
                after = [share[1]]
        last.append(share)
    came = [exchange(width, stages[-1], share[1:]) for share in last]
    encoded, between = encode(
        width, total, me, got.reshape(width * SPAN, feats), basis, centroids, rotation, [share[1] for share in last]
    )
    covariance = finish(total, between, [share[0] for share in last], came)
    return (encoded, covariance)


def solution(mesh):
    in_specs = (
        P(("groups", "wide"), None),
        P(),
        P(("groups", "wide")),
        P(("groups", "wide")),
        P("wide", None),
        P(),
    )
    out_specs = (P(("groups", "wide"), None), P(("groups", "wide"), None))
    return jax.shard_map(local, mesh=mesh, in_specs=in_specs, out_specs=out_specs, check_vma=False)
```

```python
import functools

import jax
import jax.numpy as jnp
from jax import lax
from jax.experimental import pallas as pl
from jax.experimental.pallas import tpu as pltpu
from jax.sharding import PartitionSpec as P

CAP = 128
LANES = 128
NOTES = 16
SPAN = CAP + NOTES
CHUNK = 512
TILE = 256
GROUP = 4
SHARES = 2
VMEM_ALL = 60 * 1024 * 1024
VMEM_SOME = 24 * 1024 * 1024
VMEM_MOST = 48 * 1024 * 1024


def in_three(x):
    high = x.astype(jnp.bfloat16).astype(jnp.float32)
    rest = x - high
    middle = rest.astype(jnp.bfloat16).astype(jnp.float32)
    return high, middle, (rest - middle).astype(jnp.bfloat16).astype(jnp.float32)


def rows_kernel(
    width, e_hbm, basis_hbm, owner_hbm, slot_hbm,
    rows_hbm, mean_hbm,
    owner_ref, slot_ref, mean_ref, basis_ref, e_ref, rows_ref, y_ref, yb_ref, sum_ref, total_ref, target_ref, list_ref, e_sem, small_sem, sem,
):
    step = pl.program_id(0)
    rows_here, feats = y_ref.shape
    wide = e_ref.shape[1]
    chunks = rows_here // LANES

    def e_copy(c):
        at = pl.ds(pl.multiple_of(c * CHUNK, CHUNK), CHUNK)
        return pltpu.make_async_copy(e_hbm.at[at], e_ref.at[at], e_sem.at[c])

    @pl.when(step == 0)
    def _():
        owner_copy = pltpu.make_async_copy(owner_hbm, owner_ref, small_sem.at[0])
        slot_copy = pltpu.make_async_copy(slot_hbm, slot_ref, small_sem.at[1])
        basis_copy = pltpu.make_async_copy(basis_hbm, basis_ref, small_sem.at[2])
        owner_copy.start()
        e_copy(0).start()
        slot_copy.start()
        basis_copy.start()
        for c in range(1, rows_here // CHUNK):
            e_copy(c).start()
        sum_ref[...] = jnp.zeros_like(sum_ref)
        total_ref[...] = jnp.zeros_like(total_ref)
        basis_copy.wait()

    def project():
        e_copy(step).wait()
        here = pl.ds(pl.multiple_of(step * CHUNK, CHUNK), CHUNK)
        rows = e_ref[here, :]
        y = jnp.dot(rows, basis_ref[...], preferred_element_type=jnp.float32)
        y_ref[here, :] = y
        sum_ref[...] += jnp.sum(y.reshape(CHUNK // 8, 8, feats), 0)
        total_ref[...] += jnp.sum(rows.astype(jnp.float32).reshape(CHUNK // 8, 8, wide), 0)

    @pl.when(step != 1)
    def _():
        project()

    @pl.when(step == 1)
    def _():
        pltpu.make_async_copy(owner_hbm, owner_ref, small_sem.at[0]).wait()
        owner = owner_ref[...]
        wanted = lax.broadcasted_iota(jnp.int32, (width, LANES), 0)
        hits = [jnp.where(owner[c:c + 1, :] == wanted, 1.0, 0.0) for c in range(chunks)]
        flat = jnp.concatenate(hits, 0).astype(jnp.bfloat16)
        up = lax.broadcasted_iota(jnp.int32, (LANES, LANES), 0)
        to = lax.broadcasted_iota(jnp.int32, (LANES, LANES), 1)
        before = jnp.where(up < to, 1.0, 0.0).astype(jnp.bfloat16)
        every = jnp.ones((LANES, LANES), jnp.bfloat16)
        within = jnp.dot(flat, before, preferred_element_type=jnp.float32)
        counts = jnp.dot(flat, every, preferred_element_type=jnp.float32)
        carry = jnp.zeros((width, LANES), jnp.float32)
        ranks = []
        for c in range(chunks):
            at = slice(c * width, (c + 1) * width)
            ranks.append(jnp.sum(hits[c] * (within[at] + carry), 0, keepdims=True).astype(jnp.int32))
            carry = carry + counts[at]
            target_ref[c:c + 1, :] = owner[c:c + 1, :] * CAP + ranks[c]
        project()

    @pl.when(step == pl.num_programs(0) - 1)
    def _():
        mean_y = jnp.sum(sum_ref[...], 0, keepdims=True) / rows_here
        square = jnp.zeros((8, feats), jnp.float32)
        for c in range(rows_here // CHUNK):
            at = slice(c * CHUNK, (c + 1) * CHUNK)
            centred = y_ref[at, :] - mean_y
            square = square + jnp.sum((centred * centred).reshape(CHUNK // 8, 8, feats), 0)
            yb_ref[at, :] = centred.astype(jnp.bfloat16)
        mean = jnp.sum(total_ref[...], 0, keepdims=True) / rows_here
        mean_ref[...] = mean
        mean_copy = pltpu.make_async_copy(mean_ref, mean_hbm, small_sem.at[3])
        mean_copy.start()
        parts = in_three(mean)
        common = [part[:, q * feats:(q + 1) * feats] for part in parts for q in range(wide // feats)]
        common = jnp.concatenate(common + list(in_three(jnp.sum(square, 0, keepdims=True))), 0)

        pltpu.make_async_copy(slot_hbm, slot_ref, small_sem.at[1]).wait()
        owner = owner_ref[...]
        wanted = lax.broadcasted_iota(jnp.int32, (width, LANES), 0)
        hits = [jnp.where(owner[c:c + 1, :] == wanted, 1.0, 0.0) for c in range(chunks)]
        ranks = [target_ref[c:c + 1, :] - owner[c:c + 1, :] * CAP for c in range(chunks)]
        slot = slot_ref[...] + 1
        high, low = (slot >> 5).astype(jnp.float32), (slot & 31).astype(jnp.float32)
        spots = lax.broadcasted_iota(jnp.int32, (CAP, LANES), 0)
        placed = jnp.concatenate([jnp.where(ranks[c] == spots, 1.0, 0.0) for c in range(chunks)], 1).astype(jnp.bfloat16)
        digits = jnp.concatenate(
            [
                jnp.concatenate([hits[c] * high[c:c + 1, :] for c in range(chunks)], 1),
                jnp.concatenate([hits[c] * low[c:c + 1, :] for c in range(chunks)], 1),
            ],
            0,
        ).astype(jnp.bfloat16)
        found = lax.dot_general(digits, placed, (((1,), (1,)), ((), ())), preferred_element_type=jnp.float32)
        list_ref[:, :CAP] = found[:width]
        list_ref[:, CAP:] = found[width:]


        place = lax.broadcasted_iota(jnp.int32, (GROUP * CAP, LANES), 0).astype(jnp.int16)

        def sort_group(g):
            first = g * GROUP
            pieces = []
            for c in range(chunks):
                wanted = (target_ref[c:c + 1, :] - first * CAP).astype(jnp.int32)
                wanted = jnp.broadcast_to(wanted, (16, LANES)).astype(jnp.int16)
                wanted = jnp.concatenate([wanted] * (GROUP * CAP // 16), 0)
                pieces.append(jnp.where(wanted == place, jnp.ones((), jnp.bfloat16), jnp.zeros((), jnp.bfloat16)))
            pick = jnp.concatenate(pieces, 1)
            rows = jnp.dot(pick, yb_ref[...], preferred_element_type=jnp.float32).astype(jnp.bfloat16)
            for j in range(GROUP):
                base = pl.multiple_of((first + j) * SPAN, 16)
                rows_ref[pl.ds(base, CAP), :] = rows[j * CAP:(j + 1) * CAP]
                notes = jnp.concatenate([common, list_ref[pl.ds(first + j, 1), :]], 0)
                rows_ref[pl.ds(pl.multiple_of(base + CAP, 16), NOTES), :] = notes.astype(jnp.bfloat16)
            at = pl.ds(pl.multiple_of(g * (GROUP * SPAN), 16), GROUP * SPAN)
            return pltpu.make_async_copy(rows_ref.at[at], rows_hbm.at[at], sem.at[g])

        groups = width // GROUP
        if groups <= 4:
            copies = []
            for g in range(groups):
                copies.append(sort_group(g))
                copies[g].start()
            for copy in copies:
                copy.wait()
        else:

            @pl.loop(0, groups)
            def _(g):
                copy = sort_group(g)
                copy.start()
                copy.wait()

        mean_copy.wait()


def project_and_sort(width, embeddings, basis, list_owner, list_slot):
    rows_here, wide = embeddings.shape
    feats = basis.shape[1]
    lanes = rows_here // LANES
    slots = width * SPAN
    return pl.pallas_call(
        functools.partial(rows_kernel, width),
        grid=(rows_here // CHUNK,),
        in_specs=[pl.BlockSpec(memory_space=pl.ANY)] * 4,
        out_specs=[pl.BlockSpec(memory_space=pl.ANY)] * 2,
        out_shape=[
            jax.ShapeDtypeStruct((slots, feats), jnp.bfloat16),
            jax.ShapeDtypeStruct((1, wide), jnp.float32),
        ],
        scratch_shapes=[
            pltpu.VMEM((lanes, LANES), jnp.int32),
            pltpu.VMEM((lanes, LANES), jnp.int32),
            pltpu.VMEM((1, wide), jnp.float32),
            pltpu.VMEM((wide, feats), jnp.bfloat16),
            pltpu.VMEM((rows_here, wide), jnp.bfloat16),
            pltpu.VMEM((slots, feats), jnp.bfloat16),
            pltpu.VMEM((rows_here, feats), jnp.float32),
            pltpu.VMEM((rows_here, feats), jnp.bfloat16),
            pltpu.VMEM((8, feats), jnp.float32),
            pltpu.VMEM((8, wide), jnp.float32),
            pltpu.VMEM((lanes, LANES), jnp.int32),
            pltpu.VMEM((width, 2 * CAP), jnp.float32),
            pltpu.SemaphoreType.DMA((rows_here // CHUNK,)),
            pltpu.SemaphoreType.DMA((4,)),
            pltpu.SemaphoreType.DMA((width // GROUP,)),
        ],
        compiler_params=pltpu.CompilerParams(vmem_limit_bytes=VMEM_ALL),
        cost_estimate=pl.CostEstimate(
            flops=2 * rows_here * feats * (wide + slots), bytes_accessed=2 * rows_here * wide + 2 * slots * feats, transcendentals=0
        ),
        name="project_sort",
    )(embeddings, basis, list_owner.reshape(lanes, LANES), list_slot.reshape(lanes, LANES))


def moments_kernel(width, me_ref, mean_hbm, e_hbm, keep_ref, send_ref, e_ref, mean_ref, m_ref, sem, mean_sem):
    rows_here, wide = e_ref.shape
    block = wide // width
    bits = width.bit_length() - 1
    tiles = wide // TILE
    mean_copy = pltpu.make_async_copy(mean_hbm, mean_ref, mean_sem)
    mean_copy.start()
    copies = []
    for c in range(rows_here // CHUNK):
        at = pl.ds(c * CHUNK, CHUNK)
        copies.append(pltpu.make_async_copy(e_hbm.at[at], e_ref.at[at], sem.at[c]))
        copies[c].start()
    me = me_ref[0]
    odd = (me & 1) == 1
    mean_copy.wait()
    mean = mean_ref[...]
    for t in range(tiles):
        rows, columns = slice(t * TILE, (t + 1) * TILE), slice(t * TILE, wide)
        if t == 0:
            product = jnp.zeros((TILE, wide), jnp.float32)
            for c in range(rows_here // CHUNK):
                copies[c].wait()
                at = slice(c * CHUNK, (c + 1) * CHUNK)
                product = product + lax.dot_general(
                    e_ref[at, rows], e_ref[at, :], (((0,), (0,)), ((), ())), preferred_element_type=jnp.float32
                )
        else:
            product = lax.dot_general(
                e_ref[:, rows], e_ref[:, columns], (((0,), (0,)), ((), ())), preferred_element_type=jnp.float32
            )
        down = jnp.transpose(jnp.broadcast_to(mean[:, rows] * rows_here, (LANES, TILE)))
        for u in range(t, tiles):
            pieces = []
            for j in range(u * TILE // LANES, (u + 1) * TILE // LANES):
                across = slice(j * LANES, (j + 1) * LANES)
                within = slice(j * LANES - t * TILE, (j + 1) * LANES - t * TILE)
                pieces.append((product[:, within] - down * mean[:, across]).astype(jnp.bfloat16))
            piece = jnp.concatenate(pieces, 1)
            other = slice(u * TILE, (u + 1) * TILE)
            m_ref[rows, other] = piece
            if u > t:
                m_ref[other, rows] = jnp.transpose(piece)
        for pair in range(TILE // block // 2):
            first = t * (TILE // block) + 2 * pair
            apart = (first ^ me) >> 1
            place = 0
            for k in range(bits - 1):
                place = place + (((apart >> k) & 1) << (bits - 2 - k))
            to = pl.ds(pl.multiple_of(place * block, block), block)
            even_rows = m_ref[first * block:(first + 1) * block, :]
            odd_rows = m_ref[(first + 1) * block:(first + 2) * block, :]
            keep_ref[to, :] = jnp.where(odd, odd_rows, even_rows)
            send_ref[to, :] = jnp.where(odd, even_rows, odd_rows)


def moments(width, me, embeddings, mean):
    rows_here, wide = embeddings.shape
    vmem = pl.BlockSpec(memory_space=pltpu.VMEM)
    return pl.pallas_call(
        functools.partial(moments_kernel, width),
        in_specs=[pl.BlockSpec(memory_space=pltpu.SMEM)] + [pl.BlockSpec(memory_space=pl.ANY)] * 2,
        out_specs=[vmem] * 2,
        out_shape=[
            jax.ShapeDtypeStruct((wide // 2, wide), jnp.bfloat16),
            jax.ShapeDtypeStruct((wide // 2, wide), jnp.bfloat16),
        ],
        scratch_shapes=[
            pltpu.VMEM((rows_here, wide), jnp.bfloat16),
            pltpu.VMEM((1, wide), jnp.float32),
            pltpu.VMEM((wide, wide), jnp.bfloat16),
            pltpu.SemaphoreType.DMA((rows_here // CHUNK,)),
            pltpu.SemaphoreType.DMA,
        ],
        compiler_params=pltpu.CompilerParams(vmem_limit_bytes=VMEM_MOST),
        cost_estimate=pl.CostEstimate(
            flops=2 * rows_here * wide * wide, bytes_accessed=2 * rows_here * wide + 3 * wide * wide, transcendentals=0
        ),
        name="moments",
    )(me.reshape(1), mean, embeddings)


def add_kernel(shares, pieces, keep_ref, *refs):
    outs = refs[len(refs) - shares * pieces:]
    came = refs[:len(refs) - shares * pieces]
    rows, columns = outs[0].shape
    for h in range(shares):
        across = slice(h * columns, (h + 1) * columns)
        for p in range(pieces):
            at = slice(p * rows, (p + 1) * rows)
            held = keep_ref[at, across].astype(jnp.float32)
            for ref in came:
                held = held + ref[at, across].astype(jnp.float32)
            out = outs[h * pieces + p]
            out[...] = held.astype(out.dtype)


def add_and_split(keep, came, shares, pieces):
    rows, columns = keep.shape
    vmem = pl.BlockSpec(memory_space=pltpu.VMEM)
    shape = (rows // pieces, columns // shares)
    kinds = [jnp.float32] + [jnp.bfloat16] * (pieces - 1)
    outs = pl.pallas_call(
        functools.partial(add_kernel, shares, pieces),
        in_specs=[vmem] * (1 + len(came)),
        out_specs=[vmem] * (shares * pieces),
        out_shape=[jax.ShapeDtypeStruct(shape, kind) for kind in kinds * shares],
        compiler_params=pltpu.CompilerParams(vmem_limit_bytes=VMEM_SOME),
        cost_estimate=pl.CostEstimate(flops=2 * rows * columns, bytes_accessed=10 * rows * columns, transcendentals=0),
        name="add_and_split",
    )(keep, *came)
    return [outs[h * pieces:(h + 1) * pieces] for h in range(shares)]


def finish_kernel(total, between_ref, *refs):
    out_ref = refs[-1]
    each = (len(refs) - 1) // SHARES
    columns = out_ref.shape[1] // SHARES
    for h in range(SHARES):
        across = slice(h * columns, (h + 1) * columns)
        held = refs[h * each][...]
        for ref in refs[h * each + 1:(h + 1) * each]:
            held = held + ref[...].astype(jnp.float32)
        out_ref[:, across] = (held + between_ref[:, across]) / total


def finish(total, between, keeps, came):
    parts = [part for keep, pieces in zip(keeps, came) for part in (keep, *pieces)]
    vmem = pl.BlockSpec(memory_space=pltpu.VMEM)
    return pl.pallas_call(
        functools.partial(finish_kernel, total),
        in_specs=[vmem] * (1 + len(parts)),
        out_specs=vmem,
        out_shape=jax.ShapeDtypeStruct(between.shape, jnp.float32),
        compiler_params=pltpu.CompilerParams(vmem_limit_bytes=VMEM_SOME),
        cost_estimate=pl.CostEstimate(flops=8 * between.size, bytes_accessed=16 * between.size, transcendentals=0),
        name="finish",
    )(between, *parts)


def halving_stages(width):
    strides = [1 << k for k in range(width.bit_length() - 1)]
    return [[s] for s in strides[:-2]] + [strides[-2:]]


def exchange(width, stage, out):
    came = []
    for p in range(1, 1 << len(stage)):
        apart = sum(s for k, s in enumerate(stage) if (p >> (len(stage) - 1 - k)) & 1)
        came.append(lax.ppermute(out[p - 1], "wide", [(i, i ^ apart) for i in range(width)]))
    return came


def encode_kernel(total, me_ref, got_ref, basis_ref, centroid_ref, rotation_ref, *refs):
    out_hbm, between_ref, out_ref, delta_ref, list_ref, apart_ref, sem = refs[-7:]
    width = delta_ref.shape[0]
    feats = out_ref.shape[1]
    owned = centroid_ref.shape[0]
    wide = basis_ref.shape[0]
    block = wide // width
    share = total // width

    notes = jnp.concatenate([got_ref[s * SPAN + CAP:(s + 1) * SPAN, :] for s in range(width)], 0)
    size = width * NOTES
    to = lax.broadcasted_iota(jnp.int32, (size, size), 0)
    of = lax.broadcasted_iota(jnp.int32, (size, size), 1)
    turn = jnp.where((to % width) * NOTES + to // width == of, 1.0, 0.0).astype(jnp.bfloat16)
    turned = jnp.dot(turn, notes, preferred_element_type=jnp.float32)
    row = [turned[r * width:(r + 1) * width] for r in range(NOTES)]
    digits = row[NOTES - 1]
    list_ref[...] = digits[:, :CAP] * 32.0 + digits[:, CAP:] - 1.0
    quarters = wide // feats
    shifts = jnp.zeros((width, feats), jnp.float32)
    for q in range(quarters):
        parts = [row[p * quarters + q] for p in range(3)]
        mean = parts[0] + (parts[1] + parts[2])
        apart_ref[:, q * feats:(q + 1) * feats] = mean - jnp.mean(mean, 0, keepdims=True)
        terms = jnp.dot(
            jnp.concatenate(parts, 0).astype(jnp.bfloat16),
            basis_ref[q * feats:(q + 1) * feats, :],
            preferred_element_type=jnp.float32,
        )
        shifts = shifts + (terms[:width] + (terms[width:2 * width] + terms[2 * width:]))
    square = row[3 * quarters] + (row[3 * quarters + 1] + row[3 * quarters + 2])
    delta = shifts - jnp.mean(shifts, 0, keepdims=True)
    variance = jnp.sum(square + share * (delta * delta), 0, keepdims=True) / total
    scale = lax.rsqrt(variance + 1e-05)
    delta_ref[...] = delta

    names = lax.broadcasted_iota(jnp.int32, (CAP, owned), 1).astype(jnp.int16)

    def encode_group(g):
        columns = jnp.transpose(list_ref[pl.ds(g * GROUP, GROUP), :])
        hits, projected, held = [], [], []
        for s in range(GROUP):
            listed = jnp.broadcast_to(columns[:, s:s + 1], (CAP, LANES))
            held.append(jnp.concatenate([listed] * (feats // LANES), 1) >= 0)
            wanted = jnp.concatenate([listed.astype(jnp.int32).astype(jnp.int16)] * (owned // LANES), 1)
            hits.append(jnp.where(wanted == names, jnp.ones((), jnp.bfloat16), jnp.zeros((), jnp.bfloat16)))
            base = pl.multiple_of((g * GROUP + s) * SPAN, 16)
            rows = got_ref[pl.ds(base, CAP), :].astype(jnp.float32)
            projected.append((rows + delta_ref[pl.ds(g * GROUP + s, 1), :]) * scale)
        centre = jnp.dot(jnp.concatenate(hits, 0), centroid_ref[...], preferred_element_type=jnp.float32)
        residual = jnp.where(jnp.concatenate(held, 0), jnp.concatenate(projected, 0) - centre, 0.0)
        at = pl.ds(pl.multiple_of(g * (GROUP * CAP), GROUP * CAP), GROUP * CAP)
        out_ref[at, :] = jnp.dot(
            residual.astype(jnp.bfloat16), rotation_ref[...], preferred_element_type=jnp.float32
        ).astype(jnp.bfloat16)
        return pltpu.make_async_copy(out_ref.at[at], out_hbm.at[at], sem.at[g])

    groups = width // GROUP
    copies = []
    if groups <= 4:
        for g in range(groups):
            copies.append(encode_group(g))
            copies[g].start()
    else:

        @pl.loop(0, groups)
        def _(g):
            copy = encode_group(g)
            copy.start()
            copy.wait()

    first = me_ref[0] * block
    near = apart_ref[:, pl.ds(pl.multiple_of(first // LANES * LANES, LANES), LANES)]
    near = pltpu.roll(near, (LANES - first % LANES) % LANES, 1)[:, :block]
    between_ref[...] = share * lax.dot_general(
        near,
        apart_ref[...],
        (((0,), (0,)), ((), ())),
        precision=lax.Precision.HIGHEST,
        preferred_element_type=jnp.float32,
    )
    for copy in copies:
        copy.wait()


def encode(width, total, me, got, basis, centroids, rotation, after):
    wide, feats = basis.shape
    owned = centroids.shape[0]
    slots = width * CAP
    vmem, anywhere = pl.BlockSpec(memory_space=pltpu.VMEM), pl.BlockSpec(memory_space=pl.ANY)
    return pl.pallas_call(
        functools.partial(encode_kernel, total),
        in_specs=[pl.BlockSpec(memory_space=pltpu.SMEM)] + [vmem] * 4 + [anywhere] * len(after),
        out_specs=[anywhere, vmem],
        out_shape=[
            jax.ShapeDtypeStruct((slots, feats), jnp.bfloat16),
            jax.ShapeDtypeStruct((wide // width, wide), jnp.float32),
        ],
        scratch_shapes=[
            pltpu.VMEM((slots, feats), jnp.bfloat16),
            pltpu.VMEM((width, feats), jnp.float32),
            pltpu.VMEM((width, CAP), jnp.float32),
            pltpu.VMEM((width, wide), jnp.float32),
            pltpu.SemaphoreType.DMA((width // GROUP,)),
        ],
        compiler_params=pltpu.CompilerParams(vmem_limit_bytes=VMEM_SOME),
        cost_estimate=pl.CostEstimate(
            flops=2 * slots * feats * (owned + feats), bytes_accessed=4 * slots * feats, transcendentals=0
        ),
        name="encode",
    )(me.reshape(1), got, basis, centroids, rotation, *after)


def local(embeddings, basis, list_owner, list_slot, centroids, rotation):
    width = lax.axis_size("wide")
    me = lax.axis_index("wide")
    rows_here, wide = embeddings.shape
    feats = basis.shape[1]
    total = rows_here * width

    rows, mean = project_and_sort(width, embeddings, basis, list_owner, list_slot)
    got = lax.all_to_all(rows.reshape(width, SPAN, feats), "wide", split_axis=0, concat_axis=0, tiled=True)

    keep, send = moments(width, me, embeddings, mean)
    stages = halving_stages(width)
    came = exchange(width, stages[0], [send])
    shares = add_and_split(keep, came, SHARES, 1 << len(stages[1]))
    last = []
    for share in shares:
        for n in range(1, len(stages) - 1):
            came = exchange(width, stages[n], share[1:])
            (share,) = add_and_split(share[0], came, 1, 1 << len(stages[n + 1]))
        last.append(share)
    came = [exchange(width, stages[-1], share[1:]) for share in last]
    encoded, between = encode(
        width, total, me, got.reshape(width * SPAN, feats), basis, centroids, rotation, [share[1] for share in last]
    )
    covariance = finish(total, between, [share[0] for share in last], came)
    return (encoded, covariance)


def solution(mesh):
    in_specs = (
        P(("groups", "wide"), None),
        P(),
        P(("groups", "wide")),
        P(("groups", "wide")),
        P("wide", None),
        P(),
    )
    out_specs = (P(("groups", "wide"), None), P(("groups", "wide"), None))
    return jax.shard_map(local, mesh=mesh, in_specs=in_specs, out_specs=out_specs, check_vma=False)
```

```python
import functools

import jax
import jax.numpy as jnp
from jax import lax
from jax.experimental import pallas as pl
from jax.experimental.pallas import tpu as pltpu
from jax.sharding import PartitionSpec as P

CAP = 128
LANES = 128
NOTES = 16
SPAN = CAP + NOTES
CHUNK = 512
TILE = 256
GROUP = 4
SHARES = 2
VMEM_ALL = 60 * 1024 * 1024
VMEM_SOME = 24 * 1024 * 1024
VMEM_MOST = 48 * 1024 * 1024


def in_three(x):
    high = x.astype(jnp.bfloat16).astype(jnp.float32)
    rest = x - high
    middle = rest.astype(jnp.bfloat16).astype(jnp.float32)
    return high, middle, (rest - middle).astype(jnp.bfloat16).astype(jnp.float32)


def rows_kernel(
    width, me_ref, e_hbm, basis_hbm, owner_hbm, slot_hbm,
    near_hbm, far_hbm, mean_hbm,
    owner_ref, slot_ref, mean_ref, basis_ref, e_ref, rows_ref, y_ref, yb_ref, sum_ref, total_ref, target_ref, list_ref, e_sem, small_sem, sem,
):
    step = pl.program_id(0)
    rows_here, feats = y_ref.shape
    wide = e_ref.shape[1]
    chunks = rows_here // LANES

    def e_copy(c):
        at = pl.ds(pl.multiple_of(c * CHUNK, CHUNK), CHUNK)
        return pltpu.make_async_copy(e_hbm.at[at], e_ref.at[at], e_sem.at[c])

    @pl.when(step == 0)
    def _():
        owner_copy = pltpu.make_async_copy(owner_hbm, owner_ref, small_sem.at[0])
        slot_copy = pltpu.make_async_copy(slot_hbm, slot_ref, small_sem.at[1])
        basis_copy = pltpu.make_async_copy(basis_hbm, basis_ref, small_sem.at[2])
        owner_copy.start()
        e_copy(0).start()
        slot_copy.start()
        basis_copy.start()
        for c in range(1, rows_here // CHUNK):
            e_copy(c).start()
        owner_copy.wait()
        sum_ref[...] = jnp.zeros_like(sum_ref)
        total_ref[...] = jnp.zeros_like(total_ref)
        owner = owner_ref[...]
        wanted = lax.broadcasted_iota(jnp.int32, (width, LANES), 0)
        hits = [jnp.where(owner[c:c + 1, :] == wanted, 1.0, 0.0) for c in range(chunks)]
        flat = jnp.concatenate(hits, 0).astype(jnp.bfloat16)
        up = lax.broadcasted_iota(jnp.int32, (LANES, LANES), 0)
        to = lax.broadcasted_iota(jnp.int32, (LANES, LANES), 1)
        before = jnp.where(up < to, 1.0, 0.0).astype(jnp.bfloat16)
        every = jnp.ones((LANES, LANES), jnp.bfloat16)
        within = jnp.dot(flat, before, preferred_element_type=jnp.float32)
        counts = jnp.dot(flat, every, preferred_element_type=jnp.float32)
        carry = jnp.zeros((width, LANES), jnp.float32)
        ranks = []
        for c in range(chunks):
            at = slice(c * width, (c + 1) * width)
            ranks.append(jnp.sum(hits[c] * (within[at] + carry), 0, keepdims=True).astype(jnp.int32))
            carry = carry + counts[at]
            target_ref[c:c + 1, :] = owner[c:c + 1, :] * CAP + ranks[c]

        slot_copy.wait()
        slot = slot_ref[...] + 1
        high, low = (slot >> 5).astype(jnp.float32), (slot & 31).astype(jnp.float32)
        spots = lax.broadcasted_iota(jnp.int32, (CAP, LANES), 0)
        placed = jnp.concatenate([jnp.where(ranks[c] == spots, 1.0, 0.0) for c in range(chunks)], 1).astype(jnp.bfloat16)
        digits = jnp.concatenate(
            [
                jnp.concatenate([hits[c] * high[c:c + 1, :] for c in range(chunks)], 1),
                jnp.concatenate([hits[c] * low[c:c + 1, :] for c in range(chunks)], 1),
            ],
            0,
        ).astype(jnp.bfloat16)
        found = lax.dot_general(digits, placed, (((1,), (1,)), ((), ())), preferred_element_type=jnp.float32)
        list_ref[:, :CAP] = found[:width]
        list_ref[:, CAP:] = found[width:]
        basis_copy.wait()

    e_copy(step).wait()
    here = pl.ds(pl.multiple_of(step * CHUNK, CHUNK), CHUNK)
    rows = e_ref[here, :]
    y = jnp.dot(rows, basis_ref[...], preferred_element_type=jnp.float32)
    y_ref[here, :] = y
    sum_ref[...] += jnp.sum(y.reshape(CHUNK // 8, 8, feats), 0)
    total_ref[...] += jnp.sum(rows.astype(jnp.float32).reshape(CHUNK // 8, 8, wide), 0)

    @pl.when(step == pl.num_programs(0) - 1)
    def _():
        mean_y = jnp.sum(sum_ref[...], 0, keepdims=True) / rows_here
        square = jnp.zeros((8, feats), jnp.float32)
        for c in range(rows_here // CHUNK):
            at = slice(c * CHUNK, (c + 1) * CHUNK)
            centred = y_ref[at, :] - mean_y
            square = square + jnp.sum((centred * centred).reshape(CHUNK // 8, 8, feats), 0)
            yb_ref[at, :] = centred.astype(jnp.bfloat16)
        mean = jnp.sum(total_ref[...], 0, keepdims=True) / rows_here
        mean_ref[...] = mean
        mean_copy = pltpu.make_async_copy(mean_ref, mean_hbm, small_sem.at[3])
        mean_copy.start()
        parts = in_three(mean)
        common = [part[:, q * feats:(q + 1) * feats] for part in parts for q in range(wide // feats)]
        common = jnp.concatenate(common + list(in_three(jnp.sum(square, 0, keepdims=True))), 0)

        place = lax.broadcasted_iota(jnp.int32, (GROUP * CAP, LANES), 0).astype(jnp.int16)

        half = me_ref[0] // (width // 2)
        each = width // GROUP // 2

        def sort_group(apart, q):
            first = ((half ^ apart) * each + q) * GROUP
            pieces = []
            for c in range(chunks):
                wanted = target_ref[c:c + 1, :] - first * CAP
                wanted = jnp.broadcast_to(wanted, (16, LANES)).astype(jnp.int16)
                wanted = jnp.concatenate([wanted] * (GROUP * CAP // 16), 0)
                pieces.append(jnp.where(wanted == place, jnp.ones((), jnp.bfloat16), jnp.zeros((), jnp.bfloat16)))
            pick = jnp.concatenate(pieces, 1)
            rows = jnp.dot(pick, yb_ref[...], preferred_element_type=jnp.float32).astype(jnp.bfloat16)
            start = (apart * each + q) * (GROUP * SPAN)
            for j in range(GROUP):
                base = pl.multiple_of(start + j * SPAN, 16)
                rows_ref[pl.ds(base, CAP), :] = rows[j * CAP:(j + 1) * CAP]
                notes = jnp.concatenate([common, list_ref[pl.ds(first + j, 1), :]], 0)
                rows_ref[pl.ds(pl.multiple_of(base + CAP, 16), NOTES), :] = notes.astype(jnp.bfloat16)
            here = pl.ds(pl.multiple_of(start, 16), GROUP * SPAN)
            there = pl.ds(pl.multiple_of(q * (GROUP * SPAN), 16), GROUP * SPAN)
            return pltpu.make_async_copy(
                rows_ref.at[here], (near_hbm, far_hbm)[apart].at[there], sem.at[apart * each + q]
            )

        copies = []
        for apart in (1, 0):
            if each <= 2:
                for q in range(each):
                    copies.append(sort_group(apart, q))
                    copies[-1].start()
            else:

                @pl.loop(0, each)
                def _(q):
                    copy = sort_group(apart, q)
                    copy.start()
                    copy.wait()

        for copy in copies:
            copy.wait()
        mean_copy.wait()


def project_and_sort(width, me, embeddings, basis, list_owner, list_slot):
    rows_here, wide = embeddings.shape
    feats = basis.shape[1]
    lanes = rows_here // LANES
    slots = width * SPAN
    return pl.pallas_call(
        functools.partial(rows_kernel, width),
        grid=(rows_here // CHUNK,),
        in_specs=[pl.BlockSpec(memory_space=pltpu.SMEM)] + [pl.BlockSpec(memory_space=pl.ANY)] * 4,
        out_specs=[pl.BlockSpec(memory_space=pl.ANY)] * 3,
        out_shape=[jax.ShapeDtypeStruct((slots // 2, feats), jnp.bfloat16)] * 2
        + [jax.ShapeDtypeStruct((1, wide), jnp.float32)],
        scratch_shapes=[
            pltpu.VMEM((lanes, LANES), jnp.int32),
            pltpu.VMEM((lanes, LANES), jnp.int32),
            pltpu.VMEM((1, wide), jnp.float32),
            pltpu.VMEM((wide, feats), jnp.bfloat16),
            pltpu.VMEM((rows_here, wide), jnp.bfloat16),
            pltpu.VMEM((slots, feats), jnp.bfloat16),
            pltpu.VMEM((rows_here, feats), jnp.float32),
            pltpu.VMEM((rows_here, feats), jnp.bfloat16),
            pltpu.VMEM((8, feats), jnp.float32),
            pltpu.VMEM((8, wide), jnp.float32),
            pltpu.VMEM((lanes, LANES), jnp.int32),
            pltpu.VMEM((width, 2 * CAP), jnp.float32),
            pltpu.SemaphoreType.DMA((rows_here // CHUNK,)),
            pltpu.SemaphoreType.DMA((4,)),
            pltpu.SemaphoreType.DMA((width // GROUP,)),
        ],
        compiler_params=pltpu.CompilerParams(vmem_limit_bytes=VMEM_ALL),
        cost_estimate=pl.CostEstimate(
            flops=2 * rows_here * feats * (wide + slots), bytes_accessed=2 * rows_here * wide + 2 * slots * feats, transcendentals=0
        ),
        name="project_sort",
    )(me.reshape(1), embeddings, basis, list_owner.reshape(lanes, LANES), list_slot.reshape(lanes, LANES))


def moments_kernel(width, me_ref, mean_hbm, e_hbm, keep_ref, send_ref, e_ref, mean_ref, m_ref, sem, mean_sem):
    rows_here, wide = e_ref.shape
    block = wide // width
    bits = width.bit_length() - 1
    tiles = wide // TILE
    mean_copy = pltpu.make_async_copy(mean_hbm, mean_ref, mean_sem)
    mean_copy.start()
    copies = []
    for c in range(rows_here // CHUNK):
        at = pl.ds(c * CHUNK, CHUNK)
        copies.append(pltpu.make_async_copy(e_hbm.at[at], e_ref.at[at], sem.at[c]))
        copies[c].start()
    me = me_ref[0]
    odd = (me & 1) == 1
    mean_copy.wait()
    mean = mean_ref[...]
    for t in range(tiles):
        rows, columns = slice(t * TILE, (t + 1) * TILE), slice(t * TILE, wide)
        if t == 0:
            product = jnp.zeros((TILE, wide), jnp.float32)
            for c in range(rows_here // CHUNK):
                copies[c].wait()
                at = slice(c * CHUNK, (c + 1) * CHUNK)
                product = product + lax.dot_general(
                    e_ref[at, rows], e_ref[at, :], (((0,), (0,)), ((), ())), preferred_element_type=jnp.float32
                )
        else:
            product = lax.dot_general(
                e_ref[:, rows], e_ref[:, columns], (((0,), (0,)), ((), ())), preferred_element_type=jnp.float32
            )
        down = jnp.transpose(jnp.broadcast_to(mean[:, rows] * rows_here, (LANES, TILE)))
        for u in range(t, tiles):
            pieces = []
            for j in range(u * TILE // LANES, (u + 1) * TILE // LANES):
                across = slice(j * LANES, (j + 1) * LANES)
                within = slice(j * LANES - t * TILE, (j + 1) * LANES - t * TILE)
                pieces.append((product[:, within] - down * mean[:, across]).astype(jnp.bfloat16))
            piece = jnp.concatenate(pieces, 1)
            other = slice(u * TILE, (u + 1) * TILE)
            m_ref[rows, other] = piece
            if u > t:
                m_ref[other, rows] = jnp.transpose(piece)
        for pair in range(TILE // block // 2):
            first = t * (TILE // block) + 2 * pair
            apart = (first ^ me) >> 1
            place = 0
            for k in range(bits - 1):
                place = place + (((apart >> k) & 1) << (bits - 2 - k))
            to = pl.ds(pl.multiple_of(place * block, block), block)
            even_rows = m_ref[first * block:(first + 1) * block, :]
            odd_rows = m_ref[(first + 1) * block:(first + 2) * block, :]
            keep_ref[to, :] = jnp.where(odd, odd_rows, even_rows)
            send_ref[to, :] = jnp.where(odd, even_rows, odd_rows)


def moments(width, me, embeddings, mean):
    rows_here, wide = embeddings.shape
    vmem = pl.BlockSpec(memory_space=pltpu.VMEM)
    return pl.pallas_call(
        functools.partial(moments_kernel, width),
        in_specs=[pl.BlockSpec(memory_space=pltpu.SMEM)] + [pl.BlockSpec(memory_space=pl.ANY)] * 2,
        out_specs=[vmem] * 2,
        out_shape=[
            jax.ShapeDtypeStruct((wide // 2, wide), jnp.bfloat16),
            jax.ShapeDtypeStruct((wide // 2, wide), jnp.bfloat16),
        ],
        scratch_shapes=[
            pltpu.VMEM((rows_here, wide), jnp.bfloat16),
            pltpu.VMEM((1, wide), jnp.float32),
            pltpu.VMEM((wide, wide), jnp.bfloat16),
            pltpu.SemaphoreType.DMA((rows_here // CHUNK,)),
            pltpu.SemaphoreType.DMA,
        ],
        compiler_params=pltpu.CompilerParams(vmem_limit_bytes=VMEM_MOST),
        cost_estimate=pl.CostEstimate(
            flops=2 * rows_here * wide * wide, bytes_accessed=2 * rows_here * wide + 3 * wide * wide, transcendentals=0
        ),
        name="moments",
    )(me.reshape(1), mean, embeddings)


def add_kernel(shares, pieces, keep_ref, *refs):
    outs = refs[len(refs) - shares * pieces:]
    came = refs[:len(refs) - shares * pieces]
    rows, columns = outs[0].shape
    for h in range(shares):
        across = slice(h * columns, (h + 1) * columns)
        for p in range(pieces):
            at = slice(p * rows, (p + 1) * rows)
            held = keep_ref[at, across].astype(jnp.float32)
            for ref in came:
                held = held + ref[at, across].astype(jnp.float32)
            out = outs[h * pieces + p]
            out[...] = held.astype(out.dtype)


def add_and_split(keep, came, shares, pieces):
    rows, columns = keep.shape
    vmem = pl.BlockSpec(memory_space=pltpu.VMEM)
    shape = (rows // pieces, columns // shares)
    kinds = [jnp.float32] + [jnp.bfloat16] * (pieces - 1)
    outs = pl.pallas_call(
        functools.partial(add_kernel, shares, pieces),
        in_specs=[vmem] * (1 + len(came)),
        out_specs=[vmem] * (shares * pieces),
        out_shape=[jax.ShapeDtypeStruct(shape, kind) for kind in kinds * shares],
        compiler_params=pltpu.CompilerParams(vmem_limit_bytes=VMEM_SOME),
        cost_estimate=pl.CostEstimate(flops=2 * rows * columns, bytes_accessed=10 * rows * columns, transcendentals=0),
        name="add_and_split",
    )(keep, *came)
    return [outs[h * pieces:(h + 1) * pieces] for h in range(shares)]


def finish_kernel(total, between_ref, *refs):
    out_ref = refs[-1]
    each = (len(refs) - 1) // SHARES
    columns = out_ref.shape[1] // SHARES
    for h in range(SHARES):
        across = slice(h * columns, (h + 1) * columns)
        held = refs[h * each][...]
        for ref in refs[h * each + 1:(h + 1) * each]:
            held = held + ref[...].astype(jnp.float32)
        out_ref[:, across] = (held + between_ref[:, across]) / total


def finish(total, between, keeps, came):
    parts = [part for keep, pieces in zip(keeps, came) for part in (keep, *pieces)]
    vmem = pl.BlockSpec(memory_space=pltpu.VMEM)
    return pl.pallas_call(
        functools.partial(finish_kernel, total),
        in_specs=[vmem] * (1 + len(parts)),
        out_specs=vmem,
        out_shape=jax.ShapeDtypeStruct(between.shape, jnp.float32),
        compiler_params=pltpu.CompilerParams(vmem_limit_bytes=VMEM_SOME),
        cost_estimate=pl.CostEstimate(flops=8 * between.size, bytes_accessed=16 * between.size, transcendentals=0),
        name="finish",
    )(between, *parts)


def halving_stages(width):
    strides = [1 << k for k in range(width.bit_length() - 1)]
    return [[s] for s in strides[:-2]] + [strides[-2:]]


def exchange(width, stage, out):
    came = []
    for p in range(1, 1 << len(stage)):
        apart = sum(s for k, s in enumerate(stage) if (p >> (len(stage) - 1 - k)) & 1)
        came.append(lax.ppermute(out[p - 1], "wide", [(i, i ^ apart) for i in range(width)]))
    return came


def encode_kernel(total, me_ref, near_ref, far_ref, basis_ref, centroid_ref, rotation_ref, *refs):
    out_hbm, between_ref, out_ref, delta_ref, list_ref, apart_ref, sem = refs[-7:]
    width = delta_ref.shape[0]
    feats = out_ref.shape[1]
    owned = centroid_ref.shape[0]
    wide = basis_ref.shape[0]
    block = wide // width
    share = total // width

    notes = jnp.concatenate(
        [ref[s * SPAN + CAP:(s + 1) * SPAN, :] for ref in (near_ref, far_ref) for s in range(width // 2)], 0
    )
    size = width * NOTES
    to = lax.broadcasted_iota(jnp.int32, (size, size), 0)
    of = lax.broadcasted_iota(jnp.int32, (size, size), 1)
    turn = jnp.where((to % width) * NOTES + to // width == of, 1.0, 0.0).astype(jnp.bfloat16)
    turned = jnp.dot(turn, notes, preferred_element_type=jnp.float32)
    row = [turned[r * width:(r + 1) * width] for r in range(NOTES)]
    digits = row[NOTES - 1]
    list_ref[...] = digits[:, :CAP] * 32.0 + digits[:, CAP:] - 1.0
    quarters = wide // feats
    shifts = jnp.zeros((width, feats), jnp.float32)
    for q in range(quarters):
        parts = [row[p * quarters + q] for p in range(3)]
        mean = parts[0] + (parts[1] + parts[2])
        apart_ref[:, q * feats:(q + 1) * feats] = mean - jnp.mean(mean, 0, keepdims=True)
        terms = jnp.dot(
            jnp.concatenate(parts, 0).astype(jnp.bfloat16),
            basis_ref[q * feats:(q + 1) * feats, :],
            preferred_element_type=jnp.float32,
        )
        shifts = shifts + (terms[:width] + (terms[width:2 * width] + terms[2 * width:]))
    square = row[3 * quarters] + (row[3 * quarters + 1] + row[3 * quarters + 2])
    delta = shifts - jnp.mean(shifts, 0, keepdims=True)
    variance = jnp.sum(square + share * (delta * delta), 0, keepdims=True) / total
    scale = lax.rsqrt(variance + 1e-05)
    delta_ref[...] = delta

    names = lax.broadcasted_iota(jnp.int32, (CAP, owned), 1).astype(jnp.int16)

    half = me_ref[0] // (width // 2)
    each = width // GROUP // 2

    def encode_group(apart, q):
        start = (apart * each + q) * GROUP
        columns = jnp.transpose(list_ref[pl.ds(start, GROUP), :])
        hits, projected, held = [], [], []
        for s in range(GROUP):
            listed = jnp.broadcast_to(columns[:, s:s + 1], (CAP, LANES))
            held.append(jnp.concatenate([listed] * (feats // LANES), 1) >= 0)
            wanted = jnp.concatenate([listed.astype(jnp.int32).astype(jnp.int16)] * (owned // LANES), 1)
            hits.append(jnp.where(wanted == names, jnp.ones((), jnp.bfloat16), jnp.zeros((), jnp.bfloat16)))
            base = pl.multiple_of((q * GROUP + s) * SPAN, 16)
            rows = (near_ref, far_ref)[apart][pl.ds(base, CAP), :].astype(jnp.float32)
            projected.append((rows + delta_ref[pl.ds(start + s, 1), :]) * scale)
        centre = jnp.dot(jnp.concatenate(hits, 0), centroid_ref[...], preferred_element_type=jnp.float32)
        residual = jnp.where(jnp.concatenate(held, 0), jnp.concatenate(projected, 0) - centre, 0.0)
        here = pl.ds(pl.multiple_of(start * CAP, GROUP * CAP), GROUP * CAP)
        there = pl.ds(pl.multiple_of(((half ^ apart) * each + q) * (GROUP * CAP), GROUP * CAP), GROUP * CAP)
        out_ref[here, :] = jnp.dot(
            residual.astype(jnp.bfloat16), rotation_ref[...], preferred_element_type=jnp.float32
        ).astype(jnp.bfloat16)
        return pltpu.make_async_copy(out_ref.at[here], out_hbm.at[there], sem.at[apart * each + q])

    copies = []
    for apart in (0, 1):
        if each <= 2:
            for q in range(each):
                copies.append(encode_group(apart, q))
                copies[-1].start()
        else:

            @pl.loop(0, each)
            def _(q):
                copy = encode_group(apart, q)
                copy.start()
                copy.wait()

    first = me_ref[0] * block
    near = apart_ref[:, pl.ds(pl.multiple_of(first // LANES * LANES, LANES), LANES)]
    near = pltpu.roll(near, (LANES - first % LANES) % LANES, 1)[:, :block]
    between_ref[...] = share * lax.dot_general(
        near,
        apart_ref[...],
        (((0,), (0,)), ((), ())),
        precision=lax.Precision.HIGHEST,
        preferred_element_type=jnp.float32,
    )
    for copy in copies:
        copy.wait()


def encode(width, total, me, near, far, basis, centroids, rotation, after):
    wide, feats = basis.shape
    owned = centroids.shape[0]
    slots = width * CAP
    vmem, anywhere = pl.BlockSpec(memory_space=pltpu.VMEM), pl.BlockSpec(memory_space=pl.ANY)
    return pl.pallas_call(
        functools.partial(encode_kernel, total),
        in_specs=[pl.BlockSpec(memory_space=pltpu.SMEM)] + [vmem] * 5 + [anywhere] * len(after),
        out_specs=[anywhere, vmem],
        out_shape=[
            jax.ShapeDtypeStruct((slots, feats), jnp.bfloat16),
            jax.ShapeDtypeStruct((wide // width, wide), jnp.float32),
        ],
        scratch_shapes=[
            pltpu.VMEM((slots, feats), jnp.bfloat16),
            pltpu.VMEM((width, feats), jnp.float32),
            pltpu.VMEM((width, CAP), jnp.float32),
            pltpu.VMEM((width, wide), jnp.float32),
            pltpu.SemaphoreType.DMA((width // GROUP,)),
        ],
        compiler_params=pltpu.CompilerParams(vmem_limit_bytes=VMEM_SOME),
        cost_estimate=pl.CostEstimate(
            flops=2 * slots * feats * (owned + feats), bytes_accessed=4 * slots * feats, transcendentals=0
        ),
        name="encode",
    )(me.reshape(1), near, far, basis, centroids, rotation, *after)


def local(embeddings, basis, list_owner, list_slot, centroids, rotation):
    width = lax.axis_size("wide")
    me = lax.axis_index("wide")
    rows_here, wide = embeddings.shape
    feats = basis.shape[1]
    total = rows_here * width

    near, far, mean = project_and_sort(width, me, embeddings, basis, list_owner, list_slot)
    half = width // 2
    halves = [list(range(half)), list(range(half, width))]

    def spread(blocks):
        blocks = lax.all_to_all(
            blocks.reshape(half, SPAN, feats), "wide", split_axis=0, concat_axis=0, tiled=True, axis_index_groups=halves
        )
        return blocks.reshape(half * SPAN, feats)

    far = lax.ppermute(far, "wide", [(i, i ^ half) for i in range(width)])
    near = spread(near)
    far = spread(far)
    keep, send = moments(width, me, embeddings, mean)
    stages = halving_stages(width)
    came = exchange(width, stages[0], [send])
    shares = add_and_split(keep, came, SHARES, 1 << len(stages[1]))
    last = []
    for share in shares:
        for n in range(1, len(stages) - 1):
            came = exchange(width, stages[n], share[1:])
            (share,) = add_and_split(share[0], came, 1, 1 << len(stages[n + 1]))
        last.append(share)
    came = [exchange(width, stages[-1], share[1:]) for share in last]
    encoded, between = encode(
        width, total, me, near, far, basis, centroids, rotation, [share[1] for share in last]
    )
    covariance = finish(total, between, [share[0] for share in last], came)
    return (encoded, covariance)


def solution(mesh):
    in_specs = (
        P(("groups", "wide"), None),
        P(),
        P(("groups", "wide")),
        P(("groups", "wide")),
        P("wide", None),
        P(),
    )
    out_specs = (P(("groups", "wide"), None), P(("groups", "wide"), None))
    return jax.shard_map(local, mesh=mesh, in_specs=in_specs, out_specs=out_specs, check_vma=False)
```

```python
import functools

import jax
import jax.numpy as jnp
from jax import lax
from jax.experimental import pallas as pl
from jax.experimental.pallas import tpu as pltpu
from jax.sharding import PartitionSpec as P

CAP = 128
LANES = 128
NOTES = 16
SPAN = CAP + NOTES
CHUNK = 512
TILE = 256
GROUP = 4
SHARES = 2
VMEM_ALL = 60 * 1024 * 1024
VMEM_SOME = 24 * 1024 * 1024
VMEM_MOST = 48 * 1024 * 1024


def in_three(x):
    high = x.astype(jnp.bfloat16).astype(jnp.float32)
    rest = x - high
    middle = rest.astype(jnp.bfloat16).astype(jnp.float32)
    return high, middle, (rest - middle).astype(jnp.bfloat16).astype(jnp.float32)


def sort_half(half, yb_ref, target_ref, list_ref, notes_ref, rows_ref, rows_hbm, sem):
    chunks = target_ref.shape[0]
    groups = rows_ref.shape[0] // (GROUP * SPAN)
    place = lax.broadcasted_iota(jnp.int32, (GROUP * CAP, LANES), 0).astype(jnp.int16)

    def sort_group(g):
        first = (half * groups + g) * GROUP
        pieces = []
        for c in range(chunks):
            wanted = target_ref[c:c + 1, :] - first * CAP
            wanted = jnp.broadcast_to(wanted, (16, LANES)).astype(jnp.int16)
            wanted = jnp.concatenate([wanted] * (GROUP * CAP // 16), 0)
            pieces.append(jnp.where(wanted == place, jnp.ones((), jnp.bfloat16), jnp.zeros((), jnp.bfloat16)))
        pick = jnp.concatenate(pieces, 1)
        rows = jnp.dot(pick, yb_ref[...], preferred_element_type=jnp.float32).astype(jnp.bfloat16)
        for j in range(GROUP):
            base = pl.multiple_of((g * GROUP + j) * SPAN, 16)
            rows_ref[pl.ds(base, CAP), :] = rows[j * CAP:(j + 1) * CAP]
            notes = jnp.concatenate([notes_ref[:NOTES - 1, :], list_ref[pl.ds(first + j, 1), :]], 0)
            rows_ref[pl.ds(pl.multiple_of(base + CAP, 16), NOTES), :] = notes.astype(jnp.bfloat16)
        at = pl.ds(pl.multiple_of(g * (GROUP * SPAN), 16), GROUP * SPAN)
        return pltpu.make_async_copy(rows_ref.at[at], rows_hbm.at[at], sem.at[g])

    if groups <= 4:
        copies = []
        for g in range(groups):
            copies.append(sort_group(g))
            copies[g].start()
        for copy in copies:
            copy.wait()
    else:

        @pl.loop(0, groups)
        def _(g):
            copy = sort_group(g)
            copy.start()
            copy.wait()


def near_kernel(me_ref, yb_ref, target_ref, list_ref, notes_ref, near_hbm, sorted_ref, rows_ref, sem):
    sorted_ref[...] = jnp.zeros_like(sorted_ref)
    half = me_ref[0] // (list_ref.shape[0] // 2)
    sort_half(half, yb_ref, target_ref, list_ref, notes_ref, rows_ref, near_hbm, sem)


def sort_near(me, yb, targets, lists, notes):
    rows_here, feats = yb.shape
    slots = lists.shape[0] // 2 * SPAN
    vmem, anywhere = pl.BlockSpec(memory_space=pltpu.VMEM), pl.BlockSpec(memory_space=pl.ANY)
    return pl.pallas_call(
        near_kernel,
        in_specs=[pl.BlockSpec(memory_space=pltpu.SMEM)] + [vmem] * 4,
        out_specs=[anywhere, vmem],
        out_shape=[jax.ShapeDtypeStruct((slots, feats), jnp.bfloat16), jax.ShapeDtypeStruct((8, LANES), jnp.float32)],
        scratch_shapes=[pltpu.VMEM((slots, feats), jnp.bfloat16), pltpu.SemaphoreType.DMA((slots // (GROUP * SPAN),))],
        compiler_params=pltpu.CompilerParams(vmem_limit_bytes=VMEM_ALL),
        cost_estimate=pl.CostEstimate(
            flops=2 * rows_here * feats * slots, bytes_accessed=2 * (rows_here + slots) * feats, transcendentals=0
        ),
        name="sort_near",
    )(me.reshape(1), yb, targets, lists, notes)


def tie_kernel(*refs):
    pass


def tie(x, after):
    anywhere = pl.BlockSpec(memory_space=pl.ANY)
    return pl.pallas_call(
        tie_kernel,
        in_specs=[anywhere] * (1 + len(after)),
        out_specs=anywhere,
        out_shape=jax.ShapeDtypeStruct(x.shape, x.dtype),
        input_output_aliases={0: 0},
        name="tie",
    )(x, *after)


def rows_kernel(
    width, me_ref, e_hbm, basis_hbm, owner_hbm, slot_hbm,
    far_hbm, mean_hbm, yb_hbm, target_hbm, list_hbm, notes_hbm,
    owner_ref, slot_ref, mean_ref, basis_ref, e_ref, rows_ref, y_ref, yb_ref, sum_ref, total_ref, target_ref, list_ref, notes_ref, e_sem, small_sem, sem,
):
    step = pl.program_id(0)
    rows_here, feats = y_ref.shape
    wide = e_ref.shape[1]
    chunks = rows_here // LANES

    def e_copy(c):
        at = pl.ds(pl.multiple_of(c * CHUNK, CHUNK), CHUNK)
        return pltpu.make_async_copy(e_hbm.at[at], e_ref.at[at], e_sem.at[c])

    @pl.when(step == 0)
    def _():
        owner_copy = pltpu.make_async_copy(owner_hbm, owner_ref, small_sem.at[0])
        slot_copy = pltpu.make_async_copy(slot_hbm, slot_ref, small_sem.at[1])
        basis_copy = pltpu.make_async_copy(basis_hbm, basis_ref, small_sem.at[2])
        owner_copy.start()
        e_copy(0).start()
        slot_copy.start()
        basis_copy.start()
        for c in range(1, rows_here // CHUNK):
            e_copy(c).start()
        owner_copy.wait()
        sum_ref[...] = jnp.zeros_like(sum_ref)
        total_ref[...] = jnp.zeros_like(total_ref)
        owner = owner_ref[...]
        wanted = lax.broadcasted_iota(jnp.int32, (width, LANES), 0)
        hits = [jnp.where(owner[c:c + 1, :] == wanted, 1.0, 0.0) for c in range(chunks)]
        flat = jnp.concatenate(hits, 0).astype(jnp.bfloat16)
        up = lax.broadcasted_iota(jnp.int32, (LANES, LANES), 0)
        to = lax.broadcasted_iota(jnp.int32, (LANES, LANES), 1)
        before = jnp.where(up < to, 1.0, 0.0).astype(jnp.bfloat16)
        every = jnp.ones((LANES, LANES), jnp.bfloat16)
        within = jnp.dot(flat, before, preferred_element_type=jnp.float32)
        counts = jnp.dot(flat, every, preferred_element_type=jnp.float32)
        carry = jnp.zeros((width, LANES), jnp.float32)
        ranks = []
        for c in range(chunks):
            at = slice(c * width, (c + 1) * width)
            ranks.append(jnp.sum(hits[c] * (within[at] + carry), 0, keepdims=True).astype(jnp.int32))
            carry = carry + counts[at]
            target_ref[c:c + 1, :] = owner[c:c + 1, :] * CAP + ranks[c]

        slot_copy.wait()
        slot = slot_ref[...] + 1
        high, low = (slot >> 5).astype(jnp.float32), (slot & 31).astype(jnp.float32)
        spots = lax.broadcasted_iota(jnp.int32, (CAP, LANES), 0)
        placed = jnp.concatenate([jnp.where(ranks[c] == spots, 1.0, 0.0) for c in range(chunks)], 1).astype(jnp.bfloat16)
        digits = jnp.concatenate(
            [
                jnp.concatenate([hits[c] * high[c:c + 1, :] for c in range(chunks)], 1),
                jnp.concatenate([hits[c] * low[c:c + 1, :] for c in range(chunks)], 1),
            ],
            0,
        ).astype(jnp.bfloat16)
        found = lax.dot_general(digits, placed, (((1,), (1,)), ((), ())), preferred_element_type=jnp.float32)
        list_ref[:, :CAP] = found[:width]
        list_ref[:, CAP:] = found[width:]
        basis_copy.wait()

    e_copy(step).wait()
    here = pl.ds(pl.multiple_of(step * CHUNK, CHUNK), CHUNK)
    rows = e_ref[here, :]
    y = jnp.dot(rows, basis_ref[...], preferred_element_type=jnp.float32)
    y_ref[here, :] = y
    sum_ref[...] += jnp.sum(y.reshape(CHUNK // 8, 8, feats), 0)
    total_ref[...] += jnp.sum(rows.astype(jnp.float32).reshape(CHUNK // 8, 8, wide), 0)

    @pl.when(step == pl.num_programs(0) - 1)
    def _():
        mean_y = jnp.sum(sum_ref[...], 0, keepdims=True) / rows_here
        square = jnp.zeros((8, feats), jnp.float32)
        for c in range(rows_here // CHUNK):
            at = slice(c * CHUNK, (c + 1) * CHUNK)
            centred = y_ref[at, :] - mean_y
            square = square + jnp.sum((centred * centred).reshape(CHUNK // 8, 8, feats), 0)
            yb_ref[at, :] = centred.astype(jnp.bfloat16)
        mean = jnp.sum(total_ref[...], 0, keepdims=True) / rows_here
        mean_ref[...] = mean
        mean_copy = pltpu.make_async_copy(mean_ref, mean_hbm, small_sem.at[3])
        mean_copy.start()
        parts = in_three(mean)
        common = [part[:, q * feats:(q + 1) * feats] for part in parts for q in range(wide // feats)]
        common = common + list(in_three(jnp.sum(square, 0, keepdims=True)))
        notes_ref[:NOTES - 1, :] = jnp.concatenate(common, 0)
        notes_ref[NOTES - 1:, :] = jnp.zeros((1, feats), jnp.float32)
        copies = [mean_copy]
        for n, (ref, hbm) in enumerate(
            ((yb_ref, yb_hbm), (target_ref, target_hbm), (list_ref, list_hbm), (notes_ref, notes_hbm))
        ):
            copies.append(pltpu.make_async_copy(ref, hbm, small_sem.at[4 + n]))
            copies[-1].start()
        other = 1 - me_ref[0] // (width // 2)
        sort_half(other, yb_ref, target_ref, list_ref, notes_ref, rows_ref, far_hbm, sem)
        for copy in copies:
            copy.wait()


def project_and_sort_far(width, me, embeddings, basis, list_owner, list_slot):
    rows_here, wide = embeddings.shape
    feats = basis.shape[1]
    lanes = rows_here // LANES
    slots = width * SPAN
    return pl.pallas_call(
        functools.partial(rows_kernel, width),
        grid=(rows_here // CHUNK,),
        in_specs=[pl.BlockSpec(memory_space=pltpu.SMEM)] + [pl.BlockSpec(memory_space=pl.ANY)] * 4,
        out_specs=[pl.BlockSpec(memory_space=pl.ANY)] * 6,
        out_shape=[
            jax.ShapeDtypeStruct((slots // 2, feats), jnp.bfloat16),
            jax.ShapeDtypeStruct((1, wide), jnp.float32),
            jax.ShapeDtypeStruct((rows_here, feats), jnp.bfloat16),
            jax.ShapeDtypeStruct((lanes, LANES), jnp.int32),
            jax.ShapeDtypeStruct((width, 2 * CAP), jnp.float32),
            jax.ShapeDtypeStruct((NOTES, feats), jnp.float32),
        ],
        scratch_shapes=[
            pltpu.VMEM((lanes, LANES), jnp.int32),
            pltpu.VMEM((lanes, LANES), jnp.int32),
            pltpu.VMEM((1, wide), jnp.float32),
            pltpu.VMEM((wide, feats), jnp.bfloat16),
            pltpu.VMEM((rows_here, wide), jnp.bfloat16),
            pltpu.VMEM((slots // 2, feats), jnp.bfloat16),
            pltpu.VMEM((rows_here, feats), jnp.float32),
            pltpu.VMEM((rows_here, feats), jnp.bfloat16),
            pltpu.VMEM((8, feats), jnp.float32),
            pltpu.VMEM((8, wide), jnp.float32),
            pltpu.VMEM((lanes, LANES), jnp.int32),
            pltpu.VMEM((width, 2 * CAP), jnp.float32),
            pltpu.VMEM((NOTES, feats), jnp.float32),
            pltpu.SemaphoreType.DMA((rows_here // CHUNK,)),
            pltpu.SemaphoreType.DMA((8,)),
            pltpu.SemaphoreType.DMA((width // GROUP // 2,)),
        ],
        compiler_params=pltpu.CompilerParams(vmem_limit_bytes=VMEM_ALL),
        cost_estimate=pl.CostEstimate(
            flops=2 * rows_here * feats * (wide + slots), bytes_accessed=2 * rows_here * wide + 2 * slots * feats, transcendentals=0
        ),
        name="project_sort",
    )(me.reshape(1), embeddings, basis, list_owner.reshape(lanes, LANES), list_slot.reshape(lanes, LANES))


def moments_kernel(width, me_ref, mean_hbm, e_hbm, after_hbm, keep_ref, send_ref, e_ref, mean_ref, m_ref, sem, mean_sem):
    rows_here, wide = e_ref.shape
    block = wide // width
    bits = width.bit_length() - 1
    tiles = wide // TILE
    mean_copy = pltpu.make_async_copy(mean_hbm, mean_ref, mean_sem)
    mean_copy.start()
    copies = []
    for c in range(rows_here // CHUNK):
        at = pl.ds(c * CHUNK, CHUNK)
        copies.append(pltpu.make_async_copy(e_hbm.at[at], e_ref.at[at], sem.at[c]))
        copies[c].start()
    me = me_ref[0]
    odd = (me & 1) == 1
    mean_copy.wait()
    mean = mean_ref[...]
    for t in range(tiles):
        rows, columns = slice(t * TILE, (t + 1) * TILE), slice(t * TILE, wide)
        if t == 0:
            product = jnp.zeros((TILE, wide), jnp.float32)
            for c in range(rows_here // CHUNK):
                copies[c].wait()
                at = slice(c * CHUNK, (c + 1) * CHUNK)
                product = product + lax.dot_general(
                    e_ref[at, rows], e_ref[at, :], (((0,), (0,)), ((), ())), preferred_element_type=jnp.float32
                )
        else:
            product = lax.dot_general(
                e_ref[:, rows], e_ref[:, columns], (((0,), (0,)), ((), ())), preferred_element_type=jnp.float32
            )
        down = jnp.transpose(jnp.broadcast_to(mean[:, rows] * rows_here, (LANES, TILE)))
        for u in range(t, tiles):
            pieces = []
            for j in range(u * TILE // LANES, (u + 1) * TILE // LANES):
                across = slice(j * LANES, (j + 1) * LANES)
                within = slice(j * LANES - t * TILE, (j + 1) * LANES - t * TILE)
                pieces.append((product[:, within] - down * mean[:, across]).astype(jnp.bfloat16))
            piece = jnp.concatenate(pieces, 1)
            other = slice(u * TILE, (u + 1) * TILE)
            m_ref[rows, other] = piece
            if u > t:
                m_ref[other, rows] = jnp.transpose(piece)
        for pair in range(TILE // block // 2):
            first = t * (TILE // block) + 2 * pair
            apart = (first ^ me) >> 1
            place = 0
            for k in range(bits - 1):
                place = place + (((apart >> k) & 1) << (bits - 2 - k))
            to = pl.ds(pl.multiple_of(place * block, block), block)
            even_rows = m_ref[first * block:(first + 1) * block, :]
            odd_rows = m_ref[(first + 1) * block:(first + 2) * block, :]
            keep_ref[to, :] = jnp.where(odd, odd_rows, even_rows)
            send_ref[to, :] = jnp.where(odd, even_rows, odd_rows)


def moments(width, me, embeddings, mean, after):
    rows_here, wide = embeddings.shape
    vmem = pl.BlockSpec(memory_space=pltpu.VMEM)
    return pl.pallas_call(
        functools.partial(moments_kernel, width),
        in_specs=[pl.BlockSpec(memory_space=pltpu.SMEM)] + [pl.BlockSpec(memory_space=pl.ANY)] * 3,
        out_specs=[vmem] * 2,
        out_shape=[
            jax.ShapeDtypeStruct((wide // 2, wide), jnp.bfloat16),
            jax.ShapeDtypeStruct((wide // 2, wide), jnp.bfloat16),
        ],
        scratch_shapes=[
            pltpu.VMEM((rows_here, wide), jnp.bfloat16),
            pltpu.VMEM((1, wide), jnp.float32),
            pltpu.VMEM((wide, wide), jnp.bfloat16),
            pltpu.SemaphoreType.DMA((rows_here // CHUNK,)),
            pltpu.SemaphoreType.DMA,
        ],
        compiler_params=pltpu.CompilerParams(vmem_limit_bytes=VMEM_MOST),
        cost_estimate=pl.CostEstimate(
            flops=2 * rows_here * wide * wide, bytes_accessed=2 * rows_here * wide + 3 * wide * wide, transcendentals=0
        ),
        name="moments",
    )(me.reshape(1), mean, embeddings, after)


def add_kernel(shares, pieces, arrived, keep_ref, *refs):
    outs = refs[len(refs) - shares * pieces:]
    came = refs[:arrived]
    rows, columns = outs[0].shape
    for h in range(shares):
        across = slice(h * columns, (h + 1) * columns)
        for p in range(pieces):
            at = slice(p * rows, (p + 1) * rows)
            held = keep_ref[at, across].astype(jnp.float32)
            for ref in came:
                held = held + ref[at, across].astype(jnp.float32)
            out = outs[h * pieces + p]
            out[...] = held.astype(out.dtype)


def add_and_split(keep, came, shares, pieces, after=()):
    rows, columns = keep.shape
    vmem = pl.BlockSpec(memory_space=pltpu.VMEM)
    shape = (rows // pieces, columns // shares)
    kinds = [jnp.float32] + [jnp.bfloat16] * (pieces - 1)
    outs = pl.pallas_call(
        functools.partial(add_kernel, shares, pieces, len(came)),
        in_specs=[vmem] * (1 + len(came)) + [pl.BlockSpec(memory_space=pl.ANY)] * len(after),
        out_specs=[vmem] * (shares * pieces),
        out_shape=[jax.ShapeDtypeStruct(shape, kind) for kind in kinds * shares],
        compiler_params=pltpu.CompilerParams(vmem_limit_bytes=VMEM_SOME),
        cost_estimate=pl.CostEstimate(flops=2 * rows * columns, bytes_accessed=10 * rows * columns, transcendentals=0),
        name="add_and_split",
    )(keep, *came, *after)
    return [outs[h * pieces:(h + 1) * pieces] for h in range(shares)]


def finish_kernel(total, between_ref, *refs):
    out_ref = refs[-1]
    each = (len(refs) - 1) // SHARES
    columns = out_ref.shape[1] // SHARES
    for h in range(SHARES):
        across = slice(h * columns, (h + 1) * columns)
        held = refs[h * each][...]
        for ref in refs[h * each + 1:(h + 1) * each]:
            held = held + ref[...].astype(jnp.float32)
        out_ref[:, across] = (held + between_ref[:, across]) / total


def finish(total, between, keeps, came):
    parts = [part for keep, pieces in zip(keeps, came) for part in (keep, *pieces)]
    vmem = pl.BlockSpec(memory_space=pltpu.VMEM)
    return pl.pallas_call(
        functools.partial(finish_kernel, total),
        in_specs=[vmem] * (1 + len(parts)),
        out_specs=vmem,
        out_shape=jax.ShapeDtypeStruct(between.shape, jnp.float32),
        compiler_params=pltpu.CompilerParams(vmem_limit_bytes=VMEM_SOME),
        cost_estimate=pl.CostEstimate(flops=8 * between.size, bytes_accessed=16 * between.size, transcendentals=0),
        name="finish",
    )(between, *parts)


def halving_stages(width):
    strides = [1 << k for k in range(width.bit_length() - 1)]
    return [[s] for s in strides[:-2]] + [strides[-2:]]


def exchange(width, stage, out):
    came = []
    for p in range(1, 1 << len(stage)):
        apart = sum(s for k, s in enumerate(stage) if (p >> (len(stage) - 1 - k)) & 1)
        came.append(lax.ppermute(out[p - 1], "wide", [(i, i ^ apart) for i in range(width)]))
    return came


def encode_kernel(total, me_ref, near_ref, far_ref, basis_ref, centroid_ref, rotation_ref, *refs):
    out_hbm, between_ref, out_ref, delta_ref, list_ref, apart_ref, sem = refs[-7:]
    width = delta_ref.shape[0]
    feats = out_ref.shape[1]
    owned = centroid_ref.shape[0]
    wide = basis_ref.shape[0]
    block = wide // width
    share = total // width

    notes = jnp.concatenate(
        [ref[s * SPAN + CAP:(s + 1) * SPAN, :] for ref in (near_ref, far_ref) for s in range(width // 2)], 0
    )
    size = width * NOTES
    to = lax.broadcasted_iota(jnp.int32, (size, size), 0)
    of = lax.broadcasted_iota(jnp.int32, (size, size), 1)
    turn = jnp.where((to % width) * NOTES + to // width == of, 1.0, 0.0).astype(jnp.bfloat16)
    turned = jnp.dot(turn, notes, preferred_element_type=jnp.float32)
    row = [turned[r * width:(r + 1) * width] for r in range(NOTES)]
    digits = row[NOTES - 1]
    list_ref[...] = digits[:, :CAP] * 32.0 + digits[:, CAP:] - 1.0
    quarters = wide // feats
    shifts = jnp.zeros((width, feats), jnp.float32)
    for q in range(quarters):
        parts = [row[p * quarters + q] for p in range(3)]
        mean = parts[0] + (parts[1] + parts[2])
        apart_ref[:, q * feats:(q + 1) * feats] = mean - jnp.mean(mean, 0, keepdims=True)
        terms = jnp.dot(
            jnp.concatenate(parts, 0).astype(jnp.bfloat16),
            basis_ref[q * feats:(q + 1) * feats, :],
            preferred_element_type=jnp.float32,
        )
        shifts = shifts + (terms[:width] + (terms[width:2 * width] + terms[2 * width:]))
    square = row[3 * quarters] + (row[3 * quarters + 1] + row[3 * quarters + 2])
    delta = shifts - jnp.mean(shifts, 0, keepdims=True)
    variance = jnp.sum(square + share * (delta * delta), 0, keepdims=True) / total
    scale = lax.rsqrt(variance + 1e-05)
    delta_ref[...] = delta

    names = lax.broadcasted_iota(jnp.int32, (CAP, owned), 1).astype(jnp.int16)

    half = me_ref[0] // (width // 2)
    each = width // GROUP // 2

    def encode_group(apart, q):
        start = (apart * each + q) * GROUP
        columns = jnp.transpose(list_ref[pl.ds(start, GROUP), :])
        hits, projected, held = [], [], []
        for s in range(GROUP):
            listed = jnp.broadcast_to(columns[:, s:s + 1], (CAP, LANES))
            held.append(jnp.concatenate([listed] * (feats // LANES), 1) >= 0)
            wanted = jnp.concatenate([listed.astype(jnp.int32).astype(jnp.int16)] * (owned // LANES), 1)
            hits.append(jnp.where(wanted == names, jnp.ones((), jnp.bfloat16), jnp.zeros((), jnp.bfloat16)))
            base = pl.multiple_of((q * GROUP + s) * SPAN, 16)
            rows = (near_ref, far_ref)[apart][pl.ds(base, CAP), :].astype(jnp.float32)
            projected.append((rows + delta_ref[pl.ds(start + s, 1), :]) * scale)
        centre = jnp.dot(jnp.concatenate(hits, 0), centroid_ref[...], preferred_element_type=jnp.float32)
        residual = jnp.where(jnp.concatenate(held, 0), jnp.concatenate(projected, 0) - centre, 0.0)
        here = pl.ds(pl.multiple_of(start * CAP, GROUP * CAP), GROUP * CAP)
        there = pl.ds(pl.multiple_of(((half ^ apart) * each + q) * (GROUP * CAP), GROUP * CAP), GROUP * CAP)
        out_ref[here, :] = jnp.dot(
            residual.astype(jnp.bfloat16), rotation_ref[...], preferred_element_type=jnp.float32
        ).astype(jnp.bfloat16)
        return pltpu.make_async_copy(out_ref.at[here], out_hbm.at[there], sem.at[apart * each + q])

    copies = []
    for apart in (0, 1):
        if each <= 2:
            for q in range(each):
                copies.append(encode_group(apart, q))
                copies[-1].start()
        else:

            @pl.loop(0, each)
            def _(q):
                copy = encode_group(apart, q)
                copy.start()
                copy.wait()

    first = me_ref[0] * block
    near = apart_ref[:, pl.ds(pl.multiple_of(first // LANES * LANES, LANES), LANES)]
    near = pltpu.roll(near, (LANES - first % LANES) % LANES, 1)[:, :block]
    between_ref[...] = share * lax.dot_general(
        near,
        apart_ref[...],
        (((0,), (0,)), ((), ())),
        precision=lax.Precision.HIGHEST,
        preferred_element_type=jnp.float32,
    )
    for copy in copies:
        copy.wait()


def encode(width, total, me, near, far, basis, centroids, rotation, after):
    wide, feats = basis.shape
    owned = centroids.shape[0]
    slots = width * CAP
    vmem, anywhere = pl.BlockSpec(memory_space=pltpu.VMEM), pl.BlockSpec(memory_space=pl.ANY)
    return pl.pallas_call(
        functools.partial(encode_kernel, total),
        in_specs=[pl.BlockSpec(memory_space=pltpu.SMEM)] + [vmem] * 5 + [anywhere] * len(after),
        out_specs=[anywhere, vmem],
        out_shape=[
            jax.ShapeDtypeStruct((slots, feats), jnp.bfloat16),
            jax.ShapeDtypeStruct((wide // width, wide), jnp.float32),
        ],
        scratch_shapes=[
            pltpu.VMEM((slots, feats), jnp.bfloat16),
            pltpu.VMEM((width, feats), jnp.float32),
            pltpu.VMEM((width, CAP), jnp.float32),
            pltpu.VMEM((width, wide), jnp.float32),
            pltpu.SemaphoreType.DMA((width // GROUP,)),
        ],
        compiler_params=pltpu.CompilerParams(vmem_limit_bytes=VMEM_SOME),
        cost_estimate=pl.CostEstimate(
            flops=2 * slots * feats * (owned + feats), bytes_accessed=4 * slots * feats, transcendentals=0
        ),
        name="encode",
    )(me.reshape(1), near, far, basis, centroids, rotation, *after)


def local(embeddings, basis, list_owner, list_slot, centroids, rotation):
    width = lax.axis_size("wide")
    me = lax.axis_index("wide")
    rows_here, wide = embeddings.shape
    feats = basis.shape[1]
    total = rows_here * width

    far, mean, *rest = project_and_sort_far(width, me, embeddings, basis, list_owner, list_slot)
    half = width // 2
    halves = [list(range(half)), list(range(half, width))]

    def spread(blocks):
        blocks = lax.all_to_all(
            blocks.reshape(half, SPAN, feats), "wide", split_axis=0, concat_axis=0, tiled=True, axis_index_groups=halves
        )
        return blocks.reshape(half * SPAN, feats)

    far = lax.ppermute(far, "wide", [(i, i ^ half) for i in range(width)])
    near, near_sorted = sort_near(me, *rest)
    near = spread(near)
    keep, send = moments(width, me, embeddings, mean, near_sorted)
    stages = halving_stages(width)
    came = exchange(width, stages[0], [send])
    shares = add_and_split(keep, came, SHARES, 1 << len(stages[1]))
    last, after = [], []
    for share in shares:
        for n in range(1, len(stages) - 1):
            came = exchange(width, stages[n], share[1:])
            (share,) = add_and_split(share[0], came, 1, 1 << len(stages[n + 1]), after)
        last.append(share)
        if not after:
            far = tie(far, [share[1]])
            after = [far]
    far = spread(far)
    came = [exchange(width, stages[-1], share[1:]) for share in last]
    encoded, between = encode(
        width, total, me, near, far, basis, centroids, rotation, [share[1] for share in last]
    )
    covariance = finish(total, between, [share[0] for share in last], came)
    return (encoded, covariance)


def solution(mesh):
    in_specs = (
        P(("groups", "wide"), None),
        P(),
        P(("groups", "wide")),
        P(("groups", "wide")),
        P("wide", None),
        P(),
    )
    out_specs = (P(("groups", "wide"), None), P(("groups", "wide"), None))
    return jax.shard_map(local, mesh=mesh, in_specs=in_specs, out_specs=out_specs, check_vma=False)
```

```python
import functools

import jax
import jax.numpy as jnp
from jax import lax
from jax.experimental import pallas as pl
from jax.experimental.pallas import tpu as pltpu
from jax.sharding import PartitionSpec as P

CAP = 128
LANES = 128
NOTES = 16
SPAN = CAP + NOTES
CHUNK = 512
TILE = 256
GROUP = 4
SHARES = 2
NO_COST = pl.CostEstimate(flops=0, bytes_accessed=0, transcendentals=0)
VMEM_ALL = 61840 * 1024
VMEM_SOME = 24 * 1024 * 1024
VMEM_MOST = 48 * 1024 * 1024


def in_three(x):
    high = x.astype(jnp.bfloat16).astype(jnp.float32)
    rest = x - high
    middle = rest.astype(jnp.bfloat16).astype(jnp.float32)
    return high, middle, (rest - middle).astype(jnp.bfloat16).astype(jnp.float32)


def sort_half(half, yb_ref, target_ref, list_ref, notes_ref, rows_ref, rows_hbm, sem):
    chunks = target_ref.shape[0]
    groups = rows_ref.shape[0] // (GROUP * SPAN)
    place = lax.broadcasted_iota(jnp.int32, (GROUP * CAP, LANES), 0).astype(jnp.int16)

    def sort_group(g):
        first = (half * groups + g) * GROUP
        pieces = []
        for c in range(chunks):
            wanted = target_ref[c:c + 1, :] - first * CAP
            wanted = jnp.broadcast_to(wanted, (16, LANES)).astype(jnp.int16)
            wanted = jnp.concatenate([wanted] * (GROUP * CAP // 16), 0)
            pieces.append(jnp.where(wanted == place, jnp.ones((), jnp.bfloat16), jnp.zeros((), jnp.bfloat16)))
        pick = jnp.concatenate(pieces, 1)
        rows = jnp.dot(pick, yb_ref[...], preferred_element_type=jnp.float32).astype(jnp.bfloat16)
        for j in range(GROUP):
            base = pl.multiple_of((g * GROUP + j) * SPAN, 16)
            rows_ref[pl.ds(base, CAP), :] = rows[j * CAP:(j + 1) * CAP]
            notes = jnp.concatenate([notes_ref[:NOTES - 1, :], list_ref[pl.ds(first + j, 1), :]], 0)
            rows_ref[pl.ds(pl.multiple_of(base + CAP, 16), NOTES), :] = notes.astype(jnp.bfloat16)
        at = pl.ds(pl.multiple_of(g * (GROUP * SPAN), 16), GROUP * SPAN)
        return pltpu.make_async_copy(rows_ref.at[at], rows_hbm.at[at], sem.at[g])

    if groups <= 4:
        copies = []
        for g in range(groups):
            copies.append(sort_group(g))
            copies[g].start()
        for copy in copies:
            copy.wait()
    else:

        @pl.loop(0, groups)
        def _(g):
            copy = sort_group(g)
            copy.start()
            copy.wait()


def near_kernel(me_ref, yb_ref, target_ref, list_ref, notes_ref, near_hbm, sorted_ref, rows_ref, sem):
    sorted_ref[...] = jnp.zeros_like(sorted_ref)
    half = me_ref[0] // (list_ref.shape[0] // 2)
    sort_half(half, yb_ref, target_ref, list_ref, notes_ref, rows_ref, near_hbm, sem)


def sort_near(me, yb, targets, lists, notes):
    rows_here, feats = yb.shape
    slots = lists.shape[0] // 2 * SPAN
    vmem, anywhere = pl.BlockSpec(memory_space=pltpu.VMEM), pl.BlockSpec(memory_space=pl.ANY)
    return pl.pallas_call(
        near_kernel,
        in_specs=[pl.BlockSpec(memory_space=pltpu.SMEM)] + [vmem] * 4,
        out_specs=[anywhere, vmem],
        out_shape=[jax.ShapeDtypeStruct((slots, feats), jnp.bfloat16), jax.ShapeDtypeStruct((8, LANES), jnp.float32)],
        scratch_shapes=[pltpu.VMEM((slots, feats), jnp.bfloat16), pltpu.SemaphoreType.DMA((slots // (GROUP * SPAN),))],
        compiler_params=pltpu.CompilerParams(vmem_limit_bytes=VMEM_ALL),
        cost_estimate=NO_COST,
        name="sort_near",
    )(me.reshape(1), yb, targets, lists, notes)


def tie_kernel(*refs):
    pass


def tie(x, after):
    anywhere = pl.BlockSpec(memory_space=pl.ANY)
    return pl.pallas_call(
        tie_kernel,
        in_specs=[anywhere] * (1 + len(after)),
        out_specs=anywhere,
        out_shape=jax.ShapeDtypeStruct(x.shape, x.dtype),
        input_output_aliases={0: 0},
        name="tie",
    )(x, *after)


def rows_kernel(
    width, me_ref, e_hbm, basis_hbm, owner_hbm, slot_hbm,
    far_hbm, mean_hbm, yb_hbm, target_hbm, list_hbm, notes_hbm,
    owner_ref, slot_ref, mean_ref, basis_ref, e_ref, rows_ref, y_ref, yb_ref, sum_ref, total_ref, target_ref, list_ref, notes_ref, e_sem, small_sem, sem,
):
    step = pl.program_id(0)
    rows_here, feats = y_ref.shape
    wide = e_ref.shape[1]
    chunks = rows_here // LANES

    def e_copy(c):
        at = pl.ds(pl.multiple_of(c * CHUNK, CHUNK), CHUNK)
        return pltpu.make_async_copy(e_hbm.at[at], e_ref.at[at], e_sem.at[c])

    @pl.when(step == 0)
    def _():
        owner_copy = pltpu.make_async_copy(owner_hbm, owner_ref, small_sem.at[0])
        slot_copy = pltpu.make_async_copy(slot_hbm, slot_ref, small_sem.at[1])
        basis_copy = pltpu.make_async_copy(basis_hbm, basis_ref, small_sem.at[2])
        owner_copy.start()
        e_copy(0).start()
        slot_copy.start()
        basis_copy.start()
        for c in range(1, rows_here // CHUNK):
            e_copy(c).start()
        owner_copy.wait()
        sum_ref[...] = jnp.zeros_like(sum_ref)
        total_ref[...] = jnp.zeros_like(total_ref)
        owner = owner_ref[...]
        wanted = lax.broadcasted_iota(jnp.int32, (width, LANES), 0)
        hits = [jnp.where(owner[c:c + 1, :] == wanted, 1.0, 0.0) for c in range(chunks)]
        flat = jnp.concatenate(hits, 0).astype(jnp.bfloat16)
        up = lax.broadcasted_iota(jnp.int32, (LANES, LANES), 0)
        to = lax.broadcasted_iota(jnp.int32, (LANES, LANES), 1)
        before = jnp.where(up < to, 1.0, 0.0).astype(jnp.bfloat16)
        every = jnp.ones((LANES, LANES), jnp.bfloat16)
        within = jnp.dot(flat, before, preferred_element_type=jnp.float32)
        counts = jnp.dot(flat, every, preferred_element_type=jnp.float32)
        carry = jnp.zeros((width, LANES), jnp.float32)
        ranks = []
        for c in range(chunks):
            at = slice(c * width, (c + 1) * width)
            ranks.append(jnp.sum(hits[c] * (within[at] + carry), 0, keepdims=True).astype(jnp.int32))
            carry = carry + counts[at]
            target_ref[c:c + 1, :] = owner[c:c + 1, :] * CAP + ranks[c]

        slot_copy.wait()
        slot = slot_ref[...] + 1
        high, low = (slot >> 5).astype(jnp.float32), (slot & 31).astype(jnp.float32)
        spots = lax.broadcasted_iota(jnp.int32, (CAP, LANES), 0)
        placed = jnp.concatenate([jnp.where(ranks[c] == spots, 1.0, 0.0) for c in range(chunks)], 1).astype(jnp.bfloat16)
        digits = jnp.concatenate(
            [
                jnp.concatenate([hits[c] * high[c:c + 1, :] for c in range(chunks)], 1),
                jnp.concatenate([hits[c] * low[c:c + 1, :] for c in range(chunks)], 1),
            ],
            0,
        ).astype(jnp.bfloat16)
        found = lax.dot_general(digits, placed, (((1,), (1,)), ((), ())), preferred_element_type=jnp.float32)
        list_ref[:, :CAP] = found[:width]
        list_ref[:, CAP:] = found[width:]
        basis_copy.wait()

    e_copy(step).wait()
    here = pl.ds(pl.multiple_of(step * CHUNK, CHUNK), CHUNK)
    rows = e_ref[here, :]
    y = jnp.dot(rows, basis_ref[...], preferred_element_type=jnp.float32)
    y_ref[here, :] = y
    sum_ref[...] += jnp.sum(y.reshape(CHUNK // 8, 8, feats), 0)
    total_ref[...] += jnp.sum(rows.astype(jnp.float32).reshape(CHUNK // 8, 8, wide), 0)

    @pl.when(step == pl.num_programs(0) - 1)
    def _():
        mean_y = jnp.sum(sum_ref[...], 0, keepdims=True) / rows_here
        square = jnp.zeros((8, feats), jnp.float32)
        for c in range(rows_here // CHUNK):
            at = slice(c * CHUNK, (c + 1) * CHUNK)
            centred = y_ref[at, :] - mean_y
            square = square + jnp.sum((centred * centred).reshape(CHUNK // 8, 8, feats), 0)
            yb_ref[at, :] = centred.astype(jnp.bfloat16)
        mean = jnp.sum(total_ref[...], 0, keepdims=True) / rows_here
        mean_ref[...] = mean
        mean_copy = pltpu.make_async_copy(mean_ref, mean_hbm, small_sem.at[3])
        mean_copy.start()
        parts = in_three(mean)
        common = [part[:, q * feats:(q + 1) * feats] for part in parts for q in range(wide // feats)]
        common = common + list(in_three(jnp.sum(square, 0, keepdims=True)))
        notes_ref[:NOTES - 1, :] = jnp.concatenate(common, 0)
        notes_ref[NOTES - 1:, :] = jnp.zeros((1, feats), jnp.float32)
        copies = [mean_copy]
        for n, (ref, hbm) in enumerate(
            ((yb_ref, yb_hbm), (target_ref, target_hbm), (list_ref, list_hbm), (notes_ref, notes_hbm))
        ):
            copies.append(pltpu.make_async_copy(ref, hbm, small_sem.at[4 + n]))
            copies[-1].start()
        other = 1 - me_ref[0] // (width // 2)
        sort_half(other, yb_ref, target_ref, list_ref, notes_ref, rows_ref, far_hbm, sem)
        for copy in copies:
            copy.wait()


def project_and_sort_far(width, me, embeddings, basis, list_owner, list_slot):
    rows_here, wide = embeddings.shape
    feats = basis.shape[1]
    lanes = rows_here // LANES
    slots = width * SPAN
    return pl.pallas_call(
        functools.partial(rows_kernel, width),
        grid=(rows_here // CHUNK,),
        in_specs=[pl.BlockSpec(memory_space=pltpu.SMEM)] + [pl.BlockSpec(memory_space=pl.ANY)] * 4,
        out_specs=[pl.BlockSpec(memory_space=pl.ANY)] * 6,
        out_shape=[
            jax.ShapeDtypeStruct((slots // 2, feats), jnp.bfloat16),
            jax.ShapeDtypeStruct((1, wide), jnp.float32),
            jax.ShapeDtypeStruct((rows_here, feats), jnp.bfloat16),
            jax.ShapeDtypeStruct((lanes, LANES), jnp.int32),
            jax.ShapeDtypeStruct((width, 2 * CAP), jnp.float32),
            jax.ShapeDtypeStruct((NOTES, feats), jnp.float32),
        ],
        scratch_shapes=[
            pltpu.VMEM((lanes, LANES), jnp.int32),
            pltpu.VMEM((lanes, LANES), jnp.int32),
            pltpu.VMEM((1, wide), jnp.float32),
            pltpu.VMEM((wide, feats), jnp.bfloat16),
            pltpu.VMEM((rows_here, wide), jnp.bfloat16),
            pltpu.VMEM((slots // 2, feats), jnp.bfloat16),
            pltpu.VMEM((rows_here, feats), jnp.float32),
            pltpu.VMEM((rows_here, feats), jnp.bfloat16),
            pltpu.VMEM((8, feats), jnp.float32),
            pltpu.VMEM((8, wide), jnp.float32),
            pltpu.VMEM((lanes, LANES), jnp.int32),
            pltpu.VMEM((width, 2 * CAP), jnp.float32),
            pltpu.VMEM((NOTES, feats), jnp.float32),
            pltpu.SemaphoreType.DMA((rows_here // CHUNK,)),
            pltpu.SemaphoreType.DMA((8,)),
            pltpu.SemaphoreType.DMA((width // GROUP // 2,)),
        ],
        compiler_params=pltpu.CompilerParams(vmem_limit_bytes=VMEM_ALL),
        cost_estimate=NO_COST,
        name="project_sort",
    )(me.reshape(1), embeddings, basis, list_owner.reshape(lanes, LANES), list_slot.reshape(lanes, LANES))


def moments_kernel(width, me_ref, mean_hbm, e_hbm, after_hbm, keep_ref, send_ref, e_ref, mean_ref, m_ref, sem, mean_sem):
    rows_here, wide = e_ref.shape
    block = wide // width
    bits = width.bit_length() - 1
    tiles = wide // TILE
    mean_copy = pltpu.make_async_copy(mean_hbm, mean_ref, mean_sem)
    mean_copy.start()
    copies = []
    for c in range(rows_here // CHUNK):
        at = pl.ds(c * CHUNK, CHUNK)
        copies.append(pltpu.make_async_copy(e_hbm.at[at], e_ref.at[at], sem.at[c]))
        copies[c].start()
    me = me_ref[0]
    odd = (me & 1) == 1
    mean_copy.wait()
    mean = mean_ref[...]
    for t in range(tiles):
        rows, columns = slice(t * TILE, (t + 1) * TILE), slice(t * TILE, wide)
        if t == 0:
            product = jnp.zeros((TILE, wide), jnp.float32)
            for c in range(rows_here // CHUNK):
                copies[c].wait()
                at = slice(c * CHUNK, (c + 1) * CHUNK)
                product = product + lax.dot_general(
                    e_ref[at, rows], e_ref[at, :], (((0,), (0,)), ((), ())), preferred_element_type=jnp.float32
                )
        else:
            product = lax.dot_general(
                e_ref[:, rows], e_ref[:, columns], (((0,), (0,)), ((), ())), preferred_element_type=jnp.float32
            )
        down = jnp.transpose(jnp.broadcast_to(mean[:, rows] * rows_here, (LANES, TILE)))
        for u in range(t, tiles):
            pieces = []
            for j in range(u * TILE // LANES, (u + 1) * TILE // LANES):
                across = slice(j * LANES, (j + 1) * LANES)
                within = slice(j * LANES - t * TILE, (j + 1) * LANES - t * TILE)
                pieces.append((product[:, within] - down * mean[:, across]).astype(jnp.bfloat16))
            piece = jnp.concatenate(pieces, 1)
            other = slice(u * TILE, (u + 1) * TILE)
            m_ref[rows, other] = piece
            if u > t:
                m_ref[other, rows] = jnp.transpose(piece)
        for pair in range(TILE // block // 2):
            first = t * (TILE // block) + 2 * pair
            apart = (first ^ me) >> 1
            place = 0
            for k in range(bits - 1):
                place = place + (((apart >> k) & 1) << (bits - 2 - k))
            to = pl.ds(pl.multiple_of(place * block, block), block)
            even_rows = m_ref[first * block:(first + 1) * block, :]
            odd_rows = m_ref[(first + 1) * block:(first + 2) * block, :]
            keep_ref[to, :] = jnp.where(odd, odd_rows, even_rows)
            send_ref[to, :] = jnp.where(odd, even_rows, odd_rows)


def moments(width, me, embeddings, mean, after):
    rows_here, wide = embeddings.shape
    vmem = pl.BlockSpec(memory_space=pltpu.VMEM)
    return pl.pallas_call(
        functools.partial(moments_kernel, width),
        in_specs=[pl.BlockSpec(memory_space=pltpu.SMEM)] + [pl.BlockSpec(memory_space=pl.ANY)] * 3,
        out_specs=[vmem] * 2,
        out_shape=[
            jax.ShapeDtypeStruct((wide // 2, wide), jnp.bfloat16),
            jax.ShapeDtypeStruct((wide // 2, wide), jnp.bfloat16),
        ],
        scratch_shapes=[
            pltpu.VMEM((rows_here, wide), jnp.bfloat16),
            pltpu.VMEM((1, wide), jnp.float32),
            pltpu.VMEM((wide, wide), jnp.bfloat16),
            pltpu.SemaphoreType.DMA((rows_here // CHUNK,)),
            pltpu.SemaphoreType.DMA,
        ],
        compiler_params=pltpu.CompilerParams(vmem_limit_bytes=VMEM_MOST),
        cost_estimate=NO_COST,
        name="moments",
    )(me.reshape(1), mean, embeddings, after)


def add_kernel(shares, pieces, arrived, keep_ref, *refs):
    outs = refs[len(refs) - shares * pieces:]
    came = refs[:arrived]
    rows, columns = outs[0].shape
    for h in range(shares):
        across = slice(h * columns, (h + 1) * columns)
        for p in range(pieces):
            at = slice(p * rows, (p + 1) * rows)
            held = keep_ref[at, across].astype(jnp.float32)
            for ref in came:
                held = held + ref[at, across].astype(jnp.float32)
            out = outs[h * pieces + p]
            out[...] = held.astype(out.dtype)


def add_and_split(keep, came, shares, pieces, after=()):
    rows, columns = keep.shape
    vmem = pl.BlockSpec(memory_space=pltpu.VMEM)
    shape = (rows // pieces, columns // shares)
    kinds = [jnp.float32] + [jnp.bfloat16] * (pieces - 1)
    outs = pl.pallas_call(
        functools.partial(add_kernel, shares, pieces, len(came)),
        in_specs=[vmem] * (1 + len(came)) + [pl.BlockSpec(memory_space=pl.ANY)] * len(after),
        out_specs=[vmem] * (shares * pieces),
        out_shape=[jax.ShapeDtypeStruct(shape, kind) for kind in kinds * shares],
        compiler_params=pltpu.CompilerParams(vmem_limit_bytes=VMEM_SOME),
        cost_estimate=NO_COST,
        name="add_and_split",
    )(keep, *came, *after)
    return [outs[h * pieces:(h + 1) * pieces] for h in range(shares)]


def finish_kernel(total, between_ref, *refs):
    out_ref = refs[-1]
    each = (len(refs) - 1) // SHARES
    columns = out_ref.shape[1] // SHARES
    for h in range(SHARES):
        across = slice(h * columns, (h + 1) * columns)
        held = refs[h * each][...]
        for ref in refs[h * each + 1:(h + 1) * each]:
            held = held + ref[...].astype(jnp.float32)
        out_ref[:, across] = (held + between_ref[:, across]) / total


def finish(total, between, keeps, came):
    parts = [part for keep, pieces in zip(keeps, came) for part in (keep, *pieces)]
    vmem = pl.BlockSpec(memory_space=pltpu.VMEM)
    return pl.pallas_call(
        functools.partial(finish_kernel, total),
        in_specs=[vmem] * (1 + len(parts)),
        out_specs=vmem,
        out_shape=jax.ShapeDtypeStruct(between.shape, jnp.float32),
        compiler_params=pltpu.CompilerParams(vmem_limit_bytes=VMEM_SOME),
        cost_estimate=NO_COST,
        name="finish",
    )(between, *parts)


def halving_stages(width):
    strides = [1 << k for k in range(width.bit_length() - 1)]
    return [[s] for s in strides[:-2]] + [strides[-2:]]


def exchange(width, stage, out):
    came = []
    for p in range(1, 1 << len(stage)):
        apart = sum(s for k, s in enumerate(stage) if (p >> (len(stage) - 1 - k)) & 1)
        came.append(lax.ppermute(out[p - 1], "wide", [(i, i ^ apart) for i in range(width)]))
    return came


def encode_kernel(total, me_ref, near_ref, far_ref, basis_ref, centroid_ref, rotation_ref, *refs):
    out_hbm, between_ref, out_ref, delta_ref, list_ref, apart_ref, sem = refs[-7:]
    width = delta_ref.shape[0]
    feats = out_ref.shape[1]
    owned = centroid_ref.shape[0]
    wide = basis_ref.shape[0]
    block = wide // width
    share = total // width

    notes = jnp.concatenate(
        [ref[s * SPAN + CAP:(s + 1) * SPAN, :] for ref in (near_ref, far_ref) for s in range(width // 2)], 0
    )
    size = width * NOTES
    to = lax.broadcasted_iota(jnp.int32, (size, size), 0)
    of = lax.broadcasted_iota(jnp.int32, (size, size), 1)
    turn = jnp.where((to % width) * NOTES + to // width == of, 1.0, 0.0).astype(jnp.bfloat16)
    turned = jnp.dot(turn, notes, preferred_element_type=jnp.float32)
    row = [turned[r * width:(r + 1) * width] for r in range(NOTES)]
    digits = row[NOTES - 1]
    list_ref[...] = digits[:, :CAP] * 32.0 + digits[:, CAP:] - 1.0
    quarters = wide // feats
    shifts = jnp.zeros((width, feats), jnp.float32)
    for q in range(quarters):
        parts = [row[p * quarters + q] for p in range(3)]
        mean = parts[0] + (parts[1] + parts[2])
        apart_ref[:, q * feats:(q + 1) * feats] = mean - jnp.mean(mean, 0, keepdims=True)
        terms = jnp.dot(
            jnp.concatenate(parts, 0).astype(jnp.bfloat16),
            basis_ref[q * feats:(q + 1) * feats, :],
            preferred_element_type=jnp.float32,
        )
        shifts = shifts + (terms[:width] + (terms[width:2 * width] + terms[2 * width:]))
    square = row[3 * quarters] + (row[3 * quarters + 1] + row[3 * quarters + 2])
    delta = shifts - jnp.mean(shifts, 0, keepdims=True)
    variance = jnp.sum(square + share * (delta * delta), 0, keepdims=True) / total
    scale = lax.rsqrt(variance + 1e-05)
    delta_ref[...] = delta

    names = lax.broadcasted_iota(jnp.int32, (CAP, owned), 1).astype(jnp.int16)

    half = me_ref[0] // (width // 2)
    each = width // GROUP // 2

    def encode_group(apart, q):
        start = (apart * each + q) * GROUP
        columns = jnp.transpose(list_ref[pl.ds(start, GROUP), :])
        hits, projected, held = [], [], []
        for s in range(GROUP):
            listed = jnp.broadcast_to(columns[:, s:s + 1], (CAP, LANES))
            held.append(jnp.concatenate([listed] * (feats // LANES), 1) >= 0)
            wanted = jnp.concatenate([listed.astype(jnp.int32).astype(jnp.int16)] * (owned // LANES), 1)
            hits.append(jnp.where(wanted == names, jnp.ones((), jnp.bfloat16), jnp.zeros((), jnp.bfloat16)))
            base = pl.multiple_of((q * GROUP + s) * SPAN, 16)
            rows = (near_ref, far_ref)[apart][pl.ds(base, CAP), :].astype(jnp.float32)
            projected.append((rows + delta_ref[pl.ds(start + s, 1), :]) * scale)
        centre = jnp.dot(jnp.concatenate(hits, 0), centroid_ref[...], preferred_element_type=jnp.float32)
        residual = jnp.where(jnp.concatenate(held, 0), jnp.concatenate(projected, 0) - centre, 0.0)
        here = pl.ds(pl.multiple_of(start * CAP, GROUP * CAP), GROUP * CAP)
        there = pl.ds(pl.multiple_of(((half ^ apart) * each + q) * (GROUP * CAP), GROUP * CAP), GROUP * CAP)
        out_ref[here, :] = jnp.dot(
            residual.astype(jnp.bfloat16), rotation_ref[...], preferred_element_type=jnp.float32
        ).astype(jnp.bfloat16)
        return pltpu.make_async_copy(out_ref.at[here], out_hbm.at[there], sem.at[apart * each + q])

    copies = []
    for apart in (0, 1):
        if each <= 2:
            for q in range(each):
                copies.append(encode_group(apart, q))
                copies[-1].start()
        else:

            @pl.loop(0, each)
            def _(q):
                copy = encode_group(apart, q)
                copy.start()
                copy.wait()

    first = me_ref[0] * block
    near = apart_ref[:, pl.ds(pl.multiple_of(first // LANES * LANES, LANES), LANES)]
    near = pltpu.roll(near, (LANES - first % LANES) % LANES, 1)[:, :block]
    between_ref[...] = share * lax.dot_general(
        near,
        apart_ref[...],
        (((0,), (0,)), ((), ())),
        precision=lax.Precision.HIGHEST,
        preferred_element_type=jnp.float32,
    )
    for copy in copies:
        copy.wait()


def encode(width, total, me, near, far, basis, centroids, rotation, after):
    wide, feats = basis.shape
    owned = centroids.shape[0]
    slots = width * CAP
    vmem, anywhere = pl.BlockSpec(memory_space=pltpu.VMEM), pl.BlockSpec(memory_space=pl.ANY)
    return pl.pallas_call(
        functools.partial(encode_kernel, total),
        in_specs=[pl.BlockSpec(memory_space=pltpu.SMEM)] + [vmem] * 5 + [anywhere] * len(after),
        out_specs=[anywhere, vmem],
        out_shape=[
            jax.ShapeDtypeStruct((slots, feats), jnp.bfloat16),
            jax.ShapeDtypeStruct((wide // width, wide), jnp.float32),
        ],
        scratch_shapes=[
            pltpu.VMEM((slots, feats), jnp.bfloat16),
            pltpu.VMEM((width, feats), jnp.float32),
            pltpu.VMEM((width, CAP), jnp.float32),
            pltpu.VMEM((width, wide), jnp.float32),
            pltpu.SemaphoreType.DMA((width // GROUP,)),
        ],
        compiler_params=pltpu.CompilerParams(vmem_limit_bytes=VMEM_ALL),
        cost_estimate=NO_COST,
        name="encode",
    )(me.reshape(1), near, far, basis, centroids, rotation, *after)


def local(embeddings, basis, list_owner, list_slot, centroids, rotation):
    width = lax.axis_size("wide")
    me = lax.axis_index("wide")
    rows_here, wide = embeddings.shape
    feats = basis.shape[1]
    total = rows_here * width

    far, mean, *rest = project_and_sort_far(width, me, embeddings, basis, list_owner, list_slot)
    half = width // 2
    halves = [list(range(half)), list(range(half, width))]

    def spread(blocks):
        blocks = lax.all_to_all(
            blocks.reshape(half, SPAN, feats), "wide", split_axis=0, concat_axis=0, tiled=True, axis_index_groups=halves
        )
        return blocks.reshape(half * SPAN, feats)

    far = lax.ppermute(far, "wide", [(i, i ^ half) for i in range(width)])
    near, near_sorted = sort_near(me, *rest)
    near = spread(near)
    keep, send = moments(width, me, embeddings, mean, near_sorted)
    stages = halving_stages(width)
    came = exchange(width, stages[0], [send])
    shares = add_and_split(keep, came, SHARES, 1 << len(stages[1]))
    last, after = [], []
    for share in shares:
        for n in range(1, len(stages) - 1):
            came = exchange(width, stages[n], share[1:])
            (share,) = add_and_split(share[0], came, 1, 1 << len(stages[n + 1]), after)
        last.append(share)
        if not after:
            far = tie(far, [share[1]])
            after = [far]
    far = spread(far)
    came = [exchange(width, stages[-1], share[1:]) for share in last]
    encoded, between = encode(
        width, total, me, near, far, basis, centroids, rotation, [share[1] for share in last]
    )
    covariance = finish(total, between, [share[0] for share in last], came)
    return (encoded, covariance)


def solution(mesh):
    in_specs = (
        P(("groups", "wide"), None),
        P(),
        P(("groups", "wide")),
        P(("groups", "wide")),
        P("wide", None),
        P(),
    )
    out_specs = (P(("groups", "wide"), None), P(("groups", "wide"), None))
    return jax.shard_map(local, mesh=mesh, in_specs=in_specs, out_specs=out_specs, check_vma=False)
```

```python
import functools

import jax
import jax.numpy as jnp
from jax import lax
from jax.experimental import pallas as pl
from jax.experimental.pallas import tpu as pltpu
from jax.sharding import PartitionSpec as P

CAP = 128
LANES = 128
NOTES = 16
SPAN = CAP + NOTES
CHUNK = 512
TILE = 256
GROUP = 4
SHARES = 2
VMEM_ALL = 60 * 1024 * 1024
VMEM_SOME = 24 * 1024 * 1024
VMEM_MOST = 48 * 1024 * 1024


def in_three(x):
    high = x.astype(jnp.bfloat16).astype(jnp.float32)
    rest = x - high
    middle = rest.astype(jnp.bfloat16).astype(jnp.float32)
    return high, middle, (rest - middle).astype(jnp.bfloat16).astype(jnp.float32)


def rows_kernel(
    width, e_hbm, basis_hbm, owner_hbm, slot_hbm,
    rows_hbm, mean_hbm,
    owner_ref, slot_ref, mean_ref, basis_ref, e_ref, rows_ref, y_ref, yb_ref, sum_ref, total_ref, target_ref, list_ref, e_sem, small_sem, sem,
):
    step = pl.program_id(0)
    rows_here, feats = y_ref.shape
    wide = e_ref.shape[1]
    chunks = rows_here // LANES

    def e_copy(c):
        at = pl.ds(pl.multiple_of(c * CHUNK, CHUNK), CHUNK)
        return pltpu.make_async_copy(e_hbm.at[at], e_ref.at[at], e_sem.at[c])

    @pl.when(step == 0)
    def _():
        owner_copy = pltpu.make_async_copy(owner_hbm, owner_ref, small_sem.at[0])
        slot_copy = pltpu.make_async_copy(slot_hbm, slot_ref, small_sem.at[1])
        basis_copy = pltpu.make_async_copy(basis_hbm, basis_ref, small_sem.at[2])
        owner_copy.start()
        e_copy(0).start()
        slot_copy.start()
        basis_copy.start()
        for c in range(1, rows_here // CHUNK):
            e_copy(c).start()
        owner_copy.wait()
        sum_ref[...] = jnp.zeros_like(sum_ref)
        total_ref[...] = jnp.zeros_like(total_ref)
        owner = owner_ref[...]
        wanted = lax.broadcasted_iota(jnp.int32, (width, LANES), 0)
        hits = [jnp.where(owner[c:c + 1, :] == wanted, 1.0, 0.0) for c in range(chunks)]
        flat = jnp.concatenate(hits, 0).astype(jnp.bfloat16)
        up = lax.broadcasted_iota(jnp.int32, (LANES, LANES), 0)
        to = lax.broadcasted_iota(jnp.int32, (LANES, LANES), 1)
        before = jnp.where(up < to, 1.0, 0.0).astype(jnp.bfloat16)
        every = jnp.ones((LANES, LANES), jnp.bfloat16)
        within = jnp.dot(flat, before, preferred_element_type=jnp.float32)
        counts = jnp.dot(flat, every, preferred_element_type=jnp.float32)
        carry = jnp.zeros((width, LANES), jnp.float32)
        ranks = []
        for c in range(chunks):
            at = slice(c * width, (c + 1) * width)
            ranks.append(jnp.sum(hits[c] * (within[at] + carry), 0, keepdims=True).astype(jnp.int32))
            carry = carry + counts[at]
            target_ref[c:c + 1, :] = owner[c:c + 1, :] * CAP + ranks[c]

        slot_copy.wait()
        slot = slot_ref[...] + 1
        high, low = (slot >> 5).astype(jnp.float32), (slot & 31).astype(jnp.float32)
        spots = lax.broadcasted_iota(jnp.int32, (CAP, LANES), 0)
        placed = jnp.concatenate([jnp.where(ranks[c] == spots, 1.0, 0.0) for c in range(chunks)], 1).astype(jnp.bfloat16)
        digits = jnp.concatenate(
            [
                jnp.concatenate([hits[c] * high[c:c + 1, :] for c in range(chunks)], 1),
                jnp.concatenate([hits[c] * low[c:c + 1, :] for c in range(chunks)], 1),
            ],
            0,
        ).astype(jnp.bfloat16)
        found = lax.dot_general(digits, placed, (((1,), (1,)), ((), ())), preferred_element_type=jnp.float32)
        list_ref[:, :CAP] = found[:width]
        list_ref[:, CAP:] = found[width:]
        basis_copy.wait()

    e_copy(step).wait()
    here = pl.ds(pl.multiple_of(step * CHUNK, CHUNK), CHUNK)
    rows = e_ref[here, :]
    y = jnp.dot(rows, basis_ref[...], preferred_element_type=jnp.float32)
    y_ref[here, :] = y
    sum_ref[...] += jnp.sum(y.reshape(CHUNK // 8, 8, feats), 0)
    total_ref[...] += jnp.sum(rows.astype(jnp.float32).reshape(CHUNK // 8, 8, wide), 0)

    @pl.when(step == pl.num_programs(0) - 1)
    def _():
        mean_y = jnp.sum(sum_ref[...], 0, keepdims=True) / rows_here
        square = jnp.zeros((8, feats), jnp.float32)
        for c in range(rows_here // CHUNK):
            at = slice(c * CHUNK, (c + 1) * CHUNK)
            centred = y_ref[at, :] - mean_y
            square = square + jnp.sum((centred * centred).reshape(CHUNK // 8, 8, feats), 0)
            yb_ref[at, :] = centred.astype(jnp.bfloat16)
        mean = jnp.sum(total_ref[...], 0, keepdims=True) / rows_here
        mean_ref[...] = mean
        mean_copy = pltpu.make_async_copy(mean_ref, mean_hbm, small_sem.at[3])
        mean_copy.start()
        parts = in_three(mean)
        common = [part[:, q * feats:(q + 1) * feats] for part in parts for q in range(wide // feats)]
        common = jnp.concatenate(common + list(in_three(jnp.sum(square, 0, keepdims=True))), 0)

        place = lax.broadcasted_iota(jnp.int32, (GROUP * CAP, LANES), 0).astype(jnp.int16)

        def sort_group(g):
            first = g * GROUP
            pieces = []
            for c in range(chunks):
                wanted = (target_ref[c:c + 1, :] - first * CAP).astype(jnp.int32)
                wanted = jnp.broadcast_to(wanted, (16, LANES)).astype(jnp.int16)
                wanted = jnp.concatenate([wanted] * (GROUP * CAP // 16), 0)
                pieces.append(jnp.where(wanted == place, jnp.ones((), jnp.bfloat16), jnp.zeros((), jnp.bfloat16)))
            pick = jnp.concatenate(pieces, 1)
            rows = jnp.dot(pick, yb_ref[...], preferred_element_type=jnp.float32).astype(jnp.bfloat16)
            for j in range(GROUP):
                base = pl.multiple_of((first + j) * SPAN, 16)
                rows_ref[pl.ds(base, CAP), :] = rows[j * CAP:(j + 1) * CAP]
                notes = jnp.concatenate([common, list_ref[pl.ds(first + j, 1), :]], 0)
                rows_ref[pl.ds(pl.multiple_of(base + CAP, 16), NOTES), :] = notes.astype(jnp.bfloat16)
            at = pl.ds(pl.multiple_of(g * (GROUP * SPAN), 16), GROUP * SPAN)
            return pltpu.make_async_copy(rows_ref.at[at], rows_hbm.at[at], sem.at[g])

        groups = width // GROUP
        if groups <= 4:
            copies = []
            for g in range(groups):
                copies.append(sort_group(g))
                copies[g].start()
            for copy in copies:
                copy.wait()
        else:

            @pl.loop(0, groups)
            def _(g):
                copy = sort_group(g)
                copy.start()
                copy.wait()

        mean_copy.wait()


def project_and_sort(width, embeddings, basis, list_owner, list_slot):
    rows_here, wide = embeddings.shape
    feats = basis.shape[1]
    lanes = rows_here // LANES
    slots = width * SPAN
    return pl.pallas_call(
        functools.partial(rows_kernel, width),
        grid=(rows_here // CHUNK,),
        in_specs=[pl.BlockSpec(memory_space=pl.ANY)] * 4,
        out_specs=[pl.BlockSpec(memory_space=pl.ANY)] * 2,
        out_shape=[
            jax.ShapeDtypeStruct((slots, feats), jnp.bfloat16),
            jax.ShapeDtypeStruct((1, wide), jnp.float32),
        ],
        scratch_shapes=[
            pltpu.VMEM((lanes, LANES), jnp.int32),
            pltpu.VMEM((lanes, LANES), jnp.int32),
            pltpu.VMEM((1, wide), jnp.float32),
            pltpu.VMEM((wide, feats), jnp.bfloat16),
            pltpu.VMEM((rows_here, wide), jnp.bfloat16),
            pltpu.VMEM((slots, feats), jnp.bfloat16),
            pltpu.VMEM((rows_here, feats), jnp.float32),
            pltpu.VMEM((rows_here, feats), jnp.bfloat16),
            pltpu.VMEM((8, feats), jnp.float32),
            pltpu.VMEM((8, wide), jnp.float32),
            pltpu.VMEM((lanes, LANES), jnp.int32),
            pltpu.VMEM((width, 2 * CAP), jnp.float32),
            pltpu.SemaphoreType.DMA((rows_here // CHUNK,)),
            pltpu.SemaphoreType.DMA((4,)),
            pltpu.SemaphoreType.DMA((width // GROUP,)),
        ],
        compiler_params=pltpu.CompilerParams(vmem_limit_bytes=VMEM_ALL),
        cost_estimate=pl.CostEstimate(
            flops=2 * rows_here * feats * (wide + slots), bytes_accessed=2 * rows_here * wide + 2 * slots * feats, transcendentals=0
        ),
        name="project_sort",
    )(embeddings, basis, list_owner.reshape(lanes, LANES), list_slot.reshape(lanes, LANES))


def moments_kernel(width, me_ref, mean_hbm, e_hbm, keep_ref, send_ref, e_ref, mean_ref, m_ref, sem, mean_sem):
    rows_here, wide = e_ref.shape
    block = wide // width
    bits = width.bit_length() - 1
    tiles = wide // TILE
    mean_copy = pltpu.make_async_copy(mean_hbm, mean_ref, mean_sem)
    mean_copy.start()
    copies = []
    for c in range(rows_here // CHUNK):
        at = pl.ds(c * CHUNK, CHUNK)
        copies.append(pltpu.make_async_copy(e_hbm.at[at], e_ref.at[at], sem.at[c]))
        copies[c].start()
    me = me_ref[0]
    odd = (me & 1) == 1
    mean_copy.wait()
    mean = mean_ref[...]
    for t in range(tiles):
        rows, columns = slice(t * TILE, (t + 1) * TILE), slice(t * TILE, wide)
        if t == 0:
            product = jnp.zeros((TILE, wide), jnp.float32)
            for c in range(rows_here // CHUNK):
                copies[c].wait()
                at = slice(c * CHUNK, (c + 1) * CHUNK)
                product = product + lax.dot_general(
                    e_ref[at, rows], e_ref[at, :], (((0,), (0,)), ((), ())), preferred_element_type=jnp.float32
                )
        else:
            product = lax.dot_general(
                e_ref[:, rows], e_ref[:, columns], (((0,), (0,)), ((), ())), preferred_element_type=jnp.float32
            )
        down = jnp.transpose(jnp.broadcast_to(mean[:, rows] * rows_here, (LANES, TILE)))
        for u in range(t, tiles):
            pieces = []
            for j in range(u * TILE // LANES, (u + 1) * TILE // LANES):
                across = slice(j * LANES, (j + 1) * LANES)
                within = slice(j * LANES - t * TILE, (j + 1) * LANES - t * TILE)
                pieces.append((product[:, within] - down * mean[:, across]).astype(jnp.bfloat16))
            piece = jnp.concatenate(pieces, 1)
            other = slice(u * TILE, (u + 1) * TILE)
            m_ref[rows, other] = piece
            if u > t:
                m_ref[other, rows] = jnp.transpose(piece)
        for pair in range(TILE // block // 2):
            first = t * (TILE // block) + 2 * pair
            apart = (first ^ me) >> 1
            place = 0
            for k in range(bits - 1):
                place = place + (((apart >> k) & 1) << (bits - 2 - k))
            to = pl.ds(pl.multiple_of(place * block, block), block)
            even_rows = m_ref[first * block:(first + 1) * block, :]
            odd_rows = m_ref[(first + 1) * block:(first + 2) * block, :]
            keep_ref[to, :] = jnp.where(odd, odd_rows, even_rows)
            send_ref[to, :] = jnp.where(odd, even_rows, odd_rows)


def moments(width, me, embeddings, mean):
    rows_here, wide = embeddings.shape
    vmem = pl.BlockSpec(memory_space=pltpu.VMEM)
    return pl.pallas_call(
        functools.partial(moments_kernel, width),
        in_specs=[pl.BlockSpec(memory_space=pltpu.SMEM)] + [pl.BlockSpec(memory_space=pl.ANY)] * 2,
        out_specs=[vmem] * 2,
        out_shape=[
            jax.ShapeDtypeStruct((wide // 2, wide), jnp.bfloat16),
            jax.ShapeDtypeStruct((wide // 2, wide), jnp.bfloat16),
        ],
        scratch_shapes=[
            pltpu.VMEM((rows_here, wide), jnp.bfloat16),
            pltpu.VMEM((1, wide), jnp.float32),
            pltpu.VMEM((wide, wide), jnp.bfloat16),
            pltpu.SemaphoreType.DMA((rows_here // CHUNK,)),
            pltpu.SemaphoreType.DMA,
        ],
        compiler_params=pltpu.CompilerParams(vmem_limit_bytes=VMEM_MOST),
        cost_estimate=pl.CostEstimate(
            flops=2 * rows_here * wide * wide, bytes_accessed=2 * rows_here * wide + 3 * wide * wide, transcendentals=0
        ),
        name="moments",
    )(me.reshape(1), mean, embeddings)


def add_kernel(shares, pieces, keep_ref, *refs):
    outs = refs[len(refs) - shares * pieces:]
    came = refs[:len(refs) - shares * pieces]
    rows, columns = outs[0].shape
    for h in range(shares):
        across = slice(h * columns, (h + 1) * columns)
        for p in range(pieces):
            at = slice(p * rows, (p + 1) * rows)
            held = keep_ref[at, across].astype(jnp.float32)
            for ref in came:
                held = held + ref[at, across].astype(jnp.float32)
            out = outs[h * pieces + p]
            out[...] = held.astype(out.dtype)


def add_and_split(keep, came, shares, pieces):
    rows, columns = keep.shape
    vmem = pl.BlockSpec(memory_space=pltpu.VMEM)
    shape = (rows // pieces, columns // shares)
    kinds = [jnp.float32] + [jnp.bfloat16] * (pieces - 1)
    outs = pl.pallas_call(
        functools.partial(add_kernel, shares, pieces),
        in_specs=[vmem] * (1 + len(came)),
        out_specs=[vmem] * (shares * pieces),
        out_shape=[jax.ShapeDtypeStruct(shape, kind) for kind in kinds * shares],
        compiler_params=pltpu.CompilerParams(vmem_limit_bytes=VMEM_SOME),
        cost_estimate=pl.CostEstimate(flops=2 * rows * columns, bytes_accessed=10 * rows * columns, transcendentals=0),
        name="add_and_split",
    )(keep, *came)
    return [outs[h * pieces:(h + 1) * pieces] for h in range(shares)]


def finish_kernel(total, counts, between_ref, *refs):
    out_ref = refs[-1]
    columns = out_ref.shape[1] // SHARES
    at = 0
    for h, count in enumerate(counts):
        across = slice(h * columns, (h + 1) * columns)
        held = refs[at][...]
        for ref in refs[at + 1:at + count]:
            held = held + ref[...].astype(jnp.float32)
        out_ref[:, across] = (held + between_ref[:, across]) / total
        at += count


def finish(total, between, keeps, came):
    parts = [part for keep, pieces in zip(keeps, came) for part in (keep, *pieces)]
    vmem = pl.BlockSpec(memory_space=pltpu.VMEM)
    return pl.pallas_call(
        functools.partial(finish_kernel, total, [1 + len(pieces) for pieces in came]),
        in_specs=[vmem] * (1 + len(parts)),
        out_specs=vmem,
        out_shape=jax.ShapeDtypeStruct(between.shape, jnp.float32),
        compiler_params=pltpu.CompilerParams(vmem_limit_bytes=VMEM_SOME),
        cost_estimate=pl.CostEstimate(flops=8 * between.size, bytes_accessed=16 * between.size, transcendentals=0),
        name="finish",
    )(between, *parts)


def halving_stages(width, together):
    strides = [1 << k for k in range(width.bit_length() - 1)]
    return [[s] for s in strides[:-together]] + [strides[-together:]]


def exchange(width, stage, out):
    came = []
    for p in range(1, 1 << len(stage)):
        apart = sum(s for k, s in enumerate(stage) if (p >> (len(stage) - 1 - k)) & 1)
        came.append(lax.ppermute(out[p - 1], "wide", [(i, i ^ apart) for i in range(width)]))
    return came


def encode_kernel(total, me_ref, got_ref, basis_ref, centroid_ref, rotation_ref, *refs):
    out_hbm, between_ref, out_ref, delta_ref, list_ref, apart_ref, sem = refs[-7:]
    width = delta_ref.shape[0]
    feats = out_ref.shape[1]
    owned = centroid_ref.shape[0]
    wide = basis_ref.shape[0]
    block = wide // width
    share = total // width

    notes = jnp.concatenate([got_ref[s * SPAN + CAP:(s + 1) * SPAN, :] for s in range(width)], 0)
    size = width * NOTES
    to = lax.broadcasted_iota(jnp.int32, (size, size), 0)
    of = lax.broadcasted_iota(jnp.int32, (size, size), 1)
    turn = jnp.where((to & (width - 1)) * NOTES + (to >> (width.bit_length() - 1)) == of, 1.0, 0.0).astype(jnp.bfloat16)
    turned = jnp.dot(turn, notes, preferred_element_type=jnp.float32)
    row = [turned[r * width:(r + 1) * width] for r in range(NOTES)]
    digits = row[NOTES - 1]
    list_ref[...] = digits[:, :CAP] * 32.0 + digits[:, CAP:] - 1.0
    quarters = wide // feats
    shifts = jnp.zeros((width, feats), jnp.float32)
    for q in range(quarters):
        parts = [row[p * quarters + q] for p in range(3)]
        mean = parts[0] + (parts[1] + parts[2])
        apart_ref[:, q * feats:(q + 1) * feats] = mean - jnp.mean(mean, 0, keepdims=True)
        terms = jnp.dot(
            jnp.concatenate(parts, 0).astype(jnp.bfloat16),
            basis_ref[q * feats:(q + 1) * feats, :],
            preferred_element_type=jnp.float32,
        )
        shifts = shifts + (terms[:width] + (terms[width:2 * width] + terms[2 * width:]))
    square = row[3 * quarters] + (row[3 * quarters + 1] + row[3 * quarters + 2])
    delta = shifts - jnp.mean(shifts, 0, keepdims=True)
    variance = jnp.sum(square + share * (delta * delta), 0, keepdims=True) / total
    scale = lax.rsqrt(variance + 1e-05)
    delta_ref[...] = delta

    names = lax.broadcasted_iota(jnp.int32, (CAP, owned), 1).astype(jnp.int16)

    groups = width // GROUP
    if groups <= 4:
        every = jnp.transpose(list_ref[...])

    def encode_group(g):
        if groups <= 4:
            columns = every[:, g * GROUP:(g + 1) * GROUP]
        else:
            columns = jnp.transpose(list_ref[pl.ds(g * GROUP, GROUP), :])
        hits, projected, held = [], [], []
        for s in range(GROUP):
            listed = jnp.broadcast_to(columns[:, s:s + 1], (CAP, LANES))
            held.append(jnp.concatenate([listed] * (feats // LANES), 1) >= 0)
            wanted = jnp.concatenate([listed.astype(jnp.int32).astype(jnp.int16)] * (owned // LANES), 1)
            hits.append(jnp.where(wanted == names, jnp.ones((), jnp.bfloat16), jnp.zeros((), jnp.bfloat16)))
            base = pl.multiple_of((g * GROUP + s) * SPAN, 16)
            rows = got_ref[pl.ds(base, CAP), :].astype(jnp.float32)
            projected.append((rows + delta_ref[pl.ds(g * GROUP + s, 1), :]) * scale)
        centre = jnp.dot(jnp.concatenate(hits, 0), centroid_ref[...], preferred_element_type=jnp.float32)
        residual = jnp.where(jnp.concatenate(held, 0), jnp.concatenate(projected, 0) - centre, 0.0)
        at = pl.ds(pl.multiple_of(g * (GROUP * CAP), GROUP * CAP), GROUP * CAP)
        out_ref[at, :] = jnp.dot(
            residual.astype(jnp.bfloat16), rotation_ref[...], preferred_element_type=jnp.float32
        ).astype(jnp.bfloat16)
        return pltpu.make_async_copy(out_ref.at[at], out_hbm.at[at], sem.at[g])

    copies = []
    if groups <= 4:
        for g in range(groups):
            copies.append(encode_group(g))
            copies[g].start()
    else:

        @pl.loop(0, groups)
        def _(g):
            copy = encode_group(g)
            copy.start()
            copy.wait()

    first = me_ref[0] * block
    near = apart_ref[:, pl.ds(pl.multiple_of(first // LANES * LANES, LANES), LANES)]
    near = pltpu.roll(near, (LANES - first % LANES) % LANES, 1)[:, :block]
    between_ref[...] = share * lax.dot_general(
        near,
        apart_ref[...],
        (((0,), (0,)), ((), ())),
        precision=lax.Precision.HIGHEST,
        preferred_element_type=jnp.float32,
    )
    for copy in copies:
        copy.wait()


def encode(width, total, me, got, basis, centroids, rotation, after):
    wide, feats = basis.shape
    owned = centroids.shape[0]
    slots = width * CAP
    vmem, anywhere = pl.BlockSpec(memory_space=pltpu.VMEM), pl.BlockSpec(memory_space=pl.ANY)
    return pl.pallas_call(
        functools.partial(encode_kernel, total),
        in_specs=[pl.BlockSpec(memory_space=pltpu.SMEM)] + [vmem] * 4 + [anywhere] * len(after),
        out_specs=[anywhere, vmem],
        out_shape=[
            jax.ShapeDtypeStruct((slots, feats), jnp.bfloat16),
            jax.ShapeDtypeStruct((wide // width, wide), jnp.float32),
        ],
        scratch_shapes=[
            pltpu.VMEM((slots, feats), jnp.bfloat16),
            pltpu.VMEM((width, feats), jnp.float32),
            pltpu.VMEM((width, CAP), jnp.float32),
            pltpu.VMEM((width, wide), jnp.float32),
            pltpu.SemaphoreType.DMA((width // GROUP,)),
        ],
        compiler_params=pltpu.CompilerParams(vmem_limit_bytes=VMEM_SOME),
        cost_estimate=pl.CostEstimate(
            flops=2 * slots * feats * (owned + feats), bytes_accessed=4 * slots * feats, transcendentals=0
        ),
        name="encode",
    )(me.reshape(1), got, basis, centroids, rotation, *after)


def local(embeddings, basis, list_owner, list_slot, centroids, rotation):
    width = lax.axis_size("wide")
    me = lax.axis_index("wide")
    rows_here, wide = embeddings.shape
    feats = basis.shape[1]
    total = rows_here * width

    rows, mean = project_and_sort(width, embeddings, basis, list_owner, list_slot)
    got = lax.all_to_all(rows.reshape(width, SPAN, feats), "wide", split_axis=0, concat_axis=0, tiled=True)

    keep, send = moments(width, me, embeddings, mean)
    came = exchange(width, [1], [send])
    shares = add_and_split(keep, came, SHARES, 2)
    keeps, ends, sends = [], [], []
    for together, (keep, *out) in zip((1, 2), shares):
        stages = halving_stages(width, together)[1:]
        for n, stage in enumerate(stages):
            sends.append(out[0])
            came = exchange(width, stage, out)
            if n + 1 < len(stages):
                ((keep, *out),) = add_and_split(keep, came, 1, 1 << len(stages[n + 1]))
        keeps.append(keep)
        ends.append(came)
    encoded, between = encode(
        width, total, me, got.reshape(width * SPAN, feats), basis, centroids, rotation, sends
    )
    covariance = finish(total, between, keeps, ends)
    return (encoded, covariance)


def solution(mesh):
    in_specs = (
        P(("groups", "wide"), None),
        P(),
        P(("groups", "wide")),
        P(("groups", "wide")),
        P("wide", None),
        P(),
    )
    out_specs = (P(("groups", "wide"), None), P(("groups", "wide"), None))
    return jax.shard_map(local, mesh=mesh, in_specs=in_specs, out_specs=out_specs, check_vma=False)
```

```python
import functools

import jax
import jax.numpy as jnp
from jax import lax
from jax.experimental import pallas as pl
from jax.experimental.pallas import tpu as pltpu
from jax.sharding import PartitionSpec as P

CAP = 128
LANES = 128
NOTES = 16
SPAN = CAP + NOTES
CHUNK = 512
TILE = 256
GROUP = 4
SHARES = 2
PLANE = 4
VMEM_ALL = 60 * 1024 * 1024
VMEM_SOME = 24 * 1024 * 1024
VMEM_MOST = 48 * 1024 * 1024


def place_of(width, device):
    return (device & (PLANE - 1)) * (width // PLANE) + device // PLANE


def device_at(width, place):
    return (place & (width // PLANE - 1)) * PLANE + place // (width // PLANE)


def in_three(x):
    high = x.astype(jnp.bfloat16).astype(jnp.float32)
    rest = x - high
    middle = rest.astype(jnp.bfloat16).astype(jnp.float32)
    return high, middle, (rest - middle).astype(jnp.bfloat16).astype(jnp.float32)


def rows_kernel(
    width, e_hbm, basis_hbm, owner_hbm, slot_hbm,
    rows_hbm, mean_hbm,
    owner_ref, slot_ref, mean_ref, basis_ref, e_ref, rows_ref, y_ref, yb_ref, sum_ref, total_ref, target_ref, list_ref, e_sem, small_sem, sem,
):
    step = pl.program_id(0)
    rows_here, feats = y_ref.shape
    wide = e_ref.shape[1]
    chunks = rows_here // LANES

    def e_copy(c):
        at = pl.ds(pl.multiple_of(c * CHUNK, CHUNK), CHUNK)
        return pltpu.make_async_copy(e_hbm.at[at], e_ref.at[at], e_sem.at[c])

    @pl.when(step == 0)
    def _():
        owner_copy = pltpu.make_async_copy(owner_hbm, owner_ref, small_sem.at[0])
        slot_copy = pltpu.make_async_copy(slot_hbm, slot_ref, small_sem.at[1])
        basis_copy = pltpu.make_async_copy(basis_hbm, basis_ref, small_sem.at[2])
        owner_copy.start()
        e_copy(0).start()
        slot_copy.start()
        basis_copy.start()
        for c in range(1, rows_here // CHUNK):
            e_copy(c).start()
        owner_copy.wait()
        sum_ref[...] = jnp.zeros_like(sum_ref)
        total_ref[...] = jnp.zeros_like(total_ref)
        owner = place_of(width, owner_ref[...])
        wanted = lax.broadcasted_iota(jnp.int32, (width, LANES), 0)
        hits = [jnp.where(owner[c:c + 1, :] == wanted, 1.0, 0.0) for c in range(chunks)]
        flat = jnp.concatenate(hits, 0).astype(jnp.bfloat16)
        up = lax.broadcasted_iota(jnp.int32, (LANES, LANES), 0)
        to = lax.broadcasted_iota(jnp.int32, (LANES, LANES), 1)
        before = jnp.where(up < to, 1.0, 0.0).astype(jnp.bfloat16)
        every = jnp.ones((LANES, LANES), jnp.bfloat16)
        within = jnp.dot(flat, before, preferred_element_type=jnp.float32)
        counts = jnp.dot(flat, every, preferred_element_type=jnp.float32)
        carry = jnp.zeros((width, LANES), jnp.float32)
        ranks = []
        for c in range(chunks):
            at = slice(c * width, (c + 1) * width)
            ranks.append(jnp.sum(hits[c] * (within[at] + carry), 0, keepdims=True).astype(jnp.int32))
            carry = carry + counts[at]
            target_ref[c:c + 1, :] = owner[c:c + 1, :] * CAP + ranks[c]

        slot_copy.wait()
        slot = slot_ref[...] + 1
        high, low = (slot >> 5).astype(jnp.float32), (slot & 31).astype(jnp.float32)
        spots = lax.broadcasted_iota(jnp.int32, (CAP, LANES), 0)
        placed = jnp.concatenate([jnp.where(ranks[c] == spots, 1.0, 0.0) for c in range(chunks)], 1).astype(jnp.bfloat16)
        digits = jnp.concatenate(
            [
                jnp.concatenate([hits[c] * high[c:c + 1, :] for c in range(chunks)], 1),
                jnp.concatenate([hits[c] * low[c:c + 1, :] for c in range(chunks)], 1),
            ],
            0,
        ).astype(jnp.bfloat16)
        found = lax.dot_general(digits, placed, (((1,), (1,)), ((), ())), preferred_element_type=jnp.float32)
        list_ref[:, :CAP] = found[:width]
        list_ref[:, CAP:] = found[width:]
        basis_copy.wait()

    e_copy(step).wait()
    here = pl.ds(pl.multiple_of(step * CHUNK, CHUNK), CHUNK)
    rows = e_ref[here, :]
    y = jnp.dot(rows, basis_ref[...], preferred_element_type=jnp.float32)
    y_ref[here, :] = y
    sum_ref[...] += jnp.sum(y.reshape(CHUNK // 8, 8, feats), 0)
    total_ref[...] += jnp.sum(rows.astype(jnp.float32).reshape(CHUNK // 8, 8, wide), 0)

    @pl.when(step == pl.num_programs(0) - 1)
    def _():
        mean_y = jnp.sum(sum_ref[...], 0, keepdims=True) / rows_here
        square = jnp.zeros((8, feats), jnp.float32)
        for c in range(rows_here // CHUNK):
            at = slice(c * CHUNK, (c + 1) * CHUNK)
            centred = y_ref[at, :] - mean_y
            square = square + jnp.sum((centred * centred).reshape(CHUNK // 8, 8, feats), 0)
            yb_ref[at, :] = centred.astype(jnp.bfloat16)
        mean = jnp.sum(total_ref[...], 0, keepdims=True) / rows_here
        mean_ref[...] = mean
        mean_copy = pltpu.make_async_copy(mean_ref, mean_hbm, small_sem.at[3])
        mean_copy.start()
        parts = in_three(mean)
        common = [part[:, q * feats:(q + 1) * feats] for part in parts for q in range(wide // feats)]
        common = jnp.concatenate(common + list(in_three(jnp.sum(square, 0, keepdims=True))), 0)

        place = lax.broadcasted_iota(jnp.int32, (GROUP * CAP, LANES), 0).astype(jnp.int16)

        def sort_group(g):
            first = g * GROUP
            pieces = []
            for c in range(chunks):
                wanted = (target_ref[c:c + 1, :] - first * CAP).astype(jnp.int32)
                wanted = jnp.broadcast_to(wanted, (16, LANES)).astype(jnp.int16)
                wanted = jnp.concatenate([wanted] * (GROUP * CAP // 16), 0)
                pieces.append(jnp.where(wanted == place, jnp.ones((), jnp.bfloat16), jnp.zeros((), jnp.bfloat16)))
            pick = jnp.concatenate(pieces, 1)
            rows = jnp.dot(pick, yb_ref[...], preferred_element_type=jnp.float32).astype(jnp.bfloat16)
            for j in range(GROUP):
                base = pl.multiple_of((first + j) * SPAN, 16)
                rows_ref[pl.ds(base, CAP), :] = rows[j * CAP:(j + 1) * CAP]
                notes = jnp.concatenate([common, list_ref[pl.ds(first + j, 1), :]], 0)
                rows_ref[pl.ds(pl.multiple_of(base + CAP, 16), NOTES), :] = notes.astype(jnp.bfloat16)
            at = pl.ds(pl.multiple_of(g * (GROUP * SPAN), 16), GROUP * SPAN)
            return pltpu.make_async_copy(rows_ref.at[at], rows_hbm.at[at], sem.at[g])

        groups = width // GROUP
        if groups <= 4:
            copies = []
            for g in range(groups):
                copies.append(sort_group(g))
                copies[g].start()
            for copy in copies:
                copy.wait()
        else:

            @pl.loop(0, groups)
            def _(g):
                copy = sort_group(g)
                copy.start()
                copy.wait()

        mean_copy.wait()


def project_and_sort(width, embeddings, basis, list_owner, list_slot):
    rows_here, wide = embeddings.shape
    feats = basis.shape[1]
    lanes = rows_here // LANES
    slots = width * SPAN
    return pl.pallas_call(
        functools.partial(rows_kernel, width),
        grid=(rows_here // CHUNK,),
        in_specs=[pl.BlockSpec(memory_space=pl.ANY)] * 4,
        out_specs=[pl.BlockSpec(memory_space=pl.ANY)] * 2,
        out_shape=[
            jax.ShapeDtypeStruct((slots, feats), jnp.bfloat16),
            jax.ShapeDtypeStruct((1, wide), jnp.float32),
        ],
        scratch_shapes=[
            pltpu.VMEM((lanes, LANES), jnp.int32),
            pltpu.VMEM((lanes, LANES), jnp.int32),
            pltpu.VMEM((1, wide), jnp.float32),
            pltpu.VMEM((wide, feats), jnp.bfloat16),
            pltpu.VMEM((rows_here, wide), jnp.bfloat16),
            pltpu.VMEM((slots, feats), jnp.bfloat16),
            pltpu.VMEM((rows_here, feats), jnp.float32),
            pltpu.VMEM((rows_here, feats), jnp.bfloat16),
            pltpu.VMEM((8, feats), jnp.float32),
            pltpu.VMEM((8, wide), jnp.float32),
            pltpu.VMEM((lanes, LANES), jnp.int32),
            pltpu.VMEM((width, 2 * CAP), jnp.float32),
            pltpu.SemaphoreType.DMA((rows_here // CHUNK,)),
            pltpu.SemaphoreType.DMA((4,)),
            pltpu.SemaphoreType.DMA((width // GROUP,)),
        ],
        compiler_params=pltpu.CompilerParams(vmem_limit_bytes=VMEM_ALL),
        cost_estimate=pl.CostEstimate(
            flops=2 * rows_here * feats * (wide + slots), bytes_accessed=2 * rows_here * wide + 2 * slots * feats, transcendentals=0
        ),
        name="project_sort",
    )(embeddings, basis, list_owner.reshape(lanes, LANES), list_slot.reshape(lanes, LANES))


def moments_kernel(width, me_ref, mean_hbm, e_hbm, keep_ref, send_ref, e_ref, mean_ref, m_ref, sem, mean_sem):
    rows_here, wide = e_ref.shape
    block = wide // width
    bits = width.bit_length() - 1
    tiles = wide // TILE
    mean_copy = pltpu.make_async_copy(mean_hbm, mean_ref, mean_sem)
    mean_copy.start()
    copies = []
    for c in range(rows_here // CHUNK):
        at = pl.ds(c * CHUNK, CHUNK)
        copies.append(pltpu.make_async_copy(e_hbm.at[at], e_ref.at[at], sem.at[c]))
        copies[c].start()
    me = me_ref[0]
    odd = (me & 1) == 1
    mean_copy.wait()
    mean = mean_ref[...]
    for t in range(tiles):
        rows, columns = slice(t * TILE, (t + 1) * TILE), slice(t * TILE, wide)
        if t == 0:
            product = jnp.zeros((TILE, wide), jnp.float32)
            for c in range(rows_here // CHUNK):
                copies[c].wait()
                at = slice(c * CHUNK, (c + 1) * CHUNK)
                product = product + lax.dot_general(
                    e_ref[at, rows], e_ref[at, :], (((0,), (0,)), ((), ())), preferred_element_type=jnp.float32
                )
        else:
            product = lax.dot_general(
                e_ref[:, rows], e_ref[:, columns], (((0,), (0,)), ((), ())), preferred_element_type=jnp.float32
            )
        down = jnp.transpose(jnp.broadcast_to(mean[:, rows] * rows_here, (LANES, TILE)))
        for u in range(t, tiles):
            pieces = []
            for j in range(u * TILE // LANES, (u + 1) * TILE // LANES):
                across = slice(j * LANES, (j + 1) * LANES)
                within = slice(j * LANES - t * TILE, (j + 1) * LANES - t * TILE)
                pieces.append((product[:, within] - down * mean[:, across]).astype(jnp.bfloat16))
            piece = jnp.concatenate(pieces, 1)
            other = slice(u * TILE, (u + 1) * TILE)
            m_ref[rows, other] = piece
            if u > t:
                m_ref[other, rows] = jnp.transpose(piece)
        for pair in range(TILE // block // 2):
            first = t * (TILE // block) + 2 * pair
            apart = (first ^ me) >> 1
            place = 0
            for k in range(bits - 1):
                place = place + (((apart >> k) & 1) << (bits - 2 - k))
            to = pl.ds(pl.multiple_of(place * block, block), block)
            even_rows = m_ref[first * block:(first + 1) * block, :]
            odd_rows = m_ref[(first + 1) * block:(first + 2) * block, :]
            keep_ref[to, :] = jnp.where(odd, odd_rows, even_rows)
            send_ref[to, :] = jnp.where(odd, even_rows, odd_rows)


def moments(width, me, embeddings, mean):
    rows_here, wide = embeddings.shape
    vmem = pl.BlockSpec(memory_space=pltpu.VMEM)
    return pl.pallas_call(
        functools.partial(moments_kernel, width),
        in_specs=[pl.BlockSpec(memory_space=pltpu.SMEM)] + [pl.BlockSpec(memory_space=pl.ANY)] * 2,
        out_specs=[vmem] * 2,
        out_shape=[
            jax.ShapeDtypeStruct((wide // 2, wide), jnp.bfloat16),
            jax.ShapeDtypeStruct((wide // 2, wide), jnp.bfloat16),
        ],
        scratch_shapes=[
            pltpu.VMEM((rows_here, wide), jnp.bfloat16),
            pltpu.VMEM((1, wide), jnp.float32),
            pltpu.VMEM((wide, wide), jnp.bfloat16),
            pltpu.SemaphoreType.DMA((rows_here // CHUNK,)),
            pltpu.SemaphoreType.DMA,
        ],
        compiler_params=pltpu.CompilerParams(vmem_limit_bytes=VMEM_MOST),
        cost_estimate=pl.CostEstimate(
            flops=2 * rows_here * wide * wide, bytes_accessed=2 * rows_here * wide + 3 * wide * wide, transcendentals=0
        ),
        name="moments",
    )(me.reshape(1), mean, embeddings)


def add_kernel(shares, pieces, keep_ref, *refs):
    outs = refs[len(refs) - shares * pieces:]
    came = refs[:len(refs) - shares * pieces]
    rows, columns = outs[0].shape
    for h in range(shares):
        across = slice(h * columns, (h + 1) * columns)
        for p in range(pieces):
            at = slice(p * rows, (p + 1) * rows)
            held = keep_ref[at, across].astype(jnp.float32)
            for ref in came:
                held = held + ref[at, across].astype(jnp.float32)
            out = outs[h * pieces + p]
            out[...] = held.astype(out.dtype)


def add_and_split(keep, came, shares, pieces):
    rows, columns = keep.shape
    vmem = pl.BlockSpec(memory_space=pltpu.VMEM)
    shape = (rows // pieces, columns // shares)
    kinds = [jnp.float32] + [jnp.bfloat16] * (pieces - 1)
    outs = pl.pallas_call(
        functools.partial(add_kernel, shares, pieces),
        in_specs=[vmem] * (1 + len(came)),
        out_specs=[vmem] * (shares * pieces),
        out_shape=[jax.ShapeDtypeStruct(shape, kind) for kind in kinds * shares],
        compiler_params=pltpu.CompilerParams(vmem_limit_bytes=VMEM_SOME),
        cost_estimate=pl.CostEstimate(flops=2 * rows * columns, bytes_accessed=10 * rows * columns, transcendentals=0),
        name="add_and_split",
    )(keep, *came)
    return [outs[h * pieces:(h + 1) * pieces] for h in range(shares)]


def finish_kernel(total, between_ref, *refs):
    out_ref = refs[-1]
    each = (len(refs) - 1) // SHARES
    columns = out_ref.shape[1] // SHARES
    for h in range(SHARES):
        across = slice(h * columns, (h + 1) * columns)
        held = refs[h * each][...]
        for ref in refs[h * each + 1:(h + 1) * each]:
            held = held + ref[...].astype(jnp.float32)
        out_ref[:, across] = (held + between_ref[:, across]) / total


def finish(total, between, keeps, came):
    parts = [part for keep, pieces in zip(keeps, came) for part in (keep, *pieces)]
    vmem = pl.BlockSpec(memory_space=pltpu.VMEM)
    return pl.pallas_call(
        functools.partial(finish_kernel, total),
        in_specs=[vmem] * (1 + len(parts)),
        out_specs=vmem,
        out_shape=jax.ShapeDtypeStruct(between.shape, jnp.float32),
        compiler_params=pltpu.CompilerParams(vmem_limit_bytes=VMEM_SOME),
        cost_estimate=pl.CostEstimate(flops=8 * between.size, bytes_accessed=16 * between.size, transcendentals=0),
        name="finish",
    )(between, *parts)


def halving_stages(width):
    strides = [1 << k for k in range(width.bit_length() - 1)]
    return [[s] for s in strides[:-2]] + [strides[-2:]]


def exchange(width, stage, out):
    came = []
    for p in range(1, 1 << len(stage)):
        apart = sum(s for k, s in enumerate(stage) if (p >> (len(stage) - 1 - k)) & 1)
        came.append(lax.ppermute(out[p - 1], "wide", [(i, i ^ apart) for i in range(width)]))
    return came


def encode_kernel(total, me_ref, got_ref, basis_ref, centroid_ref, rotation_ref, *refs):
    out_hbm, between_ref, out_ref, delta_ref, list_ref, apart_ref, sem = refs[-7:]
    width = delta_ref.shape[0]
    feats = out_ref.shape[1]
    owned = centroid_ref.shape[0]
    wide = basis_ref.shape[0]
    block = wide // width
    share = total // width

    notes = jnp.concatenate([got_ref[s * SPAN + CAP:(s + 1) * SPAN, :] for s in range(width)], 0)
    size = width * NOTES
    to = lax.broadcasted_iota(jnp.int32, (size, size), 0)
    of = lax.broadcasted_iota(jnp.int32, (size, size), 1)
    turn = jnp.where((to % width) * NOTES + to // width == of, 1.0, 0.0).astype(jnp.bfloat16)
    turned = jnp.dot(turn, notes, preferred_element_type=jnp.float32)
    row = [turned[r * width:(r + 1) * width] for r in range(NOTES)]
    digits = row[NOTES - 1]
    list_ref[...] = digits[:, :CAP] * 32.0 + digits[:, CAP:] - 1.0
    quarters = wide // feats
    shifts = jnp.zeros((width, feats), jnp.float32)
    for q in range(quarters):
        parts = [row[p * quarters + q] for p in range(3)]
        mean = parts[0] + (parts[1] + parts[2])
        apart_ref[:, q * feats:(q + 1) * feats] = mean - jnp.mean(mean, 0, keepdims=True)
        terms = jnp.dot(
            jnp.concatenate(parts, 0).astype(jnp.bfloat16),
            basis_ref[q * feats:(q + 1) * feats, :],
            preferred_element_type=jnp.float32,
        )
        shifts = shifts + (terms[:width] + (terms[width:2 * width] + terms[2 * width:]))
    square = row[3 * quarters] + (row[3 * quarters + 1] + row[3 * quarters + 2])
    delta = shifts - jnp.mean(shifts, 0, keepdims=True)
    variance = jnp.sum(square + share * (delta * delta), 0, keepdims=True) / total
    scale = lax.rsqrt(variance + 1e-05)
    delta_ref[...] = delta

    names = lax.broadcasted_iota(jnp.int32, (CAP, owned), 1).astype(jnp.int16)

    def encode_group(g):
        columns = jnp.transpose(list_ref[pl.ds(g * GROUP, GROUP), :])
        hits, projected, held = [], [], []
        for s in range(GROUP):
            listed = jnp.broadcast_to(columns[:, s:s + 1], (CAP, LANES))
            held.append(jnp.concatenate([listed] * (feats // LANES), 1) >= 0)
            wanted = jnp.concatenate([listed.astype(jnp.int32).astype(jnp.int16)] * (owned // LANES), 1)
            hits.append(jnp.where(wanted == names, jnp.ones((), jnp.bfloat16), jnp.zeros((), jnp.bfloat16)))
            base = pl.multiple_of((g * GROUP + s) * SPAN, 16)
            rows = got_ref[pl.ds(base, CAP), :].astype(jnp.float32)
            projected.append((rows + delta_ref[pl.ds(g * GROUP + s, 1), :]) * scale)
        centre = jnp.dot(jnp.concatenate(hits, 0), centroid_ref[...], preferred_element_type=jnp.float32)
        residual = jnp.where(jnp.concatenate(held, 0), jnp.concatenate(projected, 0) - centre, 0.0)
        at = pl.ds(pl.multiple_of(g * (GROUP * CAP), GROUP * CAP), GROUP * CAP)
        out_ref[at, :] = jnp.dot(
            residual.astype(jnp.bfloat16), rotation_ref[...], preferred_element_type=jnp.float32
        ).astype(jnp.bfloat16)
        copies = []
        for s in range(GROUP):
            place = g * GROUP + s
            here = pl.ds(pl.multiple_of(place * CAP, CAP), CAP)
            there = pl.ds(pl.multiple_of(device_at(width, place) * CAP, CAP), CAP)
            copies.append(pltpu.make_async_copy(out_ref.at[here], out_hbm.at[there], sem.at[place]))
        return copies

    groups = width // GROUP
    copies = []
    if groups <= 4:
        for g in range(groups):
            for copy in encode_group(g):
                copy.start()
                copies.append(copy)
    else:

        @pl.loop(0, groups)
        def _(g):
            for copy in encode_group(g):
                copy.start()
            for s in range(GROUP):
                at = pl.ds(pl.multiple_of((g * GROUP + s) * CAP, CAP), CAP)
                pltpu.make_async_copy(out_ref.at[at], out_hbm.at[at], sem.at[g * GROUP + s]).wait()

    first = me_ref[0] * block
    near = apart_ref[:, pl.ds(pl.multiple_of(first // LANES * LANES, LANES), LANES)]
    near = pltpu.roll(near, (LANES - first % LANES) % LANES, 1)[:, :block]
    between_ref[...] = share * lax.dot_general(
        near,
        apart_ref[...],
        (((0,), (0,)), ((), ())),
        precision=lax.Precision.HIGHEST,
        preferred_element_type=jnp.float32,
    )
    for copy in copies:
        copy.wait()


def encode(width, total, me, got, basis, centroids, rotation, after):
    wide, feats = basis.shape
    owned = centroids.shape[0]
    slots = width * CAP
    vmem, anywhere = pl.BlockSpec(memory_space=pltpu.VMEM), pl.BlockSpec(memory_space=pl.ANY)
    return pl.pallas_call(
        functools.partial(encode_kernel, total),
        in_specs=[pl.BlockSpec(memory_space=pltpu.SMEM)] + [vmem] * 4 + [anywhere] * len(after),
        out_specs=[anywhere, vmem],
        out_shape=[
            jax.ShapeDtypeStruct((slots, feats), jnp.bfloat16),
            jax.ShapeDtypeStruct((wide // width, wide), jnp.float32),
        ],
        scratch_shapes=[
            pltpu.VMEM((slots, feats), jnp.bfloat16),
            pltpu.VMEM((width, feats), jnp.float32),
            pltpu.VMEM((width, CAP), jnp.float32),
            pltpu.VMEM((width, wide), jnp.float32),
            pltpu.SemaphoreType.DMA((width,)),
        ],
        compiler_params=pltpu.CompilerParams(vmem_limit_bytes=VMEM_SOME),
        cost_estimate=pl.CostEstimate(
            flops=2 * slots * feats * (owned + feats), bytes_accessed=4 * slots * feats, transcendentals=0
        ),
        name="encode",
    )(me.reshape(1), got, basis, centroids, rotation, *after)


def local(embeddings, basis, list_owner, list_slot, centroids, rotation):
    width = lax.axis_size("wide")
    me = lax.axis_index("wide")
    rows_here, wide = embeddings.shape
    feats = basis.shape[1]
    total = rows_here * width

    rows, mean = project_and_sort(width, embeddings, basis, list_owner, list_slot)
    order = [[device_at(width, place) for place in range(width)]]
    got = lax.all_to_all(
        rows.reshape(width, SPAN, feats), "wide", split_axis=0, concat_axis=0, tiled=True, axis_index_groups=order
    )

    keep, send = moments(width, me, embeddings, mean)
    stages = halving_stages(width)
    came = exchange(width, stages[0], [send])
    shares = add_and_split(keep, came, SHARES, 1 << len(stages[1]))
    last = []
    for share in shares:
        for n in range(1, len(stages) - 1):
            came = exchange(width, stages[n], share[1:])
            (share,) = add_and_split(share[0], came, 1, 1 << len(stages[n + 1]))
        last.append(share)
    came = [exchange(width, stages[-1], share[1:]) for share in last]
    encoded, between = encode(
        width, total, me, got.reshape(width * SPAN, feats), basis, centroids, rotation, [share[1] for share in last]
    )
    covariance = finish(total, between, [share[0] for share in last], came)
    return (encoded, covariance)


def solution(mesh):
    in_specs = (
        P(("groups", "wide"), None),
        P(),
        P(("groups", "wide")),
        P(("groups", "wide")),
        P("wide", None),
        P(),
    )
    out_specs = (P(("groups", "wide"), None), P(("groups", "wide"), None))
    return jax.shard_map(local, mesh=mesh, in_specs=in_specs, out_specs=out_specs, check_vma=False)
```

```python
import functools

import jax
import jax.numpy as jnp
from jax import lax
from jax.experimental import pallas as pl
from jax.experimental.pallas import tpu as pltpu
from jax.sharding import PartitionSpec as P

CAP = 128
LANES = 128
NOTES = 16
SPAN = CAP + NOTES
CHUNK = 512
TILE = 256
GROUP = 4
SHARES = 2
PLANE = 4
VMEM_ALL = 60 * 1024 * 1024
VMEM_SOME = 24 * 1024 * 1024
VMEM_MOST = 48 * 1024 * 1024


def place_of(width, device):
    return (device & (PLANE - 1)) * (width // PLANE) + device // PLANE


def device_at(width, place):
    return (place & (width // PLANE - 1)) * PLANE + place // (width // PLANE)


def in_three(x):
    high = x.astype(jnp.bfloat16).astype(jnp.float32)
    rest = x - high
    middle = rest.astype(jnp.bfloat16).astype(jnp.float32)
    return high, middle, (rest - middle).astype(jnp.bfloat16).astype(jnp.float32)


def rows_kernel(
    width, e_hbm, basis_hbm, owner_hbm, slot_hbm,
    rows_hbm, mean_hbm,
    owner_ref, slot_ref, mean_ref, basis_ref, e_ref, rows_ref, y_ref, yb_ref, sum_ref, total_ref, target_ref, list_ref, e_sem, small_sem, sem,
):
    step = pl.program_id(0)
    rows_here, feats = y_ref.shape
    wide = e_ref.shape[1]
    chunks = rows_here // LANES

    def e_copy(c):
        at = pl.ds(pl.multiple_of(c * CHUNK, CHUNK), CHUNK)
        return pltpu.make_async_copy(e_hbm.at[at], e_ref.at[at], e_sem.at[c])

    @pl.when(step == 0)
    def _():
        owner_copy = pltpu.make_async_copy(owner_hbm, owner_ref, small_sem.at[0])
        slot_copy = pltpu.make_async_copy(slot_hbm, slot_ref, small_sem.at[1])
        basis_copy = pltpu.make_async_copy(basis_hbm, basis_ref, small_sem.at[2])
        owner_copy.start()
        e_copy(0).start()
        slot_copy.start()
        basis_copy.start()
        for c in range(1, rows_here // CHUNK):
            e_copy(c).start()
        owner_copy.wait()
        sum_ref[...] = jnp.zeros_like(sum_ref)
        total_ref[...] = jnp.zeros_like(total_ref)
        owner = place_of(width, owner_ref[...])
        wanted = lax.broadcasted_iota(jnp.int32, (width, LANES), 0)
        hits = [jnp.where(owner[c:c + 1, :] == wanted, 1.0, 0.0) for c in range(chunks)]
        flat = jnp.concatenate(hits, 0).astype(jnp.bfloat16)
        up = lax.broadcasted_iota(jnp.int32, (LANES, LANES), 0)
        to = lax.broadcasted_iota(jnp.int32, (LANES, LANES), 1)
        before = jnp.where(up < to, 1.0, 0.0).astype(jnp.bfloat16)
        every = jnp.ones((LANES, LANES), jnp.bfloat16)
        within = jnp.dot(flat, before, preferred_element_type=jnp.float32)
        counts = jnp.dot(flat, every, preferred_element_type=jnp.float32)
        carry = jnp.zeros((width, LANES), jnp.float32)
        ranks = []
        for c in range(chunks):
            at = slice(c * width, (c + 1) * width)
            ranks.append(jnp.sum(hits[c] * (within[at] + carry), 0, keepdims=True).astype(jnp.int32))
            carry = carry + counts[at]
            target_ref[c:c + 1, :] = owner[c:c + 1, :] * CAP + ranks[c]

        slot_copy.wait()
        slot = slot_ref[...] + 1
        high, low = (slot >> 5).astype(jnp.float32), (slot & 31).astype(jnp.float32)
        spots = lax.broadcasted_iota(jnp.int32, (CAP, LANES), 0)
        placed = jnp.concatenate([jnp.where(ranks[c] == spots, 1.0, 0.0) for c in range(chunks)], 1).astype(jnp.bfloat16)
        digits = jnp.concatenate(
            [
                jnp.concatenate([hits[c] * high[c:c + 1, :] for c in range(chunks)], 1),
                jnp.concatenate([hits[c] * low[c:c + 1, :] for c in range(chunks)], 1),
            ],
            0,
        ).astype(jnp.bfloat16)
        found = lax.dot_general(digits, placed, (((1,), (1,)), ((), ())), preferred_element_type=jnp.float32)
        list_ref[:, :CAP] = found[:width]
        list_ref[:, CAP:] = found[width:]
        basis_copy.wait()

    e_copy(step).wait()
    here = pl.ds(pl.multiple_of(step * CHUNK, CHUNK), CHUNK)
    rows = e_ref[here, :]
    y = jnp.dot(rows, basis_ref[...], preferred_element_type=jnp.float32)
    y_ref[here, :] = y
    sum_ref[...] += jnp.sum(y.reshape(CHUNK // 8, 8, feats), 0)
    total_ref[...] += jnp.sum(rows.astype(jnp.float32).reshape(CHUNK // 8, 8, wide), 0)

    @pl.when(step == pl.num_programs(0) - 1)
    def _():
        mean_y = jnp.sum(sum_ref[...], 0, keepdims=True) / rows_here
        square = jnp.zeros((8, feats), jnp.float32)
        for c in range(rows_here // CHUNK):
            at = slice(c * CHUNK, (c + 1) * CHUNK)
            centred = y_ref[at, :] - mean_y
            square = square + jnp.sum((centred * centred).reshape(CHUNK // 8, 8, feats), 0)
            yb_ref[at, :] = centred.astype(jnp.bfloat16)
        mean = jnp.sum(total_ref[...], 0, keepdims=True) / rows_here
        mean_ref[...] = mean
        mean_copy = pltpu.make_async_copy(mean_ref, mean_hbm, small_sem.at[3])
        mean_copy.start()
        parts = in_three(mean)
        common = [part[:, q * feats:(q + 1) * feats] for part in parts for q in range(wide // feats)]
        common = jnp.concatenate(common + list(in_three(jnp.sum(square, 0, keepdims=True))), 0)

        place = lax.broadcasted_iota(jnp.int32, (GROUP * CAP, LANES), 0).astype(jnp.int16)

        def sort_group(g):
            first = g * GROUP
            pieces = []
            for c in range(chunks):
                wanted = (target_ref[c:c + 1, :] - first * CAP).astype(jnp.int32)
                wanted = jnp.broadcast_to(wanted, (16, LANES)).astype(jnp.int16)
                wanted = jnp.concatenate([wanted] * (GROUP * CAP // 16), 0)
                pieces.append(jnp.where(wanted == place, jnp.ones((), jnp.bfloat16), jnp.zeros((), jnp.bfloat16)))
            pick = jnp.concatenate(pieces, 1)
            rows = jnp.dot(pick, yb_ref[...], preferred_element_type=jnp.float32).astype(jnp.bfloat16)
            for j in range(GROUP):
                base = pl.multiple_of((first + j) * SPAN, 16)
                rows_ref[pl.ds(base, CAP), :] = rows[j * CAP:(j + 1) * CAP]
                notes = jnp.concatenate([common, list_ref[pl.ds(first + j, 1), :]], 0)
                rows_ref[pl.ds(pl.multiple_of(base + CAP, 16), NOTES), :] = notes.astype(jnp.bfloat16)
            at = pl.ds(pl.multiple_of(g * (GROUP * SPAN), 16), GROUP * SPAN)
            return pltpu.make_async_copy(rows_ref.at[at], rows_hbm.at[at], sem.at[g])

        groups = width // GROUP
        if groups <= 4:
            copies = []
            for g in range(groups):
                copies.append(sort_group(g))
                copies[g].start()
            for copy in copies:
                copy.wait()
        else:

            @pl.loop(0, groups)
            def _(g):
                copy = sort_group(g)
                copy.start()
                copy.wait()

        mean_copy.wait()


def project_and_sort(width, embeddings, basis, list_owner, list_slot):
    rows_here, wide = embeddings.shape
    feats = basis.shape[1]
    lanes = rows_here // LANES
    slots = width * SPAN
    return pl.pallas_call(
        functools.partial(rows_kernel, width),
        grid=(rows_here // CHUNK,),
        in_specs=[pl.BlockSpec(memory_space=pl.ANY)] * 4,
        out_specs=[pl.BlockSpec(memory_space=pl.ANY)] * 2,
        out_shape=[
            jax.ShapeDtypeStruct((slots, feats), jnp.bfloat16),
            jax.ShapeDtypeStruct((1, wide), jnp.float32),
        ],
        scratch_shapes=[
            pltpu.VMEM((lanes, LANES), jnp.int32),
            pltpu.VMEM((lanes, LANES), jnp.int32),
            pltpu.VMEM((1, wide), jnp.float32),
            pltpu.VMEM((wide, feats), jnp.bfloat16),
            pltpu.VMEM((rows_here, wide), jnp.bfloat16),
            pltpu.VMEM((slots, feats), jnp.bfloat16),
            pltpu.VMEM((rows_here, feats), jnp.float32),
            pltpu.VMEM((rows_here, feats), jnp.bfloat16),
            pltpu.VMEM((8, feats), jnp.float32),
            pltpu.VMEM((8, wide), jnp.float32),
            pltpu.VMEM((lanes, LANES), jnp.int32),
            pltpu.VMEM((width, 2 * CAP), jnp.float32),
            pltpu.SemaphoreType.DMA((rows_here // CHUNK,)),
            pltpu.SemaphoreType.DMA((4,)),
            pltpu.SemaphoreType.DMA((width // GROUP,)),
        ],
        compiler_params=pltpu.CompilerParams(vmem_limit_bytes=VMEM_ALL),
        cost_estimate=pl.CostEstimate(
            flops=2 * rows_here * feats * (wide + slots), bytes_accessed=2 * rows_here * wide + 2 * slots * feats, transcendentals=0
        ),
        name="project_sort",
    )(embeddings, basis, list_owner.reshape(lanes, LANES), list_slot.reshape(lanes, LANES))


def moments_kernel(width, me_ref, mean_hbm, e_hbm, keep_ref, send_ref, e_ref, mean_ref, m_ref, sem, mean_sem):
    rows_here, wide = e_ref.shape
    block = wide // width
    bits = width.bit_length() - 1
    tiles = wide // TILE
    mean_copy = pltpu.make_async_copy(mean_hbm, mean_ref, mean_sem)
    mean_copy.start()
    copies = []
    for c in range(rows_here // CHUNK):
        at = pl.ds(c * CHUNK, CHUNK)
        copies.append(pltpu.make_async_copy(e_hbm.at[at], e_ref.at[at], sem.at[c]))
        copies[c].start()
    me = me_ref[0]
    odd = (me & 1) == 1
    mean_copy.wait()
    mean = mean_ref[...]
    for t in range(tiles):
        rows, columns = slice(t * TILE, (t + 1) * TILE), slice(t * TILE, wide)
        if t == 0:
            product = jnp.zeros((TILE, wide), jnp.float32)
            for c in range(rows_here // CHUNK):
                copies[c].wait()
                at = slice(c * CHUNK, (c + 1) * CHUNK)
                product = product + lax.dot_general(
                    e_ref[at, rows], e_ref[at, :], (((0,), (0,)), ((), ())), preferred_element_type=jnp.float32
                )
        else:
            product = lax.dot_general(
                e_ref[:, rows], e_ref[:, columns], (((0,), (0,)), ((), ())), preferred_element_type=jnp.float32
            )
        down = jnp.transpose(jnp.broadcast_to(mean[:, rows] * rows_here, (LANES, TILE)))
        for u in range(t, tiles):
            pieces = []
            for j in range(u * TILE // LANES, (u + 1) * TILE // LANES):
                across = slice(j * LANES, (j + 1) * LANES)
                within = slice(j * LANES - t * TILE, (j + 1) * LANES - t * TILE)
                pieces.append((product[:, within] - down * mean[:, across]).astype(jnp.bfloat16))
            piece = jnp.concatenate(pieces, 1)
            other = slice(u * TILE, (u + 1) * TILE)
            m_ref[rows, other] = piece
            if u > t:
                m_ref[other, rows] = jnp.transpose(piece)
        for pair in range(TILE // block // 2):
            first = t * (TILE // block) + 2 * pair
            apart = (first ^ me) >> 1
            place = 0
            for k in range(bits - 1):
                place = place + (((apart >> k) & 1) << (bits - 2 - k))
            to = pl.ds(pl.multiple_of(place * block, block), block)
            even_rows = m_ref[first * block:(first + 1) * block, :]
            odd_rows = m_ref[(first + 1) * block:(first + 2) * block, :]
            keep_ref[to, :] = jnp.where(odd, odd_rows, even_rows)
            send_ref[to, :] = jnp.where(odd, even_rows, odd_rows)


def moments(width, me, embeddings, mean):
    rows_here, wide = embeddings.shape
    vmem = pl.BlockSpec(memory_space=pltpu.VMEM)
    return pl.pallas_call(
        functools.partial(moments_kernel, width),
        in_specs=[pl.BlockSpec(memory_space=pltpu.SMEM)] + [pl.BlockSpec(memory_space=pl.ANY)] * 2,
        out_specs=[vmem] * 2,
        out_shape=[
            jax.ShapeDtypeStruct((wide // 2, wide), jnp.bfloat16),
            jax.ShapeDtypeStruct((wide // 2, wide), jnp.bfloat16),
        ],
        scratch_shapes=[
            pltpu.VMEM((rows_here, wide), jnp.bfloat16),
            pltpu.VMEM((1, wide), jnp.float32),
            pltpu.VMEM((wide, wide), jnp.bfloat16),
            pltpu.SemaphoreType.DMA((rows_here // CHUNK,)),
            pltpu.SemaphoreType.DMA,
        ],
        compiler_params=pltpu.CompilerParams(vmem_limit_bytes=VMEM_MOST),
        cost_estimate=pl.CostEstimate(
            flops=2 * rows_here * wide * wide, bytes_accessed=2 * rows_here * wide + 3 * wide * wide, transcendentals=0
        ),
        name="moments",
    )(me.reshape(1), mean, embeddings)


def add_kernel(shares, pieces, keep_ref, *refs):
    outs = refs[len(refs) - shares * pieces:]
    came = refs[:len(refs) - shares * pieces]
    rows, columns = outs[0].shape
    for h in range(shares):
        across = slice(h * columns, (h + 1) * columns)
        for p in range(pieces):
            at = slice(p * rows, (p + 1) * rows)
            held = keep_ref[at, across].astype(jnp.float32)
            for ref in came:
                held = held + ref[at, across].astype(jnp.float32)
            out = outs[h * pieces + p]
            out[...] = held.astype(out.dtype)


def add_and_split(keep, came, shares, pieces):
    rows, columns = keep.shape
    vmem = pl.BlockSpec(memory_space=pltpu.VMEM)
    shape = (rows // pieces, columns // shares)
    kinds = [jnp.float32] + [jnp.bfloat16] * (pieces - 1)
    outs = pl.pallas_call(
        functools.partial(add_kernel, shares, pieces),
        in_specs=[vmem] * (1 + len(came)),
        out_specs=[vmem] * (shares * pieces),
        out_shape=[jax.ShapeDtypeStruct(shape, kind) for kind in kinds * shares],
        compiler_params=pltpu.CompilerParams(vmem_limit_bytes=VMEM_SOME),
        cost_estimate=pl.CostEstimate(flops=2 * rows * columns, bytes_accessed=10 * rows * columns, transcendentals=0),
        name="add_and_split",
    )(keep, *came)
    return [outs[h * pieces:(h + 1) * pieces] for h in range(shares)]


def finish_kernel(total, between_ref, *refs):
    out_ref = refs[-1]
    each = (len(refs) - 1) // SHARES
    columns = out_ref.shape[1] // SHARES
    for h in range(SHARES):
        across = slice(h * columns, (h + 1) * columns)
        held = refs[h * each][...]
        for ref in refs[h * each + 1:(h + 1) * each]:
            held = held + ref[...].astype(jnp.float32)
        out_ref[:, across] = (held + between_ref[:, across]) / total


def finish(total, between, keeps, came):
    parts = [part for keep, pieces in zip(keeps, came) for part in (keep, *pieces)]
    vmem = pl.BlockSpec(memory_space=pltpu.VMEM)
    return pl.pallas_call(
        functools.partial(finish_kernel, total),
        in_specs=[vmem] * (1 + len(parts)),
        out_specs=vmem,
        out_shape=jax.ShapeDtypeStruct(between.shape, jnp.float32),
        compiler_params=pltpu.CompilerParams(vmem_limit_bytes=VMEM_SOME),
        cost_estimate=pl.CostEstimate(flops=8 * between.size, bytes_accessed=16 * between.size, transcendentals=0),
        name="finish",
    )(between, *parts)


def halving_stages(width):
    strides = [1 << k for k in range(width.bit_length() - 1)]
    return [[s] for s in strides[:-2]] + [strides[-2:]]


def exchange(width, stage, out):
    came = []
    for p in (2, 1, 3) if len(stage) == 2 else (1,):
        apart = sum(s for k, s in enumerate(stage) if (p >> (len(stage) - 1 - k)) & 1)
        came.append(lax.ppermute(out[p - 1], "wide", [(i, i ^ apart) for i in range(width)]))
    return came


def encode_kernel(total, me_ref, got_ref, basis_ref, centroid_ref, rotation_ref, *refs):
    out_hbm, between_ref, out_ref, delta_ref, list_ref, apart_ref, sem = refs[-7:]
    width = delta_ref.shape[0]
    feats = out_ref.shape[1]
    owned = centroid_ref.shape[0]
    wide = basis_ref.shape[0]
    block = wide // width
    share = total // width

    notes = jnp.concatenate([got_ref[s * SPAN + CAP:(s + 1) * SPAN, :] for s in range(width)], 0)
    size = width * NOTES
    to = lax.broadcasted_iota(jnp.int32, (size, size), 0)
    of = lax.broadcasted_iota(jnp.int32, (size, size), 1)
    turn = jnp.where((to % width) * NOTES + to // width == of, 1.0, 0.0).astype(jnp.bfloat16)
    turned = jnp.dot(turn, notes, preferred_element_type=jnp.float32)
    row = [turned[r * width:(r + 1) * width] for r in range(NOTES)]
    digits = row[NOTES - 1]
    list_ref[...] = digits[:, :CAP] * 32.0 + digits[:, CAP:] - 1.0
    quarters = wide // feats
    shifts = jnp.zeros((width, feats), jnp.float32)
    for q in range(quarters):
        parts = [row[p * quarters + q] for p in range(3)]
        mean = parts[0] + (parts[1] + parts[2])
        apart_ref[:, q * feats:(q + 1) * feats] = mean - jnp.mean(mean, 0, keepdims=True)
        terms = jnp.dot(
            jnp.concatenate(parts, 0).astype(jnp.bfloat16),
            basis_ref[q * feats:(q + 1) * feats, :],
            preferred_element_type=jnp.float32,
        )
        shifts = shifts + (terms[:width] + (terms[width:2 * width] + terms[2 * width:]))
    square = row[3 * quarters] + (row[3 * quarters + 1] + row[3 * quarters + 2])
    delta = shifts - jnp.mean(shifts, 0, keepdims=True)
    variance = jnp.sum(square + share * (delta * delta), 0, keepdims=True) / total
    scale = lax.rsqrt(variance + 1e-05)
    delta_ref[...] = delta

    names = lax.broadcasted_iota(jnp.int32, (CAP, owned), 1).astype(jnp.int16)

    def encode_group(g):
        columns = jnp.transpose(list_ref[pl.ds(g * GROUP, GROUP), :])
        hits, projected, held = [], [], []
        for s in range(GROUP):
            listed = jnp.broadcast_to(columns[:, s:s + 1], (CAP, LANES))
            held.append(jnp.concatenate([listed] * (feats // LANES), 1) >= 0)
            wanted = jnp.concatenate([listed.astype(jnp.int32).astype(jnp.int16)] * (owned // LANES), 1)
            hits.append(jnp.where(wanted == names, jnp.ones((), jnp.bfloat16), jnp.zeros((), jnp.bfloat16)))
            base = pl.multiple_of((g * GROUP + s) * SPAN, 16)
            rows = got_ref[pl.ds(base, CAP), :].astype(jnp.float32)
            projected.append((rows + delta_ref[pl.ds(g * GROUP + s, 1), :]) * scale)
        centre = jnp.dot(jnp.concatenate(hits, 0), centroid_ref[...], preferred_element_type=jnp.float32)
        residual = jnp.where(jnp.concatenate(held, 0), jnp.concatenate(projected, 0) - centre, 0.0)
        at = pl.ds(pl.multiple_of(g * (GROUP * CAP), GROUP * CAP), GROUP * CAP)
        out_ref[at, :] = jnp.dot(
            residual.astype(jnp.bfloat16), rotation_ref[...], preferred_element_type=jnp.float32
        ).astype(jnp.bfloat16)
        copies = []
        for s in range(GROUP):
            place = g * GROUP + s
            here = pl.ds(pl.multiple_of(place * CAP, CAP), CAP)
            there = pl.ds(pl.multiple_of(device_at(width, place) * CAP, CAP), CAP)
            copies.append(pltpu.make_async_copy(out_ref.at[here], out_hbm.at[there], sem.at[place]))
        return copies

    groups = width // GROUP
    copies = []
    if groups <= 4:
        for g in range(groups):
            for copy in encode_group(g):
                copy.start()
                copies.append(copy)
    else:

        @pl.loop(0, groups)
        def _(g):
            for copy in encode_group(g):
                copy.start()
            for s in range(GROUP):
                at = pl.ds(pl.multiple_of((g * GROUP + s) * CAP, CAP), CAP)
                pltpu.make_async_copy(out_ref.at[at], out_hbm.at[at], sem.at[g * GROUP + s]).wait()

    first = me_ref[0] * block
    near = apart_ref[:, pl.ds(pl.multiple_of(first // LANES * LANES, LANES), LANES)]
    near = pltpu.roll(near, (LANES - first % LANES) % LANES, 1)[:, :block]
    between_ref[...] = share * lax.dot_general(
        near,
        apart_ref[...],
        (((0,), (0,)), ((), ())),
        precision=lax.Precision.HIGHEST,
        preferred_element_type=jnp.float32,
    )
    for copy in copies:
        copy.wait()


def encode(width, total, me, got, basis, centroids, rotation, after):
    wide, feats = basis.shape
    owned = centroids.shape[0]
    slots = width * CAP
    vmem, anywhere = pl.BlockSpec(memory_space=pltpu.VMEM), pl.BlockSpec(memory_space=pl.ANY)
    return pl.pallas_call(
        functools.partial(encode_kernel, total),
        in_specs=[pl.BlockSpec(memory_space=pltpu.SMEM)] + [vmem] * 4 + [anywhere] * len(after),
        out_specs=[anywhere, vmem],
        out_shape=[
            jax.ShapeDtypeStruct((slots, feats), jnp.bfloat16),
            jax.ShapeDtypeStruct((wide // width, wide), jnp.float32),
        ],
        scratch_shapes=[
            pltpu.VMEM((slots, feats), jnp.bfloat16),
            pltpu.VMEM((width, feats), jnp.float32),
            pltpu.VMEM((width, CAP), jnp.float32),
            pltpu.VMEM((width, wide), jnp.float32),
            pltpu.SemaphoreType.DMA((width,)),
        ],
        compiler_params=pltpu.CompilerParams(vmem_limit_bytes=VMEM_SOME),
        cost_estimate=pl.CostEstimate(
            flops=2 * slots * feats * (owned + feats), bytes_accessed=4 * slots * feats, transcendentals=0
        ),
        name="encode",
    )(me.reshape(1), got, basis, centroids, rotation, *after)


def local(embeddings, basis, list_owner, list_slot, centroids, rotation):
    width = lax.axis_size("wide")
    me = lax.axis_index("wide")
    rows_here, wide = embeddings.shape
    feats = basis.shape[1]
    total = rows_here * width

    rows, mean = project_and_sort(width, embeddings, basis, list_owner, list_slot)
    order = [[device_at(width, place) for place in range(width)]]
    got = lax.all_to_all(
        rows.reshape(width, SPAN, feats), "wide", split_axis=0, concat_axis=0, tiled=True, axis_index_groups=order
    )

    keep, send = moments(width, me, embeddings, mean)
    stages = halving_stages(width)
    came = exchange(width, stages[0], [send])
    shares = add_and_split(keep, came, SHARES, 1 << len(stages[1]))
    last = []
    for share in shares:
        for n in range(1, len(stages) - 1):
            came = exchange(width, stages[n], share[1:])
            (share,) = add_and_split(share[0], came, 1, 1 << len(stages[n + 1]))
        last.append(share)
    came = [exchange(width, stages[-1], share[1:]) for share in last]
    encoded, between = encode(
        width, total, me, got.reshape(width * SPAN, feats), basis, centroids, rotation, [share[1] for share in last]
    )
    covariance = finish(total, between, [share[0] for share in last], came)
    return (encoded, covariance)


def solution(mesh):
    in_specs = (
        P(("groups", "wide"), None),
        P(),
        P(("groups", "wide")),
        P(("groups", "wide")),
        P("wide", None),
        P(),
    )
    out_specs = (P(("groups", "wide"), None), P(("groups", "wide"), None))
    return jax.shard_map(local, mesh=mesh, in_specs=in_specs, out_specs=out_specs, check_vma=False)
```

```python
import functools

import jax
import jax.numpy as jnp
from jax import lax
from jax.experimental import pallas as pl
from jax.experimental.pallas import tpu as pltpu
from jax.sharding import PartitionSpec as P

CAP = 128
LANES = 128
NOTES = 16
SPAN = CAP + NOTES
CHUNK = 512
TILE = 256
GROUP = 4
SHARES = 2
PLANE = 4
VMEM_ALL = 60 * 1024 * 1024
VMEM_SOME = 24 * 1024 * 1024
VMEM_MOST = 48 * 1024 * 1024


def place_of(width, device):
    return (device & (PLANE - 1)) * (width // PLANE) + device // PLANE


def device_at(width, place):
    return (place & (width // PLANE - 1)) * PLANE + place // (width // PLANE)


def in_three(x):
    high = x.astype(jnp.bfloat16).astype(jnp.float32)
    rest = x - high
    middle = rest.astype(jnp.bfloat16).astype(jnp.float32)
    return high, middle, (rest - middle).astype(jnp.bfloat16).astype(jnp.float32)


def rows_kernel(
    width, e_hbm, basis_hbm, owner_hbm, slot_hbm,
    rows_hbm, mean_hbm,
    owner_ref, slot_ref, mean_ref, basis_ref, e_ref, rows_ref, y_ref, yb_ref, sum_ref, total_ref, target_ref, list_ref, e_sem, small_sem, sem,
):
    step = pl.program_id(0)
    rows_here, feats = y_ref.shape
    wide = e_ref.shape[1]
    chunks = rows_here // LANES

    def e_copy(c):
        at = pl.ds(pl.multiple_of(c * CHUNK, CHUNK), CHUNK)
        return pltpu.make_async_copy(e_hbm.at[at], e_ref.at[at], e_sem.at[c])

    @pl.when(step == 0)
    def _():
        owner_copy = pltpu.make_async_copy(owner_hbm, owner_ref, small_sem.at[0])
        slot_copy = pltpu.make_async_copy(slot_hbm, slot_ref, small_sem.at[1])
        basis_copy = pltpu.make_async_copy(basis_hbm, basis_ref, small_sem.at[2])
        owner_copy.start()
        e_copy(0).start()
        slot_copy.start()
        basis_copy.start()
        for c in range(1, rows_here // CHUNK):
            e_copy(c).start()
        owner_copy.wait()
        sum_ref[...] = jnp.zeros_like(sum_ref)
        total_ref[...] = jnp.zeros_like(total_ref)
        owner = place_of(width, owner_ref[...])
        wanted = lax.broadcasted_iota(jnp.int32, (width, LANES), 0)
        hits = [jnp.where(owner[c:c + 1, :] == wanted, 1.0, 0.0) for c in range(chunks)]
        flat = jnp.concatenate(hits, 0).astype(jnp.bfloat16)
        up = lax.broadcasted_iota(jnp.int32, (LANES, LANES), 0)
        to = lax.broadcasted_iota(jnp.int32, (LANES, LANES), 1)
        before = jnp.where(up < to, 1.0, 0.0).astype(jnp.bfloat16)
        every = jnp.ones((LANES, LANES), jnp.bfloat16)
        within = jnp.dot(flat, before, preferred_element_type=jnp.float32)
        counts = jnp.dot(flat, every, preferred_element_type=jnp.float32)
        carry = jnp.zeros((width, LANES), jnp.float32)
        ranks = []
        for c in range(chunks):
            at = slice(c * width, (c + 1) * width)
            ranks.append(jnp.sum(hits[c] * (within[at] + carry), 0, keepdims=True).astype(jnp.int32))
            carry = carry + counts[at]
            target_ref[c:c + 1, :] = owner[c:c + 1, :] * CAP + ranks[c]

        slot_copy.wait()
        slot = slot_ref[...] + 1
        high, low = (slot >> 5).astype(jnp.float32), (slot & 31).astype(jnp.float32)
        spots = lax.broadcasted_iota(jnp.int32, (CAP, LANES), 0)
        placed = jnp.concatenate([jnp.where(ranks[c] == spots, 1.0, 0.0) for c in range(chunks)], 1).astype(jnp.bfloat16)
        digits = jnp.concatenate(
            [
                jnp.concatenate([hits[c] * high[c:c + 1, :] for c in range(chunks)], 1),
                jnp.concatenate([hits[c] * low[c:c + 1, :] for c in range(chunks)], 1),
            ],
            0,
        ).astype(jnp.bfloat16)
        found = lax.dot_general(digits, placed, (((1,), (1,)), ((), ())), preferred_element_type=jnp.float32)
        list_ref[:, :CAP] = found[:width]
        list_ref[:, CAP:] = found[width:]
        basis_copy.wait()

    e_copy(step).wait()
    here = pl.ds(pl.multiple_of(step * CHUNK, CHUNK), CHUNK)
    rows = e_ref[here, :]
    y = jnp.dot(rows, basis_ref[...], preferred_element_type=jnp.float32)
    y_ref[here, :] = y
    sum_ref[...] += jnp.sum(y.reshape(CHUNK // 8, 8, feats), 0)
    total_ref[...] += jnp.sum(rows.astype(jnp.float32).reshape(CHUNK // 8, 8, wide), 0)

    @pl.when(step == pl.num_programs(0) - 1)
    def _():
        mean_y = jnp.sum(sum_ref[...], 0, keepdims=True) / rows_here
        square = jnp.zeros((8, feats), jnp.float32)
        for c in range(rows_here // CHUNK):
            at = slice(c * CHUNK, (c + 1) * CHUNK)
            centred = y_ref[at, :] - mean_y
            square = square + jnp.sum((centred * centred).reshape(CHUNK // 8, 8, feats), 0)
            yb_ref[at, :] = centred.astype(jnp.bfloat16)
        mean = jnp.sum(total_ref[...], 0, keepdims=True) / rows_here
        mean_ref[...] = mean
        mean_copy = pltpu.make_async_copy(mean_ref, mean_hbm, small_sem.at[3])
        mean_copy.start()
        parts = in_three(mean)
        common = [part[:, q * feats:(q + 1) * feats] for part in parts for q in range(wide // feats)]
        common = jnp.concatenate(common + list(in_three(jnp.sum(square, 0, keepdims=True))), 0)

        place = lax.broadcasted_iota(jnp.int32, (GROUP * CAP, LANES), 0).astype(jnp.int16)

        def sort_group(g):
            first = g * GROUP
            pieces = []
            for c in range(chunks):
                wanted = (target_ref[c:c + 1, :] - first * CAP).astype(jnp.int32)
                wanted = jnp.broadcast_to(wanted, (16, LANES)).astype(jnp.int16)
                wanted = jnp.concatenate([wanted] * (GROUP * CAP // 16), 0)
                pieces.append(jnp.where(wanted == place, jnp.ones((), jnp.bfloat16), jnp.zeros((), jnp.bfloat16)))
            pick = jnp.concatenate(pieces, 1)
            rows = jnp.dot(pick, yb_ref[...], preferred_element_type=jnp.float32).astype(jnp.bfloat16)
            for j in range(GROUP):
                base = pl.multiple_of((first + j) * SPAN, 16)
                rows_ref[pl.ds(base, CAP), :] = rows[j * CAP:(j + 1) * CAP]
                notes = jnp.concatenate([common, list_ref[pl.ds(first + j, 1), :]], 0)
                rows_ref[pl.ds(pl.multiple_of(base + CAP, 16), NOTES), :] = notes.astype(jnp.bfloat16)
            at = pl.ds(pl.multiple_of(g * (GROUP * SPAN), 16), GROUP * SPAN)
            return pltpu.make_async_copy(rows_ref.at[at], rows_hbm.at[at], sem.at[g])

        groups = width // GROUP
        if groups <= 4:
            copies = []
            for g in range(groups):
                copies.append(sort_group(g))
                copies[g].start()
            for copy in copies:
                copy.wait()
        else:

            @pl.loop(0, groups)
            def _(g):
                copy = sort_group(g)
                copy.start()
                copy.wait()

        mean_copy.wait()


def project_and_sort(width, embeddings, basis, list_owner, list_slot):
    rows_here, wide = embeddings.shape
    feats = basis.shape[1]
    lanes = rows_here // LANES
    slots = width * SPAN
    return pl.pallas_call(
        functools.partial(rows_kernel, width),
        grid=(rows_here // CHUNK,),
        in_specs=[pl.BlockSpec(memory_space=pl.ANY)] * 4,
        out_specs=[pl.BlockSpec(memory_space=pl.ANY)] * 2,
        out_shape=[
            jax.ShapeDtypeStruct((slots, feats), jnp.bfloat16),
            jax.ShapeDtypeStruct((1, wide), jnp.float32),
        ],
        scratch_shapes=[
            pltpu.VMEM((lanes, LANES), jnp.int32),
            pltpu.VMEM((lanes, LANES), jnp.int32),
            pltpu.VMEM((1, wide), jnp.float32),
            pltpu.VMEM((wide, feats), jnp.bfloat16),
            pltpu.VMEM((rows_here, wide), jnp.bfloat16),
            pltpu.VMEM((slots, feats), jnp.bfloat16),
            pltpu.VMEM((rows_here, feats), jnp.float32),
            pltpu.VMEM((rows_here, feats), jnp.bfloat16),
            pltpu.VMEM((8, feats), jnp.float32),
            pltpu.VMEM((8, wide), jnp.float32),
            pltpu.VMEM((lanes, LANES), jnp.int32),
            pltpu.VMEM((width, 2 * CAP), jnp.float32),
            pltpu.SemaphoreType.DMA((rows_here // CHUNK,)),
            pltpu.SemaphoreType.DMA((4,)),
            pltpu.SemaphoreType.DMA((width // GROUP,)),
        ],
        compiler_params=pltpu.CompilerParams(vmem_limit_bytes=VMEM_ALL),
        cost_estimate=pl.CostEstimate(
            flops=2 * rows_here * feats * (wide + slots), bytes_accessed=2 * rows_here * wide + 2 * slots * feats, transcendentals=0
        ),
        name="project_sort",
    )(embeddings, basis, list_owner.reshape(lanes, LANES), list_slot.reshape(lanes, LANES))


def strides_after_core(width):
    strides = [1 << k for k in range(1, width.bit_length() - 1)]
    return strides[:-2] + strides[:-3:-1]


def moments_kernel(width, me_ref, mean_hbm, e_hbm, keep_ref, send_ref, e_ref, mean_ref, m_ref, sem, mean_sem):
    rows_here, wide = e_ref.shape
    block = wide // width
    bits = width.bit_length() - 1
    tiles = wide // TILE
    mean_copy = pltpu.make_async_copy(mean_hbm, mean_ref, mean_sem)
    mean_copy.start()
    copies = []
    for c in range(rows_here // CHUNK):
        at = pl.ds(c * CHUNK, CHUNK)
        copies.append(pltpu.make_async_copy(e_hbm.at[at], e_ref.at[at], sem.at[c]))
        copies[c].start()
    me = me_ref[0]
    odd = (me & 1) == 1
    mean_copy.wait()
    mean = mean_ref[...]
    for t in range(tiles):
        rows, columns = slice(t * TILE, (t + 1) * TILE), slice(t * TILE, wide)
        if t == 0:
            product = jnp.zeros((TILE, wide), jnp.float32)
            for c in range(rows_here // CHUNK):
                copies[c].wait()
                at = slice(c * CHUNK, (c + 1) * CHUNK)
                product = product + lax.dot_general(
                    e_ref[at, rows], e_ref[at, :], (((0,), (0,)), ((), ())), preferred_element_type=jnp.float32
                )
        else:
            product = lax.dot_general(
                e_ref[:, rows], e_ref[:, columns], (((0,), (0,)), ((), ())), preferred_element_type=jnp.float32
            )
        down = jnp.transpose(jnp.broadcast_to(mean[:, rows] * rows_here, (LANES, TILE)))
        for u in range(t, tiles):
            pieces = []
            for j in range(u * TILE // LANES, (u + 1) * TILE // LANES):
                across = slice(j * LANES, (j + 1) * LANES)
                within = slice(j * LANES - t * TILE, (j + 1) * LANES - t * TILE)
                pieces.append((product[:, within] - down * mean[:, across]).astype(jnp.bfloat16))
            piece = jnp.concatenate(pieces, 1)
            other = slice(u * TILE, (u + 1) * TILE)
            m_ref[rows, other] = piece
            if u > t:
                m_ref[other, rows] = jnp.transpose(piece)
        for pair in range(TILE // block // 2):
            first = t * (TILE // block) + 2 * pair
            place = 0
            for n, stride in enumerate(strides_after_core(width)):
                place = place + jnp.where(((first ^ me) & stride) != 0, 1 << (bits - 2 - n), 0)
            to = pl.ds(pl.multiple_of(place * block, block), block)
            even_rows = m_ref[first * block:(first + 1) * block, :]
            odd_rows = m_ref[(first + 1) * block:(first + 2) * block, :]
            keep_ref[to, :] = jnp.where(odd, odd_rows, even_rows)
            send_ref[to, :] = jnp.where(odd, even_rows, odd_rows)


def moments(width, me, embeddings, mean):
    rows_here, wide = embeddings.shape
    vmem = pl.BlockSpec(memory_space=pltpu.VMEM)
    return pl.pallas_call(
        functools.partial(moments_kernel, width),
        in_specs=[pl.BlockSpec(memory_space=pltpu.SMEM)] + [pl.BlockSpec(memory_space=pl.ANY)] * 2,
        out_specs=[vmem] * 2,
        out_shape=[
            jax.ShapeDtypeStruct((wide // 2, wide), jnp.bfloat16),
            jax.ShapeDtypeStruct((wide // 2, wide), jnp.bfloat16),
        ],
        scratch_shapes=[
            pltpu.VMEM((rows_here, wide), jnp.bfloat16),
            pltpu.VMEM((1, wide), jnp.float32),
            pltpu.VMEM((wide, wide), jnp.bfloat16),
            pltpu.SemaphoreType.DMA((rows_here // CHUNK,)),
            pltpu.SemaphoreType.DMA,
        ],
        compiler_params=pltpu.CompilerParams(vmem_limit_bytes=VMEM_MOST),
        cost_estimate=pl.CostEstimate(
            flops=2 * rows_here * wide * wide, bytes_accessed=2 * rows_here * wide + 3 * wide * wide, transcendentals=0
        ),
        name="moments",
    )(me.reshape(1), mean, embeddings)


def add_kernel(shares, pieces, keep_ref, *refs):
    outs = refs[len(refs) - shares * pieces:]
    came = refs[:len(refs) - shares * pieces]
    rows, columns = outs[0].shape
    for h in range(shares):
        across = slice(h * columns, (h + 1) * columns)
        for p in range(pieces):
            at = slice(p * rows, (p + 1) * rows)
            held = keep_ref[at, across].astype(jnp.float32)
            for ref in came:
                held = held + ref[at, across].astype(jnp.float32)
            out = outs[h * pieces + p]
            out[...] = held.astype(out.dtype)


def add_and_split(keep, came, shares, pieces):
    rows, columns = keep.shape
    vmem = pl.BlockSpec(memory_space=pltpu.VMEM)
    shape = (rows // pieces, columns // shares)
    kinds = [jnp.float32] + [jnp.bfloat16] * (pieces - 1)
    outs = pl.pallas_call(
        functools.partial(add_kernel, shares, pieces),
        in_specs=[vmem] * (1 + len(came)),
        out_specs=[vmem] * (shares * pieces),
        out_shape=[jax.ShapeDtypeStruct(shape, kind) for kind in kinds * shares],
        compiler_params=pltpu.CompilerParams(vmem_limit_bytes=VMEM_SOME),
        cost_estimate=pl.CostEstimate(flops=2 * rows * columns, bytes_accessed=10 * rows * columns, transcendentals=0),
        name="add_and_split",
    )(keep, *came)
    return [outs[h * pieces:(h + 1) * pieces] for h in range(shares)]


def finish_kernel(total, between_ref, *refs):
    out_ref = refs[-1]
    each = (len(refs) - 1) // SHARES
    columns = out_ref.shape[1] // SHARES
    for h in range(SHARES):
        across = slice(h * columns, (h + 1) * columns)
        held = refs[h * each][...]
        for ref in refs[h * each + 1:(h + 1) * each]:
            held = held + ref[...].astype(jnp.float32)
        out_ref[:, across] = (held + between_ref[:, across]) / total


def finish(total, between, keeps, came):
    parts = [part for keep, pieces in zip(keeps, came) for part in (keep, *pieces)]
    vmem = pl.BlockSpec(memory_space=pltpu.VMEM)
    return pl.pallas_call(
        functools.partial(finish_kernel, total),
        in_specs=[vmem] * (1 + len(parts)),
        out_specs=vmem,
        out_shape=jax.ShapeDtypeStruct(between.shape, jnp.float32),
        compiler_params=pltpu.CompilerParams(vmem_limit_bytes=VMEM_SOME),
        cost_estimate=pl.CostEstimate(flops=8 * between.size, bytes_accessed=16 * between.size, transcendentals=0),
        name="finish",
    )(between, *parts)


def exchange(width, stride, out):
    return lax.ppermute(out, "wide", [(i, i ^ stride) for i in range(width)])


def encode_kernel(total, me_ref, got_ref, basis_ref, centroid_ref, rotation_ref, *refs):
    out_hbm, between_ref, out_ref, delta_ref, list_ref, apart_ref, sem = refs[-7:]
    width = delta_ref.shape[0]
    feats = out_ref.shape[1]
    owned = centroid_ref.shape[0]
    wide = basis_ref.shape[0]
    block = wide // width
    share = total // width

    notes = jnp.concatenate([got_ref[s * SPAN + CAP:(s + 1) * SPAN, :] for s in range(width)], 0)
    size = width * NOTES
    to = lax.broadcasted_iota(jnp.int32, (size, size), 0)
    of = lax.broadcasted_iota(jnp.int32, (size, size), 1)
    turn = jnp.where((to % width) * NOTES + to // width == of, 1.0, 0.0).astype(jnp.bfloat16)
    turned = jnp.dot(turn, notes, preferred_element_type=jnp.float32)
    row = [turned[r * width:(r + 1) * width] for r in range(NOTES)]
    digits = row[NOTES - 1]
    list_ref[...] = digits[:, :CAP] * 32.0 + digits[:, CAP:] - 1.0
    quarters = wide // feats
    shifts = jnp.zeros((width, feats), jnp.float32)
    for q in range(quarters):
        parts = [row[p * quarters + q] for p in range(3)]
        mean = parts[0] + (parts[1] + parts[2])
        apart_ref[:, q * feats:(q + 1) * feats] = mean - jnp.mean(mean, 0, keepdims=True)
        terms = jnp.dot(
            jnp.concatenate(parts, 0).astype(jnp.bfloat16),
            basis_ref[q * feats:(q + 1) * feats, :],
            preferred_element_type=jnp.float32,
        )
        shifts = shifts + (terms[:width] + (terms[width:2 * width] + terms[2 * width:]))
    square = row[3 * quarters] + (row[3 * quarters + 1] + row[3 * quarters + 2])
    delta = shifts - jnp.mean(shifts, 0, keepdims=True)
    variance = jnp.sum(square + share * (delta * delta), 0, keepdims=True) / total
    scale = lax.rsqrt(variance + 1e-05)
    delta_ref[...] = delta

    names = lax.broadcasted_iota(jnp.int32, (CAP, owned), 1).astype(jnp.int16)

    def encode_group(g):
        columns = jnp.transpose(list_ref[pl.ds(g * GROUP, GROUP), :])
        hits, projected, held = [], [], []
        for s in range(GROUP):
            listed = jnp.broadcast_to(columns[:, s:s + 1], (CAP, LANES))
            held.append(jnp.concatenate([listed] * (feats // LANES), 1) >= 0)
            wanted = jnp.concatenate([listed.astype(jnp.int32).astype(jnp.int16)] * (owned // LANES), 1)
            hits.append(jnp.where(wanted == names, jnp.ones((), jnp.bfloat16), jnp.zeros((), jnp.bfloat16)))
            base = pl.multiple_of((g * GROUP + s) * SPAN, 16)
            rows = got_ref[pl.ds(base, CAP), :].astype(jnp.float32)
            projected.append((rows + delta_ref[pl.ds(g * GROUP + s, 1), :]) * scale)
        centre = jnp.dot(jnp.concatenate(hits, 0), centroid_ref[...], preferred_element_type=jnp.float32)
        residual = jnp.where(jnp.concatenate(held, 0), jnp.concatenate(projected, 0) - centre, 0.0)
        at = pl.ds(pl.multiple_of(g * (GROUP * CAP), GROUP * CAP), GROUP * CAP)
        out_ref[at, :] = jnp.dot(
            residual.astype(jnp.bfloat16), rotation_ref[...], preferred_element_type=jnp.float32
        ).astype(jnp.bfloat16)
        copies = []
        for s in range(GROUP):
            place = g * GROUP + s
            here = pl.ds(pl.multiple_of(place * CAP, CAP), CAP)
            there = pl.ds(pl.multiple_of(device_at(width, place) * CAP, CAP), CAP)
            copies.append(pltpu.make_async_copy(out_ref.at[here], out_hbm.at[there], sem.at[place]))
        return copies

    groups = width // GROUP
    copies = []
    if groups <= 4:
        for g in range(groups):
            for copy in encode_group(g):
                copy.start()
                copies.append(copy)
    else:

        @pl.loop(0, groups)
        def _(g):
            for copy in encode_group(g):
                copy.start()
            for s in range(GROUP):
                at = pl.ds(pl.multiple_of((g * GROUP + s) * CAP, CAP), CAP)
                pltpu.make_async_copy(out_ref.at[at], out_hbm.at[at], sem.at[g * GROUP + s]).wait()

    first = me_ref[0] * block
    near = apart_ref[:, pl.ds(pl.multiple_of(first // LANES * LANES, LANES), LANES)]
    near = pltpu.roll(near, (LANES - first % LANES) % LANES, 1)[:, :block]
    between_ref[...] = share * lax.dot_general(
        near,
        apart_ref[...],
        (((0,), (0,)), ((), ())),
        precision=lax.Precision.HIGHEST,
        preferred_element_type=jnp.float32,
    )
    for copy in copies:
        copy.wait()


def encode(width, total, me, got, basis, centroids, rotation, after):
    wide, feats = basis.shape
    owned = centroids.shape[0]
    slots = width * CAP
    vmem, anywhere = pl.BlockSpec(memory_space=pltpu.VMEM), pl.BlockSpec(memory_space=pl.ANY)
    return pl.pallas_call(
        functools.partial(encode_kernel, total),
        in_specs=[pl.BlockSpec(memory_space=pltpu.SMEM)] + [vmem] * 4 + [anywhere] * len(after),
        out_specs=[anywhere, vmem],
        out_shape=[
            jax.ShapeDtypeStruct((slots, feats), jnp.bfloat16),
            jax.ShapeDtypeStruct((wide // width, wide), jnp.float32),
        ],
        scratch_shapes=[
            pltpu.VMEM((slots, feats), jnp.bfloat16),
            pltpu.VMEM((width, feats), jnp.float32),
            pltpu.VMEM((width, CAP), jnp.float32),
            pltpu.VMEM((width, wide), jnp.float32),
            pltpu.SemaphoreType.DMA((width,)),
        ],
        compiler_params=pltpu.CompilerParams(vmem_limit_bytes=VMEM_SOME),
        cost_estimate=pl.CostEstimate(
            flops=2 * slots * feats * (owned + feats), bytes_accessed=4 * slots * feats, transcendentals=0
        ),
        name="encode",
    )(me.reshape(1), got, basis, centroids, rotation, *after)


def local(embeddings, basis, list_owner, list_slot, centroids, rotation):
    width = lax.axis_size("wide")
    me = lax.axis_index("wide")
    rows_here, wide = embeddings.shape
    feats = basis.shape[1]
    total = rows_here * width

    rows, mean = project_and_sort(width, embeddings, basis, list_owner, list_slot)
    order = [[device_at(width, place) for place in range(width)]]
    got = lax.all_to_all(
        rows.reshape(width, SPAN, feats), "wide", split_axis=0, concat_axis=0, tiled=True, axis_index_groups=order
    )

    keep, send = moments(width, me, embeddings, mean)
    came = exchange(width, 1, send)
    shares = add_and_split(keep, [came], SHARES, 2)
    strides = strides_after_core(width)
    sends, keeps, ends = [], [], []
    for keep, send in shares:
        for n, stride in enumerate(strides):
            came = exchange(width, stride, send)
            if n + 1 < len(strides):
                ((keep, send),) = add_and_split(keep, [came], 1, 2)
            if n == len(strides) - 3:
                sends.append(send)
        keeps.append(keep)
        ends.append([came])
    encoded, between = encode(
        width, total, me, got.reshape(width * SPAN, feats), basis, centroids, rotation, sends
    )
    covariance = finish(total, between, keeps, ends)
    return (encoded, covariance)


def solution(mesh):
    in_specs = (
        P(("groups", "wide"), None),
        P(),
        P(("groups", "wide")),
        P(("groups", "wide")),
        P("wide", None),
        P(),
    )
    out_specs = (P(("groups", "wide"), None), P(("groups", "wide"), None))
    return jax.shard_map(local, mesh=mesh, in_specs=in_specs, out_specs=out_specs, check_vma=False)
```

```python
import functools

import jax
import jax.numpy as jnp
from jax import lax
from jax.experimental import pallas as pl
from jax.experimental.pallas import tpu as pltpu
from jax.sharding import PartitionSpec as P

CAP = 128
LANES = 128
NOTES = 16
SPAN = CAP + NOTES
CHUNK = 512
TILE = 256
GROUP = 4
SHARES = 2
VMEM_ALL = 60 * 1024 * 1024
VMEM_SOME = 24 * 1024 * 1024
VMEM_MOST = 48 * 1024 * 1024


def in_three(x):
    high = x.astype(jnp.bfloat16).astype(jnp.float32)
    rest = x - high
    middle = rest.astype(jnp.bfloat16).astype(jnp.float32)
    return high, middle, (rest - middle).astype(jnp.bfloat16).astype(jnp.float32)


def rows_kernel(
    width, e_hbm, basis_hbm, owner_hbm, slot_hbm,
    rows_hbm, mean_hbm,
    owner_ref, slot_ref, mean_ref, basis_ref, e_ref, rows_ref, y_ref, yb_ref, sum_ref, total_ref, target_ref, list_ref, e_sem, small_sem, sem,
):
    step = pl.program_id(0)
    rows_here, feats = y_ref.shape
    wide = e_ref.shape[1]
    chunks = rows_here // LANES

    def e_copy(c):
        at = pl.ds(pl.multiple_of(c * CHUNK, CHUNK), CHUNK)
        return pltpu.make_async_copy(e_hbm.at[at], e_ref.at[at], e_sem.at[c])

    @pl.when(step == 0)
    def _():
        owner_copy = pltpu.make_async_copy(owner_hbm, owner_ref, small_sem.at[0])
        slot_copy = pltpu.make_async_copy(slot_hbm, slot_ref, small_sem.at[1])
        basis_copy = pltpu.make_async_copy(basis_hbm, basis_ref, small_sem.at[2])
        owner_copy.start()
        e_copy(0).start()
        slot_copy.start()
        basis_copy.start()
        for c in range(1, rows_here // CHUNK):
            e_copy(c).start()
        owner_copy.wait()
        sum_ref[...] = jnp.zeros_like(sum_ref)
        total_ref[...] = jnp.zeros_like(total_ref)
        owner = owner_ref[...]
        wanted = lax.broadcasted_iota(jnp.int32, (width, LANES), 0)
        hits = [jnp.where(owner[c:c + 1, :] == wanted, 1.0, 0.0) for c in range(chunks)]
        flat = jnp.concatenate(hits, 0).astype(jnp.bfloat16)
        up = lax.broadcasted_iota(jnp.int32, (LANES, LANES), 0)
        to = lax.broadcasted_iota(jnp.int32, (LANES, LANES), 1)
        before = jnp.where(up < to, 1.0, 0.0).astype(jnp.bfloat16)
        every = jnp.ones((LANES, LANES), jnp.bfloat16)
        within = jnp.dot(flat, before, preferred_element_type=jnp.float32)
        counts = jnp.dot(flat, every, preferred_element_type=jnp.float32)
        carry = jnp.zeros((width, LANES), jnp.float32)
        ranks = []
        for c in range(chunks):
            at = slice(c * width, (c + 1) * width)
            ranks.append(jnp.sum(hits[c] * (within[at] + carry), 0, keepdims=True).astype(jnp.int32))
            carry = carry + counts[at]
            target_ref[c:c + 1, :] = owner[c:c + 1, :] * CAP + ranks[c]

        slot_copy.wait()
        slot = slot_ref[...] + 1
        high, low = (slot >> 5).astype(jnp.float32), (slot & 31).astype(jnp.float32)
        spots = lax.broadcasted_iota(jnp.int32, (CAP, LANES), 0)
        placed = jnp.concatenate([jnp.where(ranks[c] == spots, 1.0, 0.0) for c in range(chunks)], 1).astype(jnp.bfloat16)
        digits = jnp.concatenate(
            [
                jnp.concatenate([hits[c] * high[c:c + 1, :] for c in range(chunks)], 1),
                jnp.concatenate([hits[c] * low[c:c + 1, :] for c in range(chunks)], 1),
            ],
            0,
        ).astype(jnp.bfloat16)
        found = lax.dot_general(digits, placed, (((1,), (1,)), ((), ())), preferred_element_type=jnp.float32)
        list_ref[:, :CAP] = found[:width]
        list_ref[:, CAP:] = found[width:]
        basis_copy.wait()

    e_copy(step).wait()
    here = pl.ds(pl.multiple_of(step * CHUNK, CHUNK), CHUNK)
    rows = e_ref[here, :]
    y = jnp.dot(rows, basis_ref[...], preferred_element_type=jnp.float32)
    y_ref[here, :] = y
    sum_ref[...] += jnp.sum(y.reshape(CHUNK // 8, 8, feats), 0)
    total_ref[...] += jnp.sum(rows.astype(jnp.float32).reshape(CHUNK // 8, 8, wide), 0)

    @pl.when(step == pl.num_programs(0) - 1)
    def _():
        mean_y = jnp.sum(sum_ref[...], 0, keepdims=True) / rows_here
        square = jnp.zeros((8, feats), jnp.float32)
        for c in range(rows_here // CHUNK):
            at = slice(c * CHUNK, (c + 1) * CHUNK)
            centred = y_ref[at, :] - mean_y
            square = square + jnp.sum((centred * centred).reshape(CHUNK // 8, 8, feats), 0)
            yb_ref[at, :] = centred.astype(jnp.bfloat16)
        mean = jnp.sum(total_ref[...], 0, keepdims=True) / rows_here
        mean_ref[...] = mean
        mean_copy = pltpu.make_async_copy(mean_ref, mean_hbm, small_sem.at[3])
        mean_copy.start()
        parts = in_three(mean)
        common = [part[:, q * feats:(q + 1) * feats] for part in parts for q in range(wide // feats)]
        common = jnp.concatenate(common + list(in_three(jnp.sum(square, 0, keepdims=True))), 0)

        place = lax.broadcasted_iota(jnp.int32, (GROUP * CAP, LANES), 0).astype(jnp.int16)

        def sort_group(g):
            first = g * GROUP
            pieces = []
            for c in range(chunks):
                wanted = (target_ref[c:c + 1, :] - first * CAP).astype(jnp.int32)
                wanted = jnp.broadcast_to(wanted, (16, LANES)).astype(jnp.int16)
                wanted = jnp.concatenate([wanted] * (GROUP * CAP // 16), 0)
                pieces.append(jnp.where(wanted == place, jnp.ones((), jnp.bfloat16), jnp.zeros((), jnp.bfloat16)))
            pick = jnp.concatenate(pieces, 1)
            rows = jnp.dot(pick, yb_ref[...], preferred_element_type=jnp.float32).astype(jnp.bfloat16)
            for j in range(GROUP):
                base = pl.multiple_of((first + j) * SPAN, 16)
                rows_ref[pl.ds(base, CAP), :] = rows[j * CAP:(j + 1) * CAP]
                notes = jnp.concatenate([common, list_ref[pl.ds(first + j, 1), :]], 0)
                rows_ref[pl.ds(pl.multiple_of(base + CAP, 16), NOTES), :] = notes.astype(jnp.bfloat16)
            at = pl.ds(pl.multiple_of(g * (GROUP * SPAN), 16), GROUP * SPAN)
            return pltpu.make_async_copy(rows_ref.at[at], rows_hbm.at[at], sem.at[g])

        groups = width // GROUP
        if groups <= 4:
            copies = []
            for g in range(groups):
                copies.append(sort_group(g))
                copies[g].start()
            for copy in copies:
                copy.wait()
        else:

            @pl.loop(0, groups)
            def _(g):
                copy = sort_group(g)
                copy.start()
                copy.wait()

        mean_copy.wait()


def project_and_sort(width, embeddings, basis, list_owner, list_slot):
    rows_here, wide = embeddings.shape
    feats = basis.shape[1]
    lanes = rows_here // LANES
    slots = width * SPAN
    return pl.pallas_call(
        functools.partial(rows_kernel, width),
        grid=(rows_here // CHUNK,),
        in_specs=[pl.BlockSpec(memory_space=pl.ANY)] * 4,
        out_specs=[pl.BlockSpec(memory_space=pl.ANY)] * 2,
        out_shape=[
            jax.ShapeDtypeStruct((slots, feats), jnp.bfloat16),
            jax.ShapeDtypeStruct((1, wide), jnp.float32),
        ],
        scratch_shapes=[
            pltpu.VMEM((lanes, LANES), jnp.int32),
            pltpu.VMEM((lanes, LANES), jnp.int32),
            pltpu.VMEM((1, wide), jnp.float32),
            pltpu.VMEM((wide, feats), jnp.bfloat16),
            pltpu.VMEM((rows_here, wide), jnp.bfloat16),
            pltpu.VMEM((slots, feats), jnp.bfloat16),
            pltpu.VMEM((rows_here, feats), jnp.float32),
            pltpu.VMEM((rows_here, feats), jnp.bfloat16),
            pltpu.VMEM((8, feats), jnp.float32),
            pltpu.VMEM((8, wide), jnp.float32),
            pltpu.VMEM((lanes, LANES), jnp.int32),
            pltpu.VMEM((width, 2 * CAP), jnp.float32),
            pltpu.SemaphoreType.DMA((rows_here // CHUNK,)),
            pltpu.SemaphoreType.DMA((4,)),
            pltpu.SemaphoreType.DMA((width // GROUP,)),
        ],
        compiler_params=pltpu.CompilerParams(vmem_limit_bytes=VMEM_ALL),
        cost_estimate=pl.CostEstimate(
            flops=2 * rows_here * feats * (wide + slots), bytes_accessed=2 * rows_here * wide + 2 * slots * feats, transcendentals=0
        ),
        name="project_sort",
    )(embeddings, basis, list_owner.reshape(lanes, LANES), list_slot.reshape(lanes, LANES))


def moments_kernel(width, me_ref, mean_hbm, e_hbm, keep_ref, send_ref, e_ref, mean_ref, m_ref, sem, mean_sem):
    rows_here, wide = e_ref.shape
    block = wide // width
    bits = width.bit_length() - 1
    tiles = wide // TILE
    mean_copy = pltpu.make_async_copy(mean_hbm, mean_ref, mean_sem)
    mean_copy.start()
    copies = []
    for c in range(rows_here // CHUNK):
        at = pl.ds(c * CHUNK, CHUNK)
        copies.append(pltpu.make_async_copy(e_hbm.at[at], e_ref.at[at], sem.at[c]))
        copies[c].start()
    me = me_ref[0]
    odd = (me & 1) == 1
    mean_copy.wait()
    mean = mean_ref[...]
    for t in range(tiles):
        rows, columns = slice(t * TILE, (t + 1) * TILE), slice(t * TILE, wide)
        if t == 0:
            product = jnp.zeros((TILE, wide), jnp.float32)
            for c in range(rows_here // CHUNK):
                copies[c].wait()
                at = slice(c * CHUNK, (c + 1) * CHUNK)
                product = product + lax.dot_general(
                    e_ref[at, rows], e_ref[at, :], (((0,), (0,)), ((), ())), preferred_element_type=jnp.float32
                )
        else:
            product = lax.dot_general(
                e_ref[:, rows], e_ref[:, columns], (((0,), (0,)), ((), ())), preferred_element_type=jnp.float32
            )
        down = jnp.transpose(jnp.broadcast_to(mean[:, rows] * rows_here, (LANES, TILE)))
        for u in range(t, tiles):
            pieces = []
            for j in range(u * TILE // LANES, (u + 1) * TILE // LANES):
                across = slice(j * LANES, (j + 1) * LANES)
                within = slice(j * LANES - t * TILE, (j + 1) * LANES - t * TILE)
                pieces.append((product[:, within] - down * mean[:, across]).astype(jnp.bfloat16))
            piece = jnp.concatenate(pieces, 1)
            other = slice(u * TILE, (u + 1) * TILE)
            m_ref[rows, other] = piece
            if u > t:
                m_ref[other, rows] = jnp.transpose(piece)
        for pair in range(TILE // block // 2):
            first = t * (TILE // block) + 2 * pair
            apart = (first ^ me) >> 1
            place = 0
            for k in range(bits - 1):
                place = place + (((apart >> k) & 1) << (bits - 2 - k))
            to = pl.ds(pl.multiple_of(place * block, block), block)
            even_rows = m_ref[first * block:(first + 1) * block, :]
            odd_rows = m_ref[(first + 1) * block:(first + 2) * block, :]
            keep_ref[to, :] = jnp.where(odd, odd_rows, even_rows)
            send_ref[to, :] = jnp.where(odd, even_rows, odd_rows)


def moments(width, me, embeddings, mean):
    rows_here, wide = embeddings.shape
    vmem = pl.BlockSpec(memory_space=pltpu.VMEM)
    return pl.pallas_call(
        functools.partial(moments_kernel, width),
        in_specs=[pl.BlockSpec(memory_space=pltpu.SMEM)] + [pl.BlockSpec(memory_space=pl.ANY)] * 2,
        out_specs=[vmem] * 2,
        out_shape=[
            jax.ShapeDtypeStruct((wide // 2, wide), jnp.bfloat16),
            jax.ShapeDtypeStruct((wide // 2, wide), jnp.bfloat16),
        ],
        scratch_shapes=[
            pltpu.VMEM((rows_here, wide), jnp.bfloat16),
            pltpu.VMEM((1, wide), jnp.float32),
            pltpu.VMEM((wide, wide), jnp.bfloat16),
            pltpu.SemaphoreType.DMA((rows_here // CHUNK,)),
            pltpu.SemaphoreType.DMA,
        ],
        compiler_params=pltpu.CompilerParams(vmem_limit_bytes=VMEM_MOST),
        cost_estimate=pl.CostEstimate(
            flops=2 * rows_here * wide * wide, bytes_accessed=2 * rows_here * wide + 3 * wide * wide, transcendentals=0
        ),
        name="moments",
    )(me.reshape(1), mean, embeddings)


def add_kernel(shares, pieces, arrived, keep_ref, *refs):
    outs = refs[len(refs) - shares * pieces:]
    came = refs[:arrived]
    rows, columns = outs[0].shape
    for h in range(shares):
        across = slice(h * columns, (h + 1) * columns)
        for p in range(pieces):
            at = slice(p * rows, (p + 1) * rows)
            held = keep_ref[at, across].astype(jnp.float32)
            for ref in came:
                held = held + ref[at, across].astype(jnp.float32)
            out = outs[h * pieces + p]
            out[...] = held.astype(out.dtype)


def add_and_split(keep, came, shares, pieces, after=()):
    rows, columns = keep.shape
    vmem = pl.BlockSpec(memory_space=pltpu.VMEM)
    shape = (rows // pieces, columns // shares)
    kinds = [jnp.float32] + [jnp.bfloat16] * (pieces - 1)
    outs = pl.pallas_call(
        functools.partial(add_kernel, shares, pieces, len(came)),
        in_specs=[vmem] * (1 + len(came)) + [pl.BlockSpec(memory_space=pl.ANY)] * len(after),
        out_specs=[vmem] * (shares * pieces),
        out_shape=[jax.ShapeDtypeStruct(shape, kind) for kind in kinds * shares],
        compiler_params=pltpu.CompilerParams(vmem_limit_bytes=VMEM_SOME),
        cost_estimate=pl.CostEstimate(flops=2 * rows * columns, bytes_accessed=10 * rows * columns, transcendentals=0),
        name="add_and_split",
    )(keep, *came, *after)
    return [outs[h * pieces:(h + 1) * pieces] for h in range(shares)]


def finish_kernel(total, counts, between_ref, *refs):
    out_ref = refs[-1]
    columns = out_ref.shape[1] // SHARES
    at = 0
    for h, count in enumerate(counts):
        across = slice(h * columns, (h + 1) * columns)
        held = refs[at][...]
        for ref in refs[at + 1:at + count]:
            held = held + ref[...].astype(jnp.float32)
        out_ref[:, across] = (held + between_ref[:, across]) / total
        at += count


def finish(total, between, keeps, came):
    parts = [part for keep, pieces in zip(keeps, came) for part in (keep, *pieces)]
    vmem = pl.BlockSpec(memory_space=pltpu.VMEM)
    return pl.pallas_call(
        functools.partial(finish_kernel, total, [1 + len(pieces) for pieces in came]),
        in_specs=[vmem] * (1 + len(parts)),
        out_specs=vmem,
        out_shape=jax.ShapeDtypeStruct(between.shape, jnp.float32),
        compiler_params=pltpu.CompilerParams(vmem_limit_bytes=VMEM_SOME),
        cost_estimate=pl.CostEstimate(flops=8 * between.size, bytes_accessed=16 * between.size, transcendentals=0),
        name="finish",
    )(between, *parts)


def halving_stages(width, together):
    strides = [1 << k for k in range(width.bit_length() - 1)]
    return [[s] for s in strides[:-together]] + [strides[-together:]]


def exchange(width, stage, out):
    came = []
    for p in range(1, 1 << len(stage)):
        apart = sum(s for k, s in enumerate(stage) if (p >> (len(stage) - 1 - k)) & 1)
        came.append(lax.ppermute(out[p - 1], "wide", [(i, i ^ apart) for i in range(width)]))
    return came


def encode_kernel(total, me_ref, got_ref, basis_ref, centroid_ref, rotation_ref, *refs):
    out_hbm, between_ref, out_ref, delta_ref, list_ref, apart_ref, sem = refs[-7:]
    width = delta_ref.shape[0]
    feats = out_ref.shape[1]
    owned = centroid_ref.shape[0]
    wide = basis_ref.shape[0]
    block = wide // width
    share = total // width

    notes = jnp.concatenate([got_ref[s * SPAN + CAP:(s + 1) * SPAN, :] for s in range(width)], 0)
    size = width * NOTES
    to = lax.broadcasted_iota(jnp.int32, (size, size), 0)
    of = lax.broadcasted_iota(jnp.int32, (size, size), 1)
    turn = jnp.where((to & (width - 1)) * NOTES + (to >> (width.bit_length() - 1)) == of, 1.0, 0.0).astype(jnp.bfloat16)
    turned = jnp.dot(turn, notes, preferred_element_type=jnp.float32)
    row = [turned[r * width:(r + 1) * width] for r in range(NOTES)]
    digits = row[NOTES - 1]
    list_ref[...] = digits[:, :CAP] * 32.0 + digits[:, CAP:] - 1.0
    quarters = wide // feats
    shifts = jnp.zeros((width, feats), jnp.float32)
    for q in range(quarters):
        parts = [row[p * quarters + q] for p in range(3)]
        mean = parts[0] + (parts[1] + parts[2])
        apart_ref[:, q * feats:(q + 1) * feats] = mean - jnp.mean(mean, 0, keepdims=True)
        terms = jnp.dot(
            jnp.concatenate(parts, 0).astype(jnp.bfloat16),
            basis_ref[q * feats:(q + 1) * feats, :],
            preferred_element_type=jnp.float32,
        )
        shifts = shifts + (terms[:width] + (terms[width:2 * width] + terms[2 * width:]))
    square = row[3 * quarters] + (row[3 * quarters + 1] + row[3 * quarters + 2])
    delta = shifts - jnp.mean(shifts, 0, keepdims=True)
    variance = jnp.sum(square + share * (delta * delta), 0, keepdims=True) / total
    scale = lax.rsqrt(variance + 1e-05)
    delta_ref[...] = delta

    names = lax.broadcasted_iota(jnp.int32, (CAP, owned), 1).astype(jnp.int16)

    groups = width // GROUP
    if groups <= 4:
        every = jnp.transpose(list_ref[...])

    def encode_group(g):
        if groups <= 4:
            columns = every[:, g * GROUP:(g + 1) * GROUP]
        else:
            columns = jnp.transpose(list_ref[pl.ds(g * GROUP, GROUP), :])
        hits, projected, held = [], [], []
        for s in range(GROUP):
            listed = jnp.broadcast_to(columns[:, s:s + 1], (CAP, LANES))
            held.append(jnp.concatenate([listed] * (feats // LANES), 1) >= 0)
            wanted = jnp.concatenate([listed.astype(jnp.int32).astype(jnp.int16)] * (owned // LANES), 1)
            hits.append(jnp.where(wanted == names, jnp.ones((), jnp.bfloat16), jnp.zeros((), jnp.bfloat16)))
            base = pl.multiple_of((g * GROUP + s) * SPAN, 16)
            rows = got_ref[pl.ds(base, CAP), :].astype(jnp.float32)
            projected.append((rows + delta_ref[pl.ds(g * GROUP + s, 1), :]) * scale)
        centre = jnp.dot(jnp.concatenate(hits, 0), centroid_ref[...], preferred_element_type=jnp.float32)
        residual = jnp.where(jnp.concatenate(held, 0), jnp.concatenate(projected, 0) - centre, 0.0)
        at = pl.ds(pl.multiple_of(g * (GROUP * CAP), GROUP * CAP), GROUP * CAP)
        out_ref[at, :] = jnp.dot(
            residual.astype(jnp.bfloat16), rotation_ref[...], preferred_element_type=jnp.float32
        ).astype(jnp.bfloat16)
        return pltpu.make_async_copy(out_ref.at[at], out_hbm.at[at], sem.at[g])

    copies = []
    if groups <= 4:
        for g in range(groups):
            copies.append(encode_group(g))
            copies[g].start()
    else:

        @pl.loop(0, groups)
        def _(g):
            copy = encode_group(g)
            copy.start()
            copy.wait()

    first = me_ref[0] * block
    near = apart_ref[:, pl.ds(pl.multiple_of(first // LANES * LANES, LANES), LANES)]
    near = pltpu.roll(near, (LANES - first % LANES) % LANES, 1)[:, :block]
    between_ref[...] = share * lax.dot_general(
        near,
        apart_ref[...],
        (((0,), (0,)), ((), ())),
        precision=lax.Precision.HIGHEST,
        preferred_element_type=jnp.float32,
    )
    for copy in copies:
        copy.wait()


def encode(width, total, me, got, basis, centroids, rotation, after):
    wide, feats = basis.shape
    owned = centroids.shape[0]
    slots = width * CAP
    vmem, anywhere = pl.BlockSpec(memory_space=pltpu.VMEM), pl.BlockSpec(memory_space=pl.ANY)
    return pl.pallas_call(
        functools.partial(encode_kernel, total),
        in_specs=[pl.BlockSpec(memory_space=pltpu.SMEM)] + [vmem] * 4 + [anywhere] * len(after),
        out_specs=[anywhere, vmem],
        out_shape=[
            jax.ShapeDtypeStruct((slots, feats), jnp.bfloat16),
            jax.ShapeDtypeStruct((wide // width, wide), jnp.float32),
        ],
        scratch_shapes=[
            pltpu.VMEM((slots, feats), jnp.bfloat16),
            pltpu.VMEM((width, feats), jnp.float32),
            pltpu.VMEM((width, CAP), jnp.float32),
            pltpu.VMEM((width, wide), jnp.float32),
            pltpu.SemaphoreType.DMA((width // GROUP,)),
        ],
        compiler_params=pltpu.CompilerParams(vmem_limit_bytes=VMEM_SOME),
        cost_estimate=pl.CostEstimate(
            flops=2 * slots * feats * (owned + feats), bytes_accessed=4 * slots * feats, transcendentals=0
        ),
        name="encode",
    )(me.reshape(1), got, basis, centroids, rotation, *after)


def local(embeddings, basis, list_owner, list_slot, centroids, rotation):
    width = lax.axis_size("wide")
    me = lax.axis_index("wide")
    rows_here, wide = embeddings.shape
    feats = basis.shape[1]
    total = rows_here * width

    rows, mean = project_and_sort(width, embeddings, basis, list_owner, list_slot)
    got = lax.all_to_all(rows.reshape(width, SPAN, feats), "wide", split_axis=0, concat_axis=0, tiled=True)

    keep, send = moments(width, me, embeddings, mean)
    came = exchange(width, [1], [send])
    shares = add_and_split(keep, came, SHARES, 2)
    keeps, ends, last = [], [], []
    for together, (keep, *out) in zip((1, 2), shares):
        stages = halving_stages(width, together)[1:]
        for n, stage in enumerate(stages):
            came = exchange(width, stage, out)
            if n + 1 < len(stages):
                ((keep, *out),) = add_and_split(keep, came, 1, 1 << len(stages[n + 1]), last if n == 0 else [])
        keeps.append(keep)
        ends.append(came)
        last = last + [out[0]]
    encoded, between = encode(width, total, me, got.reshape(width * SPAN, feats), basis, centroids, rotation, last)
    covariance = finish(total, between, keeps, ends)
    return (encoded, covariance)


def solution(mesh):
    in_specs = (
        P(("groups", "wide"), None),
        P(),
        P(("groups", "wide")),
        P(("groups", "wide")),
        P("wide", None),
        P(),
    )
    out_specs = (P(("groups", "wide"), None), P(("groups", "wide"), None))
    return jax.shard_map(local, mesh=mesh, in_specs=in_specs, out_specs=out_specs, check_vma=False)
```

```python
import functools

import jax
import jax.numpy as jnp
from jax import lax
from jax.experimental import pallas as pl
from jax.experimental.pallas import tpu as pltpu
from jax.sharding import PartitionSpec as P

CAP = 128
LANES = 128
NOTES = 16
SPAN = CAP + NOTES
CHUNK = 512
TILE = 256
GROUP = 4
SHARES = 2
PLANE = 4
VMEM_ALL = 60 * 1024 * 1024
VMEM_SOME = 24 * 1024 * 1024
VMEM_MOST = 48 * 1024 * 1024


def place_of(width, device):
    return (device & (PLANE - 1)) * (width // PLANE) + device // PLANE


def device_at(width, place):
    return (place & (width // PLANE - 1)) * PLANE + place // (width // PLANE)


def in_three(x):
    high = x.astype(jnp.bfloat16).astype(jnp.float32)
    rest = x - high
    middle = rest.astype(jnp.bfloat16).astype(jnp.float32)
    return high, middle, (rest - middle).astype(jnp.bfloat16).astype(jnp.float32)


def rows_kernel(
    width, e_hbm, basis_hbm, owner_hbm, slot_hbm,
    rows_hbm, mean_hbm,
    owner_ref, slot_ref, mean_ref, basis_ref, e_ref, rows_ref, y_ref, yb_ref, sum_ref, total_ref, target_ref, list_ref, e_sem, small_sem, sem,
):
    step = pl.program_id(0)
    rows_here, feats = y_ref.shape
    wide = e_ref.shape[1]
    chunks = rows_here // LANES

    def e_copy(c):
        at = pl.ds(pl.multiple_of(c * CHUNK, CHUNK), CHUNK)
        return pltpu.make_async_copy(e_hbm.at[at], e_ref.at[at], e_sem.at[c])

    @pl.when(step == 0)
    def _():
        owner_copy = pltpu.make_async_copy(owner_hbm, owner_ref, small_sem.at[0])
        slot_copy = pltpu.make_async_copy(slot_hbm, slot_ref, small_sem.at[1])
        basis_copy = pltpu.make_async_copy(basis_hbm, basis_ref, small_sem.at[2])
        owner_copy.start()
        e_copy(0).start()
        slot_copy.start()
        basis_copy.start()
        for c in range(1, rows_here // CHUNK):
            e_copy(c).start()
        owner_copy.wait()
        sum_ref[...] = jnp.zeros_like(sum_ref)
        total_ref[...] = jnp.zeros_like(total_ref)
        owner = place_of(width, owner_ref[...])
        wanted = lax.broadcasted_iota(jnp.int32, (width, LANES), 0)
        hits = [jnp.where(owner[c:c + 1, :] == wanted, 1.0, 0.0) for c in range(chunks)]
        flat = jnp.concatenate(hits, 0).astype(jnp.bfloat16)
        up = lax.broadcasted_iota(jnp.int32, (LANES, LANES), 0)
        to = lax.broadcasted_iota(jnp.int32, (LANES, LANES), 1)
        before = jnp.where(up < to, 1.0, 0.0).astype(jnp.bfloat16)
        every = jnp.ones((LANES, LANES), jnp.bfloat16)
        within = jnp.dot(flat, before, preferred_element_type=jnp.float32)
        counts = jnp.dot(flat, every, preferred_element_type=jnp.float32)
        carry = jnp.zeros((width, LANES), jnp.float32)
        ranks = []
        for c in range(chunks):
            at = slice(c * width, (c + 1) * width)
            ranks.append(jnp.sum(hits[c] * (within[at] + carry), 0, keepdims=True).astype(jnp.int32))
            carry = carry + counts[at]
            target_ref[c:c + 1, :] = owner[c:c + 1, :] * CAP + ranks[c]

        slot_copy.wait()
        slot = slot_ref[...] + 1
        high, low = (slot >> 5).astype(jnp.float32), (slot & 31).astype(jnp.float32)
        spots = lax.broadcasted_iota(jnp.int32, (CAP, LANES), 0)
        placed = jnp.concatenate([jnp.where(ranks[c] == spots, 1.0, 0.0) for c in range(chunks)], 1).astype(jnp.bfloat16)
        digits = jnp.concatenate(
            [
                jnp.concatenate([hits[c] * high[c:c + 1, :] for c in range(chunks)], 1),
                jnp.concatenate([hits[c] * low[c:c + 1, :] for c in range(chunks)], 1),
            ],
            0,
        ).astype(jnp.bfloat16)
        found = lax.dot_general(digits, placed, (((1,), (1,)), ((), ())), preferred_element_type=jnp.float32)
        list_ref[:, :CAP] = found[:width]
        list_ref[:, CAP:] = found[width:]
        basis_copy.wait()

    e_copy(step).wait()
    here = pl.ds(pl.multiple_of(step * CHUNK, CHUNK), CHUNK)
    rows = e_ref[here, :]
    y = jnp.dot(rows, basis_ref[...], preferred_element_type=jnp.float32)
    y_ref[here, :] = y
    sum_ref[...] += jnp.sum(y.reshape(CHUNK // 8, 8, feats), 0)
    total_ref[...] += jnp.sum(rows.astype(jnp.float32).reshape(CHUNK // 8, 8, wide), 0)

    @pl.when(step == pl.num_programs(0) - 1)
    def _():
        mean_y = jnp.sum(sum_ref[...], 0, keepdims=True) / rows_here
        square = jnp.zeros((8, feats), jnp.float32)
        for c in range(rows_here // CHUNK):
            at = slice(c * CHUNK, (c + 1) * CHUNK)
            centred = y_ref[at, :] - mean_y
            square = square + jnp.sum((centred * centred).reshape(CHUNK // 8, 8, feats), 0)
            yb_ref[at, :] = centred.astype(jnp.bfloat16)
        mean = jnp.sum(total_ref[...], 0, keepdims=True) / rows_here
        mean_ref[...] = mean
        mean_copy = pltpu.make_async_copy(mean_ref, mean_hbm, small_sem.at[3])
        mean_copy.start()
        parts = in_three(mean)
        common = [part[:, q * feats:(q + 1) * feats] for part in parts for q in range(wide // feats)]
        common = jnp.concatenate(common + list(in_three(jnp.sum(square, 0, keepdims=True))), 0)

        place = lax.broadcasted_iota(jnp.int32, (GROUP * CAP, LANES), 0).astype(jnp.int16)

        def sort_group(g):
            first = g * GROUP
            pieces = []
            for c in range(chunks):
                wanted = (target_ref[c:c + 1, :] - first * CAP).astype(jnp.int32)
                wanted = jnp.broadcast_to(wanted, (16, LANES)).astype(jnp.int16)
                wanted = jnp.concatenate([wanted] * (GROUP * CAP // 16), 0)
                pieces.append(jnp.where(wanted == place, jnp.ones((), jnp.bfloat16), jnp.zeros((), jnp.bfloat16)))
            pick = jnp.concatenate(pieces, 1)
            rows = jnp.dot(pick, yb_ref[...], preferred_element_type=jnp.float32).astype(jnp.bfloat16)
            for j in range(GROUP):
                base = pl.multiple_of((first + j) * SPAN, 16)
                rows_ref[pl.ds(base, CAP), :] = rows[j * CAP:(j + 1) * CAP]
                notes = jnp.concatenate([common, list_ref[pl.ds(first + j, 1), :]], 0)
                rows_ref[pl.ds(pl.multiple_of(base + CAP, 16), NOTES), :] = notes.astype(jnp.bfloat16)
            at = pl.ds(pl.multiple_of(g * (GROUP * SPAN), 16), GROUP * SPAN)
            return pltpu.make_async_copy(rows_ref.at[at], rows_hbm.at[at], sem.at[g])

        groups = width // GROUP
        if groups <= 4:
            copies = []
            for g in range(groups):
                copies.append(sort_group(g))
                copies[g].start()
            for copy in copies:
                copy.wait()
        else:

            @pl.loop(0, groups)
            def _(g):
                copy = sort_group(g)
                copy.start()
                copy.wait()

        mean_copy.wait()


def project_and_sort(width, embeddings, basis, list_owner, list_slot):
    rows_here, wide = embeddings.shape
    feats = basis.shape[1]
    lanes = rows_here // LANES
    slots = width * SPAN
    return pl.pallas_call(
        functools.partial(rows_kernel, width),
        grid=(rows_here // CHUNK,),
        in_specs=[pl.BlockSpec(memory_space=pl.ANY)] * 4,
        out_specs=[pl.BlockSpec(memory_space=pl.ANY)] * 2,
        out_shape=[
            jax.ShapeDtypeStruct((slots, feats), jnp.bfloat16),
            jax.ShapeDtypeStruct((1, wide), jnp.float32),
        ],
        scratch_shapes=[
            pltpu.VMEM((lanes, LANES), jnp.int32),
            pltpu.VMEM((lanes, LANES), jnp.int32),
            pltpu.VMEM((1, wide), jnp.float32),
            pltpu.VMEM((wide, feats), jnp.bfloat16),
            pltpu.VMEM((rows_here, wide), jnp.bfloat16),
            pltpu.VMEM((slots, feats), jnp.bfloat16),
            pltpu.VMEM((rows_here, feats), jnp.float32),
            pltpu.VMEM((rows_here, feats), jnp.bfloat16),
            pltpu.VMEM((8, feats), jnp.float32),
            pltpu.VMEM((8, wide), jnp.float32),
            pltpu.VMEM((lanes, LANES), jnp.int32),
            pltpu.VMEM((width, 2 * CAP), jnp.float32),
            pltpu.SemaphoreType.DMA((rows_here // CHUNK,)),
            pltpu.SemaphoreType.DMA((4,)),
            pltpu.SemaphoreType.DMA((width // GROUP,)),
        ],
        compiler_params=pltpu.CompilerParams(vmem_limit_bytes=VMEM_ALL),
        cost_estimate=pl.CostEstimate(
            flops=2 * rows_here * feats * (wide + slots), bytes_accessed=2 * rows_here * wide + 2 * slots * feats, transcendentals=0
        ),
        name="project_sort",
    )(embeddings, basis, list_owner.reshape(lanes, LANES), list_slot.reshape(lanes, LANES))


def moments_kernel(width, me_ref, mean_hbm, e_hbm, keep_ref, send_ref, e_ref, mean_ref, m_ref, sem, mean_sem):
    rows_here, wide = e_ref.shape
    block = wide // width
    bits = width.bit_length() - 1
    tiles = wide // TILE
    mean_copy = pltpu.make_async_copy(mean_hbm, mean_ref, mean_sem)
    mean_copy.start()
    copies = []
    for c in range(rows_here // CHUNK):
        at = pl.ds(c * CHUNK, CHUNK)
        copies.append(pltpu.make_async_copy(e_hbm.at[at], e_ref.at[at], sem.at[c]))
        copies[c].start()
    me = me_ref[0]
    odd = (me & 1) == 1
    mean_copy.wait()
    mean = mean_ref[...]
    for t in range(tiles):
        rows, columns = slice(t * TILE, (t + 1) * TILE), slice(t * TILE, wide)
        if t == 0:
            product = jnp.zeros((TILE, wide), jnp.float32)
            for c in range(rows_here // CHUNK):
                copies[c].wait()
                at = slice(c * CHUNK, (c + 1) * CHUNK)
                product = product + lax.dot_general(
                    e_ref[at, rows], e_ref[at, :], (((0,), (0,)), ((), ())), preferred_element_type=jnp.float32
                )
        else:
            product = lax.dot_general(
                e_ref[:, rows], e_ref[:, columns], (((0,), (0,)), ((), ())), preferred_element_type=jnp.float32
            )
        down = jnp.transpose(jnp.broadcast_to(mean[:, rows] * rows_here, (LANES, TILE)))
        for u in range(t, tiles):
            pieces = []
            for j in range(u * TILE // LANES, (u + 1) * TILE // LANES):
                across = slice(j * LANES, (j + 1) * LANES)
                within = slice(j * LANES - t * TILE, (j + 1) * LANES - t * TILE)
                pieces.append((product[:, within] - down * mean[:, across]).astype(jnp.bfloat16))
            piece = jnp.concatenate(pieces, 1)
            other = slice(u * TILE, (u + 1) * TILE)
            m_ref[rows, other] = piece
            if u > t:
                m_ref[other, rows] = jnp.transpose(piece)
        for pair in range(TILE // block // 2):
            first = t * (TILE // block) + 2 * pair
            apart = (first ^ me) >> 1
            place = 0
            for k in range(bits - 1):
                place = place + (((apart >> k) & 1) << (bits - 2 - k))
            to = pl.ds(pl.multiple_of(place * block, block), block)
            even_rows = m_ref[first * block:(first + 1) * block, :]
            odd_rows = m_ref[(first + 1) * block:(first + 2) * block, :]
            keep_ref[to, :] = jnp.where(odd, odd_rows, even_rows)
            send_ref[to, :] = jnp.where(odd, even_rows, odd_rows)


def moments(width, me, embeddings, mean):
    rows_here, wide = embeddings.shape
    vmem = pl.BlockSpec(memory_space=pltpu.VMEM)
    return pl.pallas_call(
        functools.partial(moments_kernel, width),
        in_specs=[pl.BlockSpec(memory_space=pltpu.SMEM)] + [pl.BlockSpec(memory_space=pl.ANY)] * 2,
        out_specs=[vmem] * 2,
        out_shape=[
            jax.ShapeDtypeStruct((wide // 2, wide), jnp.bfloat16),
            jax.ShapeDtypeStruct((wide // 2, wide), jnp.bfloat16),
        ],
        scratch_shapes=[
            pltpu.VMEM((rows_here, wide), jnp.bfloat16),
            pltpu.VMEM((1, wide), jnp.float32),
            pltpu.VMEM((wide, wide), jnp.bfloat16),
            pltpu.SemaphoreType.DMA((rows_here // CHUNK,)),
            pltpu.SemaphoreType.DMA,
        ],
        compiler_params=pltpu.CompilerParams(vmem_limit_bytes=VMEM_MOST),
        cost_estimate=pl.CostEstimate(
            flops=2 * rows_here * wide * wide, bytes_accessed=2 * rows_here * wide + 3 * wide * wide, transcendentals=0
        ),
        name="moments",
    )(me.reshape(1), mean, embeddings)


def add_kernel(shares, pieces, keep_ref, *refs):
    outs = refs[len(refs) - shares * pieces:]
    came = refs[:len(refs) - shares * pieces]
    rows, columns = outs[0].shape
    for h in range(shares):
        across = slice(h * columns, (h + 1) * columns)
        for p in range(pieces):
            at = slice(p * rows, (p + 1) * rows)
            held = keep_ref[at, across].astype(jnp.float32)
            for ref in came:
                held = held + ref[at, across].astype(jnp.float32)
            out = outs[h * pieces + p]
            out[...] = held.astype(out.dtype)


def add_and_split(keep, came, shares, pieces):
    rows, columns = keep.shape
    vmem = pl.BlockSpec(memory_space=pltpu.VMEM)
    shape = (rows // pieces, columns // shares)
    kinds = [jnp.float32] + [jnp.bfloat16] * (pieces - 1)
    outs = pl.pallas_call(
        functools.partial(add_kernel, shares, pieces),
        in_specs=[vmem] * (1 + len(came)),
        out_specs=[vmem] * (shares * pieces),
        out_shape=[jax.ShapeDtypeStruct(shape, kind) for kind in kinds * shares],
        compiler_params=pltpu.CompilerParams(vmem_limit_bytes=VMEM_SOME),
        cost_estimate=pl.CostEstimate(flops=2 * rows * columns, bytes_accessed=10 * rows * columns, transcendentals=0),
        name="add_and_split",
    )(keep, *came)
    return [outs[h * pieces:(h + 1) * pieces] for h in range(shares)]


def join_kernel(first_ref, second_ref, *refs):
    out_ref = refs[-1]
    columns = first_ref.shape[1]
    out_ref[:, :columns] = first_ref[...]
    out_ref[:, columns:] = second_ref[...]


def join(first, second, after):
    rows, columns = first.shape
    vmem = pl.BlockSpec(memory_space=pltpu.VMEM)
    return pl.pallas_call(
        join_kernel,
        in_specs=[vmem] * 2 + [pl.BlockSpec(memory_space=pl.ANY)] * len(after),
        out_specs=vmem,
        out_shape=jax.ShapeDtypeStruct((rows, 2 * columns), first.dtype),
        compiler_params=pltpu.CompilerParams(vmem_limit_bytes=VMEM_SOME),
        name="join",
    )(first, second, *after)


def finish_kernel(total, between_ref, near_ref, *refs):
    out_ref = refs[-1]
    each = (len(refs) - 1) // SHARES
    columns = out_ref.shape[1] // SHARES
    for h in range(SHARES):
        across = slice(h * columns, (h + 1) * columns)
        held = refs[h * each][...] + near_ref[:, across].astype(jnp.float32)
        for ref in refs[h * each + 1:(h + 1) * each]:
            held = held + ref[...].astype(jnp.float32)
        out_ref[:, across] = (held + between_ref[:, across]) / total


def finish(total, between, near, keeps, came):
    parts = [part for keep, pieces in zip(keeps, came) for part in (keep, *pieces)]
    vmem = pl.BlockSpec(memory_space=pltpu.VMEM)
    return pl.pallas_call(
        functools.partial(finish_kernel, total),
        in_specs=[vmem] * (2 + len(parts)),
        out_specs=vmem,
        out_shape=jax.ShapeDtypeStruct(between.shape, jnp.float32),
        compiler_params=pltpu.CompilerParams(vmem_limit_bytes=VMEM_SOME),
        cost_estimate=pl.CostEstimate(flops=8 * between.size, bytes_accessed=16 * between.size, transcendentals=0),
        name="finish",
    )(between, near, *parts)


def halving_stages(width):
    strides = [1 << k for k in range(width.bit_length() - 1)]
    return [[s] for s in strides[:-2]] + [strides[-2:]]


def exchange(width, apart, piece):
    return lax.ppermute(piece, "wide", [(i, i ^ apart) for i in range(width)])


def encode_kernel(total, me_ref, got_ref, basis_ref, centroid_ref, rotation_ref, *refs):
    out_hbm, between_ref, out_ref, delta_ref, list_ref, apart_ref, sem = refs[-7:]
    width = delta_ref.shape[0]
    feats = out_ref.shape[1]
    owned = centroid_ref.shape[0]
    wide = basis_ref.shape[0]
    block = wide // width
    share = total // width

    notes = jnp.concatenate([got_ref[s * SPAN + CAP:(s + 1) * SPAN, :] for s in range(width)], 0)
    size = width * NOTES
    to = lax.broadcasted_iota(jnp.int32, (size, size), 0)
    of = lax.broadcasted_iota(jnp.int32, (size, size), 1)
    turn = jnp.where((to % width) * NOTES + to // width == of, 1.0, 0.0).astype(jnp.bfloat16)
    turned = jnp.dot(turn, notes, preferred_element_type=jnp.float32)
    row = [turned[r * width:(r + 1) * width] for r in range(NOTES)]
    digits = row[NOTES - 1]
    list_ref[...] = digits[:, :CAP] * 32.0 + digits[:, CAP:] - 1.0
    quarters = wide // feats
    shifts = jnp.zeros((width, feats), jnp.float32)
    for q in range(quarters):
        parts = [row[p * quarters + q] for p in range(3)]
        mean = parts[0] + (parts[1] + parts[2])
        apart_ref[:, q * feats:(q + 1) * feats] = mean - jnp.mean(mean, 0, keepdims=True)
        terms = jnp.dot(
            jnp.concatenate(parts, 0).astype(jnp.bfloat16),
            basis_ref[q * feats:(q + 1) * feats, :],
            preferred_element_type=jnp.float32,
        )
        shifts = shifts + (terms[:width] + (terms[width:2 * width] + terms[2 * width:]))
    square = row[3 * quarters] + (row[3 * quarters + 1] + row[3 * quarters + 2])
    delta = shifts - jnp.mean(shifts, 0, keepdims=True)
    variance = jnp.sum(square + share * (delta * delta), 0, keepdims=True) / total
    scale = lax.rsqrt(variance + 1e-05)
    delta_ref[...] = delta

    names = lax.broadcasted_iota(jnp.int32, (CAP, owned), 1).astype(jnp.int16)

    def encode_group(g):
        columns = jnp.transpose(list_ref[pl.ds(g * GROUP, GROUP), :])
        hits, projected, held = [], [], []
        for s in range(GROUP):
            listed = jnp.broadcast_to(columns[:, s:s + 1], (CAP, LANES))
            held.append(jnp.concatenate([listed] * (feats // LANES), 1) >= 0)
            wanted = jnp.concatenate([listed.astype(jnp.int32).astype(jnp.int16)] * (owned // LANES), 1)
            hits.append(jnp.where(wanted == names, jnp.ones((), jnp.bfloat16), jnp.zeros((), jnp.bfloat16)))
            base = pl.multiple_of((g * GROUP + s) * SPAN, 16)
            rows = got_ref[pl.ds(base, CAP), :].astype(jnp.float32)
            projected.append((rows + delta_ref[pl.ds(g * GROUP + s, 1), :]) * scale)
        centre = jnp.dot(jnp.concatenate(hits, 0), centroid_ref[...], preferred_element_type=jnp.float32)
        residual = jnp.where(jnp.concatenate(held, 0), jnp.concatenate(projected, 0) - centre, 0.0)
        at = pl.ds(pl.multiple_of(g * (GROUP * CAP), GROUP * CAP), GROUP * CAP)
        out_ref[at, :] = jnp.dot(
            residual.astype(jnp.bfloat16), rotation_ref[...], preferred_element_type=jnp.float32
        ).astype(jnp.bfloat16)
        copies = []
        for s in range(GROUP):
            place = g * GROUP + s
            here = pl.ds(pl.multiple_of(place * CAP, CAP), CAP)
            there = pl.ds(pl.multiple_of(device_at(width, place) * CAP, CAP), CAP)
            copies.append(pltpu.make_async_copy(out_ref.at[here], out_hbm.at[there], sem.at[place]))
        return copies

    groups = width // GROUP
    copies = []
    if groups <= 4:
        for g in range(groups):
            for copy in encode_group(g):
                copy.start()
                copies.append(copy)
    else:

        @pl.loop(0, groups)
        def _(g):
            for copy in encode_group(g):
                copy.start()
            for s in range(GROUP):
                at = pl.ds(pl.multiple_of((g * GROUP + s) * CAP, CAP), CAP)
                pltpu.make_async_copy(out_ref.at[at], out_hbm.at[at], sem.at[g * GROUP + s]).wait()

    first = me_ref[0] * block
    near = apart_ref[:, pl.ds(pl.multiple_of(first // LANES * LANES, LANES), LANES)]
    near = pltpu.roll(near, (LANES - first % LANES) % LANES, 1)[:, :block]
    between_ref[...] = share * lax.dot_general(
        near,
        apart_ref[...],
        (((0,), (0,)), ((), ())),
        precision=lax.Precision.HIGHEST,
        preferred_element_type=jnp.float32,
    )
    for copy in copies:
        copy.wait()


def encode(width, total, me, got, basis, centroids, rotation, after):
    wide, feats = basis.shape
    owned = centroids.shape[0]
    slots = width * CAP
    vmem, anywhere = pl.BlockSpec(memory_space=pltpu.VMEM), pl.BlockSpec(memory_space=pl.ANY)
    return pl.pallas_call(
        functools.partial(encode_kernel, total),
        in_specs=[pl.BlockSpec(memory_space=pltpu.SMEM)] + [vmem] * 4 + [anywhere] * len(after),
        out_specs=[anywhere, vmem],
        out_shape=[
            jax.ShapeDtypeStruct((slots, feats), jnp.bfloat16),
            jax.ShapeDtypeStruct((wide // width, wide), jnp.float32),
        ],
        scratch_shapes=[
            pltpu.VMEM((slots, feats), jnp.bfloat16),
            pltpu.VMEM((width, feats), jnp.float32),
            pltpu.VMEM((width, CAP), jnp.float32),
            pltpu.VMEM((width, wide), jnp.float32),
            pltpu.SemaphoreType.DMA((width,)),
        ],
        compiler_params=pltpu.CompilerParams(vmem_limit_bytes=VMEM_SOME),
        cost_estimate=pl.CostEstimate(
            flops=2 * slots * feats * (owned + feats), bytes_accessed=4 * slots * feats, transcendentals=0
        ),
        name="encode",
    )(me.reshape(1), got, basis, centroids, rotation, *after)


def local(embeddings, basis, list_owner, list_slot, centroids, rotation):
    width = lax.axis_size("wide")
    me = lax.axis_index("wide")
    rows_here, wide = embeddings.shape
    feats = basis.shape[1]
    total = rows_here * width

    rows, mean = project_and_sort(width, embeddings, basis, list_owner, list_slot)
    order = [[device_at(width, place) for place in range(width)]]
    got = lax.all_to_all(
        rows.reshape(width, SPAN, feats), "wide", split_axis=0, concat_axis=0, tiled=True, axis_index_groups=order
    )

    keep, send = moments(width, me, embeddings, mean)
    stages = halving_stages(width)
    came = exchange(width, 1, send)
    last = []
    for share in add_and_split(keep, [came], SHARES, 1 << len(stages[1])):
        for n in range(1, len(stages) - 1):
            came = exchange(width, stages[n][0], share[1])
            (share,) = add_and_split(share[0], [came], 1, 1 << len(stages[n + 1]))
        last.append(share)
    near, far = stages[-1]
    came = [[exchange(width, far, share[1]), exchange(width, near + far, share[3])] for share in last]
    encoded, between = encode(
        width, total, me, got.reshape(width * SPAN, feats), basis, centroids, rotation, [share[1] for share in last]
    )
    came_near = exchange(width, near, join(last[0][2], last[1][2], came[1]))
    covariance = finish(total, between, came_near, [share[0] for share in last], came)
    return (encoded, covariance)


def solution(mesh):
    in_specs = (
        P(("groups", "wide"), None),
        P(),
        P(("groups", "wide")),
        P(("groups", "wide")),
        P("wide", None),
        P(),
    )
    out_specs = (P(("groups", "wide"), None), P(("groups", "wide"), None))
    return jax.shard_map(local, mesh=mesh, in_specs=in_specs, out_specs=out_specs, check_vma=False)
```

```python
import functools

import jax
import jax.numpy as jnp
from jax import lax
from jax.experimental import pallas as pl
from jax.experimental.pallas import tpu as pltpu
from jax.sharding import PartitionSpec as P

CAP = 128
LANES = 128
NOTES = 16
SPAN = CAP + NOTES
CHUNK = 512
TILE = 256
GROUP = 4
SHARES = 2
PLANE = 4
VMEM_ALL = 60 * 1024 * 1024
VMEM_SOME = 24 * 1024 * 1024
VMEM_MOST = 48 * 1024 * 1024


def place_of(width, device):
    return (device & (PLANE - 1)) * (width // PLANE) + device // PLANE


def device_at(width, place):
    return (place & (width // PLANE - 1)) * PLANE + place // (width // PLANE)


def in_three(x):
    high = x.astype(jnp.bfloat16).astype(jnp.float32)
    rest = x - high
    middle = rest.astype(jnp.bfloat16).astype(jnp.float32)
    return high, middle, (rest - middle).astype(jnp.bfloat16).astype(jnp.float32)


def rows_kernel(
    width, e_hbm, basis_hbm, owner_hbm, slot_hbm,
    rows_hbm, mean_hbm,
    owner_ref, slot_ref, mean_ref, basis_ref, e_ref, rows_ref, y_ref, yb_ref, sum_ref, total_ref, target_ref, list_ref, e_sem, small_sem, sem,
):
    step = pl.program_id(0)
    rows_here, feats = y_ref.shape
    wide = e_ref.shape[1]
    chunks = rows_here // LANES

    def e_copy(c):
        at = pl.ds(pl.multiple_of(c * CHUNK, CHUNK), CHUNK)
        return pltpu.make_async_copy(e_hbm.at[at], e_ref.at[at], e_sem.at[c])

    @pl.when(step == 0)
    def _():
        owner_copy = pltpu.make_async_copy(owner_hbm, owner_ref, small_sem.at[0])
        slot_copy = pltpu.make_async_copy(slot_hbm, slot_ref, small_sem.at[1])
        basis_copy = pltpu.make_async_copy(basis_hbm, basis_ref, small_sem.at[2])
        owner_copy.start()
        e_copy(0).start()
        slot_copy.start()
        basis_copy.start()
        for c in range(1, rows_here // CHUNK):
            e_copy(c).start()
        owner_copy.wait()
        sum_ref[...] = jnp.zeros_like(sum_ref)
        total_ref[...] = jnp.zeros_like(total_ref)
        owner = place_of(width, owner_ref[...])
        wanted = lax.broadcasted_iota(jnp.int32, (width, LANES), 0)
        hits = [jnp.where(owner[c:c + 1, :] == wanted, 1.0, 0.0) for c in range(chunks)]
        flat = jnp.concatenate(hits, 0).astype(jnp.bfloat16)
        up = lax.broadcasted_iota(jnp.int32, (LANES, LANES), 0)
        to = lax.broadcasted_iota(jnp.int32, (LANES, LANES), 1)
        before = jnp.where(up < to, 1.0, 0.0).astype(jnp.bfloat16)
        every = jnp.ones((LANES, LANES), jnp.bfloat16)
        within = jnp.dot(flat, before, preferred_element_type=jnp.float32)
        counts = jnp.dot(flat, every, preferred_element_type=jnp.float32)
        carry = jnp.zeros((width, LANES), jnp.float32)
        ranks = []
        for c in range(chunks):
            at = slice(c * width, (c + 1) * width)
            ranks.append(jnp.sum(hits[c] * (within[at] + carry), 0, keepdims=True).astype(jnp.int32))
            carry = carry + counts[at]
            target_ref[c:c + 1, :] = owner[c:c + 1, :] * CAP + ranks[c]

        slot_copy.wait()
        slot = slot_ref[...] + 1
        high, low = (slot >> 5).astype(jnp.float32), (slot & 31).astype(jnp.float32)
        spots = lax.broadcasted_iota(jnp.int32, (CAP, LANES), 0)
        placed = jnp.concatenate([jnp.where(ranks[c] == spots, 1.0, 0.0) for c in range(chunks)], 1).astype(jnp.bfloat16)
        digits = jnp.concatenate(
            [
                jnp.concatenate([hits[c] * high[c:c + 1, :] for c in range(chunks)], 1),
                jnp.concatenate([hits[c] * low[c:c + 1, :] for c in range(chunks)], 1),
            ],
            0,
        ).astype(jnp.bfloat16)
        found = lax.dot_general(digits, placed, (((1,), (1,)), ((), ())), preferred_element_type=jnp.float32)
        list_ref[:, :CAP] = found[:width]
        list_ref[:, CAP:] = found[width:]
        basis_copy.wait()

    e_copy(step).wait()
    here = pl.ds(pl.multiple_of(step * CHUNK, CHUNK), CHUNK)
    rows = e_ref[here, :]
    y = jnp.dot(rows, basis_ref[...], preferred_element_type=jnp.float32)
    y_ref[here, :] = y
    sum_ref[...] += jnp.sum(y.reshape(CHUNK // 8, 8, feats), 0)
    total_ref[...] += jnp.sum(rows.astype(jnp.float32).reshape(CHUNK // 8, 8, wide), 0)

    @pl.when(step == pl.num_programs(0) - 1)
    def _():
        mean_y = jnp.sum(sum_ref[...], 0, keepdims=True) / rows_here
        square = jnp.zeros((8, feats), jnp.float32)
        for c in range(rows_here // CHUNK):
            at = slice(c * CHUNK, (c + 1) * CHUNK)
            centred = y_ref[at, :] - mean_y
            square = square + jnp.sum((centred * centred).reshape(CHUNK // 8, 8, feats), 0)
            yb_ref[at, :] = centred.astype(jnp.bfloat16)
        mean = jnp.sum(total_ref[...], 0, keepdims=True) / rows_here
        mean_ref[...] = mean
        mean_copy = pltpu.make_async_copy(mean_ref, mean_hbm, small_sem.at[3])
        mean_copy.start()
        parts = in_three(mean)
        common = [part[:, q * feats:(q + 1) * feats] for part in parts for q in range(wide // feats)]
        common = jnp.concatenate(common + list(in_three(jnp.sum(square, 0, keepdims=True))), 0)

        place = lax.broadcasted_iota(jnp.int32, (GROUP * CAP, LANES), 0).astype(jnp.int16)

        def sort_group(g):
            first = g * GROUP
            pieces = []
            for c in range(chunks):
                wanted = (target_ref[c:c + 1, :] - first * CAP).astype(jnp.int32)
                wanted = jnp.broadcast_to(wanted, (16, LANES)).astype(jnp.int16)
                wanted = jnp.concatenate([wanted] * (GROUP * CAP // 16), 0)
                pieces.append(jnp.where(wanted == place, jnp.ones((), jnp.bfloat16), jnp.zeros((), jnp.bfloat16)))
            pick = jnp.concatenate(pieces, 1)
            rows = jnp.dot(pick, yb_ref[...], preferred_element_type=jnp.float32).astype(jnp.bfloat16)
            for j in range(GROUP):
                base = pl.multiple_of((first + j) * SPAN, 16)
                rows_ref[pl.ds(base, CAP), :] = rows[j * CAP:(j + 1) * CAP]
                notes = jnp.concatenate([common, list_ref[pl.ds(first + j, 1), :]], 0)
                rows_ref[pl.ds(pl.multiple_of(base + CAP, 16), NOTES), :] = notes.astype(jnp.bfloat16)
            at = pl.ds(pl.multiple_of(g * (GROUP * SPAN), 16), GROUP * SPAN)
            return pltpu.make_async_copy(rows_ref.at[at], rows_hbm.at[at], sem.at[g])

        groups = width // GROUP
        if groups <= 4:
            copies = []
            for g in range(groups):
                copies.append(sort_group(g))
                copies[g].start()
            for copy in copies:
                copy.wait()
        else:

            @pl.loop(0, groups)
            def _(g):
                copy = sort_group(g)
                copy.start()
                copy.wait()

        mean_copy.wait()


def project_and_sort(width, embeddings, basis, list_owner, list_slot):
    rows_here, wide = embeddings.shape
    feats = basis.shape[1]
    lanes = rows_here // LANES
    slots = width * SPAN
    return pl.pallas_call(
        functools.partial(rows_kernel, width),
        grid=(rows_here // CHUNK,),
        in_specs=[pl.BlockSpec(memory_space=pl.ANY)] * 4,
        out_specs=[pl.BlockSpec(memory_space=pl.ANY)] * 2,
        out_shape=[
            jax.ShapeDtypeStruct((slots, feats), jnp.bfloat16),
            jax.ShapeDtypeStruct((1, wide), jnp.float32),
        ],
        scratch_shapes=[
            pltpu.VMEM((lanes, LANES), jnp.int32),
            pltpu.VMEM((lanes, LANES), jnp.int32),
            pltpu.VMEM((1, wide), jnp.float32),
            pltpu.VMEM((wide, feats), jnp.bfloat16),
            pltpu.VMEM((rows_here, wide), jnp.bfloat16),
            pltpu.VMEM((slots, feats), jnp.bfloat16),
            pltpu.VMEM((rows_here, feats), jnp.float32),
            pltpu.VMEM((rows_here, feats), jnp.bfloat16),
            pltpu.VMEM((8, feats), jnp.float32),
            pltpu.VMEM((8, wide), jnp.float32),
            pltpu.VMEM((lanes, LANES), jnp.int32),
            pltpu.VMEM((width, 2 * CAP), jnp.float32),
            pltpu.SemaphoreType.DMA((rows_here // CHUNK,)),
            pltpu.SemaphoreType.DMA((4,)),
            pltpu.SemaphoreType.DMA((width // GROUP,)),
        ],
        compiler_params=pltpu.CompilerParams(vmem_limit_bytes=VMEM_ALL),
        cost_estimate=pl.CostEstimate(
            flops=2 * rows_here * feats * (wide + slots), bytes_accessed=2 * rows_here * wide + 2 * slots * feats, transcendentals=0
        ),
        name="project_sort",
    )(embeddings, basis, list_owner.reshape(lanes, LANES), list_slot.reshape(lanes, LANES))


def moments_kernel(width, me_ref, mean_hbm, e_hbm, keep_ref, send_ref, e_ref, mean_ref, m_ref, sem, mean_sem):
    rows_here, wide = e_ref.shape
    block = wide // width
    bits = width.bit_length() - 1
    tiles = wide // TILE
    mean_copy = pltpu.make_async_copy(mean_hbm, mean_ref, mean_sem)
    mean_copy.start()
    copies = []
    for c in range(rows_here // CHUNK):
        at = pl.ds(c * CHUNK, CHUNK)
        copies.append(pltpu.make_async_copy(e_hbm.at[at], e_ref.at[at], sem.at[c]))
        copies[c].start()
    me = me_ref[0]
    odd = (me & 1) == 1
    mean_copy.wait()
    mean = mean_ref[...]
    for t in range(tiles):
        rows, columns = slice(t * TILE, (t + 1) * TILE), slice(t * TILE, wide)
        if t == 0:
            product = jnp.zeros((TILE, wide), jnp.float32)
            for c in range(rows_here // CHUNK):
                copies[c].wait()
                at = slice(c * CHUNK, (c + 1) * CHUNK)
                product = product + lax.dot_general(
                    e_ref[at, rows], e_ref[at, :], (((0,), (0,)), ((), ())), preferred_element_type=jnp.float32
                )
        else:
            product = lax.dot_general(
                e_ref[:, rows], e_ref[:, columns], (((0,), (0,)), ((), ())), preferred_element_type=jnp.float32
            )
        down = jnp.transpose(jnp.broadcast_to(mean[:, rows] * rows_here, (LANES, TILE)))
        for u in range(t, tiles):
            pieces = []
            for j in range(u * TILE // LANES, (u + 1) * TILE // LANES):
                across = slice(j * LANES, (j + 1) * LANES)
                within = slice(j * LANES - t * TILE, (j + 1) * LANES - t * TILE)
                pieces.append((product[:, within] - down * mean[:, across]).astype(jnp.bfloat16))
            piece = jnp.concatenate(pieces, 1)
            other = slice(u * TILE, (u + 1) * TILE)
            m_ref[rows, other] = piece
            if u > t:
                m_ref[other, rows] = jnp.transpose(piece)
        for pair in range(TILE // block // 2):
            first = t * (TILE // block) + 2 * pair
            apart = (first ^ me) >> 1
            place = 0
            for k in range(bits - 1):
                place = place + (((apart >> k) & 1) << (bits - 2 - k))
            to = pl.ds(pl.multiple_of(place * block, block), block)
            even_rows = m_ref[first * block:(first + 1) * block, :]
            odd_rows = m_ref[(first + 1) * block:(first + 2) * block, :]
            keep_ref[to, :] = jnp.where(odd, odd_rows, even_rows)
            send_ref[to, :] = jnp.where(odd, even_rows, odd_rows)


def moments(width, me, embeddings, mean):
    rows_here, wide = embeddings.shape
    vmem = pl.BlockSpec(memory_space=pltpu.VMEM)
    return pl.pallas_call(
        functools.partial(moments_kernel, width),
        in_specs=[pl.BlockSpec(memory_space=pltpu.SMEM)] + [pl.BlockSpec(memory_space=pl.ANY)] * 2,
        out_specs=[vmem] * 2,
        out_shape=[
            jax.ShapeDtypeStruct((wide // 2, wide), jnp.bfloat16),
            jax.ShapeDtypeStruct((wide // 2, wide), jnp.bfloat16),
        ],
        scratch_shapes=[
            pltpu.VMEM((rows_here, wide), jnp.bfloat16),
            pltpu.VMEM((1, wide), jnp.float32),
            pltpu.VMEM((wide, wide), jnp.bfloat16),
            pltpu.SemaphoreType.DMA((rows_here // CHUNK,)),
            pltpu.SemaphoreType.DMA,
        ],
        compiler_params=pltpu.CompilerParams(vmem_limit_bytes=VMEM_MOST),
        cost_estimate=pl.CostEstimate(
            flops=2 * rows_here * wide * wide, bytes_accessed=2 * rows_here * wide + 3 * wide * wide, transcendentals=0
        ),
        name="moments",
    )(me.reshape(1), mean, embeddings)


def add_kernel(shares, pieces, keep_ref, *refs):
    outs = refs[len(refs) - shares * pieces:]
    came = refs[:len(refs) - shares * pieces]
    rows, columns = outs[0].shape
    for h in range(shares):
        across = slice(h * columns, (h + 1) * columns)
        for p in range(pieces):
            at = slice(p * rows, (p + 1) * rows)
            held = keep_ref[at, across].astype(jnp.float32)
            for ref in came:
                held = held + ref[at, across].astype(jnp.float32)
            out = outs[h * pieces + p]
            out[...] = held.astype(out.dtype)


def add_and_split(keep, came, shares, pieces):
    rows, columns = keep.shape
    vmem = pl.BlockSpec(memory_space=pltpu.VMEM)
    shape = (rows // pieces, columns // shares)
    kinds = [jnp.float32] + [jnp.bfloat16] * (pieces - 1)
    outs = pl.pallas_call(
        functools.partial(add_kernel, shares, pieces),
        in_specs=[vmem] * (1 + len(came)),
        out_specs=[vmem] * (shares * pieces),
        out_shape=[jax.ShapeDtypeStruct(shape, kind) for kind in kinds * shares],
        compiler_params=pltpu.CompilerParams(vmem_limit_bytes=VMEM_SOME),
        cost_estimate=pl.CostEstimate(flops=2 * rows * columns, bytes_accessed=10 * rows * columns, transcendentals=0),
        name="add_and_split",
    )(keep, *came)
    return [outs[h * pieces:(h + 1) * pieces] for h in range(shares)]


def join_kernel(first_ref, second_ref, *refs):
    out_ref = refs[-1]
    columns = first_ref.shape[1]
    out_ref[:, :columns] = first_ref[...]
    out_ref[:, columns:] = second_ref[...]


def join(first, second, after):
    rows, columns = first.shape
    vmem = pl.BlockSpec(memory_space=pltpu.VMEM)
    return pl.pallas_call(
        join_kernel,
        in_specs=[vmem] * 2 + [pl.BlockSpec(memory_space=pl.ANY)] * len(after),
        out_specs=vmem,
        out_shape=jax.ShapeDtypeStruct((rows, 2 * columns), first.dtype),
        compiler_params=pltpu.CompilerParams(vmem_limit_bytes=VMEM_SOME),
        name="join",
    )(first, second, *after)


def finish_kernel(total, between_ref, near_ref, *refs):
    out_ref = refs[-1]
    each = (len(refs) - 1) // SHARES
    columns = out_ref.shape[1] // SHARES
    for h in range(SHARES):
        across = slice(h * columns, (h + 1) * columns)
        held = refs[h * each][...] + near_ref[:, across].astype(jnp.float32)
        for ref in refs[h * each + 1:(h + 1) * each]:
            held = held + ref[...].astype(jnp.float32)
        out_ref[:, across] = (held + between_ref[:, across]) / total


def finish(total, between, near, keeps, came):
    parts = [part for keep, pieces in zip(keeps, came) for part in (keep, *pieces)]
    vmem = pl.BlockSpec(memory_space=pltpu.VMEM)
    return pl.pallas_call(
        functools.partial(finish_kernel, total),
        in_specs=[vmem] * (2 + len(parts)),
        out_specs=vmem,
        out_shape=jax.ShapeDtypeStruct(between.shape, jnp.float32),
        compiler_params=pltpu.CompilerParams(vmem_limit_bytes=VMEM_SOME),
        cost_estimate=pl.CostEstimate(flops=8 * between.size, bytes_accessed=16 * between.size, transcendentals=0),
        name="finish",
    )(between, near, *parts)


def halving_stages(width):
    strides = [1 << k for k in range(width.bit_length() - 1)]
    return [[s] for s in strides[:-2]] + [strides[-2:]]


def exchange(width, apart, piece):
    return lax.ppermute(piece, "wide", [(i, i ^ apart) for i in range(width)])


def encode_kernel(total, me_ref, got_ref, basis_ref, centroid_ref, rotation_ref, *refs):
    out_hbm, between_ref, out_ref, delta_ref, list_ref, apart_ref, sem = refs[-7:]
    width = delta_ref.shape[0]
    feats = out_ref.shape[1]
    owned = centroid_ref.shape[0]
    wide = basis_ref.shape[0]
    block = wide // width
    share = total // width

    notes = jnp.concatenate([got_ref[s * SPAN + CAP:(s + 1) * SPAN, :] for s in range(width)], 0)
    size = width * NOTES
    to = lax.broadcasted_iota(jnp.int32, (size, size), 0)
    of = lax.broadcasted_iota(jnp.int32, (size, size), 1)
    turn = jnp.where((to % width) * NOTES + to // width == of, 1.0, 0.0).astype(jnp.bfloat16)
    turned = jnp.dot(turn, notes, preferred_element_type=jnp.float32)
    row = [turned[r * width:(r + 1) * width] for r in range(NOTES)]
    digits = row[NOTES - 1]
    list_ref[...] = digits[:, :CAP] * 32.0 + digits[:, CAP:] - 1.0
    quarters = wide // feats
    shifts = jnp.zeros((width, feats), jnp.float32)
    for q in range(quarters):
        parts = [row[p * quarters + q] for p in range(3)]
        mean = parts[0] + (parts[1] + parts[2])
        apart_ref[:, q * feats:(q + 1) * feats] = mean - jnp.mean(mean, 0, keepdims=True)
        terms = jnp.dot(
            jnp.concatenate(parts, 0).astype(jnp.bfloat16),
            basis_ref[q * feats:(q + 1) * feats, :],
            preferred_element_type=jnp.float32,
        )
        shifts = shifts + (terms[:width] + (terms[width:2 * width] + terms[2 * width:]))
    square = row[3 * quarters] + (row[3 * quarters + 1] + row[3 * quarters + 2])
    delta = shifts - jnp.mean(shifts, 0, keepdims=True)
    variance = jnp.sum(square + share * (delta * delta), 0, keepdims=True) / total
    scale = lax.rsqrt(variance + 1e-05)
    delta_ref[...] = delta

    names = lax.broadcasted_iota(jnp.int32, (CAP, owned), 1).astype(jnp.int16)

    def encode_group(g):
        columns = jnp.transpose(list_ref[pl.ds(g * GROUP, GROUP), :])
        hits, projected, held = [], [], []
        for s in range(GROUP):
            listed = jnp.broadcast_to(columns[:, s:s + 1], (CAP, LANES))
            held.append(jnp.concatenate([listed] * (feats // LANES), 1) >= 0)
            wanted = jnp.concatenate([listed.astype(jnp.int32).astype(jnp.int16)] * (owned // LANES), 1)
            hits.append(jnp.where(wanted == names, jnp.ones((), jnp.bfloat16), jnp.zeros((), jnp.bfloat16)))
            base = pl.multiple_of((g * GROUP + s) * SPAN, 16)
            rows = got_ref[pl.ds(base, CAP), :].astype(jnp.float32)
            projected.append((rows + delta_ref[pl.ds(g * GROUP + s, 1), :]) * scale)
        centre = jnp.dot(jnp.concatenate(hits, 0), centroid_ref[...], preferred_element_type=jnp.float32)
        residual = jnp.where(jnp.concatenate(held, 0), jnp.concatenate(projected, 0) - centre, 0.0)
        at = pl.ds(pl.multiple_of(g * (GROUP * CAP), GROUP * CAP), GROUP * CAP)
        out_ref[at, :] = jnp.dot(
            residual.astype(jnp.bfloat16), rotation_ref[...], preferred_element_type=jnp.float32
        ).astype(jnp.bfloat16)
        copies = []
        for s in range(GROUP):
            place = g * GROUP + s
            here = pl.ds(pl.multiple_of(place * CAP, CAP), CAP)
            there = pl.ds(pl.multiple_of(device_at(width, place) * CAP, CAP), CAP)
            copies.append(pltpu.make_async_copy(out_ref.at[here], out_hbm.at[there], sem.at[place]))
        return copies

    groups = width // GROUP
    copies = []
    if groups <= 4:
        for g in range(groups):
            for copy in encode_group(g):
                copy.start()
                copies.append(copy)
    else:

        @pl.loop(0, groups)
        def _(g):
            for copy in encode_group(g):
                copy.start()
            for s in range(GROUP):
                at = pl.ds(pl.multiple_of((g * GROUP + s) * CAP, CAP), CAP)
                pltpu.make_async_copy(out_ref.at[at], out_hbm.at[at], sem.at[g * GROUP + s]).wait()

    first = me_ref[0] * block
    near = apart_ref[:, pl.ds(pl.multiple_of(first // LANES * LANES, LANES), LANES)]
    near = pltpu.roll(near, (LANES - first % LANES) % LANES, 1)[:, :block]
    between_ref[...] = share * lax.dot_general(
        near,
        apart_ref[...],
        (((0,), (0,)), ((), ())),
        precision=lax.Precision.HIGHEST,
        preferred_element_type=jnp.float32,
    )
    for copy in copies:
        copy.wait()


def encode(width, total, me, got, basis, centroids, rotation, after):
    wide, feats = basis.shape
    owned = centroids.shape[0]
    slots = width * CAP
    vmem, anywhere = pl.BlockSpec(memory_space=pltpu.VMEM), pl.BlockSpec(memory_space=pl.ANY)
    return pl.pallas_call(
        functools.partial(encode_kernel, total),
        in_specs=[pl.BlockSpec(memory_space=pltpu.SMEM)] + [vmem] * 4 + [anywhere] * len(after),
        out_specs=[anywhere, vmem],
        out_shape=[
            jax.ShapeDtypeStruct((slots, feats), jnp.bfloat16),
            jax.ShapeDtypeStruct((wide // width, wide), jnp.float32),
        ],
        scratch_shapes=[
            pltpu.VMEM((slots, feats), jnp.bfloat16),
            pltpu.VMEM((width, feats), jnp.float32),
            pltpu.VMEM((width, CAP), jnp.float32),
            pltpu.VMEM((width, wide), jnp.float32),
            pltpu.SemaphoreType.DMA((width,)),
        ],
        compiler_params=pltpu.CompilerParams(vmem_limit_bytes=VMEM_SOME),
        cost_estimate=pl.CostEstimate(
            flops=2 * slots * feats * (owned + feats), bytes_accessed=4 * slots * feats, transcendentals=0
        ),
        name="encode",
    )(me.reshape(1), got, basis, centroids, rotation, *after)


def local(embeddings, basis, list_owner, list_slot, centroids, rotation):
    width = lax.axis_size("wide")
    me = lax.axis_index("wide")
    rows_here, wide = embeddings.shape
    feats = basis.shape[1]
    total = rows_here * width

    rows, mean = project_and_sort(width, embeddings, basis, list_owner, list_slot)
    order = [[device_at(width, place) for place in range(width)]]
    got = lax.all_to_all(
        rows.reshape(width, SPAN, feats), "wide", split_axis=0, concat_axis=0, tiled=True, axis_index_groups=order
    )

    keep, send = moments(width, me, embeddings, mean)
    stages = halving_stages(width)
    came = exchange(width, 1, send)
    last = []
    for share in add_and_split(keep, [came], SHARES, 1 << len(stages[1])):
        for n in range(1, len(stages) - 1):
            came = exchange(width, stages[n][0], share[1])
            (share,) = add_and_split(share[0], [came], 1, 1 << len(stages[n + 1]))
        last.append(share)
    near, far = stages[-1]
    came = [[exchange(width, far, share[1]), exchange(width, near + far, share[3])] for share in last]
    encoded, between = encode(
        width, total, me, got.reshape(width * SPAN, feats), basis, centroids, rotation, [share[1] for share in last]
    )
    came_near = exchange(width, near, join(last[0][2], last[1][2], came[0] + came[1] + [between]))
    covariance = finish(total, between, came_near, [share[0] for share in last], came)
    return (encoded, covariance)


def solution(mesh):
    in_specs = (
        P(("groups", "wide"), None),
        P(),
        P(("groups", "wide")),
        P(("groups", "wide")),
        P("wide", None),
        P(),
    )
    out_specs = (P(("groups", "wide"), None), P(("groups", "wide"), None))
    return jax.shard_map(local, mesh=mesh, in_specs=in_specs, out_specs=out_specs, check_vma=False)
```

```python
import functools

import jax
import jax.numpy as jnp
from jax import lax
from jax.experimental import pallas as pl
from jax.experimental.pallas import tpu as pltpu
from jax.sharding import PartitionSpec as P

CAP = 128
LANES = 128
NOTES = 16
SPAN = CAP + NOTES
CHUNK = 512
STEP = 1024
TILE = 256
GROUP = 4
SHARES = 2
PLANE = 4
VMEM_ALL = 60 * 1024 * 1024
VMEM_SOME = 24 * 1024 * 1024
VMEM_MOST = 48 * 1024 * 1024


def place_of(width, device):
    return (device & (PLANE - 1)) * (width // PLANE) + device // PLANE


def device_at(width, place):
    return (place & (width // PLANE - 1)) * PLANE + place // (width // PLANE)


def in_three(x):
    high = x.astype(jnp.bfloat16).astype(jnp.float32)
    rest = x - high
    middle = rest.astype(jnp.bfloat16).astype(jnp.float32)
    return high, middle, (rest - middle).astype(jnp.bfloat16).astype(jnp.float32)


def rows_kernel(
    width, e_hbm, basis_hbm, owner_hbm, slot_hbm,
    rows_hbm, mean_hbm,
    owner_ref, slot_ref, mean_ref, basis_ref, e_ref, rows_ref, y_ref, yb_ref, sum_ref, total_ref, target_ref, list_ref, e_sem, small_sem, sem,
):
    step = pl.program_id(0)
    rows_here, feats = y_ref.shape
    wide = e_ref.shape[1]
    chunks = rows_here // LANES

    def e_copy(c):
        at = pl.ds(pl.multiple_of(c * STEP, STEP), STEP)
        return pltpu.make_async_copy(e_hbm.at[at], e_ref.at[at], e_sem.at[c])

    @pl.when(step == 0)
    def _():
        owner_copy = pltpu.make_async_copy(owner_hbm, owner_ref, small_sem.at[0])
        slot_copy = pltpu.make_async_copy(slot_hbm, slot_ref, small_sem.at[1])
        basis_copy = pltpu.make_async_copy(basis_hbm, basis_ref, small_sem.at[2])
        owner_copy.start()
        e_copy(0).start()
        slot_copy.start()
        basis_copy.start()
        for c in range(1, rows_here // STEP):
            e_copy(c).start()
        owner_copy.wait()
        sum_ref[...] = jnp.zeros_like(sum_ref)
        total_ref[...] = jnp.zeros_like(total_ref)
        owner = place_of(width, owner_ref[...])
        wanted = lax.broadcasted_iota(jnp.int32, (width, LANES), 0)
        hits = [jnp.where(owner[c:c + 1, :] == wanted, 1.0, 0.0) for c in range(chunks)]
        flat = jnp.concatenate(hits, 0).astype(jnp.bfloat16)
        up = lax.broadcasted_iota(jnp.int32, (LANES, LANES), 0)
        to = lax.broadcasted_iota(jnp.int32, (LANES, LANES), 1)
        before = jnp.where(up < to, 1.0, 0.0).astype(jnp.bfloat16)
        every = jnp.ones((LANES, LANES), jnp.bfloat16)
        within = jnp.dot(flat, before, preferred_element_type=jnp.float32)
        counts = jnp.dot(flat, every, preferred_element_type=jnp.float32)
        carry = jnp.zeros((width, LANES), jnp.float32)
        ranks = []
        for c in range(chunks):
            at = slice(c * width, (c + 1) * width)
            ranks.append(jnp.sum(hits[c] * (within[at] + carry), 0, keepdims=True).astype(jnp.int32))
            carry = carry + counts[at]
            target_ref[c:c + 1, :] = owner[c:c + 1, :] * CAP + ranks[c]

        slot_copy.wait()
        slot = slot_ref[...] + 1
        high, low = (slot >> 5).astype(jnp.float32), (slot & 31).astype(jnp.float32)
        spots = lax.broadcasted_iota(jnp.int32, (CAP, LANES), 0)
        placed = jnp.concatenate([jnp.where(ranks[c] == spots, 1.0, 0.0) for c in range(chunks)], 1).astype(jnp.bfloat16)
        digits = jnp.concatenate(
            [
                jnp.concatenate([hits[c] * high[c:c + 1, :] for c in range(chunks)], 1),
                jnp.concatenate([hits[c] * low[c:c + 1, :] for c in range(chunks)], 1),
            ],
            0,
        ).astype(jnp.bfloat16)
        found = lax.dot_general(digits, placed, (((1,), (1,)), ((), ())), preferred_element_type=jnp.float32)
        list_ref[:, :CAP] = found[:width]
        list_ref[:, CAP:] = found[width:]
        basis_copy.wait()

    e_copy(step).wait()
    here = pl.ds(pl.multiple_of(step * STEP, STEP), STEP)
    rows = e_ref[here, :]
    y = jnp.dot(rows, basis_ref[...], preferred_element_type=jnp.float32)
    y_ref[here, :] = y
    sum_ref[...] += jnp.sum(y.reshape(STEP // 8, 8, feats), 0)
    total_ref[...] += jnp.sum(rows.astype(jnp.float32).reshape(STEP // 8, 8, wide), 0)

    @pl.when(step == pl.num_programs(0) - 1)
    def _():
        mean_y = jnp.sum(sum_ref[...], 0, keepdims=True) / rows_here
        square = jnp.zeros((8, feats), jnp.float32)
        for c in range(rows_here // STEP):
            at = slice(c * STEP, (c + 1) * STEP)
            centred = y_ref[at, :] - mean_y
            square = square + jnp.sum((centred * centred).reshape(STEP // 8, 8, feats), 0)
            yb_ref[at, :] = centred.astype(jnp.bfloat16)
        mean = jnp.sum(total_ref[...], 0, keepdims=True) / rows_here
        mean_ref[...] = mean
        mean_copy = pltpu.make_async_copy(mean_ref, mean_hbm, small_sem.at[3])
        mean_copy.start()
        parts = in_three(mean)
        common = [part[:, q * feats:(q + 1) * feats] for part in parts for q in range(wide // feats)]
        common = jnp.concatenate(common + list(in_three(jnp.sum(square, 0, keepdims=True))), 0)

        place = lax.broadcasted_iota(jnp.int32, (GROUP * CAP, LANES), 0).astype(jnp.int16)

        def sort_group(g):
            first = g * GROUP
            pieces = []
            for c in range(chunks):
                wanted = (target_ref[c:c + 1, :] - first * CAP).astype(jnp.int32)
                wanted = jnp.broadcast_to(wanted, (16, LANES)).astype(jnp.int16)
                wanted = jnp.concatenate([wanted] * (GROUP * CAP // 16), 0)
                pieces.append(jnp.where(wanted == place, jnp.ones((), jnp.bfloat16), jnp.zeros((), jnp.bfloat16)))
            pick = jnp.concatenate(pieces, 1)
            rows = jnp.dot(pick, yb_ref[...], preferred_element_type=jnp.float32).astype(jnp.bfloat16)
            for j in range(GROUP):
                base = pl.multiple_of((first + j) * SPAN, 16)
                rows_ref[pl.ds(base, CAP), :] = rows[j * CAP:(j + 1) * CAP]
                notes = jnp.concatenate([common, list_ref[pl.ds(first + j, 1), :]], 0)
                rows_ref[pl.ds(pl.multiple_of(base + CAP, 16), NOTES), :] = notes.astype(jnp.bfloat16)
            at = pl.ds(pl.multiple_of(g * (GROUP * SPAN), 16), GROUP * SPAN)
            return pltpu.make_async_copy(rows_ref.at[at], rows_hbm.at[at], sem.at[g])

        groups = width // GROUP
        if groups <= 4:
            copies = []
            for g in range(groups):
                copies.append(sort_group(g))
                copies[g].start()
            for copy in copies:
                copy.wait()
        else:

            @pl.loop(0, groups)
            def _(g):
                copy = sort_group(g)
                copy.start()
                copy.wait()

        mean_copy.wait()


def project_and_sort(width, embeddings, basis, list_owner, list_slot):
    rows_here, wide = embeddings.shape
    feats = basis.shape[1]
    lanes = rows_here // LANES
    slots = width * SPAN
    return pl.pallas_call(
        functools.partial(rows_kernel, width),
        grid=(rows_here // STEP,),
        in_specs=[pl.BlockSpec(memory_space=pl.ANY)] * 4,
        out_specs=[pl.BlockSpec(memory_space=pl.ANY)] * 2,
        out_shape=[
            jax.ShapeDtypeStruct((slots, feats), jnp.bfloat16),
            jax.ShapeDtypeStruct((1, wide), jnp.float32),
        ],
        scratch_shapes=[
            pltpu.VMEM((lanes, LANES), jnp.int32),
            pltpu.VMEM((lanes, LANES), jnp.int32),
            pltpu.VMEM((1, wide), jnp.float32),
            pltpu.VMEM((wide, feats), jnp.bfloat16),
            pltpu.VMEM((rows_here, wide), jnp.bfloat16),
            pltpu.VMEM((slots, feats), jnp.bfloat16),
            pltpu.VMEM((rows_here, feats), jnp.float32),
            pltpu.VMEM((rows_here, feats), jnp.bfloat16),
            pltpu.VMEM((8, feats), jnp.float32),
            pltpu.VMEM((8, wide), jnp.float32),
            pltpu.VMEM((lanes, LANES), jnp.int32),
            pltpu.VMEM((width, 2 * CAP), jnp.float32),
            pltpu.SemaphoreType.DMA((rows_here // STEP,)),
            pltpu.SemaphoreType.DMA((4,)),
            pltpu.SemaphoreType.DMA((width // GROUP,)),
        ],
        compiler_params=pltpu.CompilerParams(vmem_limit_bytes=VMEM_ALL),
        cost_estimate=pl.CostEstimate(
            flops=2 * rows_here * feats * (wide + slots), bytes_accessed=2 * rows_here * wide + 2 * slots * feats, transcendentals=0
        ),
        name="project_sort",
    )(embeddings, basis, list_owner.reshape(lanes, LANES), list_slot.reshape(lanes, LANES))


def moments_kernel(width, me_ref, mean_hbm, e_hbm, keep_ref, send_ref, e_ref, mean_ref, m_ref, sem, mean_sem):
    rows_here, wide = e_ref.shape
    block = wide // width
    bits = width.bit_length() - 1
    tiles = wide // TILE
    mean_copy = pltpu.make_async_copy(mean_hbm, mean_ref, mean_sem)
    mean_copy.start()
    copies = []
    for c in range(rows_here // CHUNK):
        at = pl.ds(c * CHUNK, CHUNK)
        copies.append(pltpu.make_async_copy(e_hbm.at[at], e_ref.at[at], sem.at[c]))
        copies[c].start()
    me = me_ref[0]
    odd = (me & 1) == 1
    mean_copy.wait()
    mean = mean_ref[...]
    for t in range(tiles):
        rows, columns = slice(t * TILE, (t + 1) * TILE), slice(t * TILE, wide)
        if t == 0:
            product = jnp.zeros((TILE, wide), jnp.float32)
            for c in range(rows_here // CHUNK):
                copies[c].wait()
                at = slice(c * CHUNK, (c + 1) * CHUNK)
                product = product + lax.dot_general(
                    e_ref[at, rows], e_ref[at, :], (((0,), (0,)), ((), ())), preferred_element_type=jnp.float32
                )
        else:
            product = lax.dot_general(
                e_ref[:, rows], e_ref[:, columns], (((0,), (0,)), ((), ())), preferred_element_type=jnp.float32
            )
        down = jnp.transpose(jnp.broadcast_to(mean[:, rows] * rows_here, (LANES, TILE)))
        for u in range(t, tiles):
            pieces = []
            for j in range(u * TILE // LANES, (u + 1) * TILE // LANES):
                across = slice(j * LANES, (j + 1) * LANES)
                within = slice(j * LANES - t * TILE, (j + 1) * LANES - t * TILE)
                pieces.append((product[:, within] - down * mean[:, across]).astype(jnp.bfloat16))
            piece = jnp.concatenate(pieces, 1)
            other = slice(u * TILE, (u + 1) * TILE)
            m_ref[rows, other] = piece
            if u > t:
                m_ref[other, rows] = jnp.transpose(piece)
        for pair in range(TILE // block // 2):
            first = t * (TILE // block) + 2 * pair
            apart = (first ^ me) >> 1
            place = 0
            for k in range(bits - 1):
                place = place + (((apart >> k) & 1) << (bits - 2 - k))
            to = pl.ds(pl.multiple_of(place * block, block), block)
            even_rows = m_ref[first * block:(first + 1) * block, :]
            odd_rows = m_ref[(first + 1) * block:(first + 2) * block, :]
            keep_ref[to, :] = jnp.where(odd, odd_rows, even_rows)
            send_ref[to, :] = jnp.where(odd, even_rows, odd_rows)


def moments(width, me, embeddings, mean):
    rows_here, wide = embeddings.shape
    vmem = pl.BlockSpec(memory_space=pltpu.VMEM)
    return pl.pallas_call(
        functools.partial(moments_kernel, width),
        in_specs=[pl.BlockSpec(memory_space=pltpu.SMEM)] + [pl.BlockSpec(memory_space=pl.ANY)] * 2,
        out_specs=[vmem] * 2,
        out_shape=[
            jax.ShapeDtypeStruct((wide // 2, wide), jnp.bfloat16),
            jax.ShapeDtypeStruct((wide // 2, wide), jnp.bfloat16),
        ],
        scratch_shapes=[
            pltpu.VMEM((rows_here, wide), jnp.bfloat16),
            pltpu.VMEM((1, wide), jnp.float32),
            pltpu.VMEM((wide, wide), jnp.bfloat16),
            pltpu.SemaphoreType.DMA((rows_here // CHUNK,)),
            pltpu.SemaphoreType.DMA,
        ],
        compiler_params=pltpu.CompilerParams(vmem_limit_bytes=VMEM_MOST),
        cost_estimate=pl.CostEstimate(
            flops=2 * rows_here * wide * wide, bytes_accessed=2 * rows_here * wide + 3 * wide * wide, transcendentals=0
        ),
        name="moments",
    )(me.reshape(1), mean, embeddings)


def add_kernel(shares, pieces, keep_ref, *refs):
    outs = refs[len(refs) - shares * pieces:]
    came = refs[:len(refs) - shares * pieces]
    rows, columns = outs[0].shape
    for h in range(shares):
        across = slice(h * columns, (h + 1) * columns)
        for p in range(pieces):
            at = slice(p * rows, (p + 1) * rows)
            held = keep_ref[at, across].astype(jnp.float32)
            for ref in came:
                held = held + ref[at, across].astype(jnp.float32)
            out = outs[h * pieces + p]
            out[...] = held.astype(out.dtype)


def add_and_split(keep, came, shares, pieces):
    rows, columns = keep.shape
    vmem = pl.BlockSpec(memory_space=pltpu.VMEM)
    shape = (rows // pieces, columns // shares)
    kinds = [jnp.float32] + [jnp.bfloat16] * (pieces - 1)
    outs = pl.pallas_call(
        functools.partial(add_kernel, shares, pieces),
        in_specs=[vmem] * (1 + len(came)),
        out_specs=[vmem] * (shares * pieces),
        out_shape=[jax.ShapeDtypeStruct(shape, kind) for kind in kinds * shares],
        compiler_params=pltpu.CompilerParams(vmem_limit_bytes=VMEM_SOME),
        cost_estimate=pl.CostEstimate(flops=2 * rows * columns, bytes_accessed=10 * rows * columns, transcendentals=0),
        name="add_and_split",
    )(keep, *came)
    return [outs[h * pieces:(h + 1) * pieces] for h in range(shares)]


def finish_kernel(total, between_ref, *refs):
    out_ref = refs[-1]
    each = (len(refs) - 1) // SHARES
    columns = out_ref.shape[1] // SHARES
    for h in range(SHARES):
        across = slice(h * columns, (h + 1) * columns)
        held = refs[h * each][...]
        for ref in refs[h * each + 1:(h + 1) * each]:
            held = held + ref[...].astype(jnp.float32)
        out_ref[:, across] = (held + between_ref[:, across]) / total


def finish(total, between, keeps, came):
    parts = [part for keep, pieces in zip(keeps, came) for part in (keep, *pieces)]
    vmem = pl.BlockSpec(memory_space=pltpu.VMEM)
    return pl.pallas_call(
        functools.partial(finish_kernel, total),
        in_specs=[vmem] * (1 + len(parts)),
        out_specs=vmem,
        out_shape=jax.ShapeDtypeStruct(between.shape, jnp.float32),
        compiler_params=pltpu.CompilerParams(vmem_limit_bytes=VMEM_SOME),
        cost_estimate=pl.CostEstimate(flops=8 * between.size, bytes_accessed=16 * between.size, transcendentals=0),
        name="finish",
    )(between, *parts)


def halving_stages(width):
    strides = [1 << k for k in range(width.bit_length() - 1)]
    return [[s] for s in strides[:-2]] + [strides[-2:]]


def exchange(width, stage, out):
    came = []
    for p in (2, 1, 3) if len(stage) == 2 else (1,):
        apart = sum(s for k, s in enumerate(stage) if (p >> (len(stage) - 1 - k)) & 1)
        came.append(lax.ppermute(out[p - 1], "wide", [(i, i ^ apart) for i in range(width)]))
    return came


def encode_kernel(total, me_ref, got_ref, basis_ref, centroid_ref, rotation_ref, *refs):
    out_hbm, between_ref, out_ref, delta_ref, list_ref, apart_ref, sem = refs[-7:]
    width = delta_ref.shape[0]
    feats = out_ref.shape[1]
    owned = centroid_ref.shape[0]
    wide = basis_ref.shape[0]
    block = wide // width
    share = total // width

    notes = jnp.concatenate([got_ref[s * SPAN + CAP:(s + 1) * SPAN, :] for s in range(width)], 0)
    size = width * NOTES
    to = lax.broadcasted_iota(jnp.int32, (size, size), 0)
    of = lax.broadcasted_iota(jnp.int32, (size, size), 1)
    turn = jnp.where((to % width) * NOTES + to // width == of, 1.0, 0.0).astype(jnp.bfloat16)
    turned = jnp.dot(turn, notes, preferred_element_type=jnp.float32)
    row = [turned[r * width:(r + 1) * width] for r in range(NOTES)]
    digits = row[NOTES - 1]
    list_ref[...] = digits[:, :CAP] * 32.0 + digits[:, CAP:] - 1.0
    quarters = wide // feats
    shifts = jnp.zeros((width, feats), jnp.float32)
    for q in range(quarters):
        parts = [row[p * quarters + q] for p in range(3)]
        mean = parts[0] + (parts[1] + parts[2])
        apart_ref[:, q * feats:(q + 1) * feats] = mean - jnp.mean(mean, 0, keepdims=True)
        terms = jnp.dot(
            jnp.concatenate(parts, 0).astype(jnp.bfloat16),
            basis_ref[q * feats:(q + 1) * feats, :],
            preferred_element_type=jnp.float32,
        )
        shifts = shifts + (terms[:width] + (terms[width:2 * width] + terms[2 * width:]))
    square = row[3 * quarters] + (row[3 * quarters + 1] + row[3 * quarters + 2])
    delta = shifts - jnp.mean(shifts, 0, keepdims=True)
    variance = jnp.sum(square + share * (delta * delta), 0, keepdims=True) / total
    scale = lax.rsqrt(variance + 1e-05)
    delta_ref[...] = delta

    names = lax.broadcasted_iota(jnp.int32, (CAP, owned), 1).astype(jnp.int16)

    def encode_group(g):
        columns = jnp.transpose(list_ref[pl.ds(g * GROUP, GROUP), :])
        hits, projected, held = [], [], []
        for s in range(GROUP):
            listed = jnp.broadcast_to(columns[:, s:s + 1], (CAP, LANES))
            held.append(jnp.concatenate([listed] * (feats // LANES), 1) >= 0)
            wanted = jnp.concatenate([listed.astype(jnp.int32).astype(jnp.int16)] * (owned // LANES), 1)
            hits.append(jnp.where(wanted == names, jnp.ones((), jnp.bfloat16), jnp.zeros((), jnp.bfloat16)))
            base = pl.multiple_of((g * GROUP + s) * SPAN, 16)
            rows = got_ref[pl.ds(base, CAP), :].astype(jnp.float32)
            projected.append((rows + delta_ref[pl.ds(g * GROUP + s, 1), :]) * scale)
        centre = jnp.dot(jnp.concatenate(hits, 0), centroid_ref[...], preferred_element_type=jnp.float32)
        residual = jnp.where(jnp.concatenate(held, 0), jnp.concatenate(projected, 0) - centre, 0.0)
        at = pl.ds(pl.multiple_of(g * (GROUP * CAP), GROUP * CAP), GROUP * CAP)
        out_ref[at, :] = jnp.dot(
            residual.astype(jnp.bfloat16), rotation_ref[...], preferred_element_type=jnp.float32
        ).astype(jnp.bfloat16)
        copies = []
        for s in range(GROUP):
            place = g * GROUP + s
            here = pl.ds(pl.multiple_of(place * CAP, CAP), CAP)
            there = pl.ds(pl.multiple_of(device_at(width, place) * CAP, CAP), CAP)
            copies.append(pltpu.make_async_copy(out_ref.at[here], out_hbm.at[there], sem.at[place]))
        return copies

    groups = width // GROUP
    copies = []
    if groups <= 4:
        for g in range(groups):
            for copy in encode_group(g):
                copy.start()
                copies.append(copy)
    else:

        @pl.loop(0, groups)
        def _(g):
            for copy in encode_group(g):
                copy.start()
            for s in range(GROUP):
                at = pl.ds(pl.multiple_of((g * GROUP + s) * CAP, CAP), CAP)
                pltpu.make_async_copy(out_ref.at[at], out_hbm.at[at], sem.at[g * GROUP + s]).wait()

    first = me_ref[0] * block
    near = apart_ref[:, pl.ds(pl.multiple_of(first // LANES * LANES, LANES), LANES)]
    near = pltpu.roll(near, (LANES - first % LANES) % LANES, 1)[:, :block]
    between_ref[...] = share * lax.dot_general(
        near,
        apart_ref[...],
        (((0,), (0,)), ((), ())),
        precision=lax.Precision.HIGHEST,
        preferred_element_type=jnp.float32,
    )
    for copy in copies:
        copy.wait()


def encode(width, total, me, got, basis, centroids, rotation, after):
    wide, feats = basis.shape
    owned = centroids.shape[0]
    slots = width * CAP
    vmem, anywhere = pl.BlockSpec(memory_space=pltpu.VMEM), pl.BlockSpec(memory_space=pl.ANY)
    return pl.pallas_call(
        functools.partial(encode_kernel, total),
        in_specs=[pl.BlockSpec(memory_space=pltpu.SMEM)] + [vmem] * 4 + [anywhere] * len(after),
        out_specs=[anywhere, vmem],
        out_shape=[
            jax.ShapeDtypeStruct((slots, feats), jnp.bfloat16),
            jax.ShapeDtypeStruct((wide // width, wide), jnp.float32),
        ],
        scratch_shapes=[
            pltpu.VMEM((slots, feats), jnp.bfloat16),
            pltpu.VMEM((width, feats), jnp.float32),
            pltpu.VMEM((width, CAP), jnp.float32),
            pltpu.VMEM((width, wide), jnp.float32),
            pltpu.SemaphoreType.DMA((width,)),
        ],
        compiler_params=pltpu.CompilerParams(vmem_limit_bytes=VMEM_SOME),
        cost_estimate=pl.CostEstimate(
            flops=2 * slots * feats * (owned + feats), bytes_accessed=4 * slots * feats, transcendentals=0
        ),
        name="encode",
    )(me.reshape(1), got, basis, centroids, rotation, *after)


def local(embeddings, basis, list_owner, list_slot, centroids, rotation):
    width = lax.axis_size("wide")
    me = lax.axis_index("wide")
    rows_here, wide = embeddings.shape
    feats = basis.shape[1]
    total = rows_here * width

    rows, mean = project_and_sort(width, embeddings, basis, list_owner, list_slot)
    order = [[device_at(width, place) for place in range(width)]]
    got = lax.all_to_all(
        rows.reshape(width, SPAN, feats), "wide", split_axis=0, concat_axis=0, tiled=True, axis_index_groups=order
    )

    keep, send = moments(width, me, embeddings, mean)
    stages = halving_stages(width)
    came = exchange(width, stages[0], [send])
    shares = add_and_split(keep, came, SHARES, 1 << len(stages[1]))
    last = []
    for share in shares:
        for n in range(1, len(stages) - 1):
            came = exchange(width, stages[n], share[1:])
            (share,) = add_and_split(share[0], came, 1, 1 << len(stages[n + 1]))
        last.append(share)
    came = [exchange(width, stages[-1], share[1:]) for share in last]
    encoded, between = encode(
        width, total, me, got.reshape(width * SPAN, feats), basis, centroids, rotation, [share[1] for share in last]
    )
    covariance = finish(total, between, [share[0] for share in last], came)
    return (encoded, covariance)


def solution(mesh):
    in_specs = (
        P(("groups", "wide"), None),
        P(),
        P(("groups", "wide")),
        P(("groups", "wide")),
        P("wide", None),
        P(),
    )
    out_specs = (P(("groups", "wide"), None), P(("groups", "wide"), None))
    return jax.shard_map(local, mesh=mesh, in_specs=in_specs, out_specs=out_specs, check_vma=False)
```

```python
import functools

import jax
import jax.numpy as jnp
from jax import lax
from jax.experimental import pallas as pl
from jax.experimental.pallas import tpu as pltpu
from jax.sharding import PartitionSpec as P

CAP = 128
LANES = 128
NOTES = 16
SPAN = CAP + NOTES
CHUNK = 512
STEP = 2048
TILE = 256
GROUP = 4
SHARES = 2
PLANE = 4
VMEM_ALL = 60 * 1024 * 1024
VMEM_SOME = 24 * 1024 * 1024
VMEM_MOST = 48 * 1024 * 1024


def place_of(width, device):
    return (device & (PLANE - 1)) * (width // PLANE) + device // PLANE


def device_at(width, place):
    return (place & (width // PLANE - 1)) * PLANE + place // (width // PLANE)


def in_three(x):
    high = x.astype(jnp.bfloat16).astype(jnp.float32)
    rest = x - high
    middle = rest.astype(jnp.bfloat16).astype(jnp.float32)
    return high, middle, (rest - middle).astype(jnp.bfloat16).astype(jnp.float32)


def rows_kernel(
    width, e_hbm, basis_hbm, owner_hbm, slot_hbm,
    rows_hbm, mean_hbm,
    owner_ref, slot_ref, mean_ref, basis_ref, e_ref, rows_ref, y_ref, yb_ref, sum_ref, total_ref, target_ref, list_ref, e_sem, small_sem, sem,
):
    step = pl.program_id(0)
    rows_here, feats = y_ref.shape
    wide = e_ref.shape[1]
    chunks = rows_here // LANES

    def e_copy(c):
        at = pl.ds(pl.multiple_of(c * STEP, STEP), STEP)
        return pltpu.make_async_copy(e_hbm.at[at], e_ref.at[at], e_sem.at[c])

    @pl.when(step == 0)
    def _():
        owner_copy = pltpu.make_async_copy(owner_hbm, owner_ref, small_sem.at[0])
        slot_copy = pltpu.make_async_copy(slot_hbm, slot_ref, small_sem.at[1])
        basis_copy = pltpu.make_async_copy(basis_hbm, basis_ref, small_sem.at[2])
        owner_copy.start()
        e_copy(0).start()
        slot_copy.start()
        basis_copy.start()
        for c in range(1, rows_here // STEP):
            e_copy(c).start()
        owner_copy.wait()
        sum_ref[...] = jnp.zeros_like(sum_ref)
        total_ref[...] = jnp.zeros_like(total_ref)
        owner = place_of(width, owner_ref[...])
        wanted = lax.broadcasted_iota(jnp.int32, (width, LANES), 0)
        hits = [jnp.where(owner[c:c + 1, :] == wanted, 1.0, 0.0) for c in range(chunks)]
        flat = jnp.concatenate(hits, 0).astype(jnp.bfloat16)
        up = lax.broadcasted_iota(jnp.int32, (LANES, LANES), 0)
        to = lax.broadcasted_iota(jnp.int32, (LANES, LANES), 1)
        before = jnp.where(up < to, 1.0, 0.0).astype(jnp.bfloat16)
        every = jnp.ones((LANES, LANES), jnp.bfloat16)
        within = jnp.dot(flat, before, preferred_element_type=jnp.float32)
        counts = jnp.dot(flat, every, preferred_element_type=jnp.float32)
        carry = jnp.zeros((width, LANES), jnp.float32)
        ranks = []
        for c in range(chunks):
            at = slice(c * width, (c + 1) * width)
            ranks.append(jnp.sum(hits[c] * (within[at] + carry), 0, keepdims=True).astype(jnp.int32))
            carry = carry + counts[at]
            target_ref[c:c + 1, :] = owner[c:c + 1, :] * CAP + ranks[c]

        slot_copy.wait()
        slot = slot_ref[...] + 1
        high, low = (slot >> 5).astype(jnp.float32), (slot & 31).astype(jnp.float32)
        spots = lax.broadcasted_iota(jnp.int32, (CAP, LANES), 0)
        placed = jnp.concatenate([jnp.where(ranks[c] == spots, 1.0, 0.0) for c in range(chunks)], 1).astype(jnp.bfloat16)
        digits = jnp.concatenate(
            [
                jnp.concatenate([hits[c] * high[c:c + 1, :] for c in range(chunks)], 1),
                jnp.concatenate([hits[c] * low[c:c + 1, :] for c in range(chunks)], 1),
            ],
            0,
        ).astype(jnp.bfloat16)
        found = lax.dot_general(digits, placed, (((1,), (1,)), ((), ())), preferred_element_type=jnp.float32)
        list_ref[:, :CAP] = found[:width]
        list_ref[:, CAP:] = found[width:]
        basis_copy.wait()

    e_copy(step).wait()
    here = pl.ds(pl.multiple_of(step * STEP, STEP), STEP)
    rows = e_ref[here, :]
    y = jnp.dot(rows, basis_ref[...], preferred_element_type=jnp.float32)
    y_ref[here, :] = y
    sum_ref[...] += jnp.sum(y.reshape(STEP // 8, 8, feats), 0)
    total_ref[...] += jnp.sum(rows.astype(jnp.float32).reshape(STEP // 8, 8, wide), 0)

    @pl.when(step == pl.num_programs(0) - 1)
    def _():
        mean_y = jnp.sum(sum_ref[...], 0, keepdims=True) / rows_here
        square = jnp.zeros((8, feats), jnp.float32)
        for c in range(rows_here // STEP):
            at = slice(c * STEP, (c + 1) * STEP)
            centred = y_ref[at, :] - mean_y
            square = square + jnp.sum((centred * centred).reshape(STEP // 8, 8, feats), 0)
            yb_ref[at, :] = centred.astype(jnp.bfloat16)
        mean = jnp.sum(total_ref[...], 0, keepdims=True) / rows_here
        mean_ref[...] = mean
        mean_copy = pltpu.make_async_copy(mean_ref, mean_hbm, small_sem.at[3])
        mean_copy.start()
        parts = in_three(mean)
        common = [part[:, q * feats:(q + 1) * feats] for part in parts for q in range(wide // feats)]
        common = jnp.concatenate(common + list(in_three(jnp.sum(square, 0, keepdims=True))), 0)

        place = lax.broadcasted_iota(jnp.int32, (GROUP * CAP, LANES), 0).astype(jnp.int16)

        def sort_group(g):
            first = g * GROUP
            pieces = []
            for c in range(chunks):
                wanted = (target_ref[c:c + 1, :] - first * CAP).astype(jnp.int32)
                wanted = jnp.broadcast_to(wanted, (16, LANES)).astype(jnp.int16)
                wanted = jnp.concatenate([wanted] * (GROUP * CAP // 16), 0)
                pieces.append(jnp.where(wanted == place, jnp.ones((), jnp.bfloat16), jnp.zeros((), jnp.bfloat16)))
            pick = jnp.concatenate(pieces, 1)
            rows = jnp.dot(pick, yb_ref[...], preferred_element_type=jnp.float32).astype(jnp.bfloat16)
            for j in range(GROUP):
                base = pl.multiple_of((first + j) * SPAN, 16)
                rows_ref[pl.ds(base, CAP), :] = rows[j * CAP:(j + 1) * CAP]
                notes = jnp.concatenate([common, list_ref[pl.ds(first + j, 1), :]], 0)
                rows_ref[pl.ds(pl.multiple_of(base + CAP, 16), NOTES), :] = notes.astype(jnp.bfloat16)
            at = pl.ds(pl.multiple_of(g * (GROUP * SPAN), 16), GROUP * SPAN)
            return pltpu.make_async_copy(rows_ref.at[at], rows_hbm.at[at], sem.at[g])

        groups = width // GROUP
        if groups <= 4:
            copies = []
            for g in range(groups):
                copies.append(sort_group(g))
                copies[g].start()
            for copy in copies:
                copy.wait()
        else:

            @pl.loop(0, groups)
            def _(g):
                copy = sort_group(g)
                copy.start()
                copy.wait()

        mean_copy.wait()


def project_and_sort(width, embeddings, basis, list_owner, list_slot):
    rows_here, wide = embeddings.shape
    feats = basis.shape[1]
    lanes = rows_here // LANES
    slots = width * SPAN
    return pl.pallas_call(
        functools.partial(rows_kernel, width),
        grid=(rows_here // STEP,),
        in_specs=[pl.BlockSpec(memory_space=pl.ANY)] * 4,
        out_specs=[pl.BlockSpec(memory_space=pl.ANY)] * 2,
        out_shape=[
            jax.ShapeDtypeStruct((slots, feats), jnp.bfloat16),
            jax.ShapeDtypeStruct((1, wide), jnp.float32),
        ],
        scratch_shapes=[
            pltpu.VMEM((lanes, LANES), jnp.int32),
            pltpu.VMEM((lanes, LANES), jnp.int32),
            pltpu.VMEM((1, wide), jnp.float32),
            pltpu.VMEM((wide, feats), jnp.bfloat16),
            pltpu.VMEM((rows_here, wide), jnp.bfloat16),
            pltpu.VMEM((slots, feats), jnp.bfloat16),
            pltpu.VMEM((rows_here, feats), jnp.float32),
            pltpu.VMEM((rows_here, feats), jnp.bfloat16),
            pltpu.VMEM((8, feats), jnp.float32),
            pltpu.VMEM((8, wide), jnp.float32),
            pltpu.VMEM((lanes, LANES), jnp.int32),
            pltpu.VMEM((width, 2 * CAP), jnp.float32),
            pltpu.SemaphoreType.DMA((rows_here // STEP,)),
            pltpu.SemaphoreType.DMA((4,)),
            pltpu.SemaphoreType.DMA((width // GROUP,)),
        ],
        compiler_params=pltpu.CompilerParams(vmem_limit_bytes=VMEM_ALL),
        cost_estimate=pl.CostEstimate(
            flops=2 * rows_here * feats * (wide + slots), bytes_accessed=2 * rows_here * wide + 2 * slots * feats, transcendentals=0
        ),
        name="project_sort",
    )(embeddings, basis, list_owner.reshape(lanes, LANES), list_slot.reshape(lanes, LANES))


def moments_kernel(width, me_ref, mean_hbm, e_hbm, keep_ref, send_ref, e_ref, mean_ref, m_ref, sem, mean_sem):
    rows_here, wide = e_ref.shape
    block = wide // width
    bits = width.bit_length() - 1
    tiles = wide // TILE
    mean_copy = pltpu.make_async_copy(mean_hbm, mean_ref, mean_sem)
    mean_copy.start()
    copies = []
    for c in range(rows_here // CHUNK):
        at = pl.ds(c * CHUNK, CHUNK)
        copies.append(pltpu.make_async_copy(e_hbm.at[at], e_ref.at[at], sem.at[c]))
        copies[c].start()
    me = me_ref[0]
    odd = (me & 1) == 1
    mean_copy.wait()
    mean = mean_ref[...]
    for t in range(tiles):
        rows, columns = slice(t * TILE, (t + 1) * TILE), slice(t * TILE, wide)
        if t == 0:
            product = jnp.zeros((TILE, wide), jnp.float32)
            for c in range(rows_here // CHUNK):
                copies[c].wait()
                at = slice(c * CHUNK, (c + 1) * CHUNK)
                product = product + lax.dot_general(
                    e_ref[at, rows], e_ref[at, :], (((0,), (0,)), ((), ())), preferred_element_type=jnp.float32
                )
        else:
            product = lax.dot_general(
                e_ref[:, rows], e_ref[:, columns], (((0,), (0,)), ((), ())), preferred_element_type=jnp.float32
            )
        down = jnp.transpose(jnp.broadcast_to(mean[:, rows] * rows_here, (LANES, TILE)))
        for u in range(t, tiles):
            pieces = []
            for j in range(u * TILE // LANES, (u + 1) * TILE // LANES):
                across = slice(j * LANES, (j + 1) * LANES)
                within = slice(j * LANES - t * TILE, (j + 1) * LANES - t * TILE)
                pieces.append((product[:, within] - down * mean[:, across]).astype(jnp.bfloat16))
            piece = jnp.concatenate(pieces, 1)
            other = slice(u * TILE, (u + 1) * TILE)
            m_ref[rows, other] = piece
            if u > t:
                m_ref[other, rows] = jnp.transpose(piece)
        for pair in range(TILE // block // 2):
            first = t * (TILE // block) + 2 * pair
            apart = (first ^ me) >> 1
            place = 0
            for k in range(bits - 1):
                place = place + (((apart >> k) & 1) << (bits - 2 - k))
            to = pl.ds(pl.multiple_of(place * block, block), block)
            even_rows = m_ref[first * block:(first + 1) * block, :]
            odd_rows = m_ref[(first + 1) * block:(first + 2) * block, :]
            keep_ref[to, :] = jnp.where(odd, odd_rows, even_rows)
            send_ref[to, :] = jnp.where(odd, even_rows, odd_rows)


def moments(width, me, embeddings, mean):
    rows_here, wide = embeddings.shape
    vmem = pl.BlockSpec(memory_space=pltpu.VMEM)
    return pl.pallas_call(
        functools.partial(moments_kernel, width),
        in_specs=[pl.BlockSpec(memory_space=pltpu.SMEM)] + [pl.BlockSpec(memory_space=pl.ANY)] * 2,
        out_specs=[vmem] * 2,
        out_shape=[
            jax.ShapeDtypeStruct((wide // 2, wide), jnp.bfloat16),
            jax.ShapeDtypeStruct((wide // 2, wide), jnp.bfloat16),
        ],
        scratch_shapes=[
            pltpu.VMEM((rows_here, wide), jnp.bfloat16),
            pltpu.VMEM((1, wide), jnp.float32),
            pltpu.VMEM((wide, wide), jnp.bfloat16),
            pltpu.SemaphoreType.DMA((rows_here // CHUNK,)),
            pltpu.SemaphoreType.DMA,
        ],
        compiler_params=pltpu.CompilerParams(vmem_limit_bytes=VMEM_MOST),
        cost_estimate=pl.CostEstimate(
            flops=2 * rows_here * wide * wide, bytes_accessed=2 * rows_here * wide + 3 * wide * wide, transcendentals=0
        ),
        name="moments",
    )(me.reshape(1), mean, embeddings)


def add_kernel(shares, pieces, keep_ref, *refs):
    outs = refs[len(refs) - shares * pieces:]
    came = refs[:len(refs) - shares * pieces]
    rows, columns = outs[0].shape
    for h in range(shares):
        across = slice(h * columns, (h + 1) * columns)
        for p in range(pieces):
            at = slice(p * rows, (p + 1) * rows)
            held = keep_ref[at, across].astype(jnp.float32)
            for ref in came:
                held = held + ref[at, across].astype(jnp.float32)
            out = outs[h * pieces + p]
            out[...] = held.astype(out.dtype)


def add_and_split(keep, came, shares, pieces):
    rows, columns = keep.shape
    vmem = pl.BlockSpec(memory_space=pltpu.VMEM)
    shape = (rows // pieces, columns // shares)
    kinds = [jnp.float32] + [jnp.bfloat16] * (pieces - 1)
    outs = pl.pallas_call(
        functools.partial(add_kernel, shares, pieces),
        in_specs=[vmem] * (1 + len(came)),
        out_specs=[vmem] * (shares * pieces),
        out_shape=[jax.ShapeDtypeStruct(shape, kind) for kind in kinds * shares],
        compiler_params=pltpu.CompilerParams(vmem_limit_bytes=VMEM_SOME),
        cost_estimate=pl.CostEstimate(flops=2 * rows * columns, bytes_accessed=10 * rows * columns, transcendentals=0),
        name="add_and_split",
    )(keep, *came)
    return [outs[h * pieces:(h + 1) * pieces] for h in range(shares)]


def finish_kernel(total, between_ref, *refs):
    out_ref = refs[-1]
    each = (len(refs) - 1) // SHARES
    columns = out_ref.shape[1] // SHARES
    for h in range(SHARES):
        across = slice(h * columns, (h + 1) * columns)
        held = refs[h * each][...]
        for ref in refs[h * each + 1:(h + 1) * each]:
            held = held + ref[...].astype(jnp.float32)
        out_ref[:, across] = (held + between_ref[:, across]) / total


def finish(total, between, keeps, came):
    parts = [part for keep, pieces in zip(keeps, came) for part in (keep, *pieces)]
    vmem = pl.BlockSpec(memory_space=pltpu.VMEM)
    return pl.pallas_call(
        functools.partial(finish_kernel, total),
        in_specs=[vmem] * (1 + len(parts)),
        out_specs=vmem,
        out_shape=jax.ShapeDtypeStruct(between.shape, jnp.float32),
        compiler_params=pltpu.CompilerParams(vmem_limit_bytes=VMEM_SOME),
        cost_estimate=pl.CostEstimate(flops=8 * between.size, bytes_accessed=16 * between.size, transcendentals=0),
        name="finish",
    )(between, *parts)


def halving_stages(width):
    strides = [1 << k for k in range(width.bit_length() - 1)]
    return [[s] for s in strides[:-2]] + [strides[-2:]]


def exchange(width, stage, out):
    came = []
    for p in (2, 1, 3) if len(stage) == 2 else (1,):
        apart = sum(s for k, s in enumerate(stage) if (p >> (len(stage) - 1 - k)) & 1)
        came.append(lax.ppermute(out[p - 1], "wide", [(i, i ^ apart) for i in range(width)]))
    return came


def encode_kernel(total, me_ref, got_ref, basis_ref, centroid_ref, rotation_ref, *refs):
    out_hbm, between_ref, out_ref, delta_ref, list_ref, apart_ref, sem = refs[-7:]
    width = delta_ref.shape[0]
    feats = out_ref.shape[1]
    owned = centroid_ref.shape[0]
    wide = basis_ref.shape[0]
    block = wide // width
    share = total // width

    notes = jnp.concatenate([got_ref[s * SPAN + CAP:(s + 1) * SPAN, :] for s in range(width)], 0)
    size = width * NOTES
    to = lax.broadcasted_iota(jnp.int32, (size, size), 0)
    of = lax.broadcasted_iota(jnp.int32, (size, size), 1)
    turn = jnp.where((to % width) * NOTES + to // width == of, 1.0, 0.0).astype(jnp.bfloat16)
    turned = jnp.dot(turn, notes, preferred_element_type=jnp.float32)
    row = [turned[r * width:(r + 1) * width] for r in range(NOTES)]
    digits = row[NOTES - 1]
    list_ref[...] = digits[:, :CAP] * 32.0 + digits[:, CAP:] - 1.0
    quarters = wide // feats
    shifts = jnp.zeros((width, feats), jnp.float32)
    for q in range(quarters):
        parts = [row[p * quarters + q] for p in range(3)]
        mean = parts[0] + (parts[1] + parts[2])
        apart_ref[:, q * feats:(q + 1) * feats] = mean - jnp.mean(mean, 0, keepdims=True)
        terms = jnp.dot(
            jnp.concatenate(parts, 0).astype(jnp.bfloat16),
            basis_ref[q * feats:(q + 1) * feats, :],
            preferred_element_type=jnp.float32,
        )
        shifts = shifts + (terms[:width] + (terms[width:2 * width] + terms[2 * width:]))
    square = row[3 * quarters] + (row[3 * quarters + 1] + row[3 * quarters + 2])
    delta = shifts - jnp.mean(shifts, 0, keepdims=True)
    variance = jnp.sum(square + share * (delta * delta), 0, keepdims=True) / total
    scale = lax.rsqrt(variance + 1e-05)
    delta_ref[...] = delta

    names = lax.broadcasted_iota(jnp.int32, (CAP, owned), 1).astype(jnp.int16)

    def encode_group(g):
        columns = jnp.transpose(list_ref[pl.ds(g * GROUP, GROUP), :])
        hits, projected, held = [], [], []
        for s in range(GROUP):
            listed = jnp.broadcast_to(columns[:, s:s + 1], (CAP, LANES))
            held.append(jnp.concatenate([listed] * (feats // LANES), 1) >= 0)
            wanted = jnp.concatenate([listed.astype(jnp.int32).astype(jnp.int16)] * (owned // LANES), 1)
            hits.append(jnp.where(wanted == names, jnp.ones((), jnp.bfloat16), jnp.zeros((), jnp.bfloat16)))
            base = pl.multiple_of((g * GROUP + s) * SPAN, 16)
            rows = got_ref[pl.ds(base, CAP), :].astype(jnp.float32)
            projected.append((rows + delta_ref[pl.ds(g * GROUP + s, 1), :]) * scale)
        centre = jnp.dot(jnp.concatenate(hits, 0), centroid_ref[...], preferred_element_type=jnp.float32)
        residual = jnp.where(jnp.concatenate(held, 0), jnp.concatenate(projected, 0) - centre, 0.0)
        at = pl.ds(pl.multiple_of(g * (GROUP * CAP), GROUP * CAP), GROUP * CAP)
        out_ref[at, :] = jnp.dot(
            residual.astype(jnp.bfloat16), rotation_ref[...], preferred_element_type=jnp.float32
        ).astype(jnp.bfloat16)
        copies = []
        for s in range(GROUP):
            place = g * GROUP + s
            here = pl.ds(pl.multiple_of(place * CAP, CAP), CAP)
            there = pl.ds(pl.multiple_of(device_at(width, place) * CAP, CAP), CAP)
            copies.append(pltpu.make_async_copy(out_ref.at[here], out_hbm.at[there], sem.at[place]))
        return copies

    groups = width // GROUP
    copies = []
    if groups <= 4:
        for g in range(groups):
            for copy in encode_group(g):
                copy.start()
                copies.append(copy)
    else:

        @pl.loop(0, groups)
        def _(g):
            for copy in encode_group(g):
                copy.start()
            for s in range(GROUP):
                at = pl.ds(pl.multiple_of((g * GROUP + s) * CAP, CAP), CAP)
                pltpu.make_async_copy(out_ref.at[at], out_hbm.at[at], sem.at[g * GROUP + s]).wait()

    first = me_ref[0] * block
    near = apart_ref[:, pl.ds(pl.multiple_of(first // LANES * LANES, LANES), LANES)]
    near = pltpu.roll(near, (LANES - first % LANES) % LANES, 1)[:, :block]
    between_ref[...] = share * lax.dot_general(
        near,
        apart_ref[...],
        (((0,), (0,)), ((), ())),
        precision=lax.Precision.HIGHEST,
        preferred_element_type=jnp.float32,
    )
    for copy in copies:
        copy.wait()


def encode(width, total, me, got, basis, centroids, rotation, after):
    wide, feats = basis.shape
    owned = centroids.shape[0]
    slots = width * CAP
    vmem, anywhere = pl.BlockSpec(memory_space=pltpu.VMEM), pl.BlockSpec(memory_space=pl.ANY)
    return pl.pallas_call(
        functools.partial(encode_kernel, total),
        in_specs=[pl.BlockSpec(memory_space=pltpu.SMEM)] + [vmem] * 4 + [anywhere] * len(after),
        out_specs=[anywhere, vmem],
        out_shape=[
            jax.ShapeDtypeStruct((slots, feats), jnp.bfloat16),
            jax.ShapeDtypeStruct((wide // width, wide), jnp.float32),
        ],
        scratch_shapes=[
            pltpu.VMEM((slots, feats), jnp.bfloat16),
            pltpu.VMEM((width, feats), jnp.float32),
            pltpu.VMEM((width, CAP), jnp.float32),
            pltpu.VMEM((width, wide), jnp.float32),
            pltpu.SemaphoreType.DMA((width,)),
        ],
        compiler_params=pltpu.CompilerParams(vmem_limit_bytes=VMEM_SOME),
        cost_estimate=pl.CostEstimate(
            flops=2 * slots * feats * (owned + feats), bytes_accessed=4 * slots * feats, transcendentals=0
        ),
        name="encode",
    )(me.reshape(1), got, basis, centroids, rotation, *after)


def local(embeddings, basis, list_owner, list_slot, centroids, rotation):
    width = lax.axis_size("wide")
    me = lax.axis_index("wide")
    rows_here, wide = embeddings.shape
    feats = basis.shape[1]
    total = rows_here * width

    rows, mean = project_and_sort(width, embeddings, basis, list_owner, list_slot)
    order = [[device_at(width, place) for place in range(width)]]
    got = lax.all_to_all(
        rows.reshape(width, SPAN, feats), "wide", split_axis=0, concat_axis=0, tiled=True, axis_index_groups=order
    )

    keep, send = moments(width, me, embeddings, mean)
    stages = halving_stages(width)
    came = exchange(width, stages[0], [send])
    shares = add_and_split(keep, came, SHARES, 1 << len(stages[1]))
    last = []
    for share in shares:
        for n in range(1, len(stages) - 1):
            came = exchange(width, stages[n], share[1:])
            (share,) = add_and_split(share[0], came, 1, 1 << len(stages[n + 1]))
        last.append(share)
    came = [exchange(width, stages[-1], share[1:]) for share in last]
    encoded, between = encode(
        width, total, me, got.reshape(width * SPAN, feats), basis, centroids, rotation, [share[1] for share in last]
    )
    covariance = finish(total, between, [share[0] for share in last], came)
    return (encoded, covariance)


def solution(mesh):
    in_specs = (
        P(("groups", "wide"), None),
        P(),
        P(("groups", "wide")),
        P(("groups", "wide")),
        P("wide", None),
        P(),
    )
    out_specs = (P(("groups", "wide"), None), P(("groups", "wide"), None))
    return jax.shard_map(local, mesh=mesh, in_specs=in_specs, out_specs=out_specs, check_vma=False)
```

```python
import functools

import jax
import jax.numpy as jnp
from jax import lax
from jax.experimental import pallas as pl
from jax.experimental.pallas import tpu as pltpu
from jax.sharding import PartitionSpec as P

CAP = 128
LANES = 128
NOTES = 16
SPAN = CAP + NOTES
CHUNK = 512
STEP = 1024
TILE = 256
GROUP = 4
SHARES = 2
PLANE = 4
VMEM_ALL = 60 * 1024 * 1024
VMEM_SOME = 24 * 1024 * 1024
VMEM_MOST = 48 * 1024 * 1024


def place_of(width, device):
    return (device & (PLANE - 1)) * (width // PLANE) + device // PLANE


def device_at(width, place):
    return (place & (width // PLANE - 1)) * PLANE + place // (width // PLANE)


def in_three(x):
    high = x.astype(jnp.bfloat16).astype(jnp.float32)
    rest = x - high
    middle = rest.astype(jnp.bfloat16).astype(jnp.float32)
    return high, middle, (rest - middle).astype(jnp.bfloat16).astype(jnp.float32)


def rows_kernel(
    width, e_hbm, basis_hbm, owner_hbm, slot_hbm,
    rows_hbm, mean_hbm,
    owner_ref, slot_ref, mean_ref, basis_ref, e_ref, rows_ref, y_ref, yb_ref, sum_ref, total_ref, target_ref, list_ref, e_sem, small_sem, sem,
):
    step = pl.program_id(0)
    rows_here, feats = y_ref.shape
    wide = e_ref.shape[1]
    chunks = rows_here // LANES

    def e_copy(c):
        at = pl.ds(pl.multiple_of(c * CHUNK, CHUNK), CHUNK)
        return pltpu.make_async_copy(e_hbm.at[at], e_ref.at[at], e_sem.at[c])

    @pl.when(step == 0)
    def _():
        owner_copy = pltpu.make_async_copy(owner_hbm, owner_ref, small_sem.at[0])
        slot_copy = pltpu.make_async_copy(slot_hbm, slot_ref, small_sem.at[1])
        basis_copy = pltpu.make_async_copy(basis_hbm, basis_ref, small_sem.at[2])
        owner_copy.start()
        e_copy(0).start()
        slot_copy.start()
        basis_copy.start()
        for c in range(1, rows_here // CHUNK):
            e_copy(c).start()
        owner_copy.wait()
        sum_ref[...] = jnp.zeros_like(sum_ref)
        total_ref[...] = jnp.zeros_like(total_ref)
        owner = place_of(width, owner_ref[...])
        wanted = lax.broadcasted_iota(jnp.int32, (width, LANES), 0)
        hits = [jnp.where(owner[c:c + 1, :] == wanted, 1.0, 0.0) for c in range(chunks)]
        flat = jnp.concatenate(hits, 0).astype(jnp.bfloat16)
        up = lax.broadcasted_iota(jnp.int32, (LANES, LANES), 0)
        to = lax.broadcasted_iota(jnp.int32, (LANES, LANES), 1)
        before = jnp.where(up < to, 1.0, 0.0).astype(jnp.bfloat16)
        every = jnp.ones((LANES, LANES), jnp.bfloat16)
        within = jnp.dot(flat, before, preferred_element_type=jnp.float32)
        counts = jnp.dot(flat, every, preferred_element_type=jnp.float32)
        carry = jnp.zeros((width, LANES), jnp.float32)
        ranks = []
        for c in range(chunks):
            at = slice(c * width, (c + 1) * width)
            ranks.append(jnp.sum(hits[c] * (within[at] + carry), 0, keepdims=True).astype(jnp.int32))
            carry = carry + counts[at]
            target_ref[c:c + 1, :] = owner[c:c + 1, :] * CAP + ranks[c]

        slot_copy.wait()
        slot = slot_ref[...] + 1
        high, low = (slot >> 5).astype(jnp.float32), (slot & 31).astype(jnp.float32)
        spots = lax.broadcasted_iota(jnp.int32, (CAP, LANES), 0)
        placed = jnp.concatenate([jnp.where(ranks[c] == spots, 1.0, 0.0) for c in range(chunks)], 1).astype(jnp.bfloat16)
        digits = jnp.concatenate(
            [
                jnp.concatenate([hits[c] * high[c:c + 1, :] for c in range(chunks)], 1),
                jnp.concatenate([hits[c] * low[c:c + 1, :] for c in range(chunks)], 1),
            ],
            0,
        ).astype(jnp.bfloat16)
        found = lax.dot_general(digits, placed, (((1,), (1,)), ((), ())), preferred_element_type=jnp.float32)
        list_ref[:, :CAP] = found[:width]
        list_ref[:, CAP:] = found[width:]
        basis_copy.wait()

    for c in range(STEP // CHUNK):
        e_copy(step * (STEP // CHUNK) + c).wait()
    here = pl.ds(pl.multiple_of(step * STEP, STEP), STEP)
    rows = e_ref[here, :]
    y = jnp.dot(rows, basis_ref[...], preferred_element_type=jnp.float32)
    y_ref[here, :] = y
    sum_ref[...] += jnp.sum(y.reshape(STEP // 8, 8, feats), 0)
    total_ref[...] += jnp.sum(rows.astype(jnp.float32).reshape(STEP // 8, 8, wide), 0)

    @pl.when(step == pl.num_programs(0) - 1)
    def _():
        mean_y = jnp.sum(sum_ref[...], 0, keepdims=True) / rows_here
        square = jnp.zeros((8, feats), jnp.float32)
        for c in range(rows_here // STEP):
            at = slice(c * STEP, (c + 1) * STEP)
            centred = y_ref[at, :] - mean_y
            square = square + jnp.sum((centred * centred).reshape(STEP // 8, 8, feats), 0)
            yb_ref[at, :] = centred.astype(jnp.bfloat16)
        mean = jnp.sum(total_ref[...], 0, keepdims=True) / rows_here
        mean_ref[...] = mean
        mean_copy = pltpu.make_async_copy(mean_ref, mean_hbm, small_sem.at[3])
        mean_copy.start()
        parts = in_three(mean)
        common = [part[:, q * feats:(q + 1) * feats] for part in parts for q in range(wide // feats)]
        common = jnp.concatenate(common + list(in_three(jnp.sum(square, 0, keepdims=True))), 0)

        place = lax.broadcasted_iota(jnp.int32, (GROUP * CAP, LANES), 0).astype(jnp.int16)

        def sort_group(g):
            first = g * GROUP
            pieces = []
            for c in range(chunks):
                wanted = (target_ref[c:c + 1, :] - first * CAP).astype(jnp.int32)
                wanted = jnp.broadcast_to(wanted, (16, LANES)).astype(jnp.int16)
                wanted = jnp.concatenate([wanted] * (GROUP * CAP // 16), 0)
                pieces.append(jnp.where(wanted == place, jnp.ones((), jnp.bfloat16), jnp.zeros((), jnp.bfloat16)))
            pick = jnp.concatenate(pieces, 1)
            rows = jnp.dot(pick, yb_ref[...], preferred_element_type=jnp.float32).astype(jnp.bfloat16)
            for j in range(GROUP):
                base = pl.multiple_of((first + j) * SPAN, 16)
                rows_ref[pl.ds(base, CAP), :] = rows[j * CAP:(j + 1) * CAP]
                notes = jnp.concatenate([common, list_ref[pl.ds(first + j, 1), :]], 0)
                rows_ref[pl.ds(pl.multiple_of(base + CAP, 16), NOTES), :] = notes.astype(jnp.bfloat16)
            at = pl.ds(pl.multiple_of(g * (GROUP * SPAN), 16), GROUP * SPAN)
            return pltpu.make_async_copy(rows_ref.at[at], rows_hbm.at[at], sem.at[g])

        groups = width // GROUP
        if groups <= 4:
            copies = []
            for g in range(groups):
                copies.append(sort_group(g))
                copies[g].start()
            for copy in copies:
                copy.wait()
        else:

            @pl.loop(0, groups)
            def _(g):
                copy = sort_group(g)
                copy.start()
                copy.wait()

        mean_copy.wait()


def project_and_sort(width, embeddings, basis, list_owner, list_slot):
    rows_here, wide = embeddings.shape
    feats = basis.shape[1]
    lanes = rows_here // LANES
    slots = width * SPAN
    return pl.pallas_call(
        functools.partial(rows_kernel, width),
        grid=(rows_here // STEP,),
        in_specs=[pl.BlockSpec(memory_space=pl.ANY)] * 4,
        out_specs=[pl.BlockSpec(memory_space=pl.ANY)] * 2,
        out_shape=[
            jax.ShapeDtypeStruct((slots, feats), jnp.bfloat16),
            jax.ShapeDtypeStruct((1, wide), jnp.float32),
        ],
        scratch_shapes=[
            pltpu.VMEM((lanes, LANES), jnp.int32),
            pltpu.VMEM((lanes, LANES), jnp.int32),
            pltpu.VMEM((1, wide), jnp.float32),
            pltpu.VMEM((wide, feats), jnp.bfloat16),
            pltpu.VMEM((rows_here, wide), jnp.bfloat16),
            pltpu.VMEM((slots, feats), jnp.bfloat16),
            pltpu.VMEM((rows_here, feats), jnp.float32),
            pltpu.VMEM((rows_here, feats), jnp.bfloat16),
            pltpu.VMEM((8, feats), jnp.float32),
            pltpu.VMEM((8, wide), jnp.float32),
            pltpu.VMEM((lanes, LANES), jnp.int32),
            pltpu.VMEM((width, 2 * CAP), jnp.float32),
            pltpu.SemaphoreType.DMA((rows_here // CHUNK,)),
            pltpu.SemaphoreType.DMA((4,)),
            pltpu.SemaphoreType.DMA((width // GROUP,)),
        ],
        compiler_params=pltpu.CompilerParams(vmem_limit_bytes=VMEM_ALL),
        cost_estimate=pl.CostEstimate(
            flops=2 * rows_here * feats * (wide + slots), bytes_accessed=2 * rows_here * wide + 2 * slots * feats, transcendentals=0
        ),
        name="project_sort",
    )(embeddings, basis, list_owner.reshape(lanes, LANES), list_slot.reshape(lanes, LANES))


def moments_kernel(width, me_ref, mean_hbm, e_hbm, keep_ref, send_ref, e_ref, mean_ref, m_ref, sem, mean_sem):
    rows_here, wide = e_ref.shape
    block = wide // width
    bits = width.bit_length() - 1
    tiles = wide // TILE
    mean_copy = pltpu.make_async_copy(mean_hbm, mean_ref, mean_sem)
    mean_copy.start()
    copies = []
    for c in range(rows_here // CHUNK):
        at = pl.ds(c * CHUNK, CHUNK)
        copies.append(pltpu.make_async_copy(e_hbm.at[at], e_ref.at[at], sem.at[c]))
        copies[c].start()
    me = me_ref[0]
    odd = (me & 1) == 1
    mean_copy.wait()
    mean = mean_ref[...]
    for t in range(tiles):
        rows, columns = slice(t * TILE, (t + 1) * TILE), slice(t * TILE, wide)
        if t == 0:
            product = jnp.zeros((TILE, wide), jnp.float32)
            for c in range(rows_here // CHUNK):
                copies[c].wait()
                at = slice(c * CHUNK, (c + 1) * CHUNK)
                product = product + lax.dot_general(
                    e_ref[at, rows], e_ref[at, :], (((0,), (0,)), ((), ())), preferred_element_type=jnp.float32
                )
        else:
            product = lax.dot_general(
                e_ref[:, rows], e_ref[:, columns], (((0,), (0,)), ((), ())), preferred_element_type=jnp.float32
            )
        down = jnp.transpose(jnp.broadcast_to(mean[:, rows] * rows_here, (LANES, TILE)))
        for u in range(t, tiles):
            pieces = []
            for j in range(u * TILE // LANES, (u + 1) * TILE // LANES):
                across = slice(j * LANES, (j + 1) * LANES)
                within = slice(j * LANES - t * TILE, (j + 1) * LANES - t * TILE)
                pieces.append((product[:, within] - down * mean[:, across]).astype(jnp.bfloat16))
            piece = jnp.concatenate(pieces, 1)
            other = slice(u * TILE, (u + 1) * TILE)
            m_ref[rows, other] = piece
            if u > t:
                m_ref[other, rows] = jnp.transpose(piece)
        for pair in range(TILE // block // 2):
            first = t * (TILE // block) + 2 * pair
            apart = (first ^ me) >> 1
            place = 0
            for k in range(bits - 1):
                place = place + (((apart >> k) & 1) << (bits - 2 - k))
            to = pl.ds(pl.multiple_of(place * block, block), block)
            even_rows = m_ref[first * block:(first + 1) * block, :]
            odd_rows = m_ref[(first + 1) * block:(first + 2) * block, :]
            keep_ref[to, :] = jnp.where(odd, odd_rows, even_rows)
            send_ref[to, :] = jnp.where(odd, even_rows, odd_rows)


def moments(width, me, embeddings, mean):
    rows_here, wide = embeddings.shape
    vmem = pl.BlockSpec(memory_space=pltpu.VMEM)
    return pl.pallas_call(
        functools.partial(moments_kernel, width),
        in_specs=[pl.BlockSpec(memory_space=pltpu.SMEM)] + [pl.BlockSpec(memory_space=pl.ANY)] * 2,
        out_specs=[vmem] * 2,
        out_shape=[
            jax.ShapeDtypeStruct((wide // 2, wide), jnp.bfloat16),
            jax.ShapeDtypeStruct((wide // 2, wide), jnp.bfloat16),
        ],
        scratch_shapes=[
            pltpu.VMEM((rows_here, wide), jnp.bfloat16),
            pltpu.VMEM((1, wide), jnp.float32),
            pltpu.VMEM((wide, wide), jnp.bfloat16),
            pltpu.SemaphoreType.DMA((rows_here // CHUNK,)),
            pltpu.SemaphoreType.DMA,
        ],
        compiler_params=pltpu.CompilerParams(vmem_limit_bytes=VMEM_MOST),
        cost_estimate=pl.CostEstimate(
            flops=2 * rows_here * wide * wide, bytes_accessed=2 * rows_here * wide + 3 * wide * wide, transcendentals=0
        ),
        name="moments",
    )(me.reshape(1), mean, embeddings)


def add_kernel(shares, pieces, keep_ref, *refs):
    outs = refs[len(refs) - shares * pieces:]
    came = refs[:len(refs) - shares * pieces]
    rows, columns = outs[0].shape
    for h in range(shares):
        across = slice(h * columns, (h + 1) * columns)
        for p in range(pieces):
            at = slice(p * rows, (p + 1) * rows)
            held = keep_ref[at, across].astype(jnp.float32)
            for ref in came:
                held = held + ref[at, across].astype(jnp.float32)
            out = outs[h * pieces + p]
            out[...] = held.astype(out.dtype)


def add_and_split(keep, came, shares, pieces):
    rows, columns = keep.shape
    vmem = pl.BlockSpec(memory_space=pltpu.VMEM)
    shape = (rows // pieces, columns // shares)
    kinds = [jnp.float32] + [jnp.bfloat16] * (pieces - 1)
    outs = pl.pallas_call(
        functools.partial(add_kernel, shares, pieces),
        in_specs=[vmem] * (1 + len(came)),
        out_specs=[vmem] * (shares * pieces),
        out_shape=[jax.ShapeDtypeStruct(shape, kind) for kind in kinds * shares],
        compiler_params=pltpu.CompilerParams(vmem_limit_bytes=VMEM_SOME),
        cost_estimate=pl.CostEstimate(flops=2 * rows * columns, bytes_accessed=10 * rows * columns, transcendentals=0),
        name="add_and_split",
    )(keep, *came)
    return [outs[h * pieces:(h + 1) * pieces] for h in range(shares)]


def finish_kernel(total, between_ref, *refs):
    out_ref = refs[-1]
    each = (len(refs) - 1) // SHARES
    columns = out_ref.shape[1] // SHARES
    for h in range(SHARES):
        across = slice(h * columns, (h + 1) * columns)
        held = refs[h * each][...]
        for ref in refs[h * each + 1:(h + 1) * each]:
            held = held + ref[...].astype(jnp.float32)
        out_ref[:, across] = (held + between_ref[:, across]) / total


def finish(total, between, keeps, came):
    parts = [part for keep, pieces in zip(keeps, came) for part in (keep, *pieces)]
    vmem = pl.BlockSpec(memory_space=pltpu.VMEM)
    return pl.pallas_call(
        functools.partial(finish_kernel, total),
        in_specs=[vmem] * (1 + len(parts)),
        out_specs=vmem,
        out_shape=jax.ShapeDtypeStruct(between.shape, jnp.float32),
        compiler_params=pltpu.CompilerParams(vmem_limit_bytes=VMEM_SOME),
        cost_estimate=pl.CostEstimate(flops=8 * between.size, bytes_accessed=16 * between.size, transcendentals=0),
        name="finish",
    )(between, *parts)


def halving_stages(width):
    strides = [1 << k for k in range(width.bit_length() - 1)]
    return [[s] for s in strides[:-2]] + [strides[-2:]]


def exchange(width, stage, out):
    came = []
    for p in (2, 1, 3) if len(stage) == 2 else (1,):
        apart = sum(s for k, s in enumerate(stage) if (p >> (len(stage) - 1 - k)) & 1)
        came.append(lax.ppermute(out[p - 1], "wide", [(i, i ^ apart) for i in range(width)]))
    return came


def encode_kernel(total, me_ref, got_ref, basis_ref, centroid_ref, rotation_ref, *refs):
    out_hbm, between_ref, out_ref, delta_ref, list_ref, apart_ref, sem = refs[-7:]
    width = delta_ref.shape[0]
    feats = out_ref.shape[1]
    owned = centroid_ref.shape[0]
    wide = basis_ref.shape[0]
    block = wide // width
    share = total // width

    notes = jnp.concatenate([got_ref[s * SPAN + CAP:(s + 1) * SPAN, :] for s in range(width)], 0)
    size = width * NOTES
    to = lax.broadcasted_iota(jnp.int32, (size, size), 0)
    of = lax.broadcasted_iota(jnp.int32, (size, size), 1)
    turn = jnp.where((to % width) * NOTES + to // width == of, 1.0, 0.0).astype(jnp.bfloat16)
    turned = jnp.dot(turn, notes, preferred_element_type=jnp.float32)
    row = [turned[r * width:(r + 1) * width] for r in range(NOTES)]
    digits = row[NOTES - 1]
    list_ref[...] = digits[:, :CAP] * 32.0 + digits[:, CAP:] - 1.0
    quarters = wide // feats
    shifts = jnp.zeros((width, feats), jnp.float32)
    for q in range(quarters):
        parts = [row[p * quarters + q] for p in range(3)]
        mean = parts[0] + (parts[1] + parts[2])
        apart_ref[:, q * feats:(q + 1) * feats] = mean - jnp.mean(mean, 0, keepdims=True)
        terms = jnp.dot(
            jnp.concatenate(parts, 0).astype(jnp.bfloat16),
            basis_ref[q * feats:(q + 1) * feats, :],
            preferred_element_type=jnp.float32,
        )
        shifts = shifts + (terms[:width] + (terms[width:2 * width] + terms[2 * width:]))
    square = row[3 * quarters] + (row[3 * quarters + 1] + row[3 * quarters + 2])
    delta = shifts - jnp.mean(shifts, 0, keepdims=True)
    variance = jnp.sum(square + share * (delta * delta), 0, keepdims=True) / total
    scale = lax.rsqrt(variance + 1e-05)
    delta_ref[...] = delta

    names = lax.broadcasted_iota(jnp.int32, (CAP, owned), 1).astype(jnp.int16)

    def encode_group(g):
        columns = jnp.transpose(list_ref[pl.ds(g * GROUP, GROUP), :])
        hits, projected, held = [], [], []
        for s in range(GROUP):
            listed = jnp.broadcast_to(columns[:, s:s + 1], (CAP, LANES))
            held.append(jnp.concatenate([listed] * (feats // LANES), 1) >= 0)
            wanted = jnp.concatenate([listed.astype(jnp.int32).astype(jnp.int16)] * (owned // LANES), 1)
            hits.append(jnp.where(wanted == names, jnp.ones((), jnp.bfloat16), jnp.zeros((), jnp.bfloat16)))
            base = pl.multiple_of((g * GROUP + s) * SPAN, 16)
            rows = got_ref[pl.ds(base, CAP), :].astype(jnp.float32)
            projected.append((rows + delta_ref[pl.ds(g * GROUP + s, 1), :]) * scale)
        centre = jnp.dot(jnp.concatenate(hits, 0), centroid_ref[...], preferred_element_type=jnp.float32)
        residual = jnp.where(jnp.concatenate(held, 0), jnp.concatenate(projected, 0) - centre, 0.0)
        at = pl.ds(pl.multiple_of(g * (GROUP * CAP), GROUP * CAP), GROUP * CAP)
        out_ref[at, :] = jnp.dot(
            residual.astype(jnp.bfloat16), rotation_ref[...], preferred_element_type=jnp.float32
        ).astype(jnp.bfloat16)
        copies = []
        for s in range(GROUP):
            place = g * GROUP + s
            here = pl.ds(pl.multiple_of(place * CAP, CAP), CAP)
            there = pl.ds(pl.multiple_of(device_at(width, place) * CAP, CAP), CAP)
            copies.append(pltpu.make_async_copy(out_ref.at[here], out_hbm.at[there], sem.at[place]))
        return copies

    groups = width // GROUP
    copies = []
    if groups <= 4:
        for g in range(groups):
            for copy in encode_group(g):
                copy.start()
                copies.append(copy)
    else:

        @pl.loop(0, groups)
        def _(g):
            for copy in encode_group(g):
                copy.start()
            for s in range(GROUP):
                at = pl.ds(pl.multiple_of((g * GROUP + s) * CAP, CAP), CAP)
                pltpu.make_async_copy(out_ref.at[at], out_hbm.at[at], sem.at[g * GROUP + s]).wait()

    first = me_ref[0] * block
    near = apart_ref[:, pl.ds(pl.multiple_of(first // LANES * LANES, LANES), LANES)]
    near = pltpu.roll(near, (LANES - first % LANES) % LANES, 1)[:, :block]
    between_ref[...] = share * lax.dot_general(
        near,
        apart_ref[...],
        (((0,), (0,)), ((), ())),
        precision=lax.Precision.HIGHEST,
        preferred_element_type=jnp.float32,
    )
    for copy in copies:
        copy.wait()


def encode(width, total, me, got, basis, centroids, rotation, after):
    wide, feats = basis.shape
    owned = centroids.shape[0]
    slots = width * CAP
    vmem, anywhere = pl.BlockSpec(memory_space=pltpu.VMEM), pl.BlockSpec(memory_space=pl.ANY)
    return pl.pallas_call(
        functools.partial(encode_kernel, total),
        in_specs=[pl.BlockSpec(memory_space=pltpu.SMEM)] + [vmem] * 4 + [anywhere] * len(after),
        out_specs=[anywhere, vmem],
        out_shape=[
            jax.ShapeDtypeStruct((slots, feats), jnp.bfloat16),
            jax.ShapeDtypeStruct((wide // width, wide), jnp.float32),
        ],
        scratch_shapes=[
            pltpu.VMEM((slots, feats), jnp.bfloat16),
            pltpu.VMEM((width, feats), jnp.float32),
            pltpu.VMEM((width, CAP), jnp.float32),
            pltpu.VMEM((width, wide), jnp.float32),
            pltpu.SemaphoreType.DMA((width,)),
        ],
        compiler_params=pltpu.CompilerParams(vmem_limit_bytes=VMEM_SOME),
        cost_estimate=pl.CostEstimate(
            flops=2 * slots * feats * (owned + feats), bytes_accessed=4 * slots * feats, transcendentals=0
        ),
        name="encode",
    )(me.reshape(1), got, basis, centroids, rotation, *after)


def local(embeddings, basis, list_owner, list_slot, centroids, rotation):
    width = lax.axis_size("wide")
    me = lax.axis_index("wide")
    rows_here, wide = embeddings.shape
    feats = basis.shape[1]
    total = rows_here * width

    rows, mean = project_and_sort(width, embeddings, basis, list_owner, list_slot)
    order = [[device_at(width, place) for place in range(width)]]
    got = lax.all_to_all(
        rows.reshape(width, SPAN, feats), "wide", split_axis=0, concat_axis=0, tiled=True, axis_index_groups=order
    )

    keep, send = moments(width, me, embeddings, mean)
    stages = halving_stages(width)
    came = exchange(width, stages[0], [send])
    shares = add_and_split(keep, came, SHARES, 1 << len(stages[1]))
    last = []
    for share in shares:
        for n in range(1, len(stages) - 1):
            came = exchange(width, stages[n], share[1:])
            (share,) = add_and_split(share[0], came, 1, 1 << len(stages[n + 1]))
        last.append(share)
    came = [exchange(width, stages[-1], share[1:]) for share in last]
    encoded, between = encode(
        width, total, me, got.reshape(width * SPAN, feats), basis, centroids, rotation, [share[1] for share in last]
    )
    covariance = finish(total, between, [share[0] for share in last], came)
    return (encoded, covariance)


def solution(mesh):
    in_specs = (
        P(("groups", "wide"), None),
        P(),
        P(("groups", "wide")),
        P(("groups", "wide")),
        P("wide", None),
        P(),
    )
    out_specs = (P(("groups", "wide"), None), P(("groups", "wide"), None))
    return jax.shard_map(local, mesh=mesh, in_specs=in_specs, out_specs=out_specs, check_vma=False)
```
